32 devices in a mesh: box: 2 (over x), theta: 4 (over y, core), phi: 4 (over z).
Axes of the slice: x: 2, y: 2, z: 4, core: 2. Of those that a mesh axis runs over, the one named last changes fastest.
Arguments:
- coeffs: bfloat16 [256, 2, 128, 256], P(('box', 'theta', 'phi')), may hold values from -6 to 6
- near_blocks: bfloat16 [256, 12, 2, 128, 128], P(('box', 'theta', 'phi')), may hold values from -0.109375 to 0.109375
- near_ids: int32 [256, 12], P(('box', 'theta', 'phi')), may hold values from 0 to 255, as said below
- near_count: int32 [256], P(('box', 'theta', 'phi')), may hold values from 3 to 12, as said below
- radiation: bfloat16 [256, 2, 128, 128], P(('box', 'theta', 'phi')), may hold values from -0.5 to 0.5
- partners: int32 [32, 16], P('box'), may hold values from 0 to 31, as said below
- vector_ids: int32 [32, 16], P('box'), may hold values from 0 to 315
- pair_count: int32 [32], P('box'), may hold values from 4 to 16, as said below
- translation: bfloat16 [316, 2, 16, 32], P(None, None, 'theta', 'phi'), may hold values from -0.5 to 0.5
Outputs:
- product: float32 [256, 2, 128, 256], P(('box', 'theta', 'phi'))
The draws below stay inside these ranges and needn't reach their ends.
Inputs may be any that keep to these rules, and one draw needn't show every extreme that they name: `near_ids`: row b lists b itself first, then 12 - 1 further entries; the used ones (before near_count[b]) are distinct other leaf boxes whose index differs from b by at most 8, and some used entry differs by exactly 8. Entries at or after near_count[b] are not used and may repeat b. `near_count`: some leaf box uses all 12 slots. `partners`: row d holds 16 distinct upper boxes other than d whose index differs from d by at most 16; a difference of exactly 16 occurs among used entries. Entries at or after pair_count[d] are not used. `pair_count`: some upper box uses all 16 slots.
All inputs are finite; a program needn't handle non-finite values.
Results may differ from the reference program's by a relative error of at most 0.0055.
Values may be sent and summed in bfloat16 or wider, within the bound.
No kernel may reach another device: no remote copies, remote signals or barrier semaphores. Data moves between devices by JAX's collectives and lax.ppermute only.
A program may use at most 128 MiB of HBM per device.

```python
import math
import jax
import jax.numpy as jnp
from jax import lax

P_SIZE = 128
NB = 12
LB_DEV = 8
TL = 8
PL = 16
R = 256
M = 16
NV = 316
KL = 128
TU = 16
PU = 32
NL = 256
NU = 32
PAR_GROUP = 16


def near_lists(key):
    first, second = jax.random.split(jax.random.fold_in(key, 11))
    boxes = jnp.arange(NL)[:, None]
    places = jnp.arange(2 * LB_DEV)[None, :]
    offset = jnp.where(places < LB_DEV, places - LB_DEV, places - LB_DEV + 1)
    chosen = boxes + offset
    usable = (chosen >= 0) & (chosen < NL)
    scores = jax.random.randint(first, (NL, 2 * LB_DEV), 0, 65536) * 64 + places
    scores = jnp.where(usable, scores, -1 - places)
    scores = scores.at[0, 2 * LB_DEV - 1].set(2 ** 30)
    scores = scores.at[NL - 1, 0].set(2 ** 30)
    ranked, picked = lax.top_k(scores, NB - 1)
    others = jnp.take_along_axis(chosen, picked, axis=1)
    usable_count = jnp.sum(usable.astype(jnp.int32), axis=1)
    others = jnp.where(jnp.arange(NB - 1)[None, :] < usable_count[:, None], others, boxes)
    listed = jnp.concatenate([boxes, others], axis=1).astype(jnp.int32)
    counts = jax.random.randint(second, (NL,), 3, NB + 1)
    counts = jnp.minimum(counts, 1 + usable_count)
    counts = counts.at[NL // 2].set(NB).astype(jnp.int32)
    return (listed, counts)


def pair_lists(key):
    first, second = jax.random.split(jax.random.fold_in(key, 23))
    parents = jnp.arange(NU)[:, None]
    places = jnp.arange(2 * PAR_GROUP)[None, :]
    offset = jnp.where(places < PAR_GROUP, places - PAR_GROUP, places - PAR_GROUP + 1)
    chosen = parents + offset
    usable = (chosen >= 0) & (chosen < NU)
    scores = jax.random.randint(first, (NU, 2 * PAR_GROUP), 0, 65536) * 64 + places
    scores = jnp.where(usable, scores, -1 - places)
    scores = scores.at[0, 2 * PAR_GROUP - 1].set(2 ** 30)
    scores = scores.at[NU - 1, 0].set(2 ** 30)
    ranked, picked = lax.top_k(scores, M)
    listed = jnp.take_along_axis(chosen, picked, axis=1).astype(jnp.int32)
    counts = jax.random.randint(second, (NU,), M // 4, M + 1)
    counts = counts.at[NU // 2].set(M).astype(jnp.int32)
    return (listed, counts)


def draw_near_ids(key, part):
    return near_lists(key)[0]


def draw_near_count(key, part):
    return near_lists(key)[1]


def draw_partners(key, part):
    return pair_lists(key)[0]


def draw_pair_count(key, part):
    return pair_lists(key)[1]


def set_ends(result, rng, smallest, largest):
    spot = [jax.random.randint(jax.random.fold_in(rng, axis), (), 0, length) for axis, length in enumerate(result.shape)]
    main_axis = result.shape.index(max(result.shape))
    next_to = spot[:main_axis] + [(spot[main_axis] + 1) % result.shape[main_axis]] + spot[main_axis + 1:]
    return result.at[tuple(spot)].set(smallest).at[tuple(next_to)].set(largest)


def block_levels(stream_key, shape, pieces, smallest, largest):
    factor_of, own = 1.0, jax.random.fold_in(stream_key, 6)
    for position, parts in pieces:
        steps = jnp.exp(jax.random.uniform(jax.random.fold_in(own, position), (parts,), jnp.float32, smallest / len(pieces), largest / len(pieces)))
        factor_of = factor_of * jnp.repeat(steps, shape[position] // parts).reshape([-1 if axis == position else 1 for axis in range(len(shape))])
    return factor_of


def gaussian(stream_key, dims, scale, reach, shards=(), dtype=jnp.bfloat16):
    level = block_levels(stream_key, dims, shards, -0.22, 0.18) if shards else 1.0
    result = jax.random.normal(stream_key, dims, jnp.float32) * scale * level
    return jnp.minimum(jnp.maximum(result, -reach), reach).astype(dtype)


def setup_inputs(seed: int = 0) -> dict:
    keys = jax.random.split(jax.random.key(seed), 10)
    return {
        "coeffs": gaussian(keys[0], (NL, 2, P_SIZE, R), 1.0, 6.0, ((0, 32),)),
        "near_blocks": gaussian(keys[1], (NL, NB, 2, P_SIZE, P_SIZE), (2 * NB * P_SIZE) ** -0.5, 0.109375, ((0, 32),)),
        "near_ids": draw_near_ids(jax.random.fold_in(keys[9], 71), 0),
        "near_count": draw_near_count(jax.random.fold_in(keys[9], 71), 0),
        "radiation": gaussian(keys[4], (NL, 2, KL, P_SIZE), P_SIZE ** -0.5, 0.5, ((0, 32),)),
        "partners": draw_partners(jax.random.fold_in(keys[9], 71), 0),
        "vector_ids": set_ends(jax.random.randint(keys[6], (NU, M), 0, NV), jax.random.fold_in(keys[6], 1), 0, NV - 1).astype(jnp.int32),
        "pair_count": draw_pair_count(jax.random.fold_in(keys[9], 71), 0),
        "translation": gaussian(keys[8], (NV, 2, TU, PU), ((8 * M) ** -0.5), 0.5, ((2, 4), (3, 4))),
    }


WEIGHT_UP = (-0.0546875, 0.8203125, 0.2734375, -0.0390625)
WEIGHT_DOWN = (-0.0390625, 0.2734375, 0.8203125, -0.0546875)
PHASE_SCALE = 1.3


def lagrange_matrix(upper, columns, rows_in, mode, shift):
    halves = upper // 2
    parity = upper % 2
    column_ids = jnp.arange(columns)
    matrix = jnp.zeros((upper.shape[0], columns), jnp.float32)
    for order in range(4):
        node = halves + parity - 2 + order
        if mode == "wrap":
            node = node % rows_in
        elif mode == "clamp":
            node = jnp.clip(node, 0, rows_in - 1)
        node = node - shift
        weight = jnp.where(parity == 1, WEIGHT_UP[order], WEIGHT_DOWN[order]).astype(jnp.float32)
        matrix = matrix + weight[:, None] * (column_ids[None, :] == node[:, None]).astype(jnp.float32)
    return matrix


def phases(theta_ids, phi_ids, theta_total, phi_total):
    theta = math.pi * (theta_ids.astype(jnp.float32) + 0.5) / theta_total
    azimuth = 2.0 * math.pi * (phi_ids.astype(jnp.float32) + 0.5) / phi_total
    octant = jnp.arange(8)
    sign_x = (2 * (octant % 2) - 1).astype(jnp.float32)[:, None, None]
    sign_y = (2 * ((octant // 2) % 2) - 1).astype(jnp.float32)[:, None, None]
    sign_z = (2 * (octant // 4) - 1).astype(jnp.float32)[:, None, None]
    along_x = (jnp.sin(theta)[:, None] * jnp.cos(azimuth)[None, :])[None]
    along_y = (jnp.sin(theta)[:, None] * jnp.sin(azimuth)[None, :])[None]
    along_z = (jnp.cos(theta)[:, None] * jnp.ones_like(azimuth)[None, :])[None]
    angle = PHASE_SCALE * (sign_x * along_x + sign_y * along_y + sign_z * along_z)
    return jnp.cos(angle), jnp.sin(angle)


def reference(coeffs, near_blocks, near_ids, near_count, radiation, partners, vector_ids, pair_count, translation):
    highest = lax.Precision.HIGHEST
    slot_ids = jnp.arange(NB)

    def near_one(packed):
        blocks, listed, used = packed
        picked = coeffs[listed].astype(jnp.float32)
        in_use = (slot_ids < used).astype(jnp.float32)[:, None, None, None]
        picked = picked * in_use
        blocks = blocks.astype(jnp.float32)
        out_real = jnp.einsum("jpq,jqr->pr", blocks[:, 0], picked[:, 0], precision=highest) - jnp.einsum("jpq,jqr->pr", blocks[:, 1], picked[:, 1], precision=highest)
        out_imag = jnp.einsum("jpq,jqr->pr", blocks[:, 0], picked[:, 1], precision=highest) + jnp.einsum("jpq,jqr->pr", blocks[:, 1], picked[:, 0], precision=highest)
        return jnp.stack([out_real, out_imag])

    near = lax.map(near_one, (near_blocks, near_ids, near_count))

    theta_matrix = lagrange_matrix(jnp.arange(TU), TL, TL, "clamp", 0)
    phi_matrix = lagrange_matrix(jnp.arange(PU), PL, PL, "wrap", 0)
    cosine, sine = phases(jnp.arange(TU), jnp.arange(PU), TU, PU)
    cosine = cosine[:, :, :, None]
    sine = sine[:, :, :, None]
    radiation_groups = radiation.reshape(NU, LB_DEV, 2, KL, P_SIZE)
    coeff_groups = coeffs.reshape(NU, LB_DEV, 2, P_SIZE, R)

    def upward(packed):
        radiating, current = packed
        radiating = radiating.astype(jnp.float32)
        current = current.astype(jnp.float32)
        pattern_real = jnp.einsum("bkp,bpr->bkr", radiating[:, 0], current[:, 0], precision=highest) - jnp.einsum("bkp,bpr->bkr", radiating[:, 1], current[:, 1], precision=highest)
        pattern_imag = jnp.einsum("bkp,bpr->bkr", radiating[:, 0], current[:, 1], precision=highest) + jnp.einsum("bkp,bpr->bkr", radiating[:, 1], current[:, 0], precision=highest)
        leaf_pattern = lax.optimization_barrier(jnp.stack([pattern_real, pattern_imag], axis=1).astype(jnp.bfloat16)).astype(jnp.float32)
        leaf_pattern = leaf_pattern.reshape(LB_DEV, 2, TL, PL, R)
        partial_up = jnp.einsum("ut,bctlr->bculr", theta_matrix, leaf_pattern, precision=highest)
        refined = jnp.einsum("vl,bculr->bcuvr", phi_matrix, partial_up, precision=highest)
        shifted_real = cosine * refined[:, 0] - sine * refined[:, 1]
        shifted_imag = sine * refined[:, 0] + cosine * refined[:, 1]
        return jnp.stack([jnp.sum(shifted_real, axis=0), jnp.sum(shifted_imag, axis=0)]).astype(jnp.bfloat16)

    parent_pattern = lax.map(upward, (radiation_groups, coeff_groups))
    list_slots = jnp.arange(M)

    def translate(packed):
        listed, operators, used = packed
        in_use = (list_slots < used).astype(jnp.float32)[:, None, None, None]
        table = translation[operators].astype(jnp.float32) * in_use
        sources = parent_pattern[listed].astype(jnp.float32)
        field_real = jnp.sum(table[:, 0, :, :, None] * sources[:, 0] - table[:, 1, :, :, None] * sources[:, 1], axis=0)
        field_imag = jnp.sum(table[:, 0, :, :, None] * sources[:, 1] + table[:, 1, :, :, None] * sources[:, 0], axis=0)
        return jnp.stack([field_real, field_imag]).astype(jnp.bfloat16)

    incoming = lax.map(translate, (partners, vector_ids, pair_count))

    def downward(packed):
        arriving, radiating = packed
        arriving = arriving.astype(jnp.float32)
        down_real = cosine * arriving[0][None] + sine * arriving[1][None]
        down_imag = cosine * arriving[1][None] - sine * arriving[0][None]
        spread_down = jnp.stack([down_real, down_imag], axis=1)
        coarse_phi = jnp.einsum("vl,bcuvr->bculr", phi_matrix, spread_down, precision=highest)
        leaf_field = jnp.einsum("ut,bculr->bctlr", theta_matrix, coarse_phi, precision=highest)
        leaf_field = lax.optimization_barrier(leaf_field.astype(jnp.bfloat16)).astype(jnp.float32)
        leaf_field = leaf_field.reshape(LB_DEV, 2, KL, R)
        radiating = radiating.astype(jnp.float32)
        far_real = jnp.einsum("bkp,bkr->bpr", radiating[:, 0], leaf_field[:, 0], precision=highest) + jnp.einsum("bkp,bkr->bpr", radiating[:, 1], leaf_field[:, 1], precision=highest)
        far_imag = jnp.einsum("bkp,bkr->bpr", radiating[:, 0], leaf_field[:, 1], precision=highest) - jnp.einsum("bkp,bkr->bpr", radiating[:, 1], leaf_field[:, 0], precision=highest)
        return jnp.stack([far_real, far_imag], axis=1)

    far = lax.map(downward, (incoming, radiation_groups)).reshape(NL, 2, P_SIZE, R)
    return near + far
```

```python
import functools
import math

import jax
import jax.numpy as jnp
import ml_dtypes
import numpy as np
from jax import lax
from jax.experimental import pallas as pl
from jax.experimental.pallas import tpu as pltpu
from jax.sharding import PartitionSpec as P

TL = 8
PL = 16
TU = 16
PU = 32

WEIGHT_UP = (-0.0546875, 0.8203125, 0.2734375, -0.0390625)
WEIGHT_DOWN = (-0.0390625, 0.2734375, 0.8203125, -0.0546875)
PHASE_SCALE = 1.3

F32 = jnp.float32
BF16 = jnp.bfloat16
VMEM_LIMIT = 48 * 1024 * 1024


def lagrange(rows, columns, wrap):
    matrix = np.zeros((rows, columns))
    for row in range(rows):
        weights = WEIGHT_UP if row % 2 else WEIGHT_DOWN
        for order in range(4):
            node = row // 2 + row % 2 - 2 + order
            node = node % columns if wrap else min(max(node, 0), columns - 1)
            matrix[row, node] += weights[order]
    return matrix


def split_weights(matrix):
    high = matrix.astype(ml_dtypes.bfloat16)
    low = (matrix - high.astype(np.float64)).astype(ml_dtypes.bfloat16)
    return high, low


def operators(theta_size, phi_size):
    order = np.arange(TU * PU).reshape(theta_size, TU // theta_size, phi_size, PU // phi_size)
    order = order.transpose(0, 2, 1, 3).reshape(-1)
    interp = np.kron(lagrange(TU, TL, False), lagrange(PU, PL, True))
    theta = math.pi * (np.arange(TU) + 0.5) / TU
    azimuth = 2.0 * math.pi * (np.arange(PU) + 0.5) / PU
    up, down = [], []
    for octant in range(4):
        sign_x = 2 * (octant % 2) - 1
        sign_y = 2 * (octant // 2 % 2) - 1
        sign_z = 2 * (octant // 4) - 1
        angle = PHASE_SCALE * (
            sign_x * np.sin(theta)[:, None] * np.cos(azimuth)[None]
            + sign_y * np.sin(theta)[:, None] * np.sin(azimuth)[None]
            + sign_z * np.cos(theta)[:, None]
        ).reshape(-1, 1)
        cos_high, cos_low = split_weights((np.cos(angle) * interp)[order])
        sin_high, sin_low = split_weights((np.sin(angle) * interp)[order])
        up.append(np.concatenate([cos_high, sin_high, cos_low, sin_low], axis=1))
        down.append(
            np.concatenate(
                [
                    np.concatenate([cos_high.T, cos_low.T], axis=1),
                    np.concatenate([sin_high.T, sin_low.T], axis=1),
                ],
                axis=0,
            )
        )
    return np.stack(up), np.stack(down)


def dot(a, b):
    return jnp.dot(a, b, preferred_element_type=F32)


def up_kernel(x_ref, rad_ref, w_ref, out_ref, acc):
    octant = pl.program_id(0)
    points, basis = rad_ref.shape[2], rad_ref.shape[3]
    rhs = x_ref.shape[3]
    rad_re, rad_im = rad_ref[0, 0], rad_ref[0, 1]
    left = jnp.concatenate(
        [
            jnp.concatenate([rad_re, -rad_im], axis=1),
            jnp.concatenate([rad_im, rad_re], axis=1),
        ],
        axis=0,
    )
    pattern = dot(left, x_ref[0].reshape(2 * basis, rhs)).astype(BF16)
    real, imag = pattern[:points], pattern[points:]
    minus = -imag
    first = octant < 4
    swapped = jnp.concatenate(
        [jnp.where(first, minus, imag), jnp.where(first, real, -real)], axis=1
    )
    straight = jnp.concatenate([real, imag], axis=1)
    right = jnp.concatenate([straight, swapped, straight, swapped], axis=0)

    @pl.when(octant == 0)
    def _():
        acc[...] = dot(w_ref[0], right)

    @pl.when(octant > 0)
    def _():
        acc[...] += dot(w_ref[0], right)

    @pl.when(octant == pl.num_programs(0) - 1)
    def _():
        out_ref[...] = acc[...].astype(BF16).reshape(out_ref.shape)


def upward(coeffs, radiation, weights, groups):
    boxes, _, basis, rhs = coeffs.shape
    points = radiation.shape[2]
    samples = weights.shape[1]
    return pl.pallas_call(
        up_kernel,
        grid=(boxes,),
        in_specs=[
            pl.BlockSpec((1, 2, basis, rhs), lambda o: (o, 0, 0, 0)),
            pl.BlockSpec((1, 2, points, basis), lambda o: (o, 0, 0, 0)),
            pl.BlockSpec((1, samples, 4 * points), lambda o: (jnp.minimum(o, 7 - o), 0, 0)),
        ],
        out_specs=pl.BlockSpec((groups, samples // groups, 2 * rhs), lambda o: (0, 0, 0)),
        out_shape=jax.ShapeDtypeStruct((groups, samples // groups, 2 * rhs), BF16),
        scratch_shapes=[pltpu.VMEM((samples, 2 * rhs), F32)],
        compiler_params=pltpu.CompilerParams(vmem_limit_bytes=VMEM_LIMIT),
        cost_estimate=pl.CostEstimate(
            flops=3 * 10**9, bytes_accessed=5 * 2**20, transcendentals=0
        ),
        name="upward",
    )(coeffs, radiation, weights)


def translate_kernel(count, coup_ref, *refs):
    sources, out_ref, matrix, field = refs[:count], refs[count], refs[count + 1], refs[count + 2]
    targets, samples, width = out_ref.shape
    rhs = width // 2
    columns = sources[0].shape[0] * samples
    row = lax.broadcasted_iota(jnp.int32, (samples, columns), 0)
    column = lax.broadcasted_iota(jnp.int32, (samples, columns), 1)
    mask = row == column % samples
    total = None
    for group in range(count):
        for target in range(2 * targets):
            line = coup_ref[target : target + 1, group * columns : (group + 1) * columns]
            matrix[target * samples : (target + 1) * samples] = jnp.where(
                mask, jnp.broadcast_to(line, mask.shape), 0.0
            ).astype(BF16)
        part = dot(matrix[...], sources[group][...].reshape(columns, width))
        if group == 0:
            field[...] = part
        else:
            field[...] += part
    half = targets * samples
    real = field[:half, :rhs] - field[half:, rhs:]
    imag = field[:half, rhs:] + field[half:, :rhs]
    out_ref[...] = jnp.concatenate([real, imag], axis=1).astype(BF16).reshape(out_ref.shape)


def translate(coupling, sources):
    targets, samples, width = sources[0].shape
    rows = 2 * targets * samples
    return pl.pallas_call(
        functools.partial(translate_kernel, len(sources)),
        out_shape=jax.ShapeDtypeStruct((targets, samples, width), BF16),
        scratch_shapes=[
            pltpu.VMEM((rows, targets * samples), BF16),
            pltpu.VMEM((rows, width), F32),
        ],
        compiler_params=pltpu.CompilerParams(vmem_limit_bytes=VMEM_LIMIT),
        cost_estimate=pl.CostEstimate(
            flops=2 * 10**9, bytes_accessed=2 * 2**20, transcendentals=0
        ),
        name="translate",
    )(coupling, *sources)


def near_kernel(
    ids_ref, count_ref, rank_ref, blocks_ref, low_ref, own_ref, high_ref, out_ref, held, sems
):
    box = pl.program_id(0)
    boxes, _, basis, rhs = own_ref.shape

    @pl.when(box == 0)
    def _():
        copies = [
            pltpu.make_async_copy(ref, held.at[pl.ds(place * boxes, boxes)], sems.at[place])
            for place, ref in enumerate((low_ref, own_ref, high_ref))
        ]
        for copy in copies:
            copy.start()
        for copy in copies:
            copy.wait()

    used = count_ref[box]
    first = (rank_ref[0] - 1) * boxes

    def operand(slot, limit):
        real, imag = blocks_ref[0, slot, 0], blocks_ref[0, slot, 1]
        if limit:
            real = jnp.where(slot < used, real, jnp.zeros_like(real))
            imag = jnp.where(slot < used, imag, jnp.zeros_like(imag))
        return jnp.concatenate(
            [
                jnp.concatenate([real, -imag], axis=1),
                jnp.concatenate([imag, real], axis=1),
            ],
            axis=0,
        )

    def source(slot):
        return held[ids_ref[box, slot] - first].reshape(2 * basis, rhs)

    out_ref[...] = jnp.zeros_like(out_ref)

    def step(pair, carry):
        slot = 2 * pair
        last = jnp.minimum(slot + 1, used - 1)
        left = jnp.concatenate([operand(slot, False), operand(slot + 1, True)], axis=1)
        right = jnp.concatenate([source(slot), source(last)], axis=0)
        out_ref[0] += dot(left, right).reshape(2, basis, rhs)
        return carry

    lax.fori_loop(0, (used + 1) // 2, step, 0)


def near_field(ids, counts, rank, blocks, low, own, high):
    boxes, slots, _, basis, _ = blocks.shape
    rhs = own.shape[3]
    anywhere = pl.BlockSpec(memory_space=pl.ANY)
    return pl.pallas_call(
        near_kernel,
        grid_spec=pltpu.PrefetchScalarGridSpec(
            num_scalar_prefetch=3,
            grid=(boxes,),
            in_specs=[
                pl.BlockSpec((1, slots, 2, basis, basis), lambda b, *_: (b, 0, 0, 0, 0)),
                anywhere,
                anywhere,
                anywhere,
            ],
            out_specs=pl.BlockSpec((1, 2, basis, rhs), lambda b, *_: (b, 0, 0, 0)),
            scratch_shapes=[
                pltpu.VMEM((3 * boxes, 2, basis, rhs), BF16),
                pltpu.SemaphoreType.DMA((3,)),
            ],
        ),
        out_shape=jax.ShapeDtypeStruct((boxes, 2, basis, rhs), F32),
        compiler_params=pltpu.CompilerParams(vmem_limit_bytes=VMEM_LIMIT),
        cost_estimate=pl.CostEstimate(
            flops=4 * 10**9, bytes_accessed=12 * 2**20, transcendentals=0
        ),
        name="near",
    )(ids, counts, rank, blocks, low, own, high)


def down_kernel(field_ref, w_ref, rad_ref, near_ref, out_ref, held, sems):
    step = pl.program_id(0)
    last = pl.num_programs(0) - 1
    boxes, _, points, basis = rad_ref.shape
    rhs = near_ref.shape[3]
    slot = step % 2

    def writes(at, place):
        return [
            pltpu.make_async_copy(held.at[place, 0], out_ref.at[at], sems.at[place, 0]),
            pltpu.make_async_copy(held.at[place, 1], out_ref.at[boxes - 1 - at], sems.at[place, 1]),
        ]

    @pl.when(step >= 2)
    def _():
        for copy in writes(step - 2, slot):
            copy.wait()

    field = field_ref[...].reshape(-1, 2 * rhs)
    mixed = dot(w_ref[0], jnp.concatenate([field, field], axis=0))
    cos_re, cos_im = mixed[:points, :rhs], mixed[:points, rhs:]
    sin_re, sin_im = mixed[points:, :rhs], mixed[points:, rhs:]
    pairs = (
        (step, cos_re + sin_im, cos_im - sin_re),
        (boxes - 1 - step, cos_re - sin_im, cos_im + sin_re),
    )
    for place, (box, real, imag) in enumerate(pairs):
        leaf = jnp.concatenate([real, imag], axis=0).astype(BF16)
        rad_re, rad_im = rad_ref[box, 0], rad_ref[box, 1]
        left = jnp.concatenate(
            [
                jnp.concatenate([rad_re, -rad_im], axis=1),
                jnp.concatenate([rad_im, rad_re], axis=1),
            ],
            axis=0,
        )
        far = lax.dot_general(left, leaf, (((0,), (0,)), ((), ())), preferred_element_type=F32)
        held[slot, place] = near_ref[box] + far.reshape(2, basis, rhs)
    for copy in writes(step, slot):
        copy.start()

    @pl.when(step == last)
    def _():
        for copy in writes(step - 1, 1 - slot) + writes(step, slot):
            copy.wait()


def downward(field, weights, radiation, near):
    boxes, _, basis, rhs = near.shape
    whole = lambda array: pl.BlockSpec(array.shape, lambda s: (0,) * array.ndim)
    return pl.pallas_call(
        down_kernel,
        grid=(boxes // 2,),
        in_specs=[
            whole(field),
            pl.BlockSpec((1, *weights.shape[1:]), lambda s: (s, 0, 0)),
            whole(radiation),
            whole(near),
        ],
        out_specs=pl.BlockSpec(memory_space=pl.ANY),
        out_shape=jax.ShapeDtypeStruct(near.shape, F32),
        scratch_shapes=[
            pltpu.VMEM((2, 2, 2, basis, rhs), F32),
            pltpu.SemaphoreType.DMA((2, 2)),
        ],
        compiler_params=pltpu.CompilerParams(vmem_limit_bytes=VMEM_LIMIT),
        cost_estimate=pl.CostEstimate(
            flops=2 * 10**9, bytes_accessed=7 * 2**20, transcendentals=0
        ),
        name="downward",
    )(field, weights, radiation, near)


def shift(block, axis, step):
    count = lax.axis_size(axis)
    pairs = [(i, i + step) for i in range(count) if 0 <= i + step < count]
    return lax.ppermute(block, axis, pairs)


def band_sources(bands):
    count = lax.axis_size("box")
    rank = lax.axis_index("box")
    if count == 1:
        return [bands], [rank]
    if count == 2:
        return [bands, lax.ppermute(bands, "box", [(0, 1), (1, 0)])], [rank, 1 - rank]
    return [bands, shift(bands, "box", 1), shift(bands, "box", -1)], [rank, rank - 1, rank + 1]


def couplings(partners, vector_ids, pair_count, translation, per_group, group_ranks):
    operator_total = translation.shape[0]
    targets, slots = vector_ids.shape
    samples = translation.shape[2] * translation.shape[3]
    selector = (vector_ids[:, :, None] == jnp.arange(operator_total)).astype(BF16)
    table = translation.reshape(operator_total, 2 * samples)
    chosen = jnp.einsum("dmv,vs->dms", selector, table, preferred_element_type=F32).astype(BF16)
    names = jnp.concatenate([rank * per_group + jnp.arange(per_group) for rank in group_ranks])
    in_list = jnp.arange(slots)[None, :] < pair_count[:, None]
    matches = (partners[:, :, None] == names) & in_list[:, :, None]
    coupling = jnp.einsum(
        "dmj,dms->djs", matches.astype(BF16), chosen, preferred_element_type=F32
    )
    coupling = coupling.reshape(targets, names.shape[0], 2, samples).transpose(2, 0, 1, 3)
    return coupling.reshape(2 * targets, names.shape[0] * samples)


def per_device(
    up_weights,
    down_weights,
    coeffs,
    near_blocks,
    near_ids,
    near_count,
    radiation,
    partners,
    vector_ids,
    pair_count,
    translation,
):
    every = ("box", "theta", "phi")
    bands = ("theta", "phi")
    groups = lax.axis_size("theta") * lax.axis_size("phi")
    low = shift(coeffs, every, 1)
    high = shift(coeffs, every, -1)
    spread = upward(coeffs, radiation, up_weights, groups)
    parents = lax.all_to_all(spread, bands, split_axis=0, concat_axis=0, tiled=True)
    sources, group_ranks = band_sources(parents)
    coupling = couplings(
        partners, vector_ids, pair_count, translation, parents.shape[0], group_ranks
    )
    incoming = translate(coupling, sources)
    field = lax.all_to_all(incoming, bands, split_axis=0, concat_axis=0, tiled=True)
    rank = lax.axis_index(every).astype(jnp.int32).reshape(1)
    near = near_field(near_ids, near_count, rank, near_blocks, low, coeffs, high)
    return downward(field, down_weights, radiation, near)


def solution(mesh):
    up_weights, down_weights = operators(mesh.shape["theta"], mesh.shape["phi"])
    in_specs = (
        P(),
        P(),
        P(("box", "theta", "phi"), None, None, None),
        P(("box", "theta", "phi"), None, None, None, None),
        P(("box", "theta", "phi"), None),
        P(("box", "theta", "phi")),
        P(("box", "theta", "phi"), None, None, None),
        P("box", None),
        P("box", None),
        P("box"),
        P(None, None, "theta", "phi"),
    )
    out_specs = P(("box", "theta", "phi"), None, None, None)
    mapped = jax.shard_map(
        per_device, mesh=mesh, in_specs=in_specs, out_specs=out_specs, check_vma=False
    )

    def product(*arrays):
        return mapped(jnp.asarray(up_weights), jnp.asarray(down_weights), *arrays)

    return product
```

```python
import functools
import math

import jax
import jax.numpy as jnp
import ml_dtypes
import numpy as np
from jax import lax
from jax.experimental import pallas as pl
from jax.experimental.pallas import tpu as pltpu
from jax.sharding import PartitionSpec as P

TL = 8
PL = 16
TU = 16
PU = 32

WEIGHT_UP = (-0.0546875, 0.8203125, 0.2734375, -0.0390625)
WEIGHT_DOWN = (-0.0390625, 0.2734375, 0.8203125, -0.0546875)
PHASE_SCALE = 1.3

F32 = jnp.float32
BF16 = jnp.bfloat16
VMEM_LIMIT = 48 * 1024 * 1024
GROUP = 4
NOWHERE = -(2**20)


def lagrange(rows, columns, wrap):
    matrix = np.zeros((rows, columns))
    for row in range(rows):
        weights = WEIGHT_UP if row % 2 else WEIGHT_DOWN
        for order in range(4):
            node = row // 2 + row % 2 - 2 + order
            node = node % columns if wrap else min(max(node, 0), columns - 1)
            matrix[row, node] += weights[order]
    return matrix


def split_weights(matrix):
    high = matrix.astype(ml_dtypes.bfloat16)
    low = (matrix - high.astype(np.float64)).astype(ml_dtypes.bfloat16)
    return high, low


def operators(shares, theta_size, phi_size):
    theta_part = TU // theta_size // shares
    order = np.arange(TU * PU).reshape(theta_size, shares, theta_part, phi_size, PU // phi_size)
    order = order.transpose(1, 0, 3, 2, 4).reshape(-1)
    interp = np.kron(lagrange(TU, TL, False), lagrange(PU, PL, True))
    theta = math.pi * (np.arange(TU) + 0.5) / TU
    azimuth = 2.0 * math.pi * (np.arange(PU) + 0.5) / PU
    up, down = [], []
    for octant in range(4):
        sign_x = 2 * (octant % 2) - 1
        sign_y = 2 * (octant // 2 % 2) - 1
        sign_z = 2 * (octant // 4) - 1
        angle = PHASE_SCALE * (
            sign_x * np.sin(theta)[:, None] * np.cos(azimuth)[None]
            + sign_y * np.sin(theta)[:, None] * np.sin(azimuth)[None]
            + sign_z * np.cos(theta)[:, None]
        ).reshape(-1, 1)
        cos_high, cos_low = split_weights((np.cos(angle) * interp)[order])
        sin_high, sin_low = split_weights((np.sin(angle) * interp)[order])
        up.append(np.concatenate([cos_high, sin_high, cos_low, sin_low], axis=1))
        down.append(
            np.concatenate(
                [
                    np.concatenate([cos_high.T, cos_low.T], axis=1),
                    np.concatenate([sin_high.T, sin_low.T], axis=1),
                ],
                axis=0,
            )
        )
    return np.stack(up), np.stack(down)


def in_hbm(array):
    return pltpu.with_memory_space_constraint(array, pltpu.HBM)


def dot(a, b):
    return jnp.dot(a, b, preferred_element_type=F32)


def up_kernel(x_ref, rad_ref, w_ref, out_ref, acc):
    octant = pl.program_id(0)
    points, basis = rad_ref.shape[2], rad_ref.shape[3]
    rhs = x_ref.shape[3]
    rad_re, rad_im = rad_ref[0, 0], rad_ref[0, 1]
    left = jnp.concatenate(
        [
            jnp.concatenate([rad_re, -rad_im], axis=1),
            jnp.concatenate([rad_im, rad_re], axis=1),
        ],
        axis=0,
    )
    pattern = dot(left, x_ref[0].reshape(2 * basis, rhs)).astype(BF16)
    real, imag = pattern[:points], pattern[points:]
    minus = -imag
    first = octant < 4
    swapped = jnp.concatenate(
        [jnp.where(first, minus, imag), jnp.where(first, real, -real)], axis=1
    )
    straight = jnp.concatenate([real, imag], axis=1)
    right = jnp.concatenate([straight, swapped, straight, swapped], axis=0)

    @pl.when(octant == 0)
    def _():
        acc[...] = dot(w_ref[0], right)

    @pl.when(octant > 0)
    def _():
        acc[...] += dot(w_ref[0], right)

    @pl.when(octant == pl.num_programs(0) - 1)
    def _():
        out_ref[...] = acc[...].astype(BF16).reshape(out_ref.shape)


def upward(coeffs, radiation, weights, groups):
    boxes, _, basis, rhs = coeffs.shape
    points = radiation.shape[2]
    samples = weights.shape[1]
    return pl.pallas_call(
        up_kernel,
        grid=(boxes,),
        in_specs=[
            pl.BlockSpec((1, 2, basis, rhs), lambda o: (o, 0, 0, 0)),
            pl.BlockSpec((1, 2, points, basis), lambda o: (o, 0, 0, 0)),
            pl.BlockSpec((1, samples, 4 * points), lambda o: (jnp.minimum(o, 7 - o), 0, 0)),
        ],
        out_specs=pl.BlockSpec((groups, samples // groups, 2 * rhs), lambda o: (0, 0, 0)),
        out_shape=jax.ShapeDtypeStruct((groups, samples // groups, 2 * rhs), BF16),
        scratch_shapes=[pltpu.VMEM((samples, 2 * rhs), F32)],
        compiler_params=pltpu.CompilerParams(vmem_limit_bytes=VMEM_LIMIT),
        cost_estimate=pl.CostEstimate(
            flops=3 * 10**9, bytes_accessed=5 * 2**20, transcendentals=0
        ),
        name="upward",
    )(in_hbm(coeffs), in_hbm(radiation), in_hbm(weights))


def coupling_kernel(lists_ref, base_ref, table_ref, out_ref):
    rows = lists_ref.shape[0]
    samples = table_ref.shape[1] // 2
    targets = out_ref.shape[0] // (2 * samples)
    columns = out_ref.shape[1]
    slots = rows // targets
    selector = (
        lax.broadcasted_iota(jnp.int32, (rows, table_ref.shape[0]), 1) == lists_ref[:, 1:2]
    )
    chosen = dot(selector.astype(BF16), table_ref[...]).astype(BF16)
    wide = lax.broadcasted_iota(jnp.int32, (rows, columns), 1) // samples
    match = wide + base_ref[0] == lists_ref[:, 0:1]
    spread = lax.broadcasted_iota(jnp.int32, (samples, columns), 0) == (
        lax.broadcasted_iota(jnp.int32, (samples, columns), 1) % samples
    )
    gather = (
        lax.broadcasted_iota(jnp.int32, (targets, rows), 1) // slots
        == lax.broadcasted_iota(jnp.int32, (targets, rows), 0)
    ).astype(BF16)
    tile = spread.astype(BF16)
    for part in range(2):
        lines = dot(chosen[:, part * samples : (part + 1) * samples], tile)
        lines = dot(gather, jnp.where(match, lines, 0.0).astype(BF16))
        for target in range(targets):
            line = jnp.broadcast_to(lines[target : target + 1], spread.shape)
            start = (part * targets + target) * samples
            out_ref[start : start + samples] = jnp.where(spread, line, 0.0).astype(BF16)


def couplings(lists, base, table, targets, names):
    samples = table.shape[1] // 2
    shape = (2 * targets * samples, names * samples)
    vmem = pl.BlockSpec(memory_space=pltpu.VMEM)
    return pl.pallas_call(
        coupling_kernel,
        in_specs=[vmem, pl.BlockSpec(memory_space=pltpu.SMEM), vmem],
        out_specs=vmem,
        out_shape=jax.ShapeDtypeStruct(shape, BF16),
        compiler_params=pltpu.CompilerParams(vmem_limit_bytes=VMEM_LIMIT),
        cost_estimate=pl.CostEstimate(
            flops=2 * 10**8, bytes_accessed=2 * 2**20, transcendentals=0
        ),
        name="coupling",
    )(lists, base, table)


def translate_kernel(coupling_ref, *refs):
    sources, out_ref = refs[:-1], refs[-1]
    targets, samples, width = out_ref.shape
    rhs = width // 2
    total = None
    start = 0
    for source in sources:
        columns = source.shape[0] * samples
        part = dot(coupling_ref[:, start : start + columns], source[...].reshape(columns, width))
        total = part if total is None else total + part
        start += columns
    half = targets * samples
    real = total[:half, :rhs] - total[half:, rhs:]
    imag = total[:half, rhs:] + total[half:, :rhs]
    out_ref[...] = jnp.concatenate([real, imag], axis=1).astype(BF16).reshape(out_ref.shape)


def translate(coupling, sources):
    _, samples, width = sources[0].shape
    targets = coupling.shape[0] // (2 * samples)
    return pl.pallas_call(
        translate_kernel,
        out_shape=jax.ShapeDtypeStruct((targets, samples, width), BF16),
        compiler_params=pltpu.CompilerParams(vmem_limit_bytes=VMEM_LIMIT),
        cost_estimate=pl.CostEstimate(
            flops=10**9, bytes_accessed=2 * 2**20, transcendentals=0
        ),
        name="translate",
    )(coupling, *sources)


def near_kernel(
    ids_ref, count_ref, rank_ref, blocks_ref, low_ref, own_ref, high_ref, out_ref, held, sems
):
    box = pl.program_id(0)
    boxes, _, basis, rhs = own_ref.shape

    @pl.when(box == 0)
    def _():
        copies = [
            pltpu.make_async_copy(ref, held.at[pl.ds(place * boxes, boxes)], sems.at[place])
            for place, ref in enumerate((low_ref, own_ref, high_ref))
        ]
        for copy in copies:
            copy.start()
        for copy in copies:
            copy.wait()

    used = jnp.maximum(count_ref[box], 1)
    first = (rank_ref[0] - 1) * boxes

    def operand(slot, limit):
        real, imag = blocks_ref[0, slot, 0], blocks_ref[0, slot, 1]
        if limit:
            real = jnp.where(slot < used, real, jnp.zeros_like(real))
            imag = jnp.where(slot < used, imag, jnp.zeros_like(imag))
        return jnp.concatenate(
            [
                jnp.concatenate([real, -imag], axis=1),
                jnp.concatenate([imag, real], axis=1),
            ],
            axis=0,
        )

    def source(slot):
        return held[ids_ref[box, slot] - first].reshape(2 * basis, rhs)

    def group(first_slot):
        slots = range(first_slot, first_slot + GROUP)
        left = jnp.concatenate([operand(slot, slot > 0) for slot in slots], axis=1)
        right = jnp.concatenate([source(jnp.minimum(slot, used - 1)) for slot in slots], axis=0)
        return dot(left, right).reshape(2, basis, rhs)

    out_ref[0] = group(0)
    for first_slot in range(GROUP, blocks_ref.shape[1], GROUP):

        @pl.when(used > first_slot)
        def _(first_slot=first_slot):
            out_ref[0] += group(first_slot)


def near_field(ids, counts, rank, blocks, low, own, high):
    boxes, slots, _, basis, _ = blocks.shape
    rhs = own.shape[3]
    anywhere = pl.BlockSpec(memory_space=pl.ANY)
    return pl.pallas_call(
        near_kernel,
        grid_spec=pltpu.PrefetchScalarGridSpec(
            num_scalar_prefetch=3,
            grid=(boxes,),
            in_specs=[
                pl.BlockSpec((1, slots, 2, basis, basis), lambda b, *_: (b, 0, 0, 0, 0)),
                anywhere,
                anywhere,
                anywhere,
            ],
            out_specs=pl.BlockSpec((1, 2, basis, rhs), lambda b, *_: (b, 0, 0, 0)),
            scratch_shapes=[
                pltpu.VMEM((3 * boxes, 2, basis, rhs), BF16),
                pltpu.SemaphoreType.DMA((3,)),
            ],
        ),
        out_shape=jax.ShapeDtypeStruct((boxes, 2, basis, rhs), F32),
        compiler_params=pltpu.CompilerParams(vmem_limit_bytes=VMEM_LIMIT),
        cost_estimate=pl.CostEstimate(
            flops=4 * 10**9, bytes_accessed=12 * 2**20, transcendentals=0
        ),
        name="near",
    )(ids, counts, rank, in_hbm(blocks), low, own, high)


def down_kernel(
    field_ref, w_ref, rad_a_ref, rad_b_ref, near_a_ref, near_b_ref, out_ref, held, sems
):
    step = pl.program_id(0)
    last = pl.num_programs(0) - 1
    boxes = out_ref.shape[0]
    _, _, points, basis = rad_a_ref.shape
    rhs = near_a_ref.shape[3]
    slot = step % 2

    def writes(at, place):
        return [
            pltpu.make_async_copy(held.at[place, 0], out_ref.at[at], sems.at[place, 0]),
            pltpu.make_async_copy(held.at[place, 1], out_ref.at[boxes - 1 - at], sems.at[place, 1]),
        ]

    @pl.when(step >= 2)
    def _():
        for copy in writes(step - 2, slot):
            copy.wait()

    field = field_ref[...].reshape(-1, 2 * rhs)
    mixed = dot(w_ref[0], jnp.concatenate([field, field], axis=0))
    cos_re, cos_im = mixed[:points, :rhs], mixed[:points, rhs:]
    sin_re, sin_im = mixed[points:, :rhs], mixed[points:, rhs:]
    pairs = (
        (rad_a_ref, near_a_ref, cos_re + sin_im, cos_im - sin_re),
        (rad_b_ref, near_b_ref, cos_re - sin_im, cos_im + sin_re),
    )
    for place, (rad_ref, near_ref, real, imag) in enumerate(pairs):
        leaf = jnp.concatenate([real, imag], axis=0).astype(BF16)
        rad_re, rad_im = rad_ref[0, 0], rad_ref[0, 1]
        left = jnp.concatenate(
            [
                jnp.concatenate([rad_re, -rad_im], axis=1),
                jnp.concatenate([rad_im, rad_re], axis=1),
            ],
            axis=0,
        )
        far = lax.dot_general(left, leaf, (((0,), (0,)), ((), ())), preferred_element_type=F32)
        held[slot, place] = near_ref[0] + far.reshape(2, basis, rhs)
    for copy in writes(step, slot):
        copy.start()

    @pl.when(step == last)
    def _():
        for copy in writes(step - 1, 1 - slot) + writes(step, slot):
            copy.wait()


def downward(field, weights, radiation, near):
    boxes, _, basis, rhs = near.shape
    points = radiation.shape[2]
    first = lambda s: (s, 0, 0, 0)
    second = lambda s: (boxes - 1 - s, 0, 0, 0)
    return pl.pallas_call(
        down_kernel,
        grid=(boxes // 2,),
        in_specs=[
            pl.BlockSpec(field.shape, lambda s: (0, 0, 0)),
            pl.BlockSpec((1, *weights.shape[1:]), lambda s: (s, 0, 0)),
            pl.BlockSpec((1, 2, points, basis), first),
            pl.BlockSpec((1, 2, points, basis), second),
            pl.BlockSpec((1, 2, basis, rhs), first),
            pl.BlockSpec((1, 2, basis, rhs), second),
        ],
        out_specs=pl.BlockSpec(memory_space=pl.ANY),
        out_shape=jax.ShapeDtypeStruct(near.shape, F32),
        scratch_shapes=[
            pltpu.VMEM((2, 2, 2, basis, rhs), F32),
            pltpu.SemaphoreType.DMA((2, 2)),
        ],
        compiler_params=pltpu.CompilerParams(vmem_limit_bytes=VMEM_LIMIT),
        cost_estimate=pl.CostEstimate(
            flops=2 * 10**9, bytes_accessed=7 * 2**20, transcendentals=0
        ),
        name="downward",
    )(field, in_hbm(weights), *[in_hbm(radiation)] * 2, *[in_hbm(near)] * 2)


def shift(block, axis, step):
    count = lax.axis_size(axis)
    pairs = [(i, i + step) for i in range(count) if 0 <= i + step < count]
    return lax.ppermute(block, axis, pairs)


def lists_of(partners, vector_ids, pair_count):
    used = jnp.arange(partners.shape[1])[None, :] < pair_count[:, None]
    names = jnp.where(used, partners, NOWHERE)
    return jnp.stack([names, vector_ids], axis=2).reshape(-1, 2)


def far_field(spread, lists, translation, shares):
    operator_total, _, theta_band, phi_band = translation.shape
    rank = lax.axis_index("box")
    if shares == lax.axis_size("box"):
        every = ("box", "theta", "phi")
        for_all = lists
        if shares == 2:
            other = lax.ppermute(lists, "box", [(0, 1), (1, 0)])
            for_all = jnp.where(
                rank == 0, jnp.concatenate([lists, other]), jnp.concatenate([other, lists])
            )
        part = theta_band // shares
        table = lax.dynamic_slice_in_dim(translation, rank * part, part, axis=2)
        table = table.reshape(operator_total, -1)
        sources = spread.shape[0]
        base = jnp.zeros((1,), jnp.int32)
        coupling = couplings(for_all, base, table, sources, sources)
        parents = lax.all_to_all(spread, every, split_axis=0, concat_axis=0, tiled=True)
        incoming = translate(coupling, [parents])
        return lax.all_to_all(incoming, every, split_axis=0, concat_axis=0, tiled=True)
    bands = ("theta", "phi")
    per_group = spread.shape[0]
    table = translation.reshape(operator_total, -1)
    base = ((rank - 1) * per_group).astype(jnp.int32).reshape(1)
    coupling = couplings(lists, base, table, per_group, 3 * per_group)
    parents = lax.all_to_all(spread, bands, split_axis=0, concat_axis=0, tiled=True)
    sources = [shift(parents, "box", 1), parents, shift(parents, "box", -1)]
    incoming = translate(coupling, sources)
    return lax.all_to_all(incoming, bands, split_axis=0, concat_axis=0, tiled=True)


def per_device(
    shares,
    up_weights,
    down_weights,
    coeffs,
    near_blocks,
    near_ids,
    near_count,
    radiation,
    partners,
    vector_ids,
    pair_count,
    translation,
):
    every = ("box", "theta", "phi")
    low = shift(coeffs, every, 1)
    high = shift(coeffs, every, -1)
    groups = shares * lax.axis_size("theta") * lax.axis_size("phi")
    spread = upward(coeffs, radiation, up_weights, groups)
    lists = lists_of(partners, vector_ids, pair_count)
    field = far_field(spread, lists, translation, shares)
    rank = lax.axis_index(every).astype(jnp.int32).reshape(1)
    near = near_field(near_ids, near_count, rank, near_blocks, low, coeffs, high)
    return downward(field, down_weights, radiation, near)


def solution(mesh):
    box_size, theta_size, phi_size = (mesh.shape[axis] for axis in ("box", "theta", "phi"))
    shares = box_size if box_size <= 2 and TU // theta_size % box_size == 0 else 1
    up_weights, down_weights = operators(shares, theta_size, phi_size)
    in_specs = (
        P(),
        P(),
        P(("box", "theta", "phi"), None, None, None),
        P(("box", "theta", "phi"), None, None, None, None),
        P(("box", "theta", "phi"), None),
        P(("box", "theta", "phi")),
        P(("box", "theta", "phi"), None, None, None),
        P("box", None),
        P("box", None),
        P("box"),
        P(None, None, "theta", "phi"),
    )
    out_specs = P(("box", "theta", "phi"), None, None, None)
    mapped = jax.shard_map(
        functools.partial(per_device, shares),
        mesh=mesh,
        in_specs=in_specs,
        out_specs=out_specs,
        check_vma=False,
    )

    def product(*arrays):
        return mapped(jnp.asarray(up_weights), jnp.asarray(down_weights), *arrays)

    return product
```

```python
import functools
import math

import jax
import jax.numpy as jnp
import ml_dtypes
import numpy as np
from jax import lax
from jax.experimental import pallas as pl
from jax.experimental.pallas import tpu as pltpu
from jax.sharding import PartitionSpec as P

TL = 8
PL = 16
TU = 16
PU = 32

WEIGHT_UP = (-0.0546875, 0.8203125, 0.2734375, -0.0390625)
WEIGHT_DOWN = (-0.0390625, 0.2734375, 0.8203125, -0.0546875)
PHASE_SCALE = 1.3

F32 = jnp.float32
BF16 = jnp.bfloat16
MIB = 2**20
GROUP = 4
NOWHERE = -(2**20)


def lagrange(rows, columns, wrap):
    matrix = np.zeros((rows, columns))
    for row in range(rows):
        weights = WEIGHT_UP if row % 2 else WEIGHT_DOWN
        for order in range(4):
            node = row // 2 + row % 2 - 2 + order
            node = node % columns if wrap else min(max(node, 0), columns - 1)
            matrix[row, node] += weights[order]
    return matrix


def split_weights(matrix):
    high = matrix.astype(ml_dtypes.bfloat16)
    low = (matrix - high.astype(np.float64)).astype(ml_dtypes.bfloat16)
    return high, low


def operators(shares, theta_size, phi_size):
    theta_part = TU // theta_size // shares
    order = np.arange(TU * PU).reshape(theta_size, shares, theta_part, phi_size, PU // phi_size)
    order = order.transpose(1, 0, 3, 2, 4).reshape(-1)
    interp = np.kron(lagrange(TU, TL, False), lagrange(PU, PL, True))
    theta = math.pi * (np.arange(TU) + 0.5) / TU
    azimuth = 2.0 * math.pi * (np.arange(PU) + 0.5) / PU
    up, down = [], []
    for octant in range(4):
        sign_x = 2 * (octant % 2) - 1
        sign_y = 2 * (octant // 2 % 2) - 1
        sign_z = 2 * (octant // 4) - 1
        angle = PHASE_SCALE * (
            sign_x * np.sin(theta)[:, None] * np.cos(azimuth)[None]
            + sign_y * np.sin(theta)[:, None] * np.sin(azimuth)[None]
            + sign_z * np.cos(theta)[:, None]
        ).reshape(-1, 1)
        cos_high, cos_low = split_weights((np.cos(angle) * interp)[order])
        sin_high, sin_low = split_weights((np.sin(angle) * interp)[order])
        up.append(np.concatenate([cos_high, sin_high, cos_low, sin_low], axis=1))
        down.append(
            np.concatenate(
                [
                    np.concatenate([cos_high.T, cos_low.T], axis=1),
                    np.concatenate([sin_high.T, sin_low.T], axis=1),
                ],
                axis=0,
            )
        )
    return np.concatenate(up, axis=1), np.stack(down)


def in_hbm(array):
    return pltpu.with_memory_space_constraint(array, pltpu.HBM)


def dot(a, b):
    return jnp.dot(a, b, preferred_element_type=F32)


def complex_rows(real, imag):
    return jnp.concatenate(
        [
            jnp.concatenate([real, -imag], axis=1),
            jnp.concatenate([imag, real], axis=1),
        ],
        axis=0,
    )


def up_kernel(x_hbm, rad_hbm, w_hbm, out_ref, x_ref, rad_ref, w_ref, right, sems):
    boxes, _, basis, rhs = x_ref.shape
    points = rad_ref.shape[2]
    copies = [
        pltpu.make_async_copy(source, target, sems.at[place])
        for place, (source, target) in enumerate(
            ((x_hbm, x_ref), (rad_hbm, rad_ref), (w_hbm, w_ref))
        )
    ]
    for copy in copies:
        copy.start()
    copies[0].wait()
    copies[1].wait()
    half = boxes // 2
    for octant in range(boxes):
        left = complex_rows(rad_ref[octant, 0], rad_ref[octant, 1])
        pattern = dot(left, x_ref[octant].reshape(2 * basis, rhs)).astype(BF16)
        real, imag = pattern[:points], pattern[points:]
        straight = jnp.concatenate([real, imag], axis=1)
        if octant < half:
            swapped = jnp.concatenate([-imag, real], axis=1)
        else:
            swapped = jnp.concatenate([imag, -real], axis=1)
        place = octant if octant < half else boxes - 1 - octant
        for copy in range(2):
            start = (4 * place + 2 * copy) * points
            right[octant // half, start : start + points] = straight
            right[octant // half, start + points : start + 2 * points] = swapped
    copies[2].wait()
    total = dot(w_ref[...], right[0]) + dot(w_ref[...], right[1])
    out_ref[...] = total.astype(BF16).reshape(out_ref.shape)


def upward(coeffs, radiation, weights, groups):
    boxes, _, basis, rhs = coeffs.shape
    samples, columns = weights.shape
    anywhere = pl.BlockSpec(memory_space=pl.ANY)
    return pl.pallas_call(
        up_kernel,
        in_specs=[anywhere] * 3,
        out_specs=pl.BlockSpec(memory_space=pltpu.VMEM),
        out_shape=jax.ShapeDtypeStruct((groups, samples // groups, 2 * rhs), BF16),
        scratch_shapes=[
            pltpu.VMEM(coeffs.shape, BF16),
            pltpu.VMEM(radiation.shape, BF16),
            pltpu.VMEM(weights.shape, BF16),
            pltpu.VMEM((2, columns, 2 * rhs), BF16),
            pltpu.SemaphoreType.DMA((3,)),
        ],
        compiler_params=pltpu.CompilerParams(vmem_limit_bytes=24 * MIB),
        cost_estimate=pl.CostEstimate(
            flops=2 * 10**9, bytes_accessed=4 * MIB, transcendentals=0
        ),
        name="upward",
    )(in_hbm(coeffs), in_hbm(radiation), in_hbm(weights))


def coupling_kernel(lists_ref, base_ref, table_ref, out_ref):
    rows = lists_ref.shape[0]
    samples = table_ref.shape[1] // 2
    targets = out_ref.shape[0] // (2 * samples)
    columns = out_ref.shape[1]
    slots = rows // targets
    selector = (
        lax.broadcasted_iota(jnp.int32, (rows, table_ref.shape[0]), 1) == lists_ref[:, 1:2]
    )
    chosen = dot(selector.astype(BF16), table_ref[...]).astype(BF16)
    wide = lax.broadcasted_iota(jnp.int32, (rows, columns), 1) // samples
    match = wide + base_ref[0] == lists_ref[:, 0:1]
    spread = lax.broadcasted_iota(jnp.int32, (samples, columns), 0) == (
        lax.broadcasted_iota(jnp.int32, (samples, columns), 1) % samples
    )
    gather = (
        lax.broadcasted_iota(jnp.int32, (targets, rows), 1) // slots
        == lax.broadcasted_iota(jnp.int32, (targets, rows), 0)
    ).astype(BF16)
    tile = spread.astype(BF16)
    for part in range(2):
        lines = dot(chosen[:, part * samples : (part + 1) * samples], tile)
        lines = dot(gather, jnp.where(match, lines, 0.0).astype(BF16))
        for target in range(targets):
            line = jnp.broadcast_to(lines[target : target + 1], spread.shape)
            start = (part * targets + target) * samples
            out_ref[start : start + samples] = jnp.where(spread, line, 0.0).astype(BF16)


def couplings(lists, base, table, targets, names):
    samples = table.shape[1] // 2
    shape = (2 * targets * samples, names * samples)
    vmem = pl.BlockSpec(memory_space=pltpu.VMEM)
    return pl.pallas_call(
        coupling_kernel,
        in_specs=[vmem, pl.BlockSpec(memory_space=pltpu.SMEM), vmem],
        out_specs=vmem,
        out_shape=jax.ShapeDtypeStruct(shape, BF16),
        compiler_params=pltpu.CompilerParams(vmem_limit_bytes=16 * MIB),
        cost_estimate=pl.CostEstimate(
            flops=2 * 10**8, bytes_accessed=2 * 2**20, transcendentals=0
        ),
        name="coupling",
    )(lists, base, table)


def translate_kernel(coupling_ref, *refs):
    sources, out_ref = refs[:-1], refs[-1]
    targets, samples, width = out_ref.shape
    rhs = width // 2
    total = None
    start = 0
    for source in sources:
        columns = source.shape[0] * samples
        part = dot(coupling_ref[:, start : start + columns], source[...].reshape(columns, width))
        total = part if total is None else total + part
        start += columns
    half = targets * samples
    real = total[:half, :rhs] - total[half:, rhs:]
    imag = total[:half, rhs:] + total[half:, :rhs]
    out_ref[...] = jnp.concatenate([real, imag], axis=1).astype(BF16).reshape(out_ref.shape)


def translate(coupling, sources):
    _, samples, width = sources[0].shape
    targets = coupling.shape[0] // (2 * samples)
    return pl.pallas_call(
        translate_kernel,
        out_shape=jax.ShapeDtypeStruct((targets, samples, width), BF16),
        compiler_params=pltpu.CompilerParams(vmem_limit_bytes=16 * MIB),
        cost_estimate=pl.CostEstimate(
            flops=10**9, bytes_accessed=2 * 2**20, transcendentals=0
        ),
        name="translate",
    )(coupling, *sources)


def near_kernel(first, count, begun, *refs):
    ids_ref, used_ref, rank_ref, blocks_hbm = refs[:4]
    sources = refs[4 : 4 + count]
    before_ref = refs[4 + count] if begun else None
    out_ref, blocks, held, listed, sems = refs[4 + count + begun :]
    boxes, slots, _, basis, _ = blocks.shape
    rhs = held.shape[3]
    base = (rank_ref[0] - 1 + first) * boxes
    source_copies = [
        pltpu.make_async_copy(source, held.at[pl.ds(place * boxes, boxes)], sems.at[boxes + place])
        for place, source in enumerate(sources)
    ]
    block_copies = lambda box: pltpu.make_async_copy(blocks_hbm.at[box], blocks.at[box], sems.at[box])
    for copy in source_copies:
        copy.start()
    for box in range(boxes):
        block_copies(box).start()
    for copy in source_copies:
        copy.wait()

    def one_box(box, carry):
        total = jnp.int32(0)
        used = used_ref[box]
        for slot in range(slots):
            place = ids_ref[box, slot] - base
            listed[total] = jnp.int32(slot)
            wanted = (slot < used) & (place >= 0) & (place < count * boxes)
            total += wanted.astype(jnp.int32)
        out_ref[box] = before_ref[box] if begun else jnp.zeros(out_ref.shape[1:], F32)
        block_copies(box).wait()

        def group(index, carry):
            left, right = [], []
            for step in range(GROUP):
                at = index * GROUP + step
                slot = listed[jnp.minimum(at, total - 1)]
                real, imag = blocks[box, slot, 0], blocks[box, slot, 1]
                if step:
                    real = jnp.where(at < total, real, jnp.zeros_like(real))
                    imag = jnp.where(at < total, imag, jnp.zeros_like(imag))
                left.append(complex_rows(real, imag))
                right.append(held[ids_ref[box, slot] - base].reshape(2 * basis, rhs))
            part = dot(jnp.concatenate(left, axis=1), jnp.concatenate(right, axis=0))
            out_ref[box] += part.reshape(2, basis, rhs)
            return carry

        lax.fori_loop(0, (total + GROUP - 1) // GROUP, group, 0)
        return carry

    lax.fori_loop(0, boxes, one_box, 0)


def near_field(ids, used, rank, blocks, sources, first, before=None):
    boxes, slots, _, basis, _ = blocks.shape
    rhs = sources[0].shape[3]
    count = len(sources)
    begun = before is not None
    anywhere = pl.BlockSpec(memory_space=pl.ANY)
    smem = pl.BlockSpec(memory_space=pltpu.SMEM)
    vmem = pl.BlockSpec(memory_space=pltpu.VMEM)
    return pl.pallas_call(
        functools.partial(near_kernel, first, count, begun),
        in_specs=[smem] * 3 + [anywhere] * (1 + count) + [vmem] * begun,
        out_specs=vmem,
        out_shape=jax.ShapeDtypeStruct((boxes, 2, basis, rhs), F32),
        scratch_shapes=[
            pltpu.VMEM(blocks.shape, BF16),
            pltpu.VMEM((count * boxes, 2, basis, rhs), BF16),
            pltpu.SMEM((slots + 1,), jnp.int32),
            pltpu.SemaphoreType.DMA((boxes + count,)),
        ],
        compiler_params=pltpu.CompilerParams(vmem_limit_bytes=24 * MIB),
        cost_estimate=pl.CostEstimate(
            flops=2 * 10**9, bytes_accessed=8 * MIB, transcendentals=0
        ),
        name="near_first" if not begun else "near_last",
    )(ids, used, rank, in_hbm(blocks), *sources, *([before] if begun else []))


def down_kernel(field_ref, w_ref, rad_ref, near_ref, out_hbm, held, sems):
    boxes, _, points, basis = rad_ref.shape
    rhs = near_ref.shape[3]
    field = field_ref[...].reshape(-1, 2 * rhs)
    field = jnp.concatenate([field, field], axis=0)
    copies = []
    for octant in range(boxes // 2):
        mixed = dot(w_ref[octant], field)
        cos_re, cos_im = mixed[:points, :rhs], mixed[:points, rhs:]
        sin_re, sin_im = mixed[points:, :rhs], mixed[points:, rhs:]
        pairs = (
            (octant, cos_re + sin_im, cos_im - sin_re),
            (boxes - 1 - octant, cos_re - sin_im, cos_im + sin_re),
        )
        for box, real, imag in pairs:
            leaf = jnp.concatenate([real, imag], axis=0).astype(BF16)
            left = complex_rows(rad_ref[box, 0], rad_ref[box, 1])
            far = lax.dot_general(
                left, leaf, (((0,), (0,)), ((), ())), preferred_element_type=F32
            )
            held[box] = near_ref[box] + far.reshape(2, basis, rhs)
            copies.append(pltpu.make_async_copy(held.at[box], out_hbm.at[box], sems.at[box]))
            copies[-1].start()
    for copy in copies:
        copy.wait()


def downward(field, weights, radiation, near):
    boxes = near.shape[0]
    vmem = pl.BlockSpec(memory_space=pltpu.VMEM)
    return pl.pallas_call(
        down_kernel,
        in_specs=[vmem] * 4,
        out_specs=pl.BlockSpec(memory_space=pl.ANY),
        out_shape=jax.ShapeDtypeStruct(near.shape, F32),
        scratch_shapes=[
            pltpu.VMEM(near.shape, F32),
            pltpu.SemaphoreType.DMA((boxes,)),
        ],
        compiler_params=pltpu.CompilerParams(vmem_limit_bytes=16 * MIB),
        cost_estimate=pl.CostEstimate(
            flops=2 * 10**9, bytes_accessed=7 * MIB, transcendentals=0
        ),
        name="downward",
    )(field, weights, radiation, near)


def shift(block, axis, step):
    count = lax.axis_size(axis)
    pairs = [(i, i + step) for i in range(count) if 0 <= i + step < count]
    return lax.ppermute(block, axis, pairs)


def lists_of(partners, vector_ids, pair_count):
    used = jnp.arange(partners.shape[1])[None, :] < pair_count[:, None]
    names = jnp.where(used, partners, NOWHERE)
    return jnp.stack([names, vector_ids], axis=2).reshape(-1, 2)


def far_field(spread, lists, translation, shares, near):
    operator_total, _, theta_band, phi_band = translation.shape
    rank = lax.axis_index("box")
    if shares == lax.axis_size("box"):
        every = ("box", "theta", "phi")
        for_all = lists
        if shares == 2:
            other = lax.ppermute(lists, "box", [(0, 1), (1, 0)])
            for_all = jnp.where(
                rank == 0, jnp.concatenate([lists, other]), jnp.concatenate([other, lists])
            )
        part = theta_band // shares
        table = lax.dynamic_slice_in_dim(translation, rank * part, part, axis=2)
        table = table.reshape(operator_total, -1)
        sources = spread.shape[0]
        base = jnp.zeros((1,), jnp.int32)
        coupling = couplings(for_all, base, table, sources, sources)
        parents = lax.all_to_all(spread, every, split_axis=0, concat_axis=0, tiled=True)
        parents, near = lax.optimization_barrier((parents, near))
        incoming = translate(coupling, [parents])
        return lax.all_to_all(incoming, every, split_axis=0, concat_axis=0, tiled=True), near
    bands = ("theta", "phi")
    per_group = spread.shape[0]
    table = translation.reshape(operator_total, -1)
    base = ((rank - 1) * per_group).astype(jnp.int32).reshape(1)
    coupling = couplings(lists, base, table, per_group, 3 * per_group)
    parents = lax.all_to_all(spread, bands, split_axis=0, concat_axis=0, tiled=True)
    parents, near = lax.optimization_barrier((parents, near))
    sources = [shift(parents, "box", 1), parents, shift(parents, "box", -1)]
    incoming = translate(coupling, sources)
    return lax.all_to_all(incoming, bands, split_axis=0, concat_axis=0, tiled=True), near


def per_device(
    shares,
    up_weights,
    down_weights,
    coeffs,
    near_blocks,
    near_ids,
    near_count,
    radiation,
    partners,
    vector_ids,
    pair_count,
    translation,
):
    every = ("box", "theta", "phi")
    low = shift(coeffs, every, 1)
    high = shift(coeffs, every, -1)
    groups = shares * lax.axis_size("theta") * lax.axis_size("phi")
    spread = upward(coeffs, radiation, up_weights, groups)
    lists = lists_of(partners, vector_ids, pair_count)
    rank = lax.axis_index(every).astype(jnp.int32).reshape(1)
    near = near_field(near_ids, near_count, rank, near_blocks, [low, coeffs], 0)
    field, near = far_field(spread, lists, translation, shares, near)
    near = near_field(near_ids, near_count, rank, near_blocks, [high], 2, near)
    return downward(field, down_weights, radiation, near)


def solution(mesh):
    box_size, theta_size, phi_size = (mesh.shape[axis] for axis in ("box", "theta", "phi"))
    shares = box_size if box_size <= 2 and TU // theta_size % box_size == 0 else 1
    up_weights, down_weights = operators(shares, theta_size, phi_size)
    in_specs = (
        P(),
        P(),
        P(("box", "theta", "phi"), None, None, None),
        P(("box", "theta", "phi"), None, None, None, None),
        P(("box", "theta", "phi"), None),
        P(("box", "theta", "phi")),
        P(("box", "theta", "phi"), None, None, None),
        P("box", None),
        P("box", None),
        P("box"),
        P(None, None, "theta", "phi"),
    )
    out_specs = P(("box", "theta", "phi"), None, None, None)
    mapped = jax.shard_map(
        functools.partial(per_device, shares),
        mesh=mesh,
        in_specs=in_specs,
        out_specs=out_specs,
        check_vma=False,
    )

    def product(*arrays):
        return mapped(jnp.asarray(up_weights), jnp.asarray(down_weights), *arrays)

    return product
```

```python
import functools
import math

import jax
import jax.numpy as jnp
import ml_dtypes
import numpy as np
from jax import lax
from jax.experimental import pallas as pl
from jax.experimental.pallas import tpu as pltpu
from jax.sharding import PartitionSpec as P

TL = 8
PL = 16
TU = 16
PU = 32

WEIGHT_UP = (-0.0546875, 0.8203125, 0.2734375, -0.0390625)
WEIGHT_DOWN = (-0.0390625, 0.2734375, 0.8203125, -0.0546875)
PHASE_SCALE = 1.3

F32 = jnp.float32
BF16 = jnp.bfloat16
MIB = 2**20
GROUP = 4
NOWHERE = -(2**20)


def lagrange(rows, columns, wrap):
    matrix = np.zeros((rows, columns))
    for row in range(rows):
        weights = WEIGHT_UP if row % 2 else WEIGHT_DOWN
        for order in range(4):
            node = row // 2 + row % 2 - 2 + order
            node = node % columns if wrap else min(max(node, 0), columns - 1)
            matrix[row, node] += weights[order]
    return matrix


def split_weights(matrix):
    high = matrix.astype(ml_dtypes.bfloat16)
    low = (matrix - high.astype(np.float64)).astype(ml_dtypes.bfloat16)
    return high, low


def operators(shares, theta_size, phi_size):
    theta_part = TU // theta_size // shares
    order = np.arange(TU * PU).reshape(theta_size, shares, theta_part, phi_size, PU // phi_size)
    order = order.transpose(1, 0, 3, 2, 4).reshape(-1)
    interp = np.kron(lagrange(TU, TL, False), lagrange(PU, PL, True))
    theta = math.pi * (np.arange(TU) + 0.5) / TU
    azimuth = 2.0 * math.pi * (np.arange(PU) + 0.5) / PU
    up, down = [], []
    for octant in range(4):
        sign_x = 2 * (octant % 2) - 1
        sign_y = 2 * (octant // 2 % 2) - 1
        sign_z = 2 * (octant // 4) - 1
        angle = PHASE_SCALE * (
            sign_x * np.sin(theta)[:, None] * np.cos(azimuth)[None]
            + sign_y * np.sin(theta)[:, None] * np.sin(azimuth)[None]
            + sign_z * np.cos(theta)[:, None]
        ).reshape(-1, 1)
        cos_high, cos_low = split_weights((np.cos(angle) * interp)[order])
        sin_high, sin_low = split_weights((np.sin(angle) * interp)[order])
        high = np.concatenate([cos_high, sin_high], axis=1)
        low = np.concatenate([cos_low, sin_low], axis=1)
        up.append(np.concatenate([high, low], axis=0))
        down.append(np.concatenate([cos_high.T, sin_high.T, cos_low.T, sin_low.T], axis=0))
    return np.concatenate(up, axis=1), np.stack(down)


def dot(a, b):
    return jnp.dot(a, b, preferred_element_type=F32)


def complex_rows(real, imag):
    return jnp.concatenate(
        [
            jnp.concatenate([real, -imag], axis=1),
            jnp.concatenate([imag, real], axis=1),
        ],
        axis=0,
    )


def up_kernel(x_hbm, rad_hbm, w_hbm, out_ref, x_ref, rad_ref, w_ref, right, sems):
    boxes, _, basis, rhs = x_ref.shape
    points = rad_ref.shape[2]
    copies = [
        pltpu.make_async_copy(source, target, sems.at[place])
        for place, (source, target) in enumerate(
            ((x_hbm, x_ref), (rad_hbm, rad_ref), (w_hbm, w_ref))
        )
    ]
    for copy in copies:
        copy.start()
    copies[0].wait()
    copies[1].wait()
    half = boxes // 2
    for octant in range(boxes):
        left = complex_rows(rad_ref[octant, 0], rad_ref[octant, 1])
        pattern = dot(left, x_ref[octant].reshape(2 * basis, rhs)).astype(BF16)
        real, imag = pattern[:points], pattern[points:]
        straight = jnp.concatenate([real, imag], axis=1)
        if octant < half:
            swapped = jnp.concatenate([-imag, real], axis=1)
        else:
            swapped = jnp.concatenate([imag, -real], axis=1)
        place = octant if octant < half else boxes - 1 - octant
        start = 2 * place * points
        right[octant // half, start : start + points] = straight
        right[octant // half, start + points : start + 2 * points] = swapped
    copies[2].wait()
    total = dot(w_ref[...], right[0]) + dot(w_ref[...], right[1])
    samples = total.shape[0] // 2
    total = total[:samples] + total[samples:]
    out_ref[...] = total.astype(BF16).reshape(out_ref.shape)


def upward(coeffs, radiation, weights, groups):
    boxes, _, basis, rhs = coeffs.shape
    rows, columns = weights.shape
    samples = rows // 2
    hbm = pl.BlockSpec(memory_space=pltpu.HBM)
    return pl.pallas_call(
        up_kernel,
        in_specs=[hbm] * 3,
        out_specs=pl.BlockSpec(memory_space=pltpu.VMEM),
        out_shape=jax.ShapeDtypeStruct((groups, samples // groups, 2 * rhs), BF16),
        scratch_shapes=[
            pltpu.VMEM(coeffs.shape, BF16),
            pltpu.VMEM(radiation.shape, BF16),
            pltpu.VMEM(weights.shape, BF16),
            pltpu.VMEM((2, columns, 2 * rhs), BF16),
            pltpu.SemaphoreType.DMA((3,)),
        ],
        compiler_params=pltpu.CompilerParams(vmem_limit_bytes=32 * MIB),
        cost_estimate=pl.CostEstimate(
            flops=2 * 10**9, bytes_accessed=4 * MIB, transcendentals=0
        ),
        name="upward",
    )(coeffs, radiation, weights)


def coupling_kernel(lists_ref, base_ref, table_ref, out_ref):
    rows = lists_ref.shape[0]
    samples = table_ref.shape[1] // 2
    _, targets, columns = out_ref.shape
    slots = rows // targets
    selector = (
        lax.broadcasted_iota(jnp.int32, (rows, table_ref.shape[0]), 1) == lists_ref[:, 1:2]
    )
    chosen = dot(selector.astype(BF16), table_ref[...]).astype(BF16)
    wide = lax.broadcasted_iota(jnp.int32, (rows, columns), 1) // samples
    match = wide + base_ref[0] == lists_ref[:, 0:1]
    spread = lax.broadcasted_iota(jnp.int32, (samples, columns), 0) == (
        lax.broadcasted_iota(jnp.int32, (samples, columns), 1) % samples
    )
    gather = (
        lax.broadcasted_iota(jnp.int32, (targets, rows), 1) // slots
        == lax.broadcasted_iota(jnp.int32, (targets, rows), 0)
    ).astype(BF16)
    tile = spread.astype(BF16)
    for part in range(2):
        lines = dot(chosen[:, part * samples : (part + 1) * samples], tile)
        out_ref[part] = dot(gather, jnp.where(match, lines, 0.0).astype(BF16))


def couplings(lists, base, table, targets, names):
    shape = (2, targets, names * (table.shape[1] // 2))
    vmem = pl.BlockSpec(memory_space=pltpu.VMEM)
    return pl.pallas_call(
        coupling_kernel,
        in_specs=[vmem, pl.BlockSpec(memory_space=pltpu.SMEM), vmem],
        out_specs=vmem,
        out_shape=jax.ShapeDtypeStruct(shape, F32),
        compiler_params=pltpu.CompilerParams(vmem_limit_bytes=16 * MIB),
        cost_estimate=pl.CostEstimate(
            flops=2 * 10**8, bytes_accessed=2 * 2**20, transcendentals=0
        ),
        name="coupling",
    )(lists, base, table)


def translate_kernel(lines_hbm, *refs):
    count = (len(refs) - 5) // 2
    sources, out_hbm = refs[:count], refs[count]
    held, lines, matrix, result, sems = refs[count + 1 :][:count], *refs[2 * count + 1 :]
    targets, samples, width = result.shape
    rhs = width // 2
    copies = [
        pltpu.make_async_copy(source, target, sems.at[place])
        for place, (source, target) in enumerate(zip((lines_hbm, *sources), (lines, *held)))
    ]
    for copy in copies:
        copy.start()
    copies[0].wait()
    columns = matrix.shape[1]
    row = lax.broadcasted_iota(jnp.int32, (samples, columns), 0)
    diagonal = row == lax.broadcasted_iota(jnp.int32, (samples, columns), 1) % samples
    for part in range(2):
        for target in range(targets):
            line = jnp.broadcast_to(lines[part, target : target + 1], diagonal.shape)
            start = (part * targets + target) * samples
            matrix[start : start + samples] = jnp.where(diagonal, line, 0.0).astype(BF16)
    total = None
    start = 0
    for place, source in enumerate(held):
        copies[1 + place].wait()
        stop = start + source.shape[0] * samples
        part = dot(matrix[:, start:stop], source[...].reshape(stop - start, width))
        total = part if total is None else total + part
        start = stop
    half = targets * samples
    real = total[:half, :rhs] - total[half:, rhs:]
    imag = total[:half, rhs:] + total[half:, :rhs]
    result[...] = jnp.concatenate([real, imag], axis=1).astype(BF16).reshape(result.shape)
    pltpu.sync_copy(result, out_hbm)


def translate(lines, sources):
    _, samples, width = sources[0].shape
    _, targets, columns = lines.shape
    shape = (targets, samples, width)
    hbm = pl.BlockSpec(memory_space=pltpu.HBM)
    return pl.pallas_call(
        translate_kernel,
        in_specs=[hbm] * (1 + len(sources)),
        out_specs=hbm,
        out_shape=jax.ShapeDtypeStruct(shape, BF16),
        scratch_shapes=[
            *[pltpu.VMEM(source.shape, BF16) for source in sources],
            pltpu.VMEM(lines.shape, F32),
            pltpu.VMEM((2 * targets * samples, columns), BF16),
            pltpu.VMEM(shape, BF16),
            pltpu.SemaphoreType.DMA((1 + len(sources),)),
        ],
        compiler_params=pltpu.CompilerParams(vmem_limit_bytes=24 * MIB),
        cost_estimate=pl.CostEstimate(
            flops=10**9, bytes_accessed=2 * MIB, transcendentals=0
        ),
        name="translate",
    )(lines, *sources)


def near_kernel(first, count, begun, *refs):
    ids_ref, used_ref, rank_ref, blocks_hbm = refs[:4]
    sources = refs[4 : 4 + count]
    out_hbm, blocks, held, total_ref, listed, sems = refs[4 + count + begun :]
    boxes, slots, _, basis, _ = blocks.shape
    rhs = held.shape[3]
    base = (rank_ref[0] - 1 + first) * boxes
    source_copies = [
        pltpu.make_async_copy(source, held.at[pl.ds(place * boxes, boxes)], sems.at[boxes + place])
        for place, source in enumerate(sources)
    ]

    def block_copy(box):
        return pltpu.make_async_copy(blocks_hbm.at[box], blocks.at[box], sems.at[box])

    def result_copy(box, inward):
        place = boxes + count + box
        if inward:
            return pltpu.make_async_copy(refs[4 + count].at[box], total_ref.at[box], sems.at[place])
        return pltpu.make_async_copy(total_ref.at[box], out_hbm.at[box], sems.at[place])

    for copy in source_copies:
        copy.start()
    for box in range(boxes):
        block_copy(box).start()
        if begun:
            result_copy(box, True).start()
    for copy in source_copies:
        copy.wait()

    def one_box(box, carry):
        total = jnp.int32(0)
        used = used_ref[box]
        for slot in range(slots):
            place = ids_ref[box, slot] - base
            listed[total] = jnp.int32(slot)
            wanted = (slot < used) & (place >= 0) & (place < count * boxes)
            total += wanted.astype(jnp.int32)
        block_copy(box).wait()
        if begun:
            result_copy(box, True).wait()
        else:
            total_ref[box] = jnp.zeros(total_ref.shape[1:], F32)

        def group(index, carry):
            left, right = [], []
            for step in range(GROUP):
                at = index * GROUP + step
                slot = listed[jnp.minimum(at, total - 1)]
                real, imag = blocks[box, slot, 0], blocks[box, slot, 1]
                if step:
                    real = jnp.where(at < total, real, jnp.zeros_like(real))
                    imag = jnp.where(at < total, imag, jnp.zeros_like(imag))
                left.append(complex_rows(real, imag))
                right.append(held[ids_ref[box, slot] - base].reshape(2 * basis, rhs))
            part = dot(jnp.concatenate(left, axis=1), jnp.concatenate(right, axis=0))
            total_ref[box] += part.reshape(2, basis, rhs)
            return carry

        lax.fori_loop(0, (total + GROUP - 1) // GROUP, group, 0)
        result_copy(box, False).start()
        return carry

    lax.fori_loop(0, boxes, one_box, 0)
    for box in range(boxes):
        result_copy(box, False).wait()


def near_field(ids, used, rank, blocks, sources, first, before=None):
    boxes, slots, _, basis, _ = blocks.shape
    rhs = sources[0].shape[3]
    count = len(sources)
    begun = before is not None
    hbm = pl.BlockSpec(memory_space=pltpu.HBM)
    smem = pl.BlockSpec(memory_space=pltpu.SMEM)
    return pl.pallas_call(
        functools.partial(near_kernel, first, count, begun),
        in_specs=[smem] * 3 + [hbm] * (1 + count + begun),
        out_specs=hbm,
        out_shape=jax.ShapeDtypeStruct((boxes, 2, basis, rhs), F32),
        scratch_shapes=[
            pltpu.VMEM(blocks.shape, BF16),
            pltpu.VMEM((count * boxes, 2, basis, rhs), BF16),
            pltpu.VMEM((boxes, 2, basis, rhs), F32),
            pltpu.SMEM((slots + 1,), jnp.int32),
            pltpu.SemaphoreType.DMA((2 * boxes + count,)),
        ],
        compiler_params=pltpu.CompilerParams(vmem_limit_bytes=24 * MIB),
        cost_estimate=pl.CostEstimate(
            flops=10**11 if begun else 2 * 10**9, bytes_accessed=8 * MIB, transcendentals=0
        ),
        name="near_last" if begun else "near_first",
    )(ids, used, rank, blocks, *sources, *([before] if begun else []))


def adjoint_kernel(rad_ref, out_ref):
    for box in range(rad_ref.shape[0]):
        out_ref[box] = complex_rows(rad_ref[box, 0], rad_ref[box, 1]).T


def adjoint(radiation):
    boxes, _, points, basis = radiation.shape
    return pl.pallas_call(
        adjoint_kernel,
        out_shape=jax.ShapeDtypeStruct((boxes, 2 * basis, 2 * points), BF16),
        cost_estimate=pl.CostEstimate(
            flops=10**6, bytes_accessed=2 * MIB, transcendentals=0
        ),
        name="adjoint",
    )(radiation)


def down_kernel(field_hbm, w_hbm, adjoint_hbm, near_hbm, out_hbm, field, w, left, held, sems):
    boxes, width, _ = left.shape
    points = width // 2
    samples = w.shape[2]
    basis, rhs = held.shape[2], held.shape[3]
    half = boxes // 2
    field_copy = pltpu.make_async_copy(field_hbm, field, sems.at[0])
    w_copies, left_copies, near_copies, out_copies = [], [], [], []
    for pair in range(half):
        w_copies.append(pltpu.make_async_copy(w_hbm.at[pair], w.at[pair], sems.at[1 + pair]))
    for box in range(boxes):
        places = [1 + half + turn * boxes + box for turn in range(3)]
        left_copies.append(
            pltpu.make_async_copy(adjoint_hbm.at[box], left.at[box], sems.at[places[0]])
        )
        near_copies.append(
            pltpu.make_async_copy(near_hbm.at[box], held.at[box], sems.at[places[1]])
        )
        out_copies.append(
            pltpu.make_async_copy(held.at[box], out_hbm.at[box], sems.at[places[2]])
        )
    field_copy.start()
    for pair in range(half):
        w_copies[pair].start()
    for pair in range(half):
        for box in (pair, boxes - 1 - pair):
            left_copies[box].start()
            near_copies[box].start()
    field_copy.wait()
    for first in range(0, half, 2):
        for pair in (first, first + 1):
            w_copies[pair].wait()
        rows = w.shape[1]
        mixed = dot(
            w[first : first + 2].reshape(2 * rows, samples), field[...].reshape(samples, 2 * rhs)
        )
        for pair in (first, first + 1):
            part = mixed[(pair - first) * rows : (pair - first + 1) * rows]
            part = part[: rows // 2] + part[rows // 2 :]
            cos_re, cos_im = part[:points, :rhs], part[:points, rhs:]
            sin_re, sin_im = part[points:, :rhs], part[points:, rhs:]
            leaves = (
                (pair, cos_re + sin_im, cos_im - sin_re),
                (boxes - 1 - pair, cos_re - sin_im, cos_im + sin_re),
            )
            for box, real, imag in leaves:
                leaf = jnp.concatenate([real, imag], axis=0).astype(BF16)
                left_copies[box].wait()
                far = dot(left[box], leaf)
                near_copies[box].wait()
                held[box] += far.reshape(2, basis, rhs)
                out_copies[box].start()
    for copy in out_copies:
        copy.wait()


def downward(field, weights, radiation_adjoint, near):
    boxes = near.shape[0]
    hbm = pl.BlockSpec(memory_space=pltpu.HBM)
    return pl.pallas_call(
        down_kernel,
        in_specs=[hbm] * 4,
        out_specs=hbm,
        out_shape=jax.ShapeDtypeStruct(near.shape, F32),
        scratch_shapes=[
            pltpu.VMEM(field.shape, BF16),
            pltpu.VMEM(weights.shape, BF16),
            pltpu.VMEM(radiation_adjoint.shape, BF16),
            pltpu.VMEM(near.shape, F32),
            pltpu.SemaphoreType.DMA((1 + boxes // 2 + 3 * boxes,)),
        ],
        compiler_params=pltpu.CompilerParams(vmem_limit_bytes=32 * MIB),
        cost_estimate=pl.CostEstimate(
            flops=2 * 10**9, bytes_accessed=7 * MIB, transcendentals=0
        ),
        name="downward",
    )(field, weights, radiation_adjoint, near)


def shift(block, axis, step):
    count = lax.axis_size(axis)
    pairs = [(i, i + step) for i in range(count) if 0 <= i + step < count]
    return lax.ppermute(block, axis, pairs)


def lists_of(partners, vector_ids, pair_count):
    used = jnp.arange(partners.shape[1])[None, :] < pair_count[:, None]
    names = jnp.where(used, partners, NOWHERE)
    return jnp.stack([names, vector_ids], axis=2).reshape(-1, 2)


def parent_bands(spread, shares):
    axes = ("box", "theta", "phi") if shares == lax.axis_size("box") else ("theta", "phi")
    return lax.all_to_all(spread, axes, split_axis=0, concat_axis=0, tiled=True)


def translation_lines(lists, translation, shares, per_group):
    operator_total, _, theta_band, phi_band = translation.shape
    rank = lax.axis_index("box")
    if shares < lax.axis_size("box"):
        table = translation.reshape(operator_total, -1)
        base = ((rank - 1) * per_group).astype(jnp.int32).reshape(1)
        return couplings(lists, base, table, per_group, 3 * per_group)
    if shares == 2:
        other = lax.ppermute(lists, "box", [(0, 1), (1, 0)])
        lists = jnp.where(
            rank == 0, jnp.concatenate([lists, other]), jnp.concatenate([other, lists])
        )
    part = theta_band // shares
    table = lax.dynamic_slice_in_dim(translation, rank * part, part, axis=2)
    table = table.reshape(operator_total, -1)
    total = shares * per_group
    return couplings(lists, jnp.zeros((1,), jnp.int32), table, total, total)


def per_device(
    shares,
    up_weights,
    down_weights,
    coeffs,
    near_blocks,
    near_ids,
    near_count,
    radiation,
    partners,
    vector_ids,
    pair_count,
    translation,
):
    every = ("box", "theta", "phi")
    per_group = lax.axis_size("theta") * lax.axis_size("phi")
    rank = lax.axis_index(every).astype(jnp.int32).reshape(1)
    low = shift(coeffs, every, 1)
    spread = upward(coeffs, radiation, up_weights, shares * per_group)
    radiation_adjoint = adjoint(radiation)
    lists = lists_of(partners, vector_ids, pair_count)
    lines = translation_lines(lists, translation, shares, per_group)
    near = near_field(near_ids, near_count, rank, near_blocks, [low, coeffs], 0)
    parents = parent_bands(spread, shares)
    parents, near, late = lax.optimization_barrier((parents, near, coeffs))
    high = shift(late, every, -1)
    sources = [parents]
    if shares < lax.axis_size("box"):
        sources = [shift(parents, "box", 1), parents, shift(parents, "box", -1)]
    incoming = translate(lines, sources)
    field = parent_bands(incoming, shares)
    near = near_field(near_ids, near_count, rank, near_blocks, [high], 2, near)
    return downward(field, down_weights, radiation_adjoint, near)


def solution(mesh):
    box_size, theta_size, phi_size = (mesh.shape[axis] for axis in ("box", "theta", "phi"))
    shares = box_size if box_size <= 2 and TU // theta_size % box_size == 0 else 1
    up_weights, down_weights = operators(shares, theta_size, phi_size)
    in_specs = (
        P(),
        P(),
        P(("box", "theta", "phi"), None, None, None),
        P(("box", "theta", "phi"), None, None, None, None),
        P(("box", "theta", "phi"), None),
        P(("box", "theta", "phi")),
        P(("box", "theta", "phi"), None, None, None),
        P("box", None),
        P("box", None),
        P("box"),
        P(None, None, "theta", "phi"),
    )
    out_specs = P(("box", "theta", "phi"), None, None, None)
    mapped = jax.shard_map(
        functools.partial(per_device, shares),
        mesh=mesh,
        in_specs=in_specs,
        out_specs=out_specs,
        check_vma=False,
    )

    def product(*arrays):
        return mapped(jnp.asarray(up_weights), jnp.asarray(down_weights), *arrays)

    return product
```

```python
import functools
import math

import jax
import jax.numpy as jnp
import ml_dtypes
import numpy as np
from jax import lax
from jax.experimental import pallas as pl
from jax.experimental.pallas import tpu as pltpu
from jax.sharding import PartitionSpec as P

TL = 8
PL = 16
TU = 16
PU = 32

WEIGHT_UP = (-0.0546875, 0.8203125, 0.2734375, -0.0390625)
WEIGHT_DOWN = (-0.0390625, 0.2734375, 0.8203125, -0.0546875)
PHASE_SCALE = 1.3

F32 = jnp.float32
BF16 = jnp.bfloat16
MIB = 2**20
GROUP = 4
NOWHERE = -(2**20)


def lagrange(rows, columns, wrap):
    matrix = np.zeros((rows, columns))
    for row in range(rows):
        weights = WEIGHT_UP if row % 2 else WEIGHT_DOWN
        for order in range(4):
            node = row // 2 + row % 2 - 2 + order
            node = node % columns if wrap else min(max(node, 0), columns - 1)
            matrix[row, node] += weights[order]
    return matrix


def split_weights(matrix):
    high = matrix.astype(ml_dtypes.bfloat16)
    low = (matrix - high.astype(np.float64)).astype(ml_dtypes.bfloat16)
    return high, low


def operators(shares, theta_size, phi_size):
    theta_part = TU // theta_size // shares
    order = np.arange(TU * PU).reshape(theta_size, shares, theta_part, phi_size, PU // phi_size)
    order = order.transpose(1, 0, 3, 2, 4).reshape(-1)
    interp = np.kron(lagrange(TU, TL, False), lagrange(PU, PL, True))
    theta = math.pi * (np.arange(TU) + 0.5) / TU
    azimuth = 2.0 * math.pi * (np.arange(PU) + 0.5) / PU
    up, down = [], []
    for octant in range(4):
        sign_x = 2 * (octant % 2) - 1
        sign_y = 2 * (octant // 2 % 2) - 1
        sign_z = 2 * (octant // 4) - 1
        angle = PHASE_SCALE * (
            sign_x * np.sin(theta)[:, None] * np.cos(azimuth)[None]
            + sign_y * np.sin(theta)[:, None] * np.sin(azimuth)[None]
            + sign_z * np.cos(theta)[:, None]
        ).reshape(-1, 1)
        cos_high, cos_low = split_weights((np.cos(angle) * interp)[order])
        sin_high, sin_low = split_weights((np.sin(angle) * interp)[order])
        high = np.concatenate([cos_high, sin_high], axis=1)
        low = np.concatenate([cos_low, sin_low], axis=1)
        up.append(np.concatenate([high, low], axis=0))
        down.append(np.concatenate([cos_high.T, sin_high.T, cos_low.T, sin_low.T], axis=0))
    return np.concatenate(up, axis=1), np.stack(down)


def in_hbm(*arrays):
    return [pltpu.with_memory_space_constraint(array, pltpu.HBM) for array in arrays]


def dot(a, b):
    return jnp.dot(a, b, preferred_element_type=F32)


def complex_rows(real, imag):
    return jnp.concatenate(
        [
            jnp.concatenate([real, -imag], axis=1),
            jnp.concatenate([imag, real], axis=1),
        ],
        axis=0,
    )


def up_kernel(x_hbm, rad_hbm, w_hbm, out_hbm, x_ref, rad_ref, w_ref, right, result, sems):
    boxes, _, basis, rhs = x_ref.shape
    points = rad_ref.shape[2]
    copies = [
        pltpu.make_async_copy(source, target, sems.at[place])
        for place, (source, target) in enumerate(
            ((x_hbm, x_ref), (rad_hbm, rad_ref), (w_hbm, w_ref))
        )
    ]
    for copy in copies:
        copy.start()
    copies[0].wait()
    copies[1].wait()
    half = boxes // 2
    for octant in range(boxes):
        left = complex_rows(rad_ref[octant, 0], rad_ref[octant, 1])
        pattern = dot(left, x_ref[octant].reshape(2 * basis, rhs)).astype(BF16)
        real, imag = pattern[:points], pattern[points:]
        straight = jnp.concatenate([real, imag], axis=1)
        if octant < half:
            swapped = jnp.concatenate([-imag, real], axis=1)
        else:
            swapped = jnp.concatenate([imag, -real], axis=1)
        place = octant if octant < half else boxes - 1 - octant
        start = 2 * place * points
        right[octant // half, start : start + points] = straight
        right[octant // half, start + points : start + 2 * points] = swapped
    copies[2].wait()
    total = dot(w_ref[...], right[0]) + dot(w_ref[...], right[1])
    samples = total.shape[0] // 2
    total = total[:samples] + total[samples:]
    result[...] = total.astype(BF16).reshape(result.shape)
    pltpu.sync_copy(result, out_hbm)


def upward(coeffs, radiation, weights, groups):
    boxes, _, basis, rhs = coeffs.shape
    rows, columns = weights.shape
    samples = rows // 2
    hbm = pl.BlockSpec(memory_space=pltpu.HBM)
    return pl.pallas_call(
        up_kernel,
        in_specs=[hbm] * 3,
        out_specs=hbm,
        out_shape=pltpu.HBM((groups, samples // groups, 2 * rhs), BF16),
        scratch_shapes=[
            pltpu.VMEM(coeffs.shape, BF16),
            pltpu.VMEM(radiation.shape, BF16),
            pltpu.VMEM(weights.shape, BF16),
            pltpu.VMEM((2, columns, 2 * rhs), BF16),
            pltpu.VMEM((groups, samples // groups, 2 * rhs), BF16),
            pltpu.SemaphoreType.DMA((3,)),
        ],
        compiler_params=pltpu.CompilerParams(vmem_limit_bytes=32 * MIB),
        cost_estimate=pl.CostEstimate(
            flops=2 * 10**9, bytes_accessed=4 * MIB, transcendentals=0
        ),
        name="upward",
    )(*in_hbm(coeffs, radiation, weights))


def coupling_kernel(lists_ref, base_ref, table_ref, out_ref):
    rows = lists_ref.shape[0]
    samples = table_ref.shape[1] // 2
    _, targets, columns = out_ref.shape
    slots = rows // targets
    selector = (
        lax.broadcasted_iota(jnp.int32, (rows, table_ref.shape[0]), 1) == lists_ref[:, 1:2]
    )
    chosen = dot(selector.astype(BF16), table_ref[...]).astype(BF16)
    wide = lax.broadcasted_iota(jnp.int32, (rows, columns), 1) // samples
    match = wide + base_ref[0] == lists_ref[:, 0:1]
    spread = lax.broadcasted_iota(jnp.int32, (samples, columns), 0) == (
        lax.broadcasted_iota(jnp.int32, (samples, columns), 1) % samples
    )
    gather = (
        lax.broadcasted_iota(jnp.int32, (targets, rows), 1) // slots
        == lax.broadcasted_iota(jnp.int32, (targets, rows), 0)
    ).astype(BF16)
    tile = spread.astype(BF16)
    for part in range(2):
        lines = dot(chosen[:, part * samples : (part + 1) * samples], tile)
        out_ref[part] = dot(gather, jnp.where(match, lines, 0.0).astype(BF16))


def couplings(lists, base, table, targets, names):
    shape = (2, targets, names * (table.shape[1] // 2))
    vmem = pl.BlockSpec(memory_space=pltpu.VMEM)
    return pl.pallas_call(
        coupling_kernel,
        in_specs=[vmem, pl.BlockSpec(memory_space=pltpu.SMEM), vmem],
        out_specs=vmem,
        out_shape=jax.ShapeDtypeStruct(shape, F32),
        compiler_params=pltpu.CompilerParams(vmem_limit_bytes=16 * MIB),
        cost_estimate=pl.CostEstimate(
            flops=2 * 10**8, bytes_accessed=2 * 2**20, transcendentals=0
        ),
        name="coupling",
    )(lists, base, table)


def translate_kernel(lines_hbm, *refs):
    count = (len(refs) - 5) // 2
    sources, out_hbm = refs[:count], refs[count]
    held, lines, matrix, result, sems = refs[count + 1 :][:count], *refs[2 * count + 1 :]
    targets, samples, width = result.shape
    rhs = width // 2
    copies = [
        pltpu.make_async_copy(source, target, sems.at[place])
        for place, (source, target) in enumerate(zip((lines_hbm, *sources), (lines, *held)))
    ]
    for copy in copies:
        copy.start()
    copies[0].wait()
    columns = matrix.shape[1]
    row = lax.broadcasted_iota(jnp.int32, (samples, columns), 0)
    diagonal = row == lax.broadcasted_iota(jnp.int32, (samples, columns), 1) % samples
    for part in range(2):
        for target in range(targets):
            line = jnp.broadcast_to(lines[part, target : target + 1], diagonal.shape)
            start = (part * targets + target) * samples
            matrix[start : start + samples] = jnp.where(diagonal, line, 0.0).astype(BF16)
    total = None
    start = 0
    for place, source in enumerate(held):
        copies[1 + place].wait()
        stop = start + source.shape[0] * samples
        part = dot(matrix[:, start:stop], source[...].reshape(stop - start, width))
        total = part if total is None else total + part
        start = stop
    half = targets * samples
    real = total[:half, :rhs] - total[half:, rhs:]
    imag = total[:half, rhs:] + total[half:, :rhs]
    result[...] = jnp.concatenate([real, imag], axis=1).astype(BF16).reshape(result.shape)
    pltpu.sync_copy(result, out_hbm)


def translate(lines, sources):
    _, samples, width = sources[0].shape
    _, targets, columns = lines.shape
    shape = (targets, samples, width)
    hbm = pl.BlockSpec(memory_space=pltpu.HBM)
    return pl.pallas_call(
        translate_kernel,
        in_specs=[hbm] * (1 + len(sources)),
        out_specs=hbm,
        out_shape=pltpu.HBM(shape, BF16),
        scratch_shapes=[
            *[pltpu.VMEM(source.shape, BF16) for source in sources],
            pltpu.VMEM(lines.shape, F32),
            pltpu.VMEM((2 * targets * samples, columns), BF16),
            pltpu.VMEM(shape, BF16),
            pltpu.SemaphoreType.DMA((1 + len(sources),)),
        ],
        compiler_params=pltpu.CompilerParams(vmem_limit_bytes=24 * MIB),
        cost_estimate=pl.CostEstimate(
            flops=10**9, bytes_accessed=2 * MIB, transcendentals=0
        ),
        name="translate",
    )(*in_hbm(lines, *sources))


def near_kernel(first, count, begun, *refs):
    ids_ref, used_ref, rank_ref, blocks_hbm = refs[:4]
    sources = refs[4 : 4 + count]
    out_hbm, blocks, held, total_ref, listed, sems = refs[4 + count + begun :]
    boxes, slots, _, basis, _ = blocks.shape
    rhs = held.shape[3]
    base = (rank_ref[0] - 1 + first) * boxes
    source_copies = [
        pltpu.make_async_copy(source, held.at[pl.ds(place * boxes, boxes)], sems.at[boxes + place])
        for place, source in enumerate(sources)
    ]

    def block_copy(box):
        return pltpu.make_async_copy(blocks_hbm.at[box], blocks.at[box], sems.at[box])

    def result_copy(box, inward):
        place = boxes + count + box
        if inward:
            return pltpu.make_async_copy(refs[4 + count].at[box], total_ref.at[box], sems.at[place])
        return pltpu.make_async_copy(total_ref.at[box], out_hbm.at[box], sems.at[place])

    for copy in source_copies:
        copy.start()
    for box in range(boxes):
        block_copy(box).start()
        if begun:
            result_copy(box, True).start()
    for copy in source_copies:
        copy.wait()

    def one_box(box, carry):
        total = jnp.int32(0)
        used = used_ref[box]
        for slot in range(slots):
            place = ids_ref[box, slot] - base
            listed[total] = jnp.int32(slot)
            wanted = (slot < used) & (place >= 0) & (place < count * boxes)
            total += wanted.astype(jnp.int32)
        block_copy(box).wait()
        if begun:
            result_copy(box, True).wait()
        else:
            total_ref[box] = jnp.zeros(total_ref.shape[1:], F32)

        def group(index, carry):
            left, right = [], []
            for step in range(GROUP):
                at = index * GROUP + step
                slot = listed[jnp.minimum(at, total - 1)]
                real, imag = blocks[box, slot, 0], blocks[box, slot, 1]
                if step:
                    real = jnp.where(at < total, real, jnp.zeros_like(real))
                    imag = jnp.where(at < total, imag, jnp.zeros_like(imag))
                left.append(complex_rows(real, imag))
                right.append(held[ids_ref[box, slot] - base].reshape(2 * basis, rhs))
            part = dot(jnp.concatenate(left, axis=1), jnp.concatenate(right, axis=0))
            total_ref[box] += part.reshape(2, basis, rhs)
            return carry

        lax.fori_loop(0, (total + GROUP - 1) // GROUP, group, 0)
        result_copy(box, False).start()
        return carry

    lax.fori_loop(0, boxes, one_box, 0)
    for box in range(boxes):
        result_copy(box, False).wait()


def near_field(ids, used, rank, blocks, sources, first, before=None):
    boxes, slots, _, basis, _ = blocks.shape
    rhs = sources[0].shape[3]
    count = len(sources)
    begun = before is not None
    hbm = pl.BlockSpec(memory_space=pltpu.HBM)
    smem = pl.BlockSpec(memory_space=pltpu.SMEM)
    return pl.pallas_call(
        functools.partial(near_kernel, first, count, begun),
        in_specs=[smem] * 3 + [hbm] * (1 + count + begun),
        out_specs=hbm,
        out_shape=pltpu.HBM((boxes, 2, basis, rhs), F32),
        scratch_shapes=[
            pltpu.VMEM(blocks.shape, BF16),
            pltpu.VMEM((count * boxes, 2, basis, rhs), BF16),
            pltpu.VMEM((boxes, 2, basis, rhs), F32),
            pltpu.SMEM((slots + 1,), jnp.int32),
            pltpu.SemaphoreType.DMA((2 * boxes + count,)),
        ],
        compiler_params=pltpu.CompilerParams(vmem_limit_bytes=24 * MIB),
        cost_estimate=pl.CostEstimate(
            flops=10**11 if begun else 2 * 10**9, bytes_accessed=8 * MIB, transcendentals=0
        ),
        name="near_last" if begun else "near_first",
    )(ids, used, rank, *in_hbm(blocks, *sources, *([before] if begun else [])))


def adjoint_kernel(rad_ref, out_hbm, held):
    for box in range(rad_ref.shape[0]):
        held[box] = complex_rows(rad_ref[box, 0], rad_ref[box, 1]).T
    pltpu.sync_copy(held, out_hbm)


def adjoint(radiation):
    boxes, _, points, basis = radiation.shape
    return pl.pallas_call(
        adjoint_kernel,
        in_specs=[pl.BlockSpec(memory_space=pltpu.VMEM)],
        out_specs=pl.BlockSpec(memory_space=pltpu.HBM),
        scratch_shapes=[pltpu.VMEM((boxes, 2 * basis, 2 * points), BF16)],
        out_shape=pltpu.HBM((boxes, 2 * basis, 2 * points), BF16),
        cost_estimate=pl.CostEstimate(
            flops=10**6, bytes_accessed=2 * MIB, transcendentals=0
        ),
        name="adjoint",
    )(radiation)


def down_kernel(field_hbm, w_hbm, adjoint_hbm, near_hbm, out_hbm, field, w, left, held, sems):
    boxes, width, _ = left.shape
    points = width // 2
    samples = w.shape[2]
    basis, rhs = held.shape[2], held.shape[3]
    half = boxes // 2
    field_copy = pltpu.make_async_copy(field_hbm, field, sems.at[0])
    w_copies, left_copies, near_copies, out_copies = [], [], [], []
    for pair in range(half):
        w_copies.append(pltpu.make_async_copy(w_hbm.at[pair], w.at[pair], sems.at[1 + pair]))
    for box in range(boxes):
        places = [1 + half + turn * boxes + box for turn in range(3)]
        left_copies.append(
            pltpu.make_async_copy(adjoint_hbm.at[box], left.at[box], sems.at[places[0]])
        )
        near_copies.append(
            pltpu.make_async_copy(near_hbm.at[box], held.at[box], sems.at[places[1]])
        )
        out_copies.append(
            pltpu.make_async_copy(held.at[box], out_hbm.at[box], sems.at[places[2]])
        )
    field_copy.start()
    for pair in range(half):
        w_copies[pair].start()
    for pair in range(half):
        for box in (pair, boxes - 1 - pair):
            left_copies[box].start()
            near_copies[box].start()
    field_copy.wait()
    for first in range(0, half, 2):
        for pair in (first, first + 1):
            w_copies[pair].wait()
        rows = w.shape[1]
        mixed = dot(
            w[first : first + 2].reshape(2 * rows, samples), field[...].reshape(samples, 2 * rhs)
        )
        for pair in (first, first + 1):
            part = mixed[(pair - first) * rows : (pair - first + 1) * rows]
            part = part[: rows // 2] + part[rows // 2 :]
            cos_re, cos_im = part[:points, :rhs], part[:points, rhs:]
            sin_re, sin_im = part[points:, :rhs], part[points:, rhs:]
            leaves = (
                (pair, cos_re + sin_im, cos_im - sin_re),
                (boxes - 1 - pair, cos_re - sin_im, cos_im + sin_re),
            )
            for box, real, imag in leaves:
                leaf = jnp.concatenate([real, imag], axis=0).astype(BF16)
                left_copies[box].wait()
                far = dot(left[box], leaf)
                near_copies[box].wait()
                held[box] += far.reshape(2, basis, rhs)
                out_copies[box].start()
    for copy in out_copies:
        copy.wait()


def downward(field, weights, radiation_adjoint, near):
    boxes = near.shape[0]
    hbm = pl.BlockSpec(memory_space=pltpu.HBM)
    return pl.pallas_call(
        down_kernel,
        in_specs=[hbm] * 4,
        out_specs=hbm,
        out_shape=jax.ShapeDtypeStruct(near.shape, F32),
        scratch_shapes=[
            pltpu.VMEM(field.shape, BF16),
            pltpu.VMEM(weights.shape, BF16),
            pltpu.VMEM(radiation_adjoint.shape, BF16),
            pltpu.VMEM(near.shape, F32),
            pltpu.SemaphoreType.DMA((1 + boxes // 2 + 3 * boxes,)),
        ],
        compiler_params=pltpu.CompilerParams(vmem_limit_bytes=32 * MIB),
        cost_estimate=pl.CostEstimate(
            flops=2 * 10**9, bytes_accessed=7 * MIB, transcendentals=0
        ),
        name="downward",
    )(*in_hbm(field, weights, radiation_adjoint, near))


def shift(block, axis, step):
    count = lax.axis_size(axis)
    pairs = [(i, i + step) for i in range(count) if 0 <= i + step < count]
    return lax.ppermute(block, axis, pairs)


def lists_of(partners, vector_ids, pair_count):
    used = jnp.arange(partners.shape[1])[None, :] < pair_count[:, None]
    names = jnp.where(used, partners, NOWHERE)
    return jnp.stack([names, vector_ids], axis=2).reshape(-1, 2)


def parent_bands(spread, shares):
    axes = ("box", "theta", "phi") if shares == lax.axis_size("box") else ("theta", "phi")
    return lax.all_to_all(spread, axes, split_axis=0, concat_axis=0, tiled=True)


def translation_lines(lists, translation, shares, per_group):
    operator_total, _, theta_band, phi_band = translation.shape
    rank = lax.axis_index("box")
    if shares < lax.axis_size("box"):
        table = translation.reshape(operator_total, -1)
        base = ((rank - 1) * per_group).astype(jnp.int32).reshape(1)
        return couplings(lists, base, table, per_group, 3 * per_group)
    if shares == 2:
        other = lax.ppermute(lists, "box", [(0, 1), (1, 0)])
        lists = jnp.where(
            rank == 0, jnp.concatenate([lists, other]), jnp.concatenate([other, lists])
        )
    part = theta_band // shares
    table = lax.dynamic_slice_in_dim(translation, rank * part, part, axis=2)
    table = table.reshape(operator_total, -1)
    total = shares * per_group
    return couplings(lists, jnp.zeros((1,), jnp.int32), table, total, total)


def per_device(
    shares,
    up_weights,
    down_weights,
    coeffs,
    near_blocks,
    near_ids,
    near_count,
    radiation,
    partners,
    vector_ids,
    pair_count,
    translation,
):
    every = ("box", "theta", "phi")
    per_group = lax.axis_size("theta") * lax.axis_size("phi")
    rank = lax.axis_index(every).astype(jnp.int32).reshape(1)
    low = shift(coeffs, every, 1)
    spread = upward(coeffs, radiation, up_weights, shares * per_group)
    radiation_adjoint = adjoint(radiation)
    lists = lists_of(partners, vector_ids, pair_count)
    lines = translation_lines(lists, translation, shares, per_group)
    rank, lines, radiation_adjoint = lax.optimization_barrier((rank, lines, radiation_adjoint))
    low, late = lax.optimization_barrier((low, coeffs))
    high = shift(late, every, -1)
    near = near_field(near_ids, near_count, rank, near_blocks, [low, coeffs], 0)
    parents = parent_bands(spread, shares)
    parents, near = lax.optimization_barrier((parents, near))
    sources = [parents]
    if shares < lax.axis_size("box"):
        sources = [shift(parents, "box", 1), parents, shift(parents, "box", -1)]
    incoming = translate(lines, sources)
    field = parent_bands(incoming, shares)
    near = near_field(near_ids, near_count, rank, near_blocks, [high], 2, near)
    return downward(field, down_weights, radiation_adjoint, near)


def solution(mesh):
    box_size, theta_size, phi_size = (mesh.shape[axis] for axis in ("box", "theta", "phi"))
    shares = box_size if box_size <= 2 and TU // theta_size % box_size == 0 else 1
    up_weights, down_weights = operators(shares, theta_size, phi_size)
    in_specs = (
        P(),
        P(),
        P(("box", "theta", "phi"), None, None, None),
        P(("box", "theta", "phi"), None, None, None, None),
        P(("box", "theta", "phi"), None),
        P(("box", "theta", "phi")),
        P(("box", "theta", "phi"), None, None, None),
        P("box", None),
        P("box", None),
        P("box"),
        P(None, None, "theta", "phi"),
    )
    out_specs = P(("box", "theta", "phi"), None, None, None)
    mapped = jax.shard_map(
        functools.partial(per_device, shares),
        mesh=mesh,
        in_specs=in_specs,
        out_specs=out_specs,
        check_vma=False,
    )

    def product(*arrays):
        return mapped(jnp.asarray(up_weights), jnp.asarray(down_weights), *arrays)

    return product
```

```python
import functools
import math

import jax
import jax.numpy as jnp
import ml_dtypes
import numpy as np
from jax import lax
from jax.experimental import pallas as pl
from jax.experimental.pallas import tpu as pltpu
from jax.sharding import PartitionSpec as P

TL = 8
PL = 16
TU = 16
PU = 32

WEIGHT_UP = (-0.0546875, 0.8203125, 0.2734375, -0.0390625)
WEIGHT_DOWN = (-0.0390625, 0.2734375, 0.8203125, -0.0546875)
PHASE_SCALE = 1.3

F32 = jnp.float32
BF16 = jnp.bfloat16
MIB = 2**20
GROUP = 4
NOWHERE = -(2**20)


def lagrange(rows, columns, wrap):
    matrix = np.zeros((rows, columns))
    for row in range(rows):
        weights = WEIGHT_UP if row % 2 else WEIGHT_DOWN
        for order in range(4):
            node = row // 2 + row % 2 - 2 + order
            node = node % columns if wrap else min(max(node, 0), columns - 1)
            matrix[row, node] += weights[order]
    return matrix


def split_weights(matrix):
    high = matrix.astype(ml_dtypes.bfloat16)
    low = (matrix - high.astype(np.float64)).astype(ml_dtypes.bfloat16)
    return high, low


def operators(shares, theta_size, phi_size):
    theta_part = TU // theta_size // shares
    order = np.arange(TU * PU).reshape(theta_size, shares, theta_part, phi_size, PU // phi_size)
    order = order.transpose(1, 0, 3, 2, 4).reshape(-1)
    interp = np.kron(lagrange(TU, TL, False), lagrange(PU, PL, True))
    theta = math.pi * (np.arange(TU) + 0.5) / TU
    azimuth = 2.0 * math.pi * (np.arange(PU) + 0.5) / PU
    up, down = [], []
    for octant in range(4):
        sign_x = 2 * (octant % 2) - 1
        sign_y = 2 * (octant // 2 % 2) - 1
        sign_z = 2 * (octant // 4) - 1
        angle = PHASE_SCALE * (
            sign_x * np.sin(theta)[:, None] * np.cos(azimuth)[None]
            + sign_y * np.sin(theta)[:, None] * np.sin(azimuth)[None]
            + sign_z * np.cos(theta)[:, None]
        ).reshape(-1, 1)
        cos_high, cos_low = split_weights((np.cos(angle) * interp)[order])
        sin_high, sin_low = split_weights((np.sin(angle) * interp)[order])
        high = np.concatenate([cos_high, sin_high], axis=1)
        low = np.concatenate([cos_low, sin_low], axis=1)
        up.append(np.concatenate([high, low], axis=0))
        down += [cos_high.T, sin_high.T]
    return np.concatenate(up, axis=1), np.concatenate(down, axis=0)


def in_hbm(*arrays):
    return [pltpu.with_memory_space_constraint(array, pltpu.HBM) for array in arrays]


def dot(a, b):
    return jnp.dot(a, b, preferred_element_type=F32)


def complex_rows(real, imag):
    return jnp.concatenate(
        [
            jnp.concatenate([real, -imag], axis=1),
            jnp.concatenate([imag, real], axis=1),
        ],
        axis=0,
    )


def up_kernel(x_hbm, rad_hbm, w_hbm, out_hbm, x_ref, rad_ref, w_ref, right, result, sems):
    boxes, _, basis, rhs = x_ref.shape
    points = rad_ref.shape[2]
    copies = [
        pltpu.make_async_copy(source, target, sems.at[place])
        for place, (source, target) in enumerate(
            ((x_hbm, x_ref), (rad_hbm, rad_ref), (w_hbm, w_ref))
        )
    ]
    for copy in copies:
        copy.start()
    copies[0].wait()
    copies[1].wait()
    half = boxes // 2
    for octant in range(boxes):
        left = complex_rows(rad_ref[octant, 0], rad_ref[octant, 1])
        pattern = dot(left, x_ref[octant].reshape(2 * basis, rhs)).astype(BF16)
        real, imag = pattern[:points], pattern[points:]
        straight = jnp.concatenate([real, imag], axis=1)
        if octant < half:
            swapped = jnp.concatenate([-imag, real], axis=1)
        else:
            swapped = jnp.concatenate([imag, -real], axis=1)
        place = octant if octant < half else boxes - 1 - octant
        start = 2 * place * points
        right[octant // half, start : start + points] = straight
        right[octant // half, start + points : start + 2 * points] = swapped
    copies[2].wait()
    total = dot(w_ref[...], right[0]) + dot(w_ref[...], right[1])
    samples = total.shape[0] // 2
    total = total[:samples] + total[samples:]
    result[...] = total.astype(BF16).reshape(result.shape)
    pltpu.sync_copy(result, out_hbm)


def upward(coeffs, radiation, weights, groups):
    boxes, _, basis, rhs = coeffs.shape
    rows, columns = weights.shape
    samples = rows // 2
    hbm = pl.BlockSpec(memory_space=pltpu.HBM)
    return pl.pallas_call(
        up_kernel,
        in_specs=[hbm] * 3,
        out_specs=hbm,
        out_shape=pltpu.HBM((groups, samples // groups, 2 * rhs), BF16),
        scratch_shapes=[
            pltpu.VMEM(coeffs.shape, BF16),
            pltpu.VMEM(radiation.shape, BF16),
            pltpu.VMEM(weights.shape, BF16),
            pltpu.VMEM((2, columns, 2 * rhs), BF16),
            pltpu.VMEM((groups, samples // groups, 2 * rhs), BF16),
            pltpu.SemaphoreType.DMA((3,)),
        ],
        compiler_params=pltpu.CompilerParams(vmem_limit_bytes=32 * MIB),
        cost_estimate=pl.CostEstimate(
            flops=2 * 10**9, bytes_accessed=4 * MIB, transcendentals=0
        ),
        name="upward",
    )(*in_hbm(coeffs, radiation, weights))


def coupling_kernel(lists_ref, base_ref, table_ref, out_ref):
    rows = lists_ref.shape[0]
    samples = table_ref.shape[1] // 2
    _, targets, columns = out_ref.shape
    slots = rows // targets
    selector = (
        lax.broadcasted_iota(jnp.int32, (rows, table_ref.shape[0]), 1) == lists_ref[:, 1:2]
    )
    chosen = dot(selector.astype(BF16), table_ref[...]).astype(BF16)
    wide = lax.broadcasted_iota(jnp.int32, (rows, columns), 1) // samples
    match = wide + base_ref[0] == lists_ref[:, 0:1]
    spread = lax.broadcasted_iota(jnp.int32, (samples, columns), 0) == (
        lax.broadcasted_iota(jnp.int32, (samples, columns), 1) % samples
    )
    gather = (
        lax.broadcasted_iota(jnp.int32, (targets, rows), 1) // slots
        == lax.broadcasted_iota(jnp.int32, (targets, rows), 0)
    ).astype(BF16)
    tile = spread.astype(BF16)
    for part in range(2):
        lines = dot(chosen[:, part * samples : (part + 1) * samples], tile)
        out_ref[part] = dot(gather, jnp.where(match, lines, 0.0).astype(BF16))


def couplings(lists, base, table, targets, names):
    shape = (2, targets, names * (table.shape[1] // 2))
    vmem = pl.BlockSpec(memory_space=pltpu.VMEM)
    return pl.pallas_call(
        coupling_kernel,
        in_specs=[vmem, pl.BlockSpec(memory_space=pltpu.SMEM), vmem],
        out_specs=vmem,
        out_shape=jax.ShapeDtypeStruct(shape, F32),
        compiler_params=pltpu.CompilerParams(vmem_limit_bytes=16 * MIB),
        cost_estimate=pl.CostEstimate(
            flops=2 * 10**8, bytes_accessed=2 * 2**20, transcendentals=0
        ),
        name="coupling",
    )(lists, base, table)


def translate_kernel(lines_hbm, *refs):
    count = (len(refs) - 5) // 2
    sources, out_hbm = refs[:count], refs[count]
    held, lines, matrix, result, sems = refs[count + 1 :][:count], *refs[2 * count + 1 :]
    targets, samples, width = result.shape
    rhs = width // 2
    copies = [
        pltpu.make_async_copy(source, target, sems.at[place])
        for place, (source, target) in enumerate(zip((lines_hbm, *sources), (lines, *held)))
    ]
    for copy in copies:
        copy.start()
    copies[0].wait()
    columns = matrix.shape[1]
    row = lax.broadcasted_iota(jnp.int32, (samples, columns), 0)
    diagonal = row == lax.broadcasted_iota(jnp.int32, (samples, columns), 1) % samples
    for part in range(2):
        for target in range(targets):
            line = jnp.broadcast_to(lines[part, target : target + 1], diagonal.shape)
            start = (part * targets + target) * samples
            matrix[start : start + samples] = jnp.where(diagonal, line, 0.0).astype(BF16)
    total = None
    start = 0
    for place, source in enumerate(held):
        copies[1 + place].wait()
        stop = start + source.shape[0] * samples
        part = dot(matrix[:, start:stop], source[...].reshape(stop - start, width))
        total = part if total is None else total + part
        start = stop
    half = targets * samples
    real = total[:half, :rhs] - total[half:, rhs:]
    imag = total[:half, rhs:] + total[half:, :rhs]
    result[...] = jnp.concatenate([real, imag], axis=1).astype(BF16).reshape(result.shape)
    pltpu.sync_copy(result, out_hbm)


def translate(lines, sources):
    _, samples, width = sources[0].shape
    _, targets, columns = lines.shape
    shape = (targets, samples, width)
    hbm = pl.BlockSpec(memory_space=pltpu.HBM)
    anywhere = pl.BlockSpec(memory_space=pl.ANY)
    return pl.pallas_call(
        translate_kernel,
        in_specs=[hbm] + [anywhere] * len(sources),
        out_specs=hbm,
        out_shape=pltpu.HBM(shape, BF16),
        scratch_shapes=[
            *[pltpu.VMEM(source.shape, BF16) for source in sources],
            pltpu.VMEM(lines.shape, F32),
            pltpu.VMEM((2 * targets * samples, columns), BF16),
            pltpu.VMEM(shape, BF16),
            pltpu.SemaphoreType.DMA((1 + len(sources),)),
        ],
        compiler_params=pltpu.CompilerParams(vmem_limit_bytes=24 * MIB),
        cost_estimate=pl.CostEstimate(
            flops=10**9, bytes_accessed=2 * MIB, transcendentals=0
        ),
        name="translate",
    )(*in_hbm(lines), *sources)


def near_kernel(first, count, begun, *refs):
    ids_ref, used_ref, rank_ref, blocks_hbm = refs[:4]
    sources = refs[4 : 4 + count]
    out_hbm, blocks, held, total_ref, listed, sems = refs[4 + count + begun :]
    boxes, slots, _, basis, _ = blocks.shape
    rhs = held.shape[3]
    base = (rank_ref[0] - 1 + first) * boxes
    source_copies = [
        pltpu.make_async_copy(source, held.at[pl.ds(place * boxes, boxes)], sems.at[boxes + place])
        for place, source in enumerate(sources)
    ]

    def block_copy(box):
        return pltpu.make_async_copy(blocks_hbm.at[box], blocks.at[box], sems.at[box])

    def result_copy(box, inward):
        place = boxes + count + box
        if inward:
            return pltpu.make_async_copy(refs[4 + count].at[box], total_ref.at[box], sems.at[place])
        return pltpu.make_async_copy(total_ref.at[box], out_hbm.at[box], sems.at[place])

    for copy in source_copies:
        copy.start()
    for box in range(boxes):
        block_copy(box).start()
        if begun:
            result_copy(box, True).start()
    for copy in source_copies:
        copy.wait()

    def one_box(box, carry):
        total = jnp.int32(0)
        used = used_ref[box]
        for slot in range(slots):
            place = ids_ref[box, slot] - base
            listed[total] = jnp.int32(slot)
            wanted = (slot < used) & (place >= 0) & (place < count * boxes)
            total += wanted.astype(jnp.int32)
        block_copy(box).wait()
        if begun:
            result_copy(box, True).wait()
        else:
            total_ref[box] = jnp.zeros(total_ref.shape[1:], F32)

        def group(index, carry):
            left, right = [], []
            for step in range(GROUP):
                at = index * GROUP + step
                slot = listed[jnp.minimum(at, total - 1)]
                real, imag = blocks[box, slot, 0], blocks[box, slot, 1]
                if step:
                    real = jnp.where(at < total, real, jnp.zeros_like(real))
                    imag = jnp.where(at < total, imag, jnp.zeros_like(imag))
                left.append(complex_rows(real, imag))
                right.append(held[ids_ref[box, slot] - base].reshape(2 * basis, rhs))
            part = dot(jnp.concatenate(left, axis=1), jnp.concatenate(right, axis=0))
            total_ref[box] += part.reshape(2, basis, rhs)
            return carry

        lax.fori_loop(0, (total + GROUP - 1) // GROUP, group, 0)
        result_copy(box, False).start()
        return carry

    lax.fori_loop(0, boxes, one_box, 0)
    for box in range(boxes):
        result_copy(box, False).wait()


def near_field(ids, used, rank, blocks, sources, first, before=None):
    boxes, slots, _, basis, _ = blocks.shape
    rhs = sources[0].shape[3]
    count = len(sources)
    begun = before is not None
    hbm = pl.BlockSpec(memory_space=pltpu.HBM)
    smem = pl.BlockSpec(memory_space=pltpu.SMEM)
    return pl.pallas_call(
        functools.partial(near_kernel, first, count, begun),
        in_specs=[smem] * 3 + [hbm] * (1 + count + begun),
        out_specs=hbm,
        out_shape=pltpu.HBM((boxes, 2, basis, rhs), F32),
        scratch_shapes=[
            pltpu.VMEM(blocks.shape, BF16),
            pltpu.VMEM((count * boxes, 2, basis, rhs), BF16),
            pltpu.VMEM((boxes, 2, basis, rhs), F32),
            pltpu.SMEM((slots + 1,), jnp.int32),
            pltpu.SemaphoreType.DMA((2 * boxes + count,)),
        ],
        compiler_params=pltpu.CompilerParams(vmem_limit_bytes=24 * MIB),
        cost_estimate=pl.CostEstimate(
            flops=10**11 if begun else 2 * 10**9, bytes_accessed=8 * MIB, transcendentals=0
        ),
        name="near_last" if begun else "near_first",
    )(ids, used, rank, *in_hbm(blocks, *sources, *([before] if begun else [])))


def adjoint_kernel(rad_ref, out_hbm, held):
    for box in range(rad_ref.shape[0]):
        held[box] = complex_rows(rad_ref[box, 0], rad_ref[box, 1]).T
    pltpu.sync_copy(held, out_hbm)


def adjoint(radiation):
    boxes, _, points, basis = radiation.shape
    return pl.pallas_call(
        adjoint_kernel,
        in_specs=[pl.BlockSpec(memory_space=pltpu.VMEM)],
        out_specs=pl.BlockSpec(memory_space=pltpu.HBM),
        scratch_shapes=[pltpu.VMEM((boxes, 2 * basis, 2 * points), BF16)],
        out_shape=pltpu.HBM((boxes, 2 * basis, 2 * points), BF16),
        cost_estimate=pl.CostEstimate(
            flops=10**6, bytes_accessed=2 * MIB, transcendentals=0
        ),
        name="adjoint",
    )(radiation)


def down_kernel(field_ref, w_hbm, adjoint_hbm, near_hbm, out_hbm, field, w, left, held, sems):
    boxes, width, _ = left.shape
    points = width // 2
    basis, rhs = held.shape[2], held.shape[3]
    copies = [
        pltpu.make_async_copy(source, target, sems.at[boxes + place])
        for place, (source, target) in enumerate(
            ((field_ref, field), (w_hbm, w), (adjoint_hbm, left), (near_hbm, held))
        )
    ]
    out_copies = [
        pltpu.make_async_copy(held.at[box], out_hbm.at[box], sems.at[box]) for box in range(boxes)
    ]
    for copy in copies:
        copy.start()
    for copy in copies[:2]:
        copy.wait()
    mixed = dot(w[...], field[...].reshape(w.shape[1], 2 * rhs))
    for copy in copies[2:]:
        copy.wait()
    for octant in range(boxes // 2):
        start = 2 * octant * points
        cos_part = mixed[start : start + points]
        sin_part = mixed[start + points : start + 2 * points]
        cos_re, cos_im = cos_part[:, :rhs], cos_part[:, rhs:]
        sin_re, sin_im = sin_part[:, :rhs], sin_part[:, rhs:]
        leaves = (
            (octant, cos_re + sin_im, cos_im - sin_re),
            (boxes - 1 - octant, cos_re - sin_im, cos_im + sin_re),
        )
        for box, real, imag in leaves:
            leaf = jnp.concatenate([real, imag], axis=0).astype(BF16)
            held[box] += dot(left[box], leaf).reshape(2, basis, rhs)
            out_copies[box].start()
    for copy in out_copies:
        copy.wait()


def downward(field, weights, radiation_adjoint, near):
    boxes = near.shape[0]
    hbm = pl.BlockSpec(memory_space=pltpu.HBM)
    return pl.pallas_call(
        down_kernel,
        in_specs=[pl.BlockSpec(memory_space=pl.ANY)] + [hbm] * 3,
        out_specs=hbm,
        out_shape=jax.ShapeDtypeStruct(near.shape, F32),
        scratch_shapes=[
            pltpu.VMEM(field.shape, BF16),
            pltpu.VMEM(weights.shape, BF16),
            pltpu.VMEM(radiation_adjoint.shape, BF16),
            pltpu.VMEM(near.shape, F32),
            pltpu.SemaphoreType.DMA((boxes + 4,)),
        ],
        compiler_params=pltpu.CompilerParams(vmem_limit_bytes=32 * MIB),
        cost_estimate=pl.CostEstimate(
            flops=2 * 10**9, bytes_accessed=7 * MIB, transcendentals=0
        ),
        name="downward",
    )(field, *in_hbm(weights, radiation_adjoint, near))


def shift(block, axis, step):
    count = lax.axis_size(axis)
    pairs = [(i, i + step) for i in range(count) if 0 <= i + step < count]
    return lax.ppermute(block, axis, pairs)


def lists_of(partners, vector_ids, pair_count):
    used = jnp.arange(partners.shape[1])[None, :] < pair_count[:, None]
    names = jnp.where(used, partners, NOWHERE)
    return jnp.stack([names, vector_ids], axis=2).reshape(-1, 2)


def parent_bands(spread, shares):
    axes = ("box", "theta", "phi") if shares == lax.axis_size("box") else ("theta", "phi")
    return lax.all_to_all(spread, axes, split_axis=0, concat_axis=0, tiled=True)


def translation_lines(lists, translation, shares, per_group):
    operator_total, _, theta_band, phi_band = translation.shape
    rank = lax.axis_index("box")
    if shares < lax.axis_size("box"):
        table = translation.reshape(operator_total, -1)
        base = ((rank - 1) * per_group).astype(jnp.int32).reshape(1)
        return couplings(lists, base, table, per_group, 3 * per_group)
    if shares == 2:
        other = lax.ppermute(lists, "box", [(0, 1), (1, 0)])
        lists = jnp.where(
            rank == 0, jnp.concatenate([lists, other]), jnp.concatenate([other, lists])
        )
    part = theta_band // shares
    table = lax.dynamic_slice_in_dim(translation, rank * part, part, axis=2)
    table = table.reshape(operator_total, -1)
    total = shares * per_group
    return couplings(lists, jnp.zeros((1,), jnp.int32), table, total, total)


def per_device(
    shares,
    up_weights,
    down_weights,
    coeffs,
    near_blocks,
    near_ids,
    near_count,
    radiation,
    partners,
    vector_ids,
    pair_count,
    translation,
):
    every = ("box", "theta", "phi")
    per_group = lax.axis_size("theta") * lax.axis_size("phi")
    rank = lax.axis_index(every).astype(jnp.int32).reshape(1)
    low = shift(coeffs, every, 1)
    spread = upward(coeffs, radiation, up_weights, shares * per_group)
    radiation_adjoint = adjoint(radiation)
    lists = lists_of(partners, vector_ids, pair_count)
    lines = translation_lines(lists, translation, shares, per_group)
    spread, lines, radiation_adjoint = lax.optimization_barrier((spread, lines, radiation_adjoint))
    parents = parent_bands(spread, shares)
    parents, low, late = lax.optimization_barrier((parents, low, coeffs))
    high = shift(late, every, -1)
    sources = [parents]
    if shares < lax.axis_size("box"):
        sources = [shift(parents, "box", 1), parents, shift(parents, "box", -1)]
    incoming = translate(lines, sources)
    incoming, low = lax.optimization_barrier((incoming, low))
    field = parent_bands(incoming, shares)
    near = near_field(near_ids, near_count, rank, near_blocks, [low, coeffs], 0)
    near = near_field(near_ids, near_count, rank, near_blocks, [high], 2, near)
    return downward(field, down_weights, radiation_adjoint, near)


def solution(mesh):
    box_size, theta_size, phi_size = (mesh.shape[axis] for axis in ("box", "theta", "phi"))
    shares = box_size if box_size <= 2 and TU // theta_size % box_size == 0 else 1
    up_weights, down_weights = operators(shares, theta_size, phi_size)
    in_specs = (
        P(),
        P(),
        P(("box", "theta", "phi"), None, None, None),
        P(("box", "theta", "phi"), None, None, None, None),
        P(("box", "theta", "phi"), None),
        P(("box", "theta", "phi")),
        P(("box", "theta", "phi"), None, None, None),
        P("box", None),
        P("box", None),
        P("box"),
        P(None, None, "theta", "phi"),
    )
    out_specs = P(("box", "theta", "phi"), None, None, None)
    mapped = jax.shard_map(
        functools.partial(per_device, shares),
        mesh=mesh,
        in_specs=in_specs,
        out_specs=out_specs,
        check_vma=False,
    )

    def product(*arrays):
        return mapped(jnp.asarray(up_weights), jnp.asarray(down_weights), *arrays)

    return product
```

```python
import functools
import math

import jax
import jax.numpy as jnp
import ml_dtypes
import numpy as np
from jax import lax
from jax.experimental import pallas as pl
from jax.experimental.pallas import tpu as pltpu
from jax.sharding import PartitionSpec as P

TL = 8
PL = 16
TU = 16
PU = 32

WEIGHT_UP = (-0.0546875, 0.8203125, 0.2734375, -0.0390625)
WEIGHT_DOWN = (-0.0390625, 0.2734375, 0.8203125, -0.0546875)
PHASE_SCALE = 1.3

F32 = jnp.float32
BF16 = jnp.bfloat16
MIB = 2**20
GROUP = 4
NOWHERE = -(2**20)


def lagrange(rows, columns, wrap):
    matrix = np.zeros((rows, columns))
    for row in range(rows):
        weights = WEIGHT_UP if row % 2 else WEIGHT_DOWN
        for order in range(4):
            node = row // 2 + row % 2 - 2 + order
            node = node % columns if wrap else min(max(node, 0), columns - 1)
            matrix[row, node] += weights[order]
    return matrix


def split_weights(matrix):
    high = matrix.astype(ml_dtypes.bfloat16)
    low = (matrix - high.astype(np.float64)).astype(ml_dtypes.bfloat16)
    return high, low


def operators(shares, theta_size, phi_size):
    theta_part = TU // theta_size // shares
    order = np.arange(TU * PU).reshape(theta_size, shares, theta_part, phi_size, PU // phi_size)
    order = order.transpose(1, 0, 3, 2, 4).reshape(-1)
    interp = np.kron(lagrange(TU, TL, False), lagrange(PU, PL, True))
    theta = math.pi * (np.arange(TU) + 0.5) / TU
    azimuth = 2.0 * math.pi * (np.arange(PU) + 0.5) / PU
    up, down = [], []
    for octant in range(4):
        sign_x = 2 * (octant % 2) - 1
        sign_y = 2 * (octant // 2 % 2) - 1
        sign_z = 2 * (octant // 4) - 1
        angle = PHASE_SCALE * (
            sign_x * np.sin(theta)[:, None] * np.cos(azimuth)[None]
            + sign_y * np.sin(theta)[:, None] * np.sin(azimuth)[None]
            + sign_z * np.cos(theta)[:, None]
        ).reshape(-1, 1)
        cos_high, cos_low = split_weights((np.cos(angle) * interp)[order])
        sin_high, sin_low = split_weights((np.sin(angle) * interp)[order])
        high = np.concatenate([cos_high, sin_high], axis=1)
        low = np.concatenate([cos_low, sin_low], axis=1)
        up.append(np.concatenate([high, low], axis=0))
        down += [cos_high.T, sin_high.T]
    return np.concatenate(up, axis=1), np.concatenate(down, axis=0)


def in_hbm(*arrays):
    return [pltpu.with_memory_space_constraint(array, pltpu.HBM) for array in arrays]


def dot(a, b):
    return jnp.dot(a, b, preferred_element_type=F32)


def complex_rows(real, imag):
    return jnp.concatenate(
        [
            jnp.concatenate([real, -imag], axis=1),
            jnp.concatenate([imag, real], axis=1),
        ],
        axis=0,
    )


def up_kernel(x_hbm, rad_hbm, w_hbm, out_hbm, x_ref, rad_ref, w_ref, right, result, sems):
    boxes, _, basis, rhs = x_ref.shape
    points = rad_ref.shape[2]
    copies = [
        pltpu.make_async_copy(source, target, sems.at[place])
        for place, (source, target) in enumerate(
            ((x_hbm, x_ref), (rad_hbm, rad_ref), (w_hbm, w_ref))
        )
    ]
    for copy in copies:
        copy.start()
    copies[0].wait()
    copies[1].wait()
    half = boxes // 2
    for octant in range(boxes):
        left = complex_rows(rad_ref[octant, 0], rad_ref[octant, 1])
        pattern = dot(left, x_ref[octant].reshape(2 * basis, rhs)).astype(BF16)
        real, imag = pattern[:points], pattern[points:]
        straight = jnp.concatenate([real, imag], axis=1)
        if octant < half:
            swapped = jnp.concatenate([-imag, real], axis=1)
        else:
            swapped = jnp.concatenate([imag, -real], axis=1)
        place = octant if octant < half else boxes - 1 - octant
        start = 2 * place * points
        right[octant // half, start : start + points] = straight
        right[octant // half, start + points : start + 2 * points] = swapped
    copies[2].wait()
    total = dot(w_ref[...], right[0]) + dot(w_ref[...], right[1])
    samples = total.shape[0] // 2
    total = total[:samples] + total[samples:]
    result[...] = total.astype(BF16).reshape(result.shape)
    pltpu.sync_copy(result, out_hbm)


def upward(coeffs, radiation, weights, groups):
    boxes, _, basis, rhs = coeffs.shape
    rows, columns = weights.shape
    samples = rows // 2
    hbm = pl.BlockSpec(memory_space=pltpu.HBM)
    return pl.pallas_call(
        up_kernel,
        in_specs=[hbm] * 3,
        out_specs=hbm,
        out_shape=pltpu.HBM((groups, samples // groups, 2 * rhs), BF16),
        scratch_shapes=[
            pltpu.VMEM(coeffs.shape, BF16),
            pltpu.VMEM(radiation.shape, BF16),
            pltpu.VMEM(weights.shape, BF16),
            pltpu.VMEM((2, columns, 2 * rhs), BF16),
            pltpu.VMEM((groups, samples // groups, 2 * rhs), BF16),
            pltpu.SemaphoreType.DMA((3,)),
        ],
        compiler_params=pltpu.CompilerParams(vmem_limit_bytes=32 * MIB),
        cost_estimate=pl.CostEstimate(
            flops=2 * 10**9, bytes_accessed=4 * MIB, transcendentals=0
        ),
        name="upward",
    )(*in_hbm(coeffs, radiation, weights))


def coupling_kernel(lists_ref, base_ref, table_ref, out_ref):
    rows = lists_ref.shape[0]
    samples = table_ref.shape[1] // 2
    _, targets, columns = out_ref.shape
    slots = rows // targets
    selector = (
        lax.broadcasted_iota(jnp.int32, (rows, table_ref.shape[0]), 1) == lists_ref[:, 1:2]
    )
    chosen = dot(selector.astype(BF16), table_ref[...]).astype(BF16)
    wide = lax.broadcasted_iota(jnp.int32, (rows, columns), 1) // samples
    match = wide + base_ref[0] == lists_ref[:, 0:1]
    spread = lax.broadcasted_iota(jnp.int32, (samples, columns), 0) == (
        lax.broadcasted_iota(jnp.int32, (samples, columns), 1) % samples
    )
    gather = (
        lax.broadcasted_iota(jnp.int32, (targets, rows), 1) // slots
        == lax.broadcasted_iota(jnp.int32, (targets, rows), 0)
    ).astype(BF16)
    tile = spread.astype(BF16)
    for part in range(2):
        lines = dot(chosen[:, part * samples : (part + 1) * samples], tile)
        out_ref[part] = dot(gather, jnp.where(match, lines, 0.0).astype(BF16))


def couplings(lists, base, table, targets, names):
    shape = (2, targets, names * (table.shape[1] // 2))
    vmem = pl.BlockSpec(memory_space=pltpu.VMEM)
    return pl.pallas_call(
        coupling_kernel,
        in_specs=[vmem, pl.BlockSpec(memory_space=pltpu.SMEM), vmem],
        out_specs=vmem,
        out_shape=jax.ShapeDtypeStruct(shape, F32),
        compiler_params=pltpu.CompilerParams(vmem_limit_bytes=16 * MIB),
        cost_estimate=pl.CostEstimate(
            flops=2 * 10**8, bytes_accessed=2 * 2**20, transcendentals=0
        ),
        name="coupling",
    )(lists, base, table)


def translate_kernel(lines_hbm, *refs):
    count = (len(refs) - 5) // 2
    sources, out_hbm = refs[:count], refs[count]
    held, lines, matrix, result, sems = refs[count + 1 :][:count], *refs[2 * count + 1 :]
    targets, samples, width = result.shape
    rhs = width // 2
    copies = [
        pltpu.make_async_copy(source, target, sems.at[place])
        for place, (source, target) in enumerate(zip((lines_hbm, *sources), (lines, *held)))
    ]
    for copy in copies:
        copy.start()
    copies[0].wait()
    columns = matrix.shape[1]
    row = lax.broadcasted_iota(jnp.int32, (samples, columns), 0)
    diagonal = row == lax.broadcasted_iota(jnp.int32, (samples, columns), 1) % samples
    for part in range(2):
        for target in range(targets):
            line = jnp.broadcast_to(lines[part, target : target + 1], diagonal.shape)
            start = (part * targets + target) * samples
            matrix[start : start + samples] = jnp.where(diagonal, line, 0.0).astype(BF16)
    total = None
    start = 0
    for place, source in enumerate(held):
        copies[1 + place].wait()
        stop = start + source.shape[0] * samples
        part = dot(matrix[:, start:stop], source[...].reshape(stop - start, width))
        total = part if total is None else total + part
        start = stop
    half = targets * samples
    real = total[:half, :rhs] - total[half:, rhs:]
    imag = total[:half, rhs:] + total[half:, :rhs]
    result[...] = jnp.concatenate([real, imag], axis=1).astype(BF16).reshape(result.shape)
    pltpu.sync_copy(result, out_hbm)


def translate(lines, sources):
    _, samples, width = sources[0].shape
    _, targets, columns = lines.shape
    shape = (targets, samples, width)
    hbm = pl.BlockSpec(memory_space=pltpu.HBM)
    anywhere = pl.BlockSpec(memory_space=pl.ANY)
    return pl.pallas_call(
        translate_kernel,
        in_specs=[hbm] + [anywhere] * len(sources),
        out_specs=hbm,
        out_shape=pltpu.HBM(shape, BF16),
        scratch_shapes=[
            *[pltpu.VMEM(source.shape, BF16) for source in sources],
            pltpu.VMEM(lines.shape, F32),
            pltpu.VMEM((2 * targets * samples, columns), BF16),
            pltpu.VMEM(shape, BF16),
            pltpu.SemaphoreType.DMA((1 + len(sources),)),
        ],
        compiler_params=pltpu.CompilerParams(vmem_limit_bytes=24 * MIB),
        cost_estimate=pl.CostEstimate(
            flops=10**9, bytes_accessed=2 * MIB, transcendentals=0
        ),
        name="translate",
    )(*in_hbm(lines), *sources)


def near_kernel(first, count, begun, *refs):
    ids_ref, used_ref, rank_ref, blocks_hbm = refs[:4]
    sources = refs[4 : 4 + count]
    out_hbm, blocks, held, total_ref, listed, sems = refs[4 + count + begun :]
    boxes, slots, _, basis, _ = blocks.shape
    rhs = held.shape[3]
    base = (rank_ref[0] - 1 + first) * boxes
    source_copies = [
        pltpu.make_async_copy(source, held.at[pl.ds(place * boxes, boxes)], sems.at[boxes + place])
        for place, source in enumerate(sources)
    ]

    def block_copy(box):
        return pltpu.make_async_copy(blocks_hbm.at[box], blocks.at[box], sems.at[box])

    def result_copy(box, inward):
        place = boxes + count + box
        if inward:
            return pltpu.make_async_copy(refs[4 + count].at[box], total_ref.at[box], sems.at[place])
        return pltpu.make_async_copy(total_ref.at[box], out_hbm.at[box], sems.at[place])

    for copy in source_copies:
        copy.start()
    for box in range(boxes):
        block_copy(box).start()
        if begun:
            result_copy(box, True).start()
    for copy in source_copies:
        copy.wait()

    def one_box(box, carry):
        total = jnp.int32(0)
        used = used_ref[box]
        for slot in range(slots):
            place = ids_ref[box, slot] - base
            listed[total] = jnp.int32(slot)
            wanted = (slot < used) & (place >= 0) & (place < count * boxes)
            total += wanted.astype(jnp.int32)
        block_copy(box).wait()
        if begun:
            result_copy(box, True).wait()
        else:
            total_ref[box] = jnp.zeros(total_ref.shape[1:], F32)

        def group(index, carry):
            left, right = [], []
            for step in range(GROUP):
                at = index * GROUP + step
                slot = listed[jnp.minimum(at, total - 1)]
                real, imag = blocks[box, slot, 0], blocks[box, slot, 1]
                if step:
                    real = jnp.where(at < total, real, jnp.zeros_like(real))
                    imag = jnp.where(at < total, imag, jnp.zeros_like(imag))
                left.append(complex_rows(real, imag))
                right.append(held[ids_ref[box, slot] - base].reshape(2 * basis, rhs))
            part = dot(jnp.concatenate(left, axis=1), jnp.concatenate(right, axis=0))
            total_ref[box] += part.reshape(2, basis, rhs)
            return carry

        lax.fori_loop(0, (total + GROUP - 1) // GROUP, group, 0)
        result_copy(box, False).start()
        return carry

    lax.fori_loop(0, boxes, one_box, 0)
    for box in range(boxes):
        result_copy(box, False).wait()


def near_field(ids, used, rank, blocks, sources, first, before=None):
    boxes, slots, _, basis, _ = blocks.shape
    rhs = sources[0].shape[3]
    count = len(sources)
    begun = before is not None
    hbm = pl.BlockSpec(memory_space=pltpu.HBM)
    smem = pl.BlockSpec(memory_space=pltpu.SMEM)
    return pl.pallas_call(
        functools.partial(near_kernel, first, count, begun),
        in_specs=[smem] * 3 + [hbm] * (1 + count + begun),
        out_specs=hbm,
        out_shape=pltpu.HBM((boxes, 2, basis, rhs), F32),
        scratch_shapes=[
            pltpu.VMEM(blocks.shape, BF16),
            pltpu.VMEM((count * boxes, 2, basis, rhs), BF16),
            pltpu.VMEM((boxes, 2, basis, rhs), F32),
            pltpu.SMEM((slots + 1,), jnp.int32),
            pltpu.SemaphoreType.DMA((2 * boxes + count,)),
        ],
        compiler_params=pltpu.CompilerParams(vmem_limit_bytes=24 * MIB),
        cost_estimate=pl.CostEstimate(
            flops=10**11 if begun else 2 * 10**9, bytes_accessed=8 * MIB, transcendentals=0
        ),
        name="near_last" if begun else "near_first",
    )(ids, used, rank, *in_hbm(blocks, *sources, *([before] if begun else [])))


def adjoint_kernel(rad_ref, out_hbm, held):
    for box in range(rad_ref.shape[0]):
        held[box] = complex_rows(rad_ref[box, 0], rad_ref[box, 1]).T
    pltpu.sync_copy(held, out_hbm)


def adjoint(radiation):
    boxes, _, points, basis = radiation.shape
    return pl.pallas_call(
        adjoint_kernel,
        in_specs=[pl.BlockSpec(memory_space=pltpu.VMEM)],
        out_specs=pl.BlockSpec(memory_space=pltpu.HBM),
        scratch_shapes=[pltpu.VMEM((boxes, 2 * basis, 2 * points), BF16)],
        out_shape=pltpu.HBM((boxes, 2 * basis, 2 * points), BF16),
        cost_estimate=pl.CostEstimate(
            flops=10**6, bytes_accessed=2 * MIB, transcendentals=0
        ),
        name="adjoint",
    )(radiation)


def down_kernel(field_ref, w_hbm, adjoint_hbm, near_hbm, out_hbm, field, w, left, held, sems):
    boxes, width, _ = left.shape
    points = width // 2
    basis, rhs = held.shape[2], held.shape[3]
    copies = [
        pltpu.make_async_copy(source, target, sems.at[boxes + place])
        for place, (source, target) in enumerate(
            ((field_ref, field), (w_hbm, w), (adjoint_hbm, left), (near_hbm, held))
        )
    ]
    out_copies = [
        pltpu.make_async_copy(held.at[box], out_hbm.at[box], sems.at[box]) for box in range(boxes)
    ]
    for copy in copies:
        copy.start()
    for copy in copies[:2]:
        copy.wait()
    mixed = dot(w[...], field[...].reshape(w.shape[1], 2 * rhs))
    for copy in copies[2:]:
        copy.wait()
    for octant in range(boxes // 2):
        start = 2 * octant * points
        cos_part = mixed[start : start + points]
        sin_part = mixed[start + points : start + 2 * points]
        cos_re, cos_im = cos_part[:, :rhs], cos_part[:, rhs:]
        sin_re, sin_im = sin_part[:, :rhs], sin_part[:, rhs:]
        leaves = (
            (octant, cos_re + sin_im, cos_im - sin_re),
            (boxes - 1 - octant, cos_re - sin_im, cos_im + sin_re),
        )
        for box, real, imag in leaves:
            leaf = jnp.concatenate([real, imag], axis=0).astype(BF16)
            held[box] += dot(left[box], leaf).reshape(2, basis, rhs)
            out_copies[box].start()
    for copy in out_copies:
        copy.wait()


def downward(field, weights, radiation_adjoint, near):
    boxes = near.shape[0]
    hbm = pl.BlockSpec(memory_space=pltpu.HBM)
    return pl.pallas_call(
        down_kernel,
        in_specs=[pl.BlockSpec(memory_space=pl.ANY)] + [hbm] * 3,
        out_specs=hbm,
        out_shape=jax.ShapeDtypeStruct(near.shape, F32),
        scratch_shapes=[
            pltpu.VMEM(field.shape, BF16),
            pltpu.VMEM(weights.shape, BF16),
            pltpu.VMEM(radiation_adjoint.shape, BF16),
            pltpu.VMEM(near.shape, F32),
            pltpu.SemaphoreType.DMA((boxes + 4,)),
        ],
        compiler_params=pltpu.CompilerParams(vmem_limit_bytes=32 * MIB),
        cost_estimate=pl.CostEstimate(
            flops=2 * 10**9, bytes_accessed=7 * MIB, transcendentals=0
        ),
        name="downward",
    )(field, *in_hbm(weights, radiation_adjoint, near))


def shift(block, axis, step):
    count = lax.axis_size(axis)
    pairs = [(i, i + step) for i in range(count) if 0 <= i + step < count]
    return lax.ppermute(block, axis, pairs)


def lists_of(partners, vector_ids, pair_count):
    used = jnp.arange(partners.shape[1])[None, :] < pair_count[:, None]
    names = jnp.where(used, partners, NOWHERE)
    return jnp.stack([names, vector_ids], axis=2).reshape(-1, 2)


def parent_bands(spread, shares):
    axes = ("box", "theta", "phi") if shares == lax.axis_size("box") else ("theta", "phi")
    return lax.all_to_all(spread, axes, split_axis=0, concat_axis=0, tiled=True)


def translation_lines(lists, translation, shares, per_group):
    operator_total, _, theta_band, phi_band = translation.shape
    rank = lax.axis_index("box")
    if shares < lax.axis_size("box"):
        table = translation.reshape(operator_total, -1)
        base = ((rank - 1) * per_group).astype(jnp.int32).reshape(1)
        return couplings(lists, base, table, per_group, 3 * per_group)
    if shares == 2:
        other = lax.ppermute(lists, "box", [(0, 1), (1, 0)])
        lists = jnp.where(
            rank == 0, jnp.concatenate([lists, other]), jnp.concatenate([other, lists])
        )
    part = theta_band // shares
    table = lax.dynamic_slice_in_dim(translation, rank * part, part, axis=2)
    table = table.reshape(operator_total, -1)
    total = shares * per_group
    return couplings(lists, jnp.zeros((1,), jnp.int32), table, total, total)


def per_device(
    shares,
    up_weights,
    down_weights,
    coeffs,
    near_blocks,
    near_ids,
    near_count,
    radiation,
    partners,
    vector_ids,
    pair_count,
    translation,
):
    every = ("box", "theta", "phi")
    per_group = lax.axis_size("theta") * lax.axis_size("phi")
    rank = lax.axis_index(every).astype(jnp.int32).reshape(1)
    low = shift(coeffs, every, 1)
    spread = upward(coeffs, radiation, up_weights, shares * per_group)
    radiation_adjoint = adjoint(radiation)
    lists = lists_of(partners, vector_ids, pair_count)
    spread, lists = lax.optimization_barrier((spread, lists))
    lines = translation_lines(lists, translation, shares, per_group)
    spread, lines, radiation_adjoint = lax.optimization_barrier((spread, lines, radiation_adjoint))
    parents = parent_bands(spread, shares)
    near = near_field(near_ids, near_count, rank, near_blocks, [low, coeffs], 0)
    near, late = lax.optimization_barrier((near, coeffs))
    high = shift(late, every, -1)
    parents, near = lax.optimization_barrier((parents, near))
    sources = [parents]
    if shares < lax.axis_size("box"):
        sources = [shift(parents, "box", 1), parents, shift(parents, "box", -1)]
    incoming = translate(lines, sources)
    field = parent_bands(incoming, shares)
    near = near_field(near_ids, near_count, rank, near_blocks, [high], 2, near)
    return downward(field, down_weights, radiation_adjoint, near)


def solution(mesh):
    box_size, theta_size, phi_size = (mesh.shape[axis] for axis in ("box", "theta", "phi"))
    shares = box_size if box_size <= 2 and TU // theta_size % box_size == 0 else 1
    up_weights, down_weights = operators(shares, theta_size, phi_size)
    in_specs = (
        P(),
        P(),
        P(("box", "theta", "phi"), None, None, None),
        P(("box", "theta", "phi"), None, None, None, None),
        P(("box", "theta", "phi"), None),
        P(("box", "theta", "phi")),
        P(("box", "theta", "phi"), None, None, None),
        P("box", None),
        P("box", None),
        P("box"),
        P(None, None, "theta", "phi"),
    )
    out_specs = P(("box", "theta", "phi"), None, None, None)
    mapped = jax.shard_map(
        functools.partial(per_device, shares),
        mesh=mesh,
        in_specs=in_specs,
        out_specs=out_specs,
        check_vma=False,
    )

    def product(*arrays):
        return mapped(jnp.asarray(up_weights), jnp.asarray(down_weights), *arrays)

    return product
```

```python
import functools
import math

import jax
import jax.numpy as jnp
import ml_dtypes
import numpy as np
from jax import lax
from jax.experimental import pallas as pl
from jax.experimental.pallas import tpu as pltpu
from jax.sharding import PartitionSpec as P

TL = 8
PL = 16
TU = 16
PU = 32

WEIGHT_UP = (-0.0546875, 0.8203125, 0.2734375, -0.0390625)
WEIGHT_DOWN = (-0.0390625, 0.2734375, 0.8203125, -0.0546875)
PHASE_SCALE = 1.3

F32 = jnp.float32
BF16 = jnp.bfloat16
MIB = 2**20
GROUP = 4
NOWHERE = -(2**20)


def lagrange(rows, columns, wrap):
    matrix = np.zeros((rows, columns))
    for row in range(rows):
        weights = WEIGHT_UP if row % 2 else WEIGHT_DOWN
        for order in range(4):
            node = row // 2 + row % 2 - 2 + order
            node = node % columns if wrap else min(max(node, 0), columns - 1)
            matrix[row, node] += weights[order]
    return matrix


def split_weights(matrix):
    high = matrix.astype(ml_dtypes.bfloat16)
    low = (matrix - high.astype(np.float64)).astype(ml_dtypes.bfloat16)
    return high, low


def operators(shares, theta_size, phi_size):
    theta_part = TU // theta_size // shares
    order = np.arange(TU * PU).reshape(theta_size, shares, theta_part, phi_size, PU // phi_size)
    order = order.transpose(1, 0, 3, 2, 4).reshape(-1)
    interp = np.kron(lagrange(TU, TL, False), lagrange(PU, PL, True))
    theta = math.pi * (np.arange(TU) + 0.5) / TU
    azimuth = 2.0 * math.pi * (np.arange(PU) + 0.5) / PU
    up, down = [], []
    for octant in range(4):
        sign_x = 2 * (octant % 2) - 1
        sign_y = 2 * (octant // 2 % 2) - 1
        sign_z = 2 * (octant // 4) - 1
        angle = PHASE_SCALE * (
            sign_x * np.sin(theta)[:, None] * np.cos(azimuth)[None]
            + sign_y * np.sin(theta)[:, None] * np.sin(azimuth)[None]
            + sign_z * np.cos(theta)[:, None]
        ).reshape(-1, 1)
        cos_high, cos_low = split_weights((np.cos(angle) * interp)[order])
        sin_high, sin_low = split_weights((np.sin(angle) * interp)[order])
        high = np.concatenate([cos_high, sin_high], axis=1)
        low = np.concatenate([cos_low, sin_low], axis=1)
        up.append(np.concatenate([high, low], axis=0))
        down += [cos_high.T, sin_high.T]
    return np.concatenate(up, axis=1), np.concatenate(down, axis=0)


def in_hbm(*arrays):
    return [pltpu.with_memory_space_constraint(array, pltpu.HBM) for array in arrays]


def dot(a, b):
    return jnp.dot(a, b, preferred_element_type=F32)


def complex_rows(real, imag):
    return jnp.concatenate(
        [
            jnp.concatenate([real, -imag], axis=1),
            jnp.concatenate([imag, real], axis=1),
        ],
        axis=0,
    )


def up_kernel(x_hbm, rad_hbm, w_hbm, out_hbm, x_ref, rad_ref, w_ref, right, result, sems):
    boxes, _, basis, rhs = x_ref.shape
    points = rad_ref.shape[2]
    copies = [
        pltpu.make_async_copy(source, target, sems.at[place])
        for place, (source, target) in enumerate(
            ((x_hbm, x_ref), (rad_hbm, rad_ref), (w_hbm, w_ref))
        )
    ]
    for copy in copies:
        copy.start()
    copies[0].wait()
    copies[1].wait()
    half = boxes // 2
    for octant in range(boxes):
        left = complex_rows(rad_ref[octant, 0], rad_ref[octant, 1])
        pattern = dot(left, x_ref[octant].reshape(2 * basis, rhs)).astype(BF16)
        real, imag = pattern[:points], pattern[points:]
        straight = jnp.concatenate([real, imag], axis=1)
        if octant < half:
            swapped = jnp.concatenate([-imag, real], axis=1)
        else:
            swapped = jnp.concatenate([imag, -real], axis=1)
        place = octant if octant < half else boxes - 1 - octant
        start = 2 * place * points
        right[octant // half, start : start + points] = straight
        right[octant // half, start + points : start + 2 * points] = swapped
    copies[2].wait()
    total = dot(w_ref[...], right[0]) + dot(w_ref[...], right[1])
    samples = total.shape[0] // 2
    total = total[:samples] + total[samples:]
    result[...] = total.astype(BF16).reshape(result.shape)
    pltpu.sync_copy(result, out_hbm)


def upward(coeffs, radiation, weights, groups):
    boxes, _, basis, rhs = coeffs.shape
    rows, columns = weights.shape
    samples = rows // 2
    hbm = pl.BlockSpec(memory_space=pltpu.HBM)
    return pl.pallas_call(
        up_kernel,
        in_specs=[hbm] * 3,
        out_specs=hbm,
        out_shape=pltpu.HBM((groups, samples // groups, 2 * rhs), BF16),
        scratch_shapes=[
            pltpu.VMEM(coeffs.shape, BF16),
            pltpu.VMEM(radiation.shape, BF16),
            pltpu.VMEM(weights.shape, BF16),
            pltpu.VMEM((2, columns, 2 * rhs), BF16),
            pltpu.VMEM((groups, samples // groups, 2 * rhs), BF16),
            pltpu.SemaphoreType.DMA((3,)),
        ],
        compiler_params=pltpu.CompilerParams(vmem_limit_bytes=32 * MIB),
        cost_estimate=pl.CostEstimate(
            flops=2 * 10**9, bytes_accessed=4 * MIB, transcendentals=0
        ),
        name="upward",
    )(*in_hbm(coeffs, radiation, weights))


def coupling_kernel(lists_ref, base_ref, table_ref, out_ref):
    rows = lists_ref.shape[0]
    samples = table_ref.shape[1] // 2
    _, targets, columns = out_ref.shape
    slots = rows // targets
    selector = (
        lax.broadcasted_iota(jnp.int32, (rows, table_ref.shape[0]), 1) == lists_ref[:, 1:2]
    )
    chosen = dot(selector.astype(BF16), table_ref[...]).astype(BF16)
    wide = lax.broadcasted_iota(jnp.int32, (rows, columns), 1) // samples
    match = wide + base_ref[0] == lists_ref[:, 0:1]
    spread = lax.broadcasted_iota(jnp.int32, (samples, columns), 0) == (
        lax.broadcasted_iota(jnp.int32, (samples, columns), 1) % samples
    )
    gather = (
        lax.broadcasted_iota(jnp.int32, (targets, rows), 1) // slots
        == lax.broadcasted_iota(jnp.int32, (targets, rows), 0)
    ).astype(BF16)
    tile = spread.astype(BF16)
    for part in range(2):
        lines = dot(chosen[:, part * samples : (part + 1) * samples], tile)
        out_ref[part] = dot(gather, jnp.where(match, lines, 0.0).astype(BF16))


def couplings(lists, base, table, targets, names):
    shape = (2, targets, names * (table.shape[1] // 2))
    vmem = pl.BlockSpec(memory_space=pltpu.VMEM)
    return pl.pallas_call(
        coupling_kernel,
        in_specs=[vmem, pl.BlockSpec(memory_space=pltpu.SMEM), vmem],
        out_specs=vmem,
        out_shape=jax.ShapeDtypeStruct(shape, F32),
        compiler_params=pltpu.CompilerParams(vmem_limit_bytes=16 * MIB),
        cost_estimate=pl.CostEstimate(
            flops=2 * 10**8, bytes_accessed=2 * 2**20, transcendentals=0
        ),
        name="coupling",
    )(lists, base, table)


def translate_kernel(lines_hbm, *refs):
    count = (len(refs) - 5) // 2
    sources, out_hbm = refs[:count], refs[count]
    held, lines, matrix, result, sems = refs[count + 1 :][:count], *refs[2 * count + 1 :]
    targets, samples, width = result.shape
    rhs = width // 2
    copies = [
        pltpu.make_async_copy(source, target, sems.at[place])
        for place, (source, target) in enumerate(zip((lines_hbm, *sources), (lines, *held)))
    ]
    for copy in copies:
        copy.start()
    copies[0].wait()
    columns = matrix.shape[1]
    row = lax.broadcasted_iota(jnp.int32, (samples, columns), 0)
    diagonal = row == lax.broadcasted_iota(jnp.int32, (samples, columns), 1) % samples
    for part in range(2):
        for target in range(targets):
            line = jnp.broadcast_to(lines[part, target : target + 1], diagonal.shape)
            start = (part * targets + target) * samples
            matrix[start : start + samples] = jnp.where(diagonal, line, 0.0).astype(BF16)
    total = None
    start = 0
    for place, source in enumerate(held):
        copies[1 + place].wait()
        stop = start + source.shape[0] * samples
        part = dot(matrix[:, start:stop], source[...].reshape(stop - start, width))
        total = part if total is None else total + part
        start = stop
    half = targets * samples
    real = total[:half, :rhs] - total[half:, rhs:]
    imag = total[:half, rhs:] + total[half:, :rhs]
    result[...] = jnp.concatenate([real, imag], axis=1).astype(BF16).reshape(result.shape)
    pltpu.sync_copy(result, out_hbm)


def translate(lines, sources):
    _, samples, width = sources[0].shape
    _, targets, columns = lines.shape
    shape = (targets, samples, width)
    hbm = pl.BlockSpec(memory_space=pltpu.HBM)
    anywhere = pl.BlockSpec(memory_space=pl.ANY)
    return pl.pallas_call(
        translate_kernel,
        in_specs=[hbm] + [anywhere] * len(sources),
        out_specs=hbm,
        out_shape=pltpu.HBM(shape, BF16),
        scratch_shapes=[
            *[pltpu.VMEM(source.shape, BF16) for source in sources],
            pltpu.VMEM(lines.shape, F32),
            pltpu.VMEM((2 * targets * samples, columns), BF16),
            pltpu.VMEM(shape, BF16),
            pltpu.SemaphoreType.DMA((1 + len(sources),)),
        ],
        compiler_params=pltpu.CompilerParams(vmem_limit_bytes=24 * MIB),
        cost_estimate=pl.CostEstimate(
            flops=10**9, bytes_accessed=2 * MIB, transcendentals=0
        ),
        name="translate",
    )(*in_hbm(lines), *sources)


def near_kernel(first, count, begun, *refs):
    ids_ref, used_ref, rank_ref, blocks_hbm = refs[:4]
    sources = refs[4 : 4 + count]
    out_hbm, blocks, held, total_ref, listed, sems = refs[4 + count + begun :]
    boxes, slots, _, basis, _ = blocks.shape
    rhs = held.shape[3]
    base = (rank_ref[0] - 1 + first) * boxes
    source_copies = [
        pltpu.make_async_copy(source, held.at[pl.ds(place * boxes, boxes)], sems.at[boxes + place])
        for place, source in enumerate(sources)
    ]

    def block_copy(box):
        return pltpu.make_async_copy(blocks_hbm.at[box], blocks.at[box], sems.at[box])

    def result_copy(box, inward):
        place = boxes + count + box
        if inward:
            return pltpu.make_async_copy(refs[4 + count].at[box], total_ref.at[box], sems.at[place])
        return pltpu.make_async_copy(total_ref.at[box], out_hbm.at[box], sems.at[place])

    for copy in source_copies:
        copy.start()
    for box in range(boxes):
        block_copy(box).start()
        if begun:
            result_copy(box, True).start()
    for copy in source_copies:
        copy.wait()

    def one_box(box, carry):
        total = jnp.int32(0)
        used = used_ref[box]
        for slot in range(slots):
            place = ids_ref[box, slot] - base
            listed[total] = jnp.int32(slot)
            wanted = (slot < used) & (place >= 0) & (place < count * boxes)
            total += wanted.astype(jnp.int32)
        block_copy(box).wait()
        if begun:
            result_copy(box, True).wait()
        else:
            total_ref[box] = jnp.zeros(total_ref.shape[1:], F32)

        def group(index, carry):
            left, right = [], []
            for step in range(GROUP):
                at = index * GROUP + step
                slot = listed[jnp.minimum(at, total - 1)]
                real, imag = blocks[box, slot, 0], blocks[box, slot, 1]
                if step:
                    real = jnp.where(at < total, real, jnp.zeros_like(real))
                    imag = jnp.where(at < total, imag, jnp.zeros_like(imag))
                left.append(complex_rows(real, imag))
                right.append(held[ids_ref[box, slot] - base].reshape(2 * basis, rhs))
            part = dot(jnp.concatenate(left, axis=1), jnp.concatenate(right, axis=0))
            total_ref[box] += part.reshape(2, basis, rhs)
            return carry

        lax.fori_loop(0, (total + GROUP - 1) // GROUP, group, 0)
        result_copy(box, False).start()
        return carry

    lax.fori_loop(0, boxes, one_box, 0)
    for box in range(boxes):
        result_copy(box, False).wait()


def near_field(ids, used, rank, blocks, sources, first, before=None):
    boxes, slots, _, basis, _ = blocks.shape
    rhs = sources[0].shape[3]
    count = len(sources)
    begun = before is not None
    hbm = pl.BlockSpec(memory_space=pltpu.HBM)
    smem = pl.BlockSpec(memory_space=pltpu.SMEM)
    return pl.pallas_call(
        functools.partial(near_kernel, first, count, begun),
        in_specs=[smem] * 3 + [hbm] * (1 + count + begun),
        out_specs=hbm,
        out_shape=pltpu.HBM((boxes, 2, basis, rhs), F32),
        scratch_shapes=[
            pltpu.VMEM(blocks.shape, BF16),
            pltpu.VMEM((count * boxes, 2, basis, rhs), BF16),
            pltpu.VMEM((boxes, 2, basis, rhs), F32),
            pltpu.SMEM((slots + 1,), jnp.int32),
            pltpu.SemaphoreType.DMA((2 * boxes + count,)),
        ],
        compiler_params=pltpu.CompilerParams(vmem_limit_bytes=24 * MIB),
        cost_estimate=pl.CostEstimate(
            flops=10**11 if first == 2 else 2 * 10**9, bytes_accessed=8 * MIB, transcendentals=0
        ),
        name=("near_low", "near_own", "near_high")[first],
    )(ids, used, rank, *in_hbm(blocks, *sources, *([before] if begun else [])))


def adjoint_kernel(rad_ref, out_hbm, held):
    for box in range(rad_ref.shape[0]):
        held[box] = complex_rows(rad_ref[box, 0], rad_ref[box, 1]).T
    pltpu.sync_copy(held, out_hbm)


def adjoint(radiation):
    boxes, _, points, basis = radiation.shape
    return pl.pallas_call(
        adjoint_kernel,
        in_specs=[pl.BlockSpec(memory_space=pltpu.VMEM)],
        out_specs=pl.BlockSpec(memory_space=pltpu.HBM),
        scratch_shapes=[pltpu.VMEM((boxes, 2 * basis, 2 * points), BF16)],
        out_shape=pltpu.HBM((boxes, 2 * basis, 2 * points), BF16),
        cost_estimate=pl.CostEstimate(
            flops=10**6, bytes_accessed=2 * MIB, transcendentals=0
        ),
        name="adjoint",
    )(radiation)


def down_kernel(field_ref, w_hbm, adjoint_hbm, near_hbm, out_hbm, field, w, left, held, sems):
    boxes, width, _ = left.shape
    points = width // 2
    basis, rhs = held.shape[2], held.shape[3]
    copies = [
        pltpu.make_async_copy(source, target, sems.at[boxes + place])
        for place, (source, target) in enumerate(
            ((field_ref, field), (w_hbm, w), (adjoint_hbm, left), (near_hbm, held))
        )
    ]
    out_copies = [
        pltpu.make_async_copy(held.at[box], out_hbm.at[box], sems.at[box]) for box in range(boxes)
    ]
    for copy in copies:
        copy.start()
    for copy in copies[:2]:
        copy.wait()
    mixed = dot(w[...], field[...].reshape(w.shape[1], 2 * rhs))
    for copy in copies[2:]:
        copy.wait()
    for octant in range(boxes // 2):
        start = 2 * octant * points
        cos_part = mixed[start : start + points]
        sin_part = mixed[start + points : start + 2 * points]
        cos_re, cos_im = cos_part[:, :rhs], cos_part[:, rhs:]
        sin_re, sin_im = sin_part[:, :rhs], sin_part[:, rhs:]
        leaves = (
            (octant, cos_re + sin_im, cos_im - sin_re),
            (boxes - 1 - octant, cos_re - sin_im, cos_im + sin_re),
        )
        for box, real, imag in leaves:
            leaf = jnp.concatenate([real, imag], axis=0).astype(BF16)
            held[box] += dot(left[box], leaf).reshape(2, basis, rhs)
            out_copies[box].start()
    for copy in out_copies:
        copy.wait()


def downward(field, weights, radiation_adjoint, near):
    boxes = near.shape[0]
    hbm = pl.BlockSpec(memory_space=pltpu.HBM)
    return pl.pallas_call(
        down_kernel,
        in_specs=[pl.BlockSpec(memory_space=pl.ANY)] + [hbm] * 3,
        out_specs=hbm,
        out_shape=jax.ShapeDtypeStruct(near.shape, F32),
        scratch_shapes=[
            pltpu.VMEM(field.shape, BF16),
            pltpu.VMEM(weights.shape, BF16),
            pltpu.VMEM(radiation_adjoint.shape, BF16),
            pltpu.VMEM(near.shape, F32),
            pltpu.SemaphoreType.DMA((boxes + 4,)),
        ],
        compiler_params=pltpu.CompilerParams(vmem_limit_bytes=32 * MIB),
        cost_estimate=pl.CostEstimate(
            flops=2 * 10**9, bytes_accessed=7 * MIB, transcendentals=0
        ),
        name="downward",
    )(field, *in_hbm(weights, radiation_adjoint, near))


def shift(block, axis, step):
    count = lax.axis_size(axis)
    pairs = [(i, i + step) for i in range(count) if 0 <= i + step < count]
    return lax.ppermute(block, axis, pairs)


def lists_of(partners, vector_ids, pair_count):
    used = jnp.arange(partners.shape[1])[None, :] < pair_count[:, None]
    names = jnp.where(used, partners, NOWHERE)
    return jnp.stack([names, vector_ids], axis=2).reshape(-1, 2)


def parent_bands(spread, shares):
    axes = ("box", "theta", "phi") if shares == lax.axis_size("box") else ("theta", "phi")
    return lax.all_to_all(spread, axes, split_axis=0, concat_axis=0, tiled=True)


def translation_lines(lists, translation, shares, per_group):
    operator_total, _, theta_band, phi_band = translation.shape
    rank = lax.axis_index("box")
    if shares < lax.axis_size("box"):
        table = translation.reshape(operator_total, -1)
        base = ((rank - 1) * per_group).astype(jnp.int32).reshape(1)
        return couplings(lists, base, table, per_group, 3 * per_group)
    if shares == 2:
        other = lax.ppermute(lists, "box", [(0, 1), (1, 0)])
        lists = jnp.where(
            rank == 0, jnp.concatenate([lists, other]), jnp.concatenate([other, lists])
        )
    part = theta_band // shares
    table = lax.dynamic_slice_in_dim(translation, rank * part, part, axis=2)
    table = table.reshape(operator_total, -1)
    total = shares * per_group
    return couplings(lists, jnp.zeros((1,), jnp.int32), table, total, total)


def per_device(
    shares,
    up_weights,
    down_weights,
    coeffs,
    near_blocks,
    near_ids,
    near_count,
    radiation,
    partners,
    vector_ids,
    pair_count,
    translation,
):
    every = ("box", "theta", "phi")
    per_group = lax.axis_size("theta") * lax.axis_size("phi")
    rank = lax.axis_index(every).astype(jnp.int32).reshape(1)
    low = shift(coeffs, every, 1)
    spread = upward(coeffs, radiation, up_weights, shares * per_group)
    radiation_adjoint = adjoint(radiation)
    lists = lists_of(partners, vector_ids, pair_count)
    spread, lists = lax.optimization_barrier((spread, lists))
    lines = translation_lines(lists, translation, shares, per_group)
    spread, lines, radiation_adjoint = lax.optimization_barrier((spread, lines, radiation_adjoint))
    parents = parent_bands(spread, shares)
    near = near_field(near_ids, near_count, rank, near_blocks, [coeffs], 1)
    near = near_field(near_ids, near_count, rank, near_blocks, [low], 0, near)
    near, late = lax.optimization_barrier((near, coeffs))
    high = shift(late, every, -1)
    parents, near = lax.optimization_barrier((parents, near))
    sources = [parents]
    if shares < lax.axis_size("box"):
        sources = [shift(parents, "box", 1), parents, shift(parents, "box", -1)]
    incoming = translate(lines, sources)
    field = parent_bands(incoming, shares)
    near = near_field(near_ids, near_count, rank, near_blocks, [high], 2, near)
    return downward(field, down_weights, radiation_adjoint, near)


def solution(mesh):
    box_size, theta_size, phi_size = (mesh.shape[axis] for axis in ("box", "theta", "phi"))
    shares = box_size if box_size <= 2 and TU // theta_size % box_size == 0 else 1
    up_weights, down_weights = operators(shares, theta_size, phi_size)
    in_specs = (
        P(),
        P(),
        P(("box", "theta", "phi"), None, None, None),
        P(("box", "theta", "phi"), None, None, None, None),
        P(("box", "theta", "phi"), None),
        P(("box", "theta", "phi")),
        P(("box", "theta", "phi"), None, None, None),
        P("box", None),
        P("box", None),
        P("box"),
        P(None, None, "theta", "phi"),
    )
    out_specs = P(("box", "theta", "phi"), None, None, None)
    mapped = jax.shard_map(
        functools.partial(per_device, shares),
        mesh=mesh,
        in_specs=in_specs,
        out_specs=out_specs,
        check_vma=False,
    )

    def product(*arrays):
        return mapped(jnp.asarray(up_weights), jnp.asarray(down_weights), *arrays)

    return product
```

```python
import functools
import math

import jax
import jax.numpy as jnp
import ml_dtypes
import numpy as np
from jax import lax
from jax.experimental import pallas as pl
from jax.experimental.pallas import tpu as pltpu
from jax.sharding import PartitionSpec as P

TL = 8
PL = 16
TU = 16
PU = 32

WEIGHT_UP = (-0.0546875, 0.8203125, 0.2734375, -0.0390625)
WEIGHT_DOWN = (-0.0390625, 0.2734375, 0.8203125, -0.0546875)
PHASE_SCALE = 1.3

F32 = jnp.float32
BF16 = jnp.bfloat16
MIB = 2**20
GROUP = 4
NOWHERE = -(2**20)


def lagrange(rows, columns, wrap):
    matrix = np.zeros((rows, columns))
    for row in range(rows):
        weights = WEIGHT_UP if row % 2 else WEIGHT_DOWN
        for order in range(4):
            node = row // 2 + row % 2 - 2 + order
            node = node % columns if wrap else min(max(node, 0), columns - 1)
            matrix[row, node] += weights[order]
    return matrix


def split_weights(matrix):
    high = matrix.astype(ml_dtypes.bfloat16)
    low = (matrix - high.astype(np.float64)).astype(ml_dtypes.bfloat16)
    return high, low


def operators(shares, theta_size, phi_size):
    theta_part = TU // theta_size // shares
    order = np.arange(TU * PU).reshape(theta_size, shares, theta_part, phi_size, PU // phi_size)
    order = order.transpose(1, 0, 3, 2, 4).reshape(-1)
    interp = np.kron(lagrange(TU, TL, False), lagrange(PU, PL, True))
    theta = math.pi * (np.arange(TU) + 0.5) / TU
    azimuth = 2.0 * math.pi * (np.arange(PU) + 0.5) / PU
    up, down = [], []
    for octant in range(4):
        sign_x = 2 * (octant % 2) - 1
        sign_y = 2 * (octant // 2 % 2) - 1
        sign_z = 2 * (octant // 4) - 1
        angle = PHASE_SCALE * (
            sign_x * np.sin(theta)[:, None] * np.cos(azimuth)[None]
            + sign_y * np.sin(theta)[:, None] * np.sin(azimuth)[None]
            + sign_z * np.cos(theta)[:, None]
        ).reshape(-1, 1)
        cos_high, cos_low = split_weights((np.cos(angle) * interp)[order])
        sin_high, sin_low = split_weights((np.sin(angle) * interp)[order])
        high = np.concatenate([cos_high, sin_high], axis=1)
        low = np.concatenate([cos_low, sin_low], axis=1)
        up.append(np.concatenate([high, low], axis=0))
        down += [cos_high.T, sin_high.T]
    return np.concatenate(up, axis=1), np.concatenate(down, axis=0)


def in_hbm(*arrays):
    return [pltpu.with_memory_space_constraint(array, pltpu.HBM) for array in arrays]


def dot(a, b):
    return jnp.dot(a, b, preferred_element_type=F32)


def side_by_side(real, imag):
    return jnp.concatenate([real, imag], axis=1)


def complex_columns(real, imag):
    return jnp.concatenate([side_by_side(real, imag), side_by_side(-imag, real)], axis=0)


def up_kernel(x_hbm, rad_hbm, w_hbm, out_hbm, x_ref, rad_ref, w_ref, right, result, sems):
    boxes, _, _, rhs = x_ref.shape
    points = rad_ref.shape[2]
    copies = [
        pltpu.make_async_copy(source, target, sems.at[place])
        for place, (source, target) in enumerate(
            ((x_hbm, x_ref), (rad_hbm, rad_ref), (w_hbm, w_ref))
        )
    ]
    for copy in copies:
        copy.start()
    copies[0].wait()
    copies[1].wait()
    half = boxes // 2
    for octant in range(boxes):
        left = side_by_side(rad_ref[octant, 0], rad_ref[octant, 1])
        straight = dot(left, complex_columns(x_ref[octant, 0], x_ref[octant, 1])).astype(BF16)
        real, imag = straight[:, :rhs], straight[:, rhs:]
        if octant < half:
            swapped = side_by_side(-imag, real)
        else:
            swapped = side_by_side(imag, -real)
        place = octant if octant < half else boxes - 1 - octant
        start = 2 * place * points
        right[octant // half, start : start + points] = straight
        right[octant // half, start + points : start + 2 * points] = swapped
    copies[2].wait()
    total = dot(w_ref[...], right[0]) + dot(w_ref[...], right[1])
    samples = total.shape[0] // 2
    total = total[:samples] + total[samples:]
    result[...] = total.astype(BF16).reshape(result.shape)
    pltpu.sync_copy(result, out_hbm)


def upward(coeffs, radiation, weights, groups):
    boxes, _, basis, rhs = coeffs.shape
    rows, columns = weights.shape
    samples = rows // 2
    hbm = pl.BlockSpec(memory_space=pltpu.HBM)
    return pl.pallas_call(
        up_kernel,
        in_specs=[hbm] * 3,
        out_specs=hbm,
        out_shape=pltpu.HBM((groups, samples // groups, 2 * rhs), BF16),
        scratch_shapes=[
            pltpu.VMEM(coeffs.shape, BF16),
            pltpu.VMEM(radiation.shape, BF16),
            pltpu.VMEM(weights.shape, BF16),
            pltpu.VMEM((2, columns, 2 * rhs), BF16),
            pltpu.VMEM((groups, samples // groups, 2 * rhs), BF16),
            pltpu.SemaphoreType.DMA((3,)),
        ],
        compiler_params=pltpu.CompilerParams(vmem_limit_bytes=32 * MIB),
        cost_estimate=pl.CostEstimate(
            flops=2 * 10**9, bytes_accessed=4 * MIB, transcendentals=0
        ),
        name="upward",
    )(*in_hbm(coeffs, radiation, weights))


def coupling_kernel(lists_ref, base_ref, table_ref, out_ref):
    rows = lists_ref.shape[0]
    samples = table_ref.shape[1] // 2
    _, targets, columns = out_ref.shape
    slots = rows // targets
    selector = (
        lax.broadcasted_iota(jnp.int32, (rows, table_ref.shape[0]), 1) == lists_ref[:, 1:2]
    )
    chosen = dot(selector.astype(BF16), table_ref[...]).astype(BF16)
    wide = lax.broadcasted_iota(jnp.int32, (rows, columns), 1) // samples
    match = wide + base_ref[0] == lists_ref[:, 0:1]
    spread = lax.broadcasted_iota(jnp.int32, (samples, columns), 0) == (
        lax.broadcasted_iota(jnp.int32, (samples, columns), 1) % samples
    )
    gather = (
        lax.broadcasted_iota(jnp.int32, (targets, rows), 1) // slots
        == lax.broadcasted_iota(jnp.int32, (targets, rows), 0)
    ).astype(BF16)
    tile = spread.astype(BF16)
    for part in range(2):
        lines = dot(chosen[:, part * samples : (part + 1) * samples], tile)
        out_ref[part] = dot(gather, jnp.where(match, lines, 0.0).astype(BF16))


def couplings(lists, base, table, targets, names):
    shape = (2, targets, names * (table.shape[1] // 2))
    vmem = pl.BlockSpec(memory_space=pltpu.VMEM)
    return pl.pallas_call(
        coupling_kernel,
        in_specs=[vmem, pl.BlockSpec(memory_space=pltpu.SMEM), vmem],
        out_specs=vmem,
        out_shape=jax.ShapeDtypeStruct(shape, F32),
        compiler_params=pltpu.CompilerParams(vmem_limit_bytes=16 * MIB),
        cost_estimate=pl.CostEstimate(
            flops=2 * 10**8, bytes_accessed=2 * 2**20, transcendentals=0
        ),
        name="coupling",
    )(lists, base, table)


def translate_kernel(lines_hbm, *refs):
    count = (len(refs) - 5) // 2
    sources, out_hbm = refs[:count], refs[count]
    held, lines, matrix, result, sems = refs[count + 1 :][:count], *refs[2 * count + 1 :]
    targets, samples, width = result.shape
    rhs = width // 2
    copies = [
        pltpu.make_async_copy(source, target, sems.at[place])
        for place, (source, target) in enumerate(zip((lines_hbm, *sources), (lines, *held)))
    ]
    for copy in copies:
        copy.start()
    copies[0].wait()
    columns = matrix.shape[1]
    row = lax.broadcasted_iota(jnp.int32, (samples, columns), 0)
    diagonal = row == lax.broadcasted_iota(jnp.int32, (samples, columns), 1) % samples
    for part in range(2):
        for target in range(targets):
            line = jnp.broadcast_to(lines[part, target : target + 1], diagonal.shape)
            start = (part * targets + target) * samples
            matrix[start : start + samples] = jnp.where(diagonal, line, 0.0).astype(BF16)
    total = None
    start = 0
    for place, source in enumerate(held):
        copies[1 + place].wait()
        stop = start + source.shape[0] * samples
        part = dot(matrix[:, start:stop], source[...].reshape(stop - start, width))
        total = part if total is None else total + part
        start = stop
    half = targets * samples
    real = total[:half, :rhs] - total[half:, rhs:]
    imag = total[:half, rhs:] + total[half:, :rhs]
    result[...] = jnp.concatenate([real, imag], axis=1).astype(BF16).reshape(result.shape)
    pltpu.sync_copy(result, out_hbm)


def translate(lines, sources):
    _, samples, width = sources[0].shape
    _, targets, columns = lines.shape
    shape = (targets, samples, width)
    hbm = pl.BlockSpec(memory_space=pltpu.HBM)
    anywhere = pl.BlockSpec(memory_space=pl.ANY)
    return pl.pallas_call(
        translate_kernel,
        in_specs=[hbm] + [anywhere] * len(sources),
        out_specs=hbm,
        out_shape=pltpu.HBM(shape, BF16),
        scratch_shapes=[
            *[pltpu.VMEM(source.shape, BF16) for source in sources],
            pltpu.VMEM(lines.shape, F32),
            pltpu.VMEM((2 * targets * samples, columns), BF16),
            pltpu.VMEM(shape, BF16),
            pltpu.SemaphoreType.DMA((1 + len(sources),)),
        ],
        compiler_params=pltpu.CompilerParams(vmem_limit_bytes=24 * MIB),
        cost_estimate=pl.CostEstimate(
            flops=10**9, bytes_accessed=2 * MIB, transcendentals=0
        ),
        name="translate",
    )(*in_hbm(lines), *sources)


def near_kernel(first, count, begun, *refs):
    ids_ref, used_ref, rank_ref, blocks_hbm = refs[:4]
    sources = refs[4 : 4 + count]
    out_hbm, blocks, held, wide, total_ref, listed, sems = refs[4 + count + begun :]
    boxes, slots, _, basis, _ = blocks.shape
    rhs = held.shape[3]
    base = (rank_ref[0] - 1 + first) * boxes
    source_copies = [
        pltpu.make_async_copy(source, held.at[pl.ds(place * boxes, boxes)], sems.at[boxes + place])
        for place, source in enumerate(sources)
    ]

    def block_copy(box):
        return pltpu.make_async_copy(blocks_hbm.at[box], blocks.at[box], sems.at[box])

    def result_copy(box, inward):
        place = boxes + count + box
        if inward:
            return pltpu.make_async_copy(refs[4 + count].at[box], total_ref.at[box], sems.at[place])
        return pltpu.make_async_copy(total_ref.at[box], out_hbm.at[box], sems.at[place])

    for copy in source_copies:
        copy.start()
    for box in range(boxes):
        block_copy(box).start()
        if begun:
            result_copy(box, True).start()
    for copy in source_copies:
        copy.wait()

    def widen(place, carry):
        wide[place] = complex_columns(held[place, 0], held[place, 1])
        return carry

    lax.fori_loop(0, count * boxes, widen, 0)

    def one_box(box, carry):
        total = jnp.int32(0)
        used = used_ref[box]
        for slot in range(slots):
            place = ids_ref[box, slot] - base
            listed[total] = jnp.int32(slot)
            wanted = (slot < used) & (place >= 0) & (place < count * boxes)
            total += wanted.astype(jnp.int32)
        block_copy(box).wait()
        if begun:
            result_copy(box, True).wait()
        else:
            total_ref[box] = jnp.zeros(total_ref.shape[1:], F32)

        def group(index, carry):
            left, right = [], []
            for step in range(GROUP):
                at = index * GROUP + step
                slot = listed[jnp.minimum(at, total - 1)]
                real, imag = blocks[box, slot, 0], blocks[box, slot, 1]
                if step:
                    real = jnp.where(at < total, real, jnp.zeros_like(real))
                    imag = jnp.where(at < total, imag, jnp.zeros_like(imag))
                left.append(side_by_side(real, imag))
                right.append(wide[ids_ref[box, slot] - base])
            part = dot(jnp.concatenate(left, axis=1), jnp.concatenate(right, axis=0))
            total_ref[box, 0] += part[:, :rhs]
            total_ref[box, 1] += part[:, rhs:]
            return carry

        lax.fori_loop(0, (total + GROUP - 1) // GROUP, group, 0)
        result_copy(box, False).start()
        return carry

    lax.fori_loop(0, boxes, one_box, 0)
    for box in range(boxes):
        result_copy(box, False).wait()


def near_field(ids, used, rank, blocks, sources, first, before=None):
    boxes, slots, _, basis, _ = blocks.shape
    rhs = sources[0].shape[3]
    count = len(sources)
    begun = before is not None
    hbm = pl.BlockSpec(memory_space=pltpu.HBM)
    smem = pl.BlockSpec(memory_space=pltpu.SMEM)
    return pl.pallas_call(
        functools.partial(near_kernel, first, count, begun),
        in_specs=[smem] * 3 + [hbm] * (1 + count + begun),
        out_specs=hbm,
        out_shape=pltpu.HBM((boxes, 2, basis, rhs), F32),
        scratch_shapes=[
            pltpu.VMEM(blocks.shape, BF16),
            pltpu.VMEM((count * boxes, 2, basis, rhs), BF16),
            pltpu.VMEM((count * boxes, 2 * basis, 2 * rhs), BF16),
            pltpu.VMEM((boxes, 2, basis, rhs), F32),
            pltpu.SMEM((slots + 1,), jnp.int32),
            pltpu.SemaphoreType.DMA((2 * boxes + count,)),
        ],
        compiler_params=pltpu.CompilerParams(vmem_limit_bytes=24 * MIB),
        cost_estimate=pl.CostEstimate(
            flops=10**11 if first == 2 else 2 * 10**9, bytes_accessed=8 * MIB, transcendentals=0
        ),
        name=("near_low", "near_own", "near_high")[first],
    )(ids, used, rank, *in_hbm(blocks, *sources, *([before] if begun else [])))


def adjoint_kernel(rad_ref, out_hbm, held):
    for box in range(rad_ref.shape[0]):
        held[box] = side_by_side(rad_ref[box, 0].T, rad_ref[box, 1].T)
    pltpu.sync_copy(held, out_hbm)


def adjoint(radiation):
    boxes, _, points, basis = radiation.shape
    return pl.pallas_call(
        adjoint_kernel,
        in_specs=[pl.BlockSpec(memory_space=pltpu.VMEM)],
        out_specs=pl.BlockSpec(memory_space=pltpu.HBM),
        scratch_shapes=[pltpu.VMEM((boxes, basis, 2 * points), BF16)],
        out_shape=pltpu.HBM((boxes, basis, 2 * points), BF16),
        cost_estimate=pl.CostEstimate(
            flops=10**6, bytes_accessed=2 * MIB, transcendentals=0
        ),
        name="adjoint",
    )(radiation)


def down_kernel(field_ref, w_hbm, adjoint_hbm, near_hbm, out_hbm, field, w, left, held, sems):
    boxes, _, width = left.shape
    points = width // 2
    rhs = held.shape[3]
    copies = [
        pltpu.make_async_copy(source, target, sems.at[boxes + place])
        for place, (source, target) in enumerate(
            ((field_ref, field), (w_hbm, w), (adjoint_hbm, left), (near_hbm, held))
        )
    ]
    out_copies = [
        pltpu.make_async_copy(held.at[box], out_hbm.at[box], sems.at[box]) for box in range(boxes)
    ]
    for copy in copies:
        copy.start()
    for copy in copies[:2]:
        copy.wait()
    mixed = dot(w[...], field[...].reshape(w.shape[1], 2 * rhs))
    for copy in copies[2:]:
        copy.wait()
    for octant in range(boxes // 2):
        start = 2 * octant * points
        cos_part = mixed[start : start + points]
        sin_part = mixed[start + points : start + 2 * points]
        cos_re, cos_im = cos_part[:, :rhs], cos_part[:, rhs:]
        sin_re, sin_im = sin_part[:, :rhs], sin_part[:, rhs:]
        leaves = (
            (octant, cos_re + sin_im, cos_im - sin_re),
            (boxes - 1 - octant, cos_re - sin_im, cos_im + sin_re),
        )
        for box, real, imag in leaves:
            real, imag = real.astype(BF16), imag.astype(BF16)
            right = jnp.concatenate([side_by_side(real, imag), side_by_side(imag, -real)], axis=0)
            far = dot(left[box], right)
            held[box, 0] += far[:, :rhs]
            held[box, 1] += far[:, rhs:]
            out_copies[box].start()
    for copy in out_copies:
        copy.wait()


def downward(field, weights, radiation_adjoint, near):
    boxes = near.shape[0]
    hbm = pl.BlockSpec(memory_space=pltpu.HBM)
    return pl.pallas_call(
        down_kernel,
        in_specs=[pl.BlockSpec(memory_space=pl.ANY)] + [hbm] * 3,
        out_specs=hbm,
        out_shape=jax.ShapeDtypeStruct(near.shape, F32),
        scratch_shapes=[
            pltpu.VMEM(field.shape, BF16),
            pltpu.VMEM(weights.shape, BF16),
            pltpu.VMEM(radiation_adjoint.shape, BF16),
            pltpu.VMEM(near.shape, F32),
            pltpu.SemaphoreType.DMA((boxes + 4,)),
        ],
        compiler_params=pltpu.CompilerParams(vmem_limit_bytes=32 * MIB),
        cost_estimate=pl.CostEstimate(
            flops=2 * 10**9, bytes_accessed=7 * MIB, transcendentals=0
        ),
        name="downward",
    )(field, *in_hbm(weights, radiation_adjoint, near))


def shift(block, axis, step):
    count = lax.axis_size(axis)
    pairs = [(i, i + step) for i in range(count) if 0 <= i + step < count]
    return lax.ppermute(block, axis, pairs)


def lists_of(partners, vector_ids, pair_count):
    used = jnp.arange(partners.shape[1])[None, :] < pair_count[:, None]
    names = jnp.where(used, partners, NOWHERE)
    return jnp.stack([names, vector_ids], axis=2).reshape(-1, 2)


def parent_bands(spread, shares):
    axes = ("box", "theta", "phi") if shares == lax.axis_size("box") else ("theta", "phi")
    return lax.all_to_all(spread, axes, split_axis=0, concat_axis=0, tiled=True)


def translation_lines(lists, translation, shares, per_group):
    operator_total, _, theta_band, phi_band = translation.shape
    rank = lax.axis_index("box")
    if shares < lax.axis_size("box"):
        table = translation.reshape(operator_total, -1)
        base = ((rank - 1) * per_group).astype(jnp.int32).reshape(1)
        return couplings(lists, base, table, per_group, 3 * per_group)
    if shares == 2:
        other = lax.ppermute(lists, "box", [(0, 1), (1, 0)])
        lists = jnp.where(
            rank == 0, jnp.concatenate([lists, other]), jnp.concatenate([other, lists])
        )
    part = theta_band // shares
    table = lax.dynamic_slice_in_dim(translation, rank * part, part, axis=2)
    table = table.reshape(operator_total, -1)
    total = shares * per_group
    return couplings(lists, jnp.zeros((1,), jnp.int32), table, total, total)


def per_device(
    shares,
    up_weights,
    down_weights,
    coeffs,
    near_blocks,
    near_ids,
    near_count,
    radiation,
    partners,
    vector_ids,
    pair_count,
    translation,
):
    every = ("box", "theta", "phi")
    per_group = lax.axis_size("theta") * lax.axis_size("phi")
    rank = lax.axis_index(every).astype(jnp.int32).reshape(1)
    low = shift(coeffs, every, 1)
    spread = upward(coeffs, radiation, up_weights, shares * per_group)
    radiation_adjoint = adjoint(radiation)
    lists = lists_of(partners, vector_ids, pair_count)
    spread, lists = lax.optimization_barrier((spread, lists))
    lines = translation_lines(lists, translation, shares, per_group)
    spread, lines, radiation_adjoint = lax.optimization_barrier((spread, lines, radiation_adjoint))
    parents = parent_bands(spread, shares)
    near = near_field(near_ids, near_count, rank, near_blocks, [low], 0)
    near, late = lax.optimization_barrier((near, coeffs))
    high = shift(late, every, -1)
    parents, near = lax.optimization_barrier((parents, near))
    sources = [parents]
    if shares < lax.axis_size("box"):
        sources = [shift(parents, "box", 1), parents, shift(parents, "box", -1)]
    incoming = translate(lines, sources)
    incoming, near = lax.optimization_barrier((incoming, near))
    field = parent_bands(incoming, shares)
    near = near_field(near_ids, near_count, rank, near_blocks, [coeffs], 1, near)
    near = near_field(near_ids, near_count, rank, near_blocks, [high], 2, near)
    return downward(field, down_weights, radiation_adjoint, near)


def solution(mesh):
    box_size, theta_size, phi_size = (mesh.shape[axis] for axis in ("box", "theta", "phi"))
    shares = box_size if box_size <= 2 and TU // theta_size % box_size == 0 else 1
    up_weights, down_weights = operators(shares, theta_size, phi_size)
    in_specs = (
        P(),
        P(),
        P(("box", "theta", "phi"), None, None, None),
        P(("box", "theta", "phi"), None, None, None, None),
        P(("box", "theta", "phi"), None),
        P(("box", "theta", "phi")),
        P(("box", "theta", "phi"), None, None, None),
        P("box", None),
        P("box", None),
        P("box"),
        P(None, None, "theta", "phi"),
    )
    out_specs = P(("box", "theta", "phi"), None, None, None)
    mapped = jax.shard_map(
        functools.partial(per_device, shares),
        mesh=mesh,
        in_specs=in_specs,
        out_specs=out_specs,
        check_vma=False,
    )

    def product(*arrays):
        return mapped(jnp.asarray(up_weights), jnp.asarray(down_weights), *arrays)

    return product
```

```python
import functools
import math

import jax
import jax.numpy as jnp
import ml_dtypes
import numpy as np
from jax import lax
from jax.experimental import pallas as pl
from jax.experimental.pallas import tpu as pltpu
from jax.sharding import PartitionSpec as P

TL = 8
PL = 16
TU = 16
PU = 32

WEIGHT_UP = (-0.0546875, 0.8203125, 0.2734375, -0.0390625)
WEIGHT_DOWN = (-0.0390625, 0.2734375, 0.8203125, -0.0546875)
PHASE_SCALE = 1.3

F32 = jnp.float32
BF16 = jnp.bfloat16
MIB = 2**20
GROUP = 4
NOWHERE = -(2**20)


def lagrange(rows, columns, wrap):
    matrix = np.zeros((rows, columns))
    for row in range(rows):
        weights = WEIGHT_UP if row % 2 else WEIGHT_DOWN
        for order in range(4):
            node = row // 2 + row % 2 - 2 + order
            node = node % columns if wrap else min(max(node, 0), columns - 1)
            matrix[row, node] += weights[order]
    return matrix


def split_weights(matrix):
    high = matrix.astype(ml_dtypes.bfloat16)
    low = (matrix - high.astype(np.float64)).astype(ml_dtypes.bfloat16)
    return high, low


def operators(shares, theta_size, phi_size):
    theta_part = TU // theta_size // shares
    order = np.arange(TU * PU).reshape(theta_size, shares, theta_part, phi_size, PU // phi_size)
    order = order.transpose(1, 0, 3, 2, 4).reshape(-1)
    interp = np.kron(lagrange(TU, TL, False), lagrange(PU, PL, True))
    theta = math.pi * (np.arange(TU) + 0.5) / TU
    azimuth = 2.0 * math.pi * (np.arange(PU) + 0.5) / PU
    up, down = [], []
    for octant in range(4):
        sign_x = 2 * (octant % 2) - 1
        sign_y = 2 * (octant // 2 % 2) - 1
        sign_z = 2 * (octant // 4) - 1
        angle = PHASE_SCALE * (
            sign_x * np.sin(theta)[:, None] * np.cos(azimuth)[None]
            + sign_y * np.sin(theta)[:, None] * np.sin(azimuth)[None]
            + sign_z * np.cos(theta)[:, None]
        ).reshape(-1, 1)
        cos_high, cos_low = split_weights((np.cos(angle) * interp)[order])
        sin_high, sin_low = split_weights((np.sin(angle) * interp)[order])
        high = np.concatenate([cos_high, sin_high], axis=1)
        low = np.concatenate([cos_low, sin_low], axis=1)
        up.append(np.concatenate([high, low], axis=0))
        down += [cos_high.T, sin_high.T]
    return np.concatenate(up, axis=1), np.concatenate(down, axis=0)


def in_hbm(*arrays):
    return [pltpu.with_memory_space_constraint(array, pltpu.HBM) for array in arrays]


def dot(a, b):
    return jnp.dot(a, b, preferred_element_type=F32)


def side_by_side(real, imag):
    return jnp.concatenate([real, imag], axis=1)


def complex_columns(real, imag):
    return jnp.concatenate([side_by_side(real, imag), side_by_side(-imag, real)], axis=0)


def up_kernel(x_hbm, rad_hbm, w_hbm, out_hbm, x_ref, rad_ref, w_ref, right, result, sems):
    boxes, _, _, rhs = x_ref.shape
    points = rad_ref.shape[2]
    copies = [
        pltpu.make_async_copy(source, target, sems.at[place])
        for place, (source, target) in enumerate(
            ((x_hbm, x_ref), (rad_hbm, rad_ref), (w_hbm, w_ref))
        )
    ]
    for copy in copies:
        copy.start()
    copies[0].wait()
    copies[1].wait()
    half = boxes // 2
    for octant in range(boxes):
        left = side_by_side(rad_ref[octant, 0], rad_ref[octant, 1])
        straight = dot(left, complex_columns(x_ref[octant, 0], x_ref[octant, 1])).astype(BF16)
        real, imag = straight[:, :rhs], straight[:, rhs:]
        if octant < half:
            swapped = side_by_side(-imag, real)
        else:
            swapped = side_by_side(imag, -real)
        place = octant if octant < half else boxes - 1 - octant
        start = 2 * place * points
        right[octant // half, start : start + points] = straight
        right[octant // half, start + points : start + 2 * points] = swapped
    copies[2].wait()
    total = dot(w_ref[...], right[0]) + dot(w_ref[...], right[1])
    samples = total.shape[0] // 2
    total = total[:samples] + total[samples:]
    result[...] = total.astype(BF16).reshape(result.shape)
    pltpu.sync_copy(result, out_hbm)


def upward(coeffs, radiation, weights, groups):
    boxes, _, basis, rhs = coeffs.shape
    rows, columns = weights.shape
    samples = rows // 2
    hbm = pl.BlockSpec(memory_space=pltpu.HBM)
    return pl.pallas_call(
        up_kernel,
        in_specs=[hbm] * 3,
        out_specs=hbm,
        out_shape=pltpu.HBM((groups, samples // groups, 2 * rhs), BF16),
        scratch_shapes=[
            pltpu.VMEM(coeffs.shape, BF16),
            pltpu.VMEM(radiation.shape, BF16),
            pltpu.VMEM(weights.shape, BF16),
            pltpu.VMEM((2, columns, 2 * rhs), BF16),
            pltpu.VMEM((groups, samples // groups, 2 * rhs), BF16),
            pltpu.SemaphoreType.DMA((3,)),
        ],
        compiler_params=pltpu.CompilerParams(vmem_limit_bytes=32 * MIB),
        cost_estimate=pl.CostEstimate(
            flops=2 * 10**9, bytes_accessed=4 * MIB, transcendentals=0
        ),
        name="upward",
    )(*in_hbm(coeffs, radiation, weights))


def coupling_kernel(lists_ref, base_ref, table_ref, out_ref):
    rows = lists_ref.shape[0]
    samples = table_ref.shape[1] // 2
    _, targets, columns = out_ref.shape
    slots = rows // targets
    selector = (
        lax.broadcasted_iota(jnp.int32, (rows, table_ref.shape[0]), 1) == lists_ref[:, 1:2]
    )
    chosen = dot(selector.astype(BF16), table_ref[...]).astype(BF16)
    wide = lax.broadcasted_iota(jnp.int32, (rows, columns), 1) // samples
    match = wide + base_ref[0] == lists_ref[:, 0:1]
    spread = lax.broadcasted_iota(jnp.int32, (samples, columns), 0) == (
        lax.broadcasted_iota(jnp.int32, (samples, columns), 1) % samples
    )
    gather = (
        lax.broadcasted_iota(jnp.int32, (targets, rows), 1) // slots
        == lax.broadcasted_iota(jnp.int32, (targets, rows), 0)
    ).astype(BF16)
    tile = spread.astype(BF16)
    for part in range(2):
        lines = dot(chosen[:, part * samples : (part + 1) * samples], tile)
        out_ref[part] = dot(gather, jnp.where(match, lines, 0.0).astype(BF16))


def couplings(lists, base, table, targets, names):
    shape = (2, targets, names * (table.shape[1] // 2))
    vmem = pl.BlockSpec(memory_space=pltpu.VMEM)
    return pl.pallas_call(
        coupling_kernel,
        in_specs=[vmem, pl.BlockSpec(memory_space=pltpu.SMEM), vmem],
        out_specs=vmem,
        out_shape=jax.ShapeDtypeStruct(shape, F32),
        compiler_params=pltpu.CompilerParams(vmem_limit_bytes=16 * MIB),
        cost_estimate=pl.CostEstimate(
            flops=2 * 10**8, bytes_accessed=2 * 2**20, transcendentals=0
        ),
        name="coupling",
    )(lists, base, table)


def translate_kernel(lines_hbm, *refs):
    count = (len(refs) - 5) // 2
    sources, out_hbm = refs[:count], refs[count]
    held, lines, matrix, result, sems = refs[count + 1 :][:count], *refs[2 * count + 1 :]
    targets, samples, width = result.shape
    rhs = width // 2
    copies = [
        pltpu.make_async_copy(source, target, sems.at[place])
        for place, (source, target) in enumerate(zip((lines_hbm, *sources), (lines, *held)))
    ]
    for copy in copies:
        copy.start()
    copies[0].wait()
    columns = matrix.shape[1]
    row = lax.broadcasted_iota(jnp.int32, (samples, columns), 0)
    diagonal = row == lax.broadcasted_iota(jnp.int32, (samples, columns), 1) % samples
    for part in range(2):
        for target in range(targets):
            line = jnp.broadcast_to(lines[part, target : target + 1], diagonal.shape)
            start = (part * targets + target) * samples
            matrix[start : start + samples] = jnp.where(diagonal, line, 0.0).astype(BF16)
    total = None
    start = 0
    for place, source in enumerate(held):
        copies[1 + place].wait()
        stop = start + source.shape[0] * samples
        part = dot(matrix[:, start:stop], source[...].reshape(stop - start, width))
        total = part if total is None else total + part
        start = stop
    half = targets * samples
    real = total[:half, :rhs] - total[half:, rhs:]
    imag = total[:half, rhs:] + total[half:, :rhs]
    result[...] = jnp.concatenate([real, imag], axis=1).astype(BF16).reshape(result.shape)
    pltpu.sync_copy(result, out_hbm)


def translate(lines, sources):
    _, samples, width = sources[0].shape
    _, targets, columns = lines.shape
    shape = (targets, samples, width)
    hbm = pl.BlockSpec(memory_space=pltpu.HBM)
    anywhere = pl.BlockSpec(memory_space=pl.ANY)
    return pl.pallas_call(
        translate_kernel,
        in_specs=[hbm] + [anywhere] * len(sources),
        out_specs=hbm,
        out_shape=pltpu.HBM(shape, BF16),
        scratch_shapes=[
            *[pltpu.VMEM(source.shape, BF16) for source in sources],
            pltpu.VMEM(lines.shape, F32),
            pltpu.VMEM((2 * targets * samples, columns), BF16),
            pltpu.VMEM(shape, BF16),
            pltpu.SemaphoreType.DMA((1 + len(sources),)),
        ],
        compiler_params=pltpu.CompilerParams(vmem_limit_bytes=24 * MIB),
        cost_estimate=pl.CostEstimate(
            flops=10**9, bytes_accessed=2 * MIB, transcendentals=0
        ),
        name="translate",
    )(*in_hbm(lines), *sources)


def near_kernel(first, count, begun, *refs):
    ids_ref, used_ref, rank_ref, blocks_hbm = refs[:4]
    sources = refs[4 : 4 + count]
    out_hbm, blocks, held, wide, total_ref, listed, sems = refs[4 + count + begun :]
    boxes, slots, _, basis, _ = blocks.shape
    rhs = held.shape[3]
    base = (rank_ref[0] - 1 + first) * boxes
    source_copies = [
        pltpu.make_async_copy(source, held.at[pl.ds(place * boxes, boxes)], sems.at[boxes + place])
        for place, source in enumerate(sources)
    ]

    def block_copy(box):
        return pltpu.make_async_copy(blocks_hbm.at[box], blocks.at[box], sems.at[box])

    def result_copy(box, inward):
        place = boxes + count + box
        if inward:
            return pltpu.make_async_copy(refs[4 + count].at[box], total_ref.at[box], sems.at[place])
        return pltpu.make_async_copy(total_ref.at[box], out_hbm.at[box], sems.at[place])

    for copy in source_copies:
        copy.start()
    for box in range(boxes):
        block_copy(box).start()
        if begun:
            result_copy(box, True).start()
    for copy in source_copies:
        copy.wait()

    def widen(place, carry):
        wide[place] = complex_columns(held[place, 0], held[place, 1])
        return carry

    lax.fori_loop(0, count * boxes, widen, 0)

    def one_box(box, carry):
        total = jnp.int32(0)
        used = used_ref[box]
        for slot in range(slots):
            place = ids_ref[box, slot] - base
            listed[total] = jnp.int32(slot)
            wanted = (slot < used) & (place >= 0) & (place < count * boxes)
            total += wanted.astype(jnp.int32)
        block_copy(box).wait()
        if begun:
            result_copy(box, True).wait()
        else:
            total_ref[box] = jnp.zeros(total_ref.shape[1:], F32)

        def group(index, carry):
            left, right = [], []
            for step in range(GROUP):
                at = index * GROUP + step
                slot = listed[jnp.minimum(at, total - 1)]
                real, imag = blocks[box, slot, 0], blocks[box, slot, 1]
                if step:
                    real = jnp.where(at < total, real, jnp.zeros_like(real))
                    imag = jnp.where(at < total, imag, jnp.zeros_like(imag))
                left.append(side_by_side(real, imag))
                right.append(wide[ids_ref[box, slot] - base])
            part = dot(jnp.concatenate(left, axis=1), jnp.concatenate(right, axis=0))
            total_ref[box, 0] += part[:, :rhs]
            total_ref[box, 1] += part[:, rhs:]
            return carry

        lax.fori_loop(0, (total + GROUP - 1) // GROUP, group, 0)
        result_copy(box, False).start()
        return carry

    lax.fori_loop(0, boxes, one_box, 0)
    for box in range(boxes):
        result_copy(box, False).wait()


def near_field(ids, used, rank, blocks, sources, first, before=None):
    boxes, slots, _, basis, _ = blocks.shape
    rhs = sources[0].shape[3]
    count = len(sources)
    begun = before is not None
    hbm = pl.BlockSpec(memory_space=pltpu.HBM)
    smem = pl.BlockSpec(memory_space=pltpu.SMEM)
    return pl.pallas_call(
        functools.partial(near_kernel, first, count, begun),
        in_specs=[smem] * 3 + [hbm] * (1 + count + begun),
        out_specs=hbm,
        out_shape=pltpu.HBM((boxes, 2, basis, rhs), F32),
        scratch_shapes=[
            pltpu.VMEM(blocks.shape, BF16),
            pltpu.VMEM((count * boxes, 2, basis, rhs), BF16),
            pltpu.VMEM((count * boxes, 2 * basis, 2 * rhs), BF16),
            pltpu.VMEM((boxes, 2, basis, rhs), F32),
            pltpu.SMEM((slots + 1,), jnp.int32),
            pltpu.SemaphoreType.DMA((2 * boxes + count,)),
        ],
        compiler_params=pltpu.CompilerParams(vmem_limit_bytes=24 * MIB),
        cost_estimate=pl.CostEstimate(
            flops=10**11 if first == 2 else 2 * 10**9, bytes_accessed=8 * MIB, transcendentals=0
        ),
        name=("near_low", "near_own", "near_high")[first],
    )(ids, used, rank, *in_hbm(blocks, *sources, *([before] if begun else [])))


def adjoint_kernel(rad_ref, out_hbm, held):
    for box in range(rad_ref.shape[0]):
        held[box] = side_by_side(rad_ref[box, 0].T, rad_ref[box, 1].T)
    pltpu.sync_copy(held, out_hbm)


def adjoint(radiation):
    boxes, _, points, basis = radiation.shape
    return pl.pallas_call(
        adjoint_kernel,
        in_specs=[pl.BlockSpec(memory_space=pltpu.VMEM)],
        out_specs=pl.BlockSpec(memory_space=pltpu.HBM),
        scratch_shapes=[pltpu.VMEM((boxes, basis, 2 * points), BF16)],
        out_shape=pltpu.HBM((boxes, basis, 2 * points), BF16),
        cost_estimate=pl.CostEstimate(
            flops=10**6, bytes_accessed=2 * MIB, transcendentals=0
        ),
        name="adjoint",
    )(radiation)


def down_kernel(phi_ref, w_hbm, adjoint_hbm, near_hbm, *refs):
    bands_ref, received = refs[0], refs[1:-6]
    out_hbm, field, w, left, held, sems = refs[-6:]
    boxes, _, width = left.shape
    points = width // 2
    rhs = held.shape[3]
    phi = phi_ref[0]
    phi_size = field.shape[1]
    pairs = [(w_hbm, w), (bands_ref.at[:, phi], field.at[:, phi])]
    for distance, piece in enumerate(received, 1):
        pairs.append((piece, field.at[:, lax.rem(phi + phi_size - distance, phi_size)]))
    first = len(pairs)
    pairs += [(adjoint_hbm, left), (near_hbm, held)]
    copies = [
        pltpu.make_async_copy(source, target, sems.at[boxes + place])
        for place, (source, target) in enumerate(pairs)
    ]
    out_copies = [
        pltpu.make_async_copy(held.at[box], out_hbm.at[box], sems.at[box]) for box in range(boxes)
    ]
    for copy in copies:
        copy.start()
    for copy in copies[:first]:
        copy.wait()
    mixed = dot(w[...], field[...].reshape(w.shape[1], 2 * rhs))
    for copy in copies[first:]:
        copy.wait()
    for octant in range(boxes // 2):
        start = 2 * octant * points
        cos_part = mixed[start : start + points]
        sin_part = mixed[start + points : start + 2 * points]
        cos_re, cos_im = cos_part[:, :rhs], cos_part[:, rhs:]
        sin_re, sin_im = sin_part[:, :rhs], sin_part[:, rhs:]
        leaves = (
            (octant, cos_re + sin_im, cos_im - sin_re),
            (boxes - 1 - octant, cos_re - sin_im, cos_im + sin_re),
        )
        for box, real, imag in leaves:
            real, imag = real.astype(BF16), imag.astype(BF16)
            right = jnp.concatenate([side_by_side(real, imag), side_by_side(imag, -real)], axis=0)
            far = dot(left[box], right)
            held[box, 0] += far[:, :rhs]
            held[box, 1] += far[:, rhs:]
            out_copies[box].start()
    for copy in out_copies:
        copy.wait()


def downward(phi, bands, received, weights, radiation_adjoint, near):
    boxes = near.shape[0]
    anywhere = pl.BlockSpec(memory_space=pl.ANY)
    hbm = pl.BlockSpec(memory_space=pltpu.HBM)
    return pl.pallas_call(
        down_kernel,
        in_specs=[pl.BlockSpec(memory_space=pltpu.SMEM)]
        + [hbm] * 3
        + [anywhere] * (1 + len(received)),
        out_specs=hbm,
        out_shape=jax.ShapeDtypeStruct(near.shape, F32),
        scratch_shapes=[
            pltpu.VMEM(bands.shape, BF16),
            pltpu.VMEM(weights.shape, BF16),
            pltpu.VMEM(radiation_adjoint.shape, BF16),
            pltpu.VMEM(near.shape, F32),
            pltpu.SemaphoreType.DMA((boxes + 4 + len(received),)),
        ],
        compiler_params=pltpu.CompilerParams(vmem_limit_bytes=32 * MIB),
        cost_estimate=pl.CostEstimate(
            flops=2 * 10**9, bytes_accessed=7 * MIB, transcendentals=0
        ),
        name="downward",
    )(phi, *in_hbm(weights, radiation_adjoint, near), bands, *received)


def shift(block, axis, step):
    count = lax.axis_size(axis)
    pairs = [(i, i + step) for i in range(count) if 0 <= i + step < count]
    return lax.ppermute(block, axis, pairs)


def lists_of(partners, vector_ids, pair_count):
    used = jnp.arange(partners.shape[1])[None, :] < pair_count[:, None]
    names = jnp.where(used, partners, NOWHERE)
    return jnp.stack([names, vector_ids], axis=2).reshape(-1, 2)


def parent_bands(spread, shares):
    axes = ("box", "theta", "phi") if shares == lax.axis_size("box") else ("theta", "phi")
    return lax.all_to_all(spread, axes, split_axis=0, concat_axis=0, tiled=True)


def staged_bands(incoming, shares):
    axes = ("box", "theta") if shares == lax.axis_size("box") else ("theta",)
    phi_size = lax.axis_size("phi")
    phi = lax.axis_index("phi")
    bands = incoming.reshape(-1, phi_size, *incoming.shape[1:])
    bands = lax.all_to_all(bands, axes, split_axis=0, concat_axis=0, tiled=True)
    received = []
    for distance in range(1, phi_size):
        piece = lax.dynamic_index_in_dim(bands, (phi + distance) % phi_size, 1, keepdims=False)
        ring = [(place, (place + distance) % phi_size) for place in range(phi_size)]
        received.append(lax.ppermute(piece, "phi", ring))
    return phi.astype(jnp.int32).reshape(1), bands, received


def translation_lines(lists, translation, shares, per_group):
    operator_total, _, theta_band, phi_band = translation.shape
    rank = lax.axis_index("box")
    if shares < lax.axis_size("box"):
        table = translation.reshape(operator_total, -1)
        base = ((rank - 1) * per_group).astype(jnp.int32).reshape(1)
        return couplings(lists, base, table, per_group, 3 * per_group)
    if shares == 2:
        other = lax.ppermute(lists, "box", [(0, 1), (1, 0)])
        lists = jnp.where(
            rank == 0, jnp.concatenate([lists, other]), jnp.concatenate([other, lists])
        )
    part = theta_band // shares
    table = lax.dynamic_slice_in_dim(translation, rank * part, part, axis=2)
    table = table.reshape(operator_total, -1)
    total = shares * per_group
    return couplings(lists, jnp.zeros((1,), jnp.int32), table, total, total)


def per_device(
    shares,
    up_weights,
    down_weights,
    coeffs,
    near_blocks,
    near_ids,
    near_count,
    radiation,
    partners,
    vector_ids,
    pair_count,
    translation,
):
    every = ("box", "theta", "phi")
    per_group = lax.axis_size("theta") * lax.axis_size("phi")
    rank = lax.axis_index(every).astype(jnp.int32).reshape(1)
    low = shift(coeffs, every, 1)
    spread = upward(coeffs, radiation, up_weights, shares * per_group)
    radiation_adjoint = adjoint(radiation)
    lists = lists_of(partners, vector_ids, pair_count)
    spread, lists = lax.optimization_barrier((spread, lists))
    lines = translation_lines(lists, translation, shares, per_group)
    spread, lines, radiation_adjoint = lax.optimization_barrier((spread, lines, radiation_adjoint))
    parents = parent_bands(spread, shares)
    near = near_field(near_ids, near_count, rank, near_blocks, [low], 0)
    near, late = lax.optimization_barrier((near, coeffs))
    high = shift(late, every, -1)
    parents, near = lax.optimization_barrier((parents, near))
    sources = [parents]
    if shares < lax.axis_size("box"):
        sources = [shift(parents, "box", 1), parents, shift(parents, "box", -1)]
    incoming = translate(lines, sources)
    incoming, near = lax.optimization_barrier((incoming, near))
    phi, bands, received = staged_bands(incoming, shares)
    near = near_field(near_ids, near_count, rank, near_blocks, [coeffs], 1, near)
    near = near_field(near_ids, near_count, rank, near_blocks, [high], 2, near)
    return downward(phi, bands, received, down_weights, radiation_adjoint, near)


def solution(mesh):
    box_size, theta_size, phi_size = (mesh.shape[axis] for axis in ("box", "theta", "phi"))
    shares = box_size if box_size <= 2 and TU // theta_size % box_size == 0 else 1
    up_weights, down_weights = operators(shares, theta_size, phi_size)
    in_specs = (
        P(),
        P(),
        P(("box", "theta", "phi"), None, None, None),
        P(("box", "theta", "phi"), None, None, None, None),
        P(("box", "theta", "phi"), None),
        P(("box", "theta", "phi")),
        P(("box", "theta", "phi"), None, None, None),
        P("box", None),
        P("box", None),
        P("box"),
        P(None, None, "theta", "phi"),
    )
    out_specs = P(("box", "theta", "phi"), None, None, None)
    mapped = jax.shard_map(
        functools.partial(per_device, shares),
        mesh=mesh,
        in_specs=in_specs,
        out_specs=out_specs,
        check_vma=False,
    )

    def product(*arrays):
        return mapped(jnp.asarray(up_weights), jnp.asarray(down_weights), *arrays)

    return product
```

```python
import functools
import math

import jax
import jax.numpy as jnp
import ml_dtypes
import numpy as np
from jax import lax
from jax.experimental import pallas as pl
from jax.experimental.pallas import tpu as pltpu
from jax.sharding import PartitionSpec as P

TL = 8
PL = 16
TU = 16
PU = 32

WEIGHT_UP = (-0.0546875, 0.8203125, 0.2734375, -0.0390625)
WEIGHT_DOWN = (-0.0390625, 0.2734375, 0.8203125, -0.0546875)
PHASE_SCALE = 1.3

F32 = jnp.float32
BF16 = jnp.bfloat16
MIB = 2**20
GROUP = 4
NOWHERE = -(2**20)


def lagrange(rows, columns, wrap):
    matrix = np.zeros((rows, columns))
    for row in range(rows):
        weights = WEIGHT_UP if row % 2 else WEIGHT_DOWN
        for order in range(4):
            node = row // 2 + row % 2 - 2 + order
            node = node % columns if wrap else min(max(node, 0), columns - 1)
            matrix[row, node] += weights[order]
    return matrix


def split_weights(matrix):
    high = matrix.astype(ml_dtypes.bfloat16)
    low = (matrix - high.astype(np.float64)).astype(ml_dtypes.bfloat16)
    return high, low


def operators(shares, theta_size, phi_size):
    theta_part = TU // theta_size // shares
    order = np.arange(TU * PU).reshape(theta_size, shares, theta_part, phi_size, PU // phi_size)
    order = order.transpose(1, 0, 3, 2, 4).reshape(-1)
    interp = np.kron(lagrange(TU, TL, False), lagrange(PU, PL, True))
    theta = math.pi * (np.arange(TU) + 0.5) / TU
    azimuth = 2.0 * math.pi * (np.arange(PU) + 0.5) / PU
    up, down = [], []
    for octant in range(4):
        sign_x = 2 * (octant % 2) - 1
        sign_y = 2 * (octant // 2 % 2) - 1
        sign_z = 2 * (octant // 4) - 1
        angle = PHASE_SCALE * (
            sign_x * np.sin(theta)[:, None] * np.cos(azimuth)[None]
            + sign_y * np.sin(theta)[:, None] * np.sin(azimuth)[None]
            + sign_z * np.cos(theta)[:, None]
        ).reshape(-1, 1)
        cos_high, cos_low = split_weights((np.cos(angle) * interp)[order])
        sin_high, sin_low = split_weights((np.sin(angle) * interp)[order])
        high = np.concatenate([cos_high, sin_high], axis=1)
        low = np.concatenate([cos_low, sin_low], axis=1)
        up.append(np.concatenate([high, low], axis=0))
        down += [cos_high.T, sin_high.T]
    return np.concatenate(up, axis=1), np.concatenate(down, axis=0)


def in_hbm(*arrays):
    return [pltpu.with_memory_space_constraint(array, pltpu.HBM) for array in arrays]


def dot(a, b):
    return jnp.dot(a, b, preferred_element_type=F32)


def side_by_side(real, imag):
    return jnp.concatenate([real, imag], axis=1)


def complex_columns(real, imag):
    return jnp.concatenate([side_by_side(real, imag), side_by_side(-imag, real)], axis=0)


def up_kernel(x_hbm, rad_hbm, w_hbm, out_hbm, x_ref, rad_ref, w_ref, right, result, sems):
    boxes, _, _, rhs = x_ref.shape
    points = rad_ref.shape[2]
    copies = [
        pltpu.make_async_copy(source, target, sems.at[place])
        for place, (source, target) in enumerate(
            ((x_hbm, x_ref), (rad_hbm, rad_ref), (w_hbm, w_ref))
        )
    ]
    for copy in copies:
        copy.start()
    copies[0].wait()
    copies[1].wait()
    half = boxes // 2
    for octant in range(boxes):
        left = side_by_side(rad_ref[octant, 0], rad_ref[octant, 1])
        straight = dot(left, complex_columns(x_ref[octant, 0], x_ref[octant, 1])).astype(BF16)
        real, imag = straight[:, :rhs], straight[:, rhs:]
        if octant < half:
            swapped = side_by_side(-imag, real)
        else:
            swapped = side_by_side(imag, -real)
        place = octant if octant < half else boxes - 1 - octant
        start = 2 * place * points
        right[octant // half, start : start + points] = straight
        right[octant // half, start + points : start + 2 * points] = swapped
    copies[2].wait()
    total = dot(w_ref[...], right[0]) + dot(w_ref[...], right[1])
    samples = total.shape[0] // 2
    total = total[:samples] + total[samples:]
    result[...] = total.astype(BF16).reshape(result.shape)
    pltpu.sync_copy(result, out_hbm)


def upward(coeffs, radiation, weights, groups):
    boxes, _, basis, rhs = coeffs.shape
    rows, columns = weights.shape
    samples = rows // 2
    hbm = pl.BlockSpec(memory_space=pltpu.HBM)
    return pl.pallas_call(
        up_kernel,
        in_specs=[hbm] * 3,
        out_specs=hbm,
        out_shape=pltpu.HBM((groups, samples // groups, 2 * rhs), BF16),
        scratch_shapes=[
            pltpu.VMEM(coeffs.shape, BF16),
            pltpu.VMEM(radiation.shape, BF16),
            pltpu.VMEM(weights.shape, BF16),
            pltpu.VMEM((2, columns, 2 * rhs), BF16),
            pltpu.VMEM((groups, samples // groups, 2 * rhs), BF16),
            pltpu.SemaphoreType.DMA((3,)),
        ],
        compiler_params=pltpu.CompilerParams(vmem_limit_bytes=32 * MIB),
        cost_estimate=pl.CostEstimate(
            flops=2 * 10**9, bytes_accessed=4 * MIB, transcendentals=0
        ),
        name="upward",
    )(*in_hbm(coeffs, radiation, weights))


def coupling_kernel(lists_ref, base_ref, table_ref, out_ref):
    rows = lists_ref.shape[0]
    samples = table_ref.shape[1] // 2
    _, targets, columns = out_ref.shape
    slots = rows // targets
    selector = (
        lax.broadcasted_iota(jnp.int32, (rows, table_ref.shape[0]), 1) == lists_ref[:, 1:2]
    )
    chosen = dot(selector.astype(BF16), table_ref[...]).astype(BF16)
    wide = lax.broadcasted_iota(jnp.int32, (rows, columns), 1) // samples
    match = wide + base_ref[0] == lists_ref[:, 0:1]
    spread = lax.broadcasted_iota(jnp.int32, (samples, columns), 0) == (
        lax.broadcasted_iota(jnp.int32, (samples, columns), 1) % samples
    )
    gather = (
        lax.broadcasted_iota(jnp.int32, (targets, rows), 1) // slots
        == lax.broadcasted_iota(jnp.int32, (targets, rows), 0)
    ).astype(BF16)
    tile = spread.astype(BF16)
    for part in range(2):
        lines = dot(chosen[:, part * samples : (part + 1) * samples], tile)
        out_ref[part] = dot(gather, jnp.where(match, lines, 0.0).astype(BF16))


def couplings(lists, base, table, targets, names):
    shape = (2, targets, names * (table.shape[1] // 2))
    vmem = pl.BlockSpec(memory_space=pltpu.VMEM)
    return pl.pallas_call(
        coupling_kernel,
        in_specs=[vmem, pl.BlockSpec(memory_space=pltpu.SMEM), vmem],
        out_specs=vmem,
        out_shape=jax.ShapeDtypeStruct(shape, F32),
        compiler_params=pltpu.CompilerParams(vmem_limit_bytes=16 * MIB),
        cost_estimate=pl.CostEstimate(
            flops=2 * 10**8, bytes_accessed=2 * 2**20, transcendentals=0
        ),
        name="coupling",
    )(lists, base, table)


def translate_kernel(lines_hbm, *refs):
    count = (len(refs) - 5) // 2
    sources, out_hbm = refs[:count], refs[count]
    held, lines, matrix, result, sems = refs[count + 1 :][:count], *refs[2 * count + 1 :]
    targets, samples, width = result.shape
    rhs = width // 2
    copies = [
        pltpu.make_async_copy(source, target, sems.at[place])
        for place, (source, target) in enumerate(zip((lines_hbm, *sources), (lines, *held)))
    ]
    for copy in copies:
        copy.start()
    copies[0].wait()
    columns = matrix.shape[1]
    row = lax.broadcasted_iota(jnp.int32, (samples, columns), 0)
    diagonal = row == lax.broadcasted_iota(jnp.int32, (samples, columns), 1) % samples
    for part in range(2):
        for target in range(targets):
            line = jnp.broadcast_to(lines[part, target : target + 1], diagonal.shape)
            start = (part * targets + target) * samples
            matrix[start : start + samples] = jnp.where(diagonal, line, 0.0).astype(BF16)
    total = None
    start = 0
    for place, source in enumerate(held):
        copies[1 + place].wait()
        stop = start + source.shape[0] * samples
        part = dot(matrix[:, start:stop], source[...].reshape(stop - start, width))
        total = part if total is None else total + part
        start = stop
    half = targets * samples
    real = total[:half, :rhs] - total[half:, rhs:]
    imag = total[:half, rhs:] + total[half:, :rhs]
    result[...] = jnp.concatenate([real, imag], axis=1).astype(BF16).reshape(result.shape)
    pltpu.sync_copy(result, out_hbm)


def translate(lines, sources):
    _, samples, width = sources[0].shape
    _, targets, columns = lines.shape
    shape = (targets, samples, width)
    hbm = pl.BlockSpec(memory_space=pltpu.HBM)
    anywhere = pl.BlockSpec(memory_space=pl.ANY)
    return pl.pallas_call(
        translate_kernel,
        in_specs=[hbm] + [anywhere] * len(sources),
        out_specs=hbm,
        out_shape=pltpu.HBM(shape, BF16),
        scratch_shapes=[
            *[pltpu.VMEM(source.shape, BF16) for source in sources],
            pltpu.VMEM(lines.shape, F32),
            pltpu.VMEM((2 * targets * samples, columns), BF16),
            pltpu.VMEM(shape, BF16),
            pltpu.SemaphoreType.DMA((1 + len(sources),)),
        ],
        compiler_params=pltpu.CompilerParams(vmem_limit_bytes=24 * MIB),
        cost_estimate=pl.CostEstimate(
            flops=10**9, bytes_accessed=2 * MIB, transcendentals=0
        ),
        name="translate",
    )(*in_hbm(lines), *sources)


def near_kernel(first, begun, kept, *refs):
    refs = list(refs)
    ids_ref, used_ref, rank_ref, blocks_hbm, source_hbm = refs[:5]
    before_hbm = refs[5] if begun else None
    kept_hbm = refs[5 + begun : 5 + begun + kept]
    out_ref = refs[5 + begun + kept]
    kept_refs = refs[6 + begun + kept : 6 + begun + 2 * kept]
    blocks, held, wide, total_ref, listed, sems = refs[6 + begun + 2 * kept :]
    boxes, _, basis, rhs = held.shape
    slots = blocks_hbm.shape[1]
    most = boxes * slots
    base = (rank_ref[0] - 1 + first) * boxes
    others = [pltpu.make_async_copy(source_hbm, held, sems.at[most])]
    if begun:
        others.append(pltpu.make_async_copy(before_hbm, total_ref, sems.at[most + 1]))
    for place in range(kept):
        others.append(
            pltpu.make_async_copy(kept_hbm[place], kept_refs[place], sems.at[most + 2 + place])
        )
    for copy in others:
        copy.start()

    def block_copy(box, slot, place):
        return pltpu.make_async_copy(blocks_hbm.at[box, slot], blocks.at[place], sems.at[place])

    starts = [jnp.int32(0)]
    for box in range(boxes):
        place = starts[box]
        for slot in range(slots):
            source = ids_ref[box, slot] - base
            wanted = (slot < used_ref[box]) & (source >= 0) & (source < boxes)

            @pl.when(wanted)
            def _(box=box, slot=slot, place=place, source=source):
                listed[place] = source
                block_copy(box, slot, place).start()

            place += wanted.astype(jnp.int32)
        starts.append(place)
    others[0].wait()
    for place in range(boxes):
        wide[place] = complex_columns(held[place, 0], held[place, 1])

    def landed(place, carry):
        block_copy(0, 0, place).wait()
        return carry

    lax.fori_loop(0, starts[boxes], landed, 0)
    for copy in others[1:]:
        copy.wait()

    def group(box, index):
        left, right = [], []
        for step in range(GROUP):
            place = starts[box] + index * GROUP + step
            valid = place < starts[box + 1]
            place = jnp.where(valid, place, 0)
            real, imag = blocks[place, 0], blocks[place, 1]
            real = jnp.where(valid, real, jnp.zeros_like(real))
            imag = jnp.where(valid, imag, jnp.zeros_like(imag))
            left.append(side_by_side(real, imag))
            right.append(wide[jnp.where(valid, listed[place], 0)])
        return dot(jnp.concatenate(left, axis=1), jnp.concatenate(right, axis=0))

    for box in range(boxes):
        part = group(box, 0)
        if begun:
            total_ref[box, 0] += part[:, :rhs]
            total_ref[box, 1] += part[:, rhs:]
        else:
            total_ref[box, 0] = part[:, :rhs]
            total_ref[box, 1] = part[:, rhs:]
    for box in range(boxes):

        def more(index, carry, box=box):
            part = group(box, index)
            total_ref[box, 0] += part[:, :rhs]
            total_ref[box, 1] += part[:, rhs:]
            return carry

        lax.fori_loop(1, (starts[box + 1] - starts[box] + GROUP - 1) // GROUP, more, 0)
    if not kept:
        pltpu.sync_copy(total_ref, out_ref)


def near_field(ids, used, rank, blocks, source, first, before=None, keep=()):
    boxes, slots, _, basis, _ = blocks.shape
    rhs = source.shape[3]
    begun, kept = before is not None, len(keep)
    hbm = pl.BlockSpec(memory_space=pltpu.HBM)
    smem = pl.BlockSpec(memory_space=pltpu.SMEM)
    vmem = pl.BlockSpec(memory_space=pltpu.VMEM)
    shape = (boxes, 2, basis, rhs)
    scratch = [
        pltpu.VMEM((boxes * slots, *blocks.shape[2:]), BF16),
        pltpu.VMEM(source.shape, BF16),
        pltpu.VMEM((boxes, 2 * basis, 2 * rhs), BF16),
        pltpu.VMEM(shape, F32),
        pltpu.SMEM((boxes * slots,), jnp.int32),
        pltpu.SemaphoreType.DMA((boxes * slots + 2 + kept,)),
    ]
    kernel = functools.partial(near_kernel, first, begun, kept)
    if kept:
        del scratch[3]
        inner = kernel

        def kernel(*refs):
            place = 5 + begun + kept
            inner(*refs[:-2], refs[place], *refs[-2:])

    return pl.pallas_call(
        kernel,
        in_specs=[smem] * 3 + [hbm] * (2 + begun + kept),
        out_specs=[vmem] * (1 + kept) if kept else hbm,
        out_shape=[
            pltpu.VMEM(shape, F32),
            *[pltpu.VMEM(array.shape, array.dtype) for array in keep],
        ]
        if kept
        else pltpu.HBM(shape, F32),
        scratch_shapes=scratch,
        compiler_params=pltpu.CompilerParams(vmem_limit_bytes=32 * MIB),
        cost_estimate=pl.CostEstimate(
            flops=10**11 if first == 2 else 2 * 10**9, bytes_accessed=8 * MIB, transcendentals=0
        ),
        name=("near_low", "near_own", "near_high")[first],
    )(ids, used, rank, *in_hbm(blocks, source, *([before] if begun else []), *keep))


def adjoint_kernel(rad_ref, out_hbm, held):
    for box in range(rad_ref.shape[0]):
        held[box] = side_by_side(rad_ref[box, 0].T, rad_ref[box, 1].T)
    pltpu.sync_copy(held, out_hbm)


def adjoint(radiation):
    boxes, _, points, basis = radiation.shape
    return pl.pallas_call(
        adjoint_kernel,
        in_specs=[pl.BlockSpec(memory_space=pltpu.VMEM)],
        out_specs=pl.BlockSpec(memory_space=pltpu.HBM),
        scratch_shapes=[pltpu.VMEM((boxes, basis, 2 * points), BF16)],
        out_shape=pltpu.HBM((boxes, basis, 2 * points), BF16),
        cost_estimate=pl.CostEstimate(
            flops=10**6, bytes_accessed=2 * MIB, transcendentals=0
        ),
        name="adjoint",
    )(radiation)


def down_kernel(phi_ref, near_ref, w_ref, adjoint_ref, *refs):
    bands_ref, received = refs[0], refs[1:-4]
    out_hbm, field, held, sems = refs[-4:]
    boxes, _, width = adjoint_ref.shape
    points = width // 2
    rhs = held.shape[3]
    phi = phi_ref[0]
    phi_size = field.shape[1]
    pairs = [(bands_ref.at[:, phi], field.at[:, phi])]
    for distance, piece in enumerate(received, 1):
        pairs.append((piece, field.at[:, lax.rem(phi + phi_size - distance, phi_size)]))
    copies = [
        pltpu.make_async_copy(source, target, sems.at[boxes + place])
        for place, (source, target) in enumerate(pairs)
    ]
    out_copies = [
        pltpu.make_async_copy(held.at[box], out_hbm.at[box], sems.at[box]) for box in range(boxes)
    ]
    for copy in copies:
        copy.start()
    for copy in copies:
        copy.wait()
    mixed = dot(w_ref[...], field[...].reshape(w_ref.shape[1], 2 * rhs))
    for octant in range(boxes // 2):
        start = 2 * octant * points
        cos_part = mixed[start : start + points]
        sin_part = mixed[start + points : start + 2 * points]
        cos_re, cos_im = cos_part[:, :rhs], cos_part[:, rhs:]
        sin_re, sin_im = sin_part[:, :rhs], sin_part[:, rhs:]
        leaves = (
            (octant, cos_re + sin_im, cos_im - sin_re),
            (boxes - 1 - octant, cos_re - sin_im, cos_im + sin_re),
        )
        for box, real, imag in leaves:
            real, imag = real.astype(BF16), imag.astype(BF16)
            right = jnp.concatenate([side_by_side(real, imag), side_by_side(imag, -real)], axis=0)
            far = dot(adjoint_ref[box], right)
            held[box, 0] = near_ref[box, 0] + far[:, :rhs]
            held[box, 1] = near_ref[box, 1] + far[:, rhs:]
            out_copies[box].start()
    for copy in out_copies:
        copy.wait()


def downward(phi, bands, received, near, weights, radiation_adjoint):
    boxes = near.shape[0]
    anywhere = pl.BlockSpec(memory_space=pl.ANY)
    ready = [
        pltpu.with_memory_space_constraint(array, pltpu.VMEM)
        for array in (near, weights, radiation_adjoint)
    ]
    return pl.pallas_call(
        down_kernel,
        in_specs=[pl.BlockSpec(memory_space=pltpu.SMEM)]
        + [pl.BlockSpec(memory_space=pltpu.VMEM)] * 3
        + [anywhere] * (1 + len(received)),
        out_specs=pl.BlockSpec(memory_space=pltpu.HBM),
        out_shape=jax.ShapeDtypeStruct(near.shape, F32),
        scratch_shapes=[
            pltpu.VMEM(bands.shape, BF16),
            pltpu.VMEM(near.shape, F32),
            pltpu.SemaphoreType.DMA((boxes + 1 + len(received),)),
        ],
        compiler_params=pltpu.CompilerParams(vmem_limit_bytes=32 * MIB),
        cost_estimate=pl.CostEstimate(
            flops=2 * 10**9, bytes_accessed=7 * MIB, transcendentals=0
        ),
        name="downward",
    )(phi, *ready, bands, *received)


def shift(block, axis, step):
    count = lax.axis_size(axis)
    pairs = [(i, i + step) for i in range(count) if 0 <= i + step < count]
    return lax.ppermute(block, axis, pairs)


def lists_of(partners, vector_ids, pair_count):
    used = jnp.arange(partners.shape[1])[None, :] < pair_count[:, None]
    names = jnp.where(used, partners, NOWHERE)
    return jnp.stack([names, vector_ids], axis=2).reshape(-1, 2)


def parent_bands(spread, shares):
    axes = ("box", "theta", "phi") if shares == lax.axis_size("box") else ("theta", "phi")
    return lax.all_to_all(spread, axes, split_axis=0, concat_axis=0, tiled=True)


def staged_bands(incoming, shares):
    axes = ("box", "theta") if shares == lax.axis_size("box") else ("theta",)
    phi_size = lax.axis_size("phi")
    phi = lax.axis_index("phi")
    bands = incoming.reshape(-1, phi_size, *incoming.shape[1:])
    bands = lax.all_to_all(bands, axes, split_axis=0, concat_axis=0, tiled=True)
    received = []
    for distance in range(1, phi_size):
        piece = lax.dynamic_index_in_dim(bands, (phi + distance) % phi_size, 1, keepdims=False)
        ring = [(place, (place + distance) % phi_size) for place in range(phi_size)]
        received.append(lax.ppermute(piece, "phi", ring))
    return phi.astype(jnp.int32).reshape(1), bands, received


def translation_lines(lists, translation, shares, per_group):
    operator_total, _, theta_band, phi_band = translation.shape
    rank = lax.axis_index("box")
    if shares < lax.axis_size("box"):
        table = translation.reshape(operator_total, -1)
        base = ((rank - 1) * per_group).astype(jnp.int32).reshape(1)
        return couplings(lists, base, table, per_group, 3 * per_group)
    if shares == 2:
        other = lax.ppermute(lists, "box", [(0, 1), (1, 0)])
        lists = jnp.where(
            rank == 0, jnp.concatenate([lists, other]), jnp.concatenate([other, lists])
        )
    part = theta_band // shares
    table = lax.dynamic_slice_in_dim(translation, rank * part, part, axis=2)
    table = table.reshape(operator_total, -1)
    total = shares * per_group
    return couplings(lists, jnp.zeros((1,), jnp.int32), table, total, total)


def per_device(
    shares,
    up_weights,
    down_weights,
    coeffs,
    near_blocks,
    near_ids,
    near_count,
    radiation,
    partners,
    vector_ids,
    pair_count,
    translation,
):
    every = ("box", "theta", "phi")
    per_group = lax.axis_size("theta") * lax.axis_size("phi")
    rank = lax.axis_index(every).astype(jnp.int32).reshape(1)
    low = shift(coeffs, every, 1)
    spread = upward(coeffs, radiation, up_weights, shares * per_group)
    radiation_adjoint = adjoint(radiation)
    lists = lists_of(partners, vector_ids, pair_count)
    spread, lists = lax.optimization_barrier((spread, lists))
    lines = translation_lines(lists, translation, shares, per_group)
    spread, lines, radiation_adjoint = lax.optimization_barrier((spread, lines, radiation_adjoint))
    parents = parent_bands(spread, shares)
    slots = (near_ids, near_count, rank, near_blocks)
    near = near_field(*slots, low, 0)
    near, late = lax.optimization_barrier((near, coeffs))
    high = shift(late, every, -1)
    parents, near = lax.optimization_barrier((parents, near))
    sources = [parents]
    if shares < lax.axis_size("box"):
        sources = [shift(parents, "box", 1), parents, shift(parents, "box", -1)]
    incoming = translate(lines, sources)
    incoming, near = lax.optimization_barrier((incoming, near))
    phi, bands, received = staged_bands(incoming, shares)
    near = near_field(*slots, coeffs, 1, near)
    ready = near_field(*slots, high, 2, near, keep=(down_weights, radiation_adjoint))
    return downward(phi, bands, received, *ready)


def solution(mesh):
    box_size, theta_size, phi_size = (mesh.shape[axis] for axis in ("box", "theta", "phi"))
    shares = box_size if box_size <= 2 and TU // theta_size % box_size == 0 else 1
    up_weights, down_weights = operators(shares, theta_size, phi_size)
    in_specs = (
        P(),
        P(),
        P(("box", "theta", "phi"), None, None, None),
        P(("box", "theta", "phi"), None, None, None, None),
        P(("box", "theta", "phi"), None),
        P(("box", "theta", "phi")),
        P(("box", "theta", "phi"), None, None, None),
        P("box", None),
        P("box", None),
        P("box"),
        P(None, None, "theta", "phi"),
    )
    out_specs = P(("box", "theta", "phi"), None, None, None)
    mapped = jax.shard_map(
        functools.partial(per_device, shares),
        mesh=mesh,
        in_specs=in_specs,
        out_specs=out_specs,
        check_vma=False,
    )

    def product(*arrays):
        return mapped(jnp.asarray(up_weights), jnp.asarray(down_weights), *arrays)

    return product
```

```python
import functools
import math

import jax
import jax.numpy as jnp
import ml_dtypes
import numpy as np
from jax import lax
from jax.experimental import pallas as pl
from jax.experimental.pallas import tpu as pltpu
from jax.sharding import PartitionSpec as P

TL = 8
PL = 16
TU = 16
PU = 32

WEIGHT_UP = (-0.0546875, 0.8203125, 0.2734375, -0.0390625)
WEIGHT_DOWN = (-0.0390625, 0.2734375, 0.8203125, -0.0546875)
PHASE_SCALE = 1.3

F32 = jnp.float32
BF16 = jnp.bfloat16
MIB = 2**20
GROUP = 4
NOWHERE = -(2**20)


def lagrange(rows, columns, wrap):
    matrix = np.zeros((rows, columns))
    for row in range(rows):
        weights = WEIGHT_UP if row % 2 else WEIGHT_DOWN
        for order in range(4):
            node = row // 2 + row % 2 - 2 + order
            node = node % columns if wrap else min(max(node, 0), columns - 1)
            matrix[row, node] += weights[order]
    return matrix


def split_weights(matrix):
    high = matrix.astype(ml_dtypes.bfloat16)
    low = (matrix - high.astype(np.float64)).astype(ml_dtypes.bfloat16)
    return high, low


def operators(shares, theta_size, phi_size):
    theta_part = TU // theta_size // shares
    order = np.arange(TU * PU).reshape(theta_size, shares, theta_part, phi_size, PU // phi_size)
    order = order.transpose(1, 0, 3, 2, 4).reshape(-1)
    interp = np.kron(lagrange(TU, TL, False), lagrange(PU, PL, True))
    theta = math.pi * (np.arange(TU) + 0.5) / TU
    azimuth = 2.0 * math.pi * (np.arange(PU) + 0.5) / PU
    up, down = [], []
    for octant in range(4):
        sign_x = 2 * (octant % 2) - 1
        sign_y = 2 * (octant // 2 % 2) - 1
        sign_z = 2 * (octant // 4) - 1
        angle = PHASE_SCALE * (
            sign_x * np.sin(theta)[:, None] * np.cos(azimuth)[None]
            + sign_y * np.sin(theta)[:, None] * np.sin(azimuth)[None]
            + sign_z * np.cos(theta)[:, None]
        ).reshape(-1, 1)
        cos_high, cos_low = split_weights((np.cos(angle) * interp)[order])
        sin_high, sin_low = split_weights((np.sin(angle) * interp)[order])
        high = np.concatenate([cos_high, sin_high], axis=1)
        low = np.concatenate([cos_low, sin_low], axis=1)
        up.append(np.concatenate([high, low], axis=0))
        down += [cos_high.T, sin_high.T]
    return np.concatenate(up, axis=1), np.concatenate(down, axis=0)


def in_hbm(*arrays):
    return [pltpu.with_memory_space_constraint(array, pltpu.HBM) for array in arrays]


def dot(a, b):
    return jnp.dot(a, b, preferred_element_type=F32)


def side_by_side(real, imag):
    return jnp.concatenate([real, imag], axis=1)


def complex_columns(real, imag):
    return jnp.concatenate([side_by_side(real, imag), side_by_side(-imag, real)], axis=0)


def up_kernel(x_hbm, rad_hbm, w_hbm, out_hbm, x_ref, rad_ref, w_ref, right, result, sems):
    boxes, _, _, rhs = x_ref.shape
    points = rad_ref.shape[2]
    copies = [
        pltpu.make_async_copy(source, target, sems.at[place])
        for place, (source, target) in enumerate(
            ((x_hbm, x_ref), (rad_hbm, rad_ref), (w_hbm, w_ref))
        )
    ]
    for copy in copies:
        copy.start()
    copies[0].wait()
    copies[1].wait()
    half = boxes // 2
    for octant in range(boxes):
        left = side_by_side(rad_ref[octant, 0], rad_ref[octant, 1])
        straight = dot(left, complex_columns(x_ref[octant, 0], x_ref[octant, 1])).astype(BF16)
        real, imag = straight[:, :rhs], straight[:, rhs:]
        if octant < half:
            swapped = side_by_side(-imag, real)
        else:
            swapped = side_by_side(imag, -real)
        place = octant if octant < half else boxes - 1 - octant
        start = 2 * place * points
        right[octant // half, start : start + points] = straight
        right[octant // half, start + points : start + 2 * points] = swapped
    copies[2].wait()
    total = dot(w_ref[...], right[0]) + dot(w_ref[...], right[1])
    samples = total.shape[0] // 2
    total = total[:samples] + total[samples:]
    result[...] = total.astype(BF16).reshape(result.shape)
    pltpu.sync_copy(result, out_hbm)


def upward(coeffs, radiation, weights, groups):
    boxes, _, basis, rhs = coeffs.shape
    rows, columns = weights.shape
    samples = rows // 2
    hbm = pl.BlockSpec(memory_space=pltpu.HBM)
    return pl.pallas_call(
        up_kernel,
        in_specs=[hbm] * 3,
        out_specs=hbm,
        out_shape=pltpu.HBM((groups, samples // groups, 2 * rhs), BF16),
        scratch_shapes=[
            pltpu.VMEM(coeffs.shape, BF16),
            pltpu.VMEM(radiation.shape, BF16),
            pltpu.VMEM(weights.shape, BF16),
            pltpu.VMEM((2, columns, 2 * rhs), BF16),
            pltpu.VMEM((groups, samples // groups, 2 * rhs), BF16),
            pltpu.SemaphoreType.DMA((3,)),
        ],
        compiler_params=pltpu.CompilerParams(vmem_limit_bytes=32 * MIB),
        cost_estimate=pl.CostEstimate(
            flops=2 * 10**9, bytes_accessed=4 * MIB, transcendentals=0
        ),
        name="upward",
    )(*in_hbm(coeffs, radiation, weights))


def coupling_kernel(lists_ref, base_ref, table_ref, out_ref):
    rows = lists_ref.shape[0]
    samples = table_ref.shape[1] // 2
    _, targets, columns = out_ref.shape
    slots = rows // targets
    selector = (
        lax.broadcasted_iota(jnp.int32, (rows, table_ref.shape[0]), 1) == lists_ref[:, 1:2]
    )
    chosen = dot(selector.astype(BF16), table_ref[...]).astype(BF16)
    wide = lax.broadcasted_iota(jnp.int32, (rows, columns), 1) // samples
    match = wide + base_ref[0] == lists_ref[:, 0:1]
    spread = lax.broadcasted_iota(jnp.int32, (samples, columns), 0) == (
        lax.broadcasted_iota(jnp.int32, (samples, columns), 1) % samples
    )
    gather = (
        lax.broadcasted_iota(jnp.int32, (targets, rows), 1) // slots
        == lax.broadcasted_iota(jnp.int32, (targets, rows), 0)
    ).astype(BF16)
    tile = spread.astype(BF16)
    for part in range(2):
        lines = dot(chosen[:, part * samples : (part + 1) * samples], tile)
        out_ref[part] = dot(gather, jnp.where(match, lines, 0.0).astype(BF16))


def couplings(lists, base, table, targets, names):
    shape = (2, targets, names * (table.shape[1] // 2))
    vmem = pl.BlockSpec(memory_space=pltpu.VMEM)
    return pl.pallas_call(
        coupling_kernel,
        in_specs=[vmem, pl.BlockSpec(memory_space=pltpu.SMEM), vmem],
        out_specs=vmem,
        out_shape=jax.ShapeDtypeStruct(shape, F32),
        compiler_params=pltpu.CompilerParams(vmem_limit_bytes=16 * MIB),
        cost_estimate=pl.CostEstimate(
            flops=2 * 10**8, bytes_accessed=2 * 2**20, transcendentals=0
        ),
        name="coupling",
    )(lists, base, table)


def translate_kernel(lines_hbm, *refs):
    count = (len(refs) - 5) // 2
    sources, out_hbm = refs[:count], refs[count]
    held, lines, matrix, result, sems = refs[count + 1 :][:count], *refs[2 * count + 1 :]
    targets, samples, width = result.shape
    rhs = width // 2
    copies = [
        pltpu.make_async_copy(source, target, sems.at[place])
        for place, (source, target) in enumerate(zip((lines_hbm, *sources), (lines, *held)))
    ]
    for copy in copies:
        copy.start()
    copies[0].wait()
    columns = matrix.shape[1]
    row = lax.broadcasted_iota(jnp.int32, (samples, columns), 0)
    diagonal = row == lax.broadcasted_iota(jnp.int32, (samples, columns), 1) % samples
    for part in range(2):
        for target in range(targets):
            line = jnp.broadcast_to(lines[part, target : target + 1], diagonal.shape)
            start = (part * targets + target) * samples
            matrix[start : start + samples] = jnp.where(diagonal, line, 0.0).astype(BF16)
    total = None
    start = 0
    for place, source in enumerate(held):
        copies[1 + place].wait()
        stop = start + source.shape[0] * samples
        part = dot(matrix[:, start:stop], source[...].reshape(stop - start, width))
        total = part if total is None else total + part
        start = stop
    half = targets * samples
    real = total[:half, :rhs] - total[half:, rhs:]
    imag = total[:half, rhs:] + total[half:, :rhs]
    result[...] = jnp.concatenate([real, imag], axis=1).astype(BF16).reshape(result.shape)
    pltpu.sync_copy(result, out_hbm)


def translate(lines, sources):
    _, samples, width = sources[0].shape
    _, targets, columns = lines.shape
    shape = (targets, samples, width)
    hbm = pl.BlockSpec(memory_space=pltpu.HBM)
    anywhere = pl.BlockSpec(memory_space=pl.ANY)
    return pl.pallas_call(
        translate_kernel,
        in_specs=[hbm] + [anywhere] * len(sources),
        out_specs=hbm,
        out_shape=pltpu.HBM(shape, BF16),
        scratch_shapes=[
            *[pltpu.VMEM(source.shape, BF16) for source in sources],
            pltpu.VMEM(lines.shape, F32),
            pltpu.VMEM((2 * targets * samples, columns), BF16),
            pltpu.VMEM(shape, BF16),
            pltpu.SemaphoreType.DMA((1 + len(sources),)),
        ],
        compiler_params=pltpu.CompilerParams(vmem_limit_bytes=24 * MIB),
        cost_estimate=pl.CostEstimate(
            flops=10**9, bytes_accessed=2 * MIB, transcendentals=0
        ),
        name="translate",
    )(*in_hbm(lines), *sources)


def near_kernel(first, begun, kept, *refs):
    refs = list(refs)
    ids_ref, used_ref, rank_ref, blocks_hbm, source_hbm = refs[:5]
    before_hbm = refs[5] if begun else None
    kept_hbm = refs[5 + begun : 5 + begun + kept]
    out_ref = refs[5 + begun + kept]
    kept_refs = refs[6 + begun + kept : 6 + begun + 2 * kept]
    blocks, held, wide, total_ref, listed, sems = refs[6 + begun + 2 * kept :]
    boxes, _, basis, rhs = held.shape
    slots = blocks_hbm.shape[1]
    most = boxes * slots
    base = (rank_ref[0] - 1 + first) * boxes

    def by_box(source, target, turn):
        return [
            pltpu.make_async_copy(
                source.at[box], target.at[box], sems.at[most + turn * boxes + box]
            )
            for box in range(boxes)
        ]

    source_copies = by_box(source_hbm, held, 0)
    before_copies = by_box(before_hbm, total_ref, 1) if begun else []
    out_copies = [] if kept else by_box(total_ref, out_ref, 2)
    kept_copies = [
        pltpu.make_async_copy(kept_hbm[place], kept_refs[place], sems.at[most + 3 * boxes + place])
        for place in range(kept)
    ]
    for copy in source_copies:
        copy.start()

    def block_copy(box, slot, place):
        return pltpu.make_async_copy(blocks_hbm.at[box, slot], blocks.at[place], sems.at[place])

    starts = [jnp.int32(0)]
    for box in range(boxes):
        place = starts[box]
        for slot in range(slots):
            source = ids_ref[box, slot] - base
            wanted = (slot < used_ref[box]) & (source >= 0) & (source < boxes)

            @pl.when(wanted)
            def _(box=box, slot=slot, place=place, source=source):
                listed[place] = source
                block_copy(box, slot, place).start()

            place += wanted.astype(jnp.int32)
        starts.append(place)
    for copy in before_copies + kept_copies:
        copy.start()
    for copy in source_copies:
        copy.wait()
    for place in range(boxes):
        wide[place] = complex_columns(held[place, 0], held[place, 1])

    def landed(place, carry):
        block_copy(0, 0, place).wait()
        return carry

    lax.fori_loop(0, starts[boxes], landed, 0)
    for copy in before_copies:
        copy.wait()

    def group(box, index):
        left, right = [], []
        for step in range(GROUP):
            place = starts[box] + index * GROUP + step
            valid = place < starts[box + 1]
            place = jnp.where(valid, place, 0)
            real, imag = blocks[place, 0], blocks[place, 1]
            real = jnp.where(valid, real, jnp.zeros_like(real))
            imag = jnp.where(valid, imag, jnp.zeros_like(imag))
            left.append(side_by_side(real, imag))
            right.append(wide[jnp.where(valid, listed[place], 0)])
        return dot(jnp.concatenate(left, axis=1), jnp.concatenate(right, axis=0))

    for box in range(boxes):
        part = group(box, 0)
        if begun:
            total_ref[box, 0] += part[:, :rhs]
            total_ref[box, 1] += part[:, rhs:]
        else:
            total_ref[box, 0] = part[:, :rhs]
            total_ref[box, 1] = part[:, rhs:]
    for box in range(boxes):

        def more(index, carry, box=box):
            part = group(box, index)
            total_ref[box, 0] += part[:, :rhs]
            total_ref[box, 1] += part[:, rhs:]
            return carry

        lax.fori_loop(1, (starts[box + 1] - starts[box] + GROUP - 1) // GROUP, more, 0)
        if out_copies:
            out_copies[box].start()
    for copy in out_copies + kept_copies:
        copy.wait()


def near_field(ids, used, rank, blocks, source, first, before=None, keep=()):
    boxes, slots, _, basis, _ = blocks.shape
    rhs = source.shape[3]
    begun, kept = before is not None, len(keep)
    hbm = pl.BlockSpec(memory_space=pltpu.HBM)
    smem = pl.BlockSpec(memory_space=pltpu.SMEM)
    vmem = pl.BlockSpec(memory_space=pltpu.VMEM)
    shape = (boxes, 2, basis, rhs)
    scratch = [
        pltpu.VMEM((boxes * slots, *blocks.shape[2:]), BF16),
        pltpu.VMEM(source.shape, BF16),
        pltpu.VMEM((boxes, 2 * basis, 2 * rhs), BF16),
        pltpu.VMEM(shape, F32),
        pltpu.SMEM((boxes * slots,), jnp.int32),
        pltpu.SemaphoreType.DMA((boxes * slots + 3 * boxes + kept,)),
    ]
    kernel = functools.partial(near_kernel, first, begun, kept)
    if kept:
        del scratch[3]
        inner = kernel

        def kernel(*refs):
            place = 5 + begun + kept
            inner(*refs[:-2], refs[place], *refs[-2:])

    return pl.pallas_call(
        kernel,
        in_specs=[smem] * 3 + [hbm] * (2 + begun + kept),
        out_specs=[vmem] * (1 + kept) if kept else hbm,
        out_shape=[
            pltpu.VMEM(shape, F32),
            *[pltpu.VMEM(array.shape, array.dtype) for array in keep],
        ]
        if kept
        else pltpu.HBM(shape, F32),
        scratch_shapes=scratch,
        compiler_params=pltpu.CompilerParams(vmem_limit_bytes=32 * MIB),
        cost_estimate=pl.CostEstimate(
            flops=10**11 if first == 2 else 2 * 10**9, bytes_accessed=8 * MIB, transcendentals=0
        ),
        name=("near_low", "near_own", "near_high")[first],
    )(ids, used, rank, *in_hbm(blocks, source, *([before] if begun else []), *keep))


def adjoint_kernel(rad_ref, out_hbm, held):
    for box in range(rad_ref.shape[0]):
        held[box] = side_by_side(rad_ref[box, 0].T, rad_ref[box, 1].T)
    pltpu.sync_copy(held, out_hbm)


def adjoint(radiation):
    boxes, _, points, basis = radiation.shape
    return pl.pallas_call(
        adjoint_kernel,
        in_specs=[pl.BlockSpec(memory_space=pltpu.VMEM)],
        out_specs=pl.BlockSpec(memory_space=pltpu.HBM),
        scratch_shapes=[pltpu.VMEM((boxes, basis, 2 * points), BF16)],
        out_shape=pltpu.HBM((boxes, basis, 2 * points), BF16),
        cost_estimate=pl.CostEstimate(
            flops=10**6, bytes_accessed=2 * MIB, transcendentals=0
        ),
        name="adjoint",
    )(radiation)


def down_kernel(phi_ref, near_ref, w_ref, adjoint_ref, *refs):
    bands_ref, received = refs[0], refs[1:-4]
    out_hbm, field, held, sems = refs[-4:]
    boxes, _, width = adjoint_ref.shape
    points = width // 2
    rhs = held.shape[3]
    phi = phi_ref[0]
    phi_size = field.shape[1]
    pairs = [(bands_ref.at[:, phi], field.at[:, phi])]
    for distance, piece in enumerate(received, 1):
        pairs.append((piece, field.at[:, lax.rem(phi + phi_size - distance, phi_size)]))
    copies = [
        pltpu.make_async_copy(source, target, sems.at[boxes + place])
        for place, (source, target) in enumerate(pairs)
    ]
    out_copies = [
        pltpu.make_async_copy(held.at[box], out_hbm.at[box], sems.at[box]) for box in range(boxes)
    ]
    for copy in copies:
        copy.start()
    for copy in copies:
        copy.wait()
    mixed = dot(w_ref[...], field[...].reshape(w_ref.shape[1], 2 * rhs))
    for octant in range(boxes // 2):
        start = 2 * octant * points
        cos_part = mixed[start : start + points]
        sin_part = mixed[start + points : start + 2 * points]
        cos_re, cos_im = cos_part[:, :rhs], cos_part[:, rhs:]
        sin_re, sin_im = sin_part[:, :rhs], sin_part[:, rhs:]
        leaves = (
            (octant, cos_re + sin_im, cos_im - sin_re),
            (boxes - 1 - octant, cos_re - sin_im, cos_im + sin_re),
        )
        for box, real, imag in leaves:
            real, imag = real.astype(BF16), imag.astype(BF16)
            right = jnp.concatenate([side_by_side(real, imag), side_by_side(imag, -real)], axis=0)
            far = dot(adjoint_ref[box], right)
            held[box, 0] = near_ref[box, 0] + far[:, :rhs]
            held[box, 1] = near_ref[box, 1] + far[:, rhs:]
            out_copies[box].start()
    for copy in out_copies:
        copy.wait()


def downward(phi, bands, received, near, weights, radiation_adjoint):
    boxes = near.shape[0]
    anywhere = pl.BlockSpec(memory_space=pl.ANY)
    ready = [
        pltpu.with_memory_space_constraint(array, pltpu.VMEM)
        for array in (near, weights, radiation_adjoint)
    ]
    return pl.pallas_call(
        down_kernel,
        in_specs=[pl.BlockSpec(memory_space=pltpu.SMEM)]
        + [pl.BlockSpec(memory_space=pltpu.VMEM)] * 3
        + [anywhere] * (1 + len(received)),
        out_specs=pl.BlockSpec(memory_space=pltpu.HBM),
        out_shape=jax.ShapeDtypeStruct(near.shape, F32),
        scratch_shapes=[
            pltpu.VMEM(bands.shape, BF16),
            pltpu.VMEM(near.shape, F32),
            pltpu.SemaphoreType.DMA((boxes + 1 + len(received),)),
        ],
        compiler_params=pltpu.CompilerParams(vmem_limit_bytes=32 * MIB),
        cost_estimate=pl.CostEstimate(
            flops=2 * 10**9, bytes_accessed=7 * MIB, transcendentals=0
        ),
        name="downward",
    )(phi, *ready, bands, *received)


def shift(block, axis, step):
    count = lax.axis_size(axis)
    pairs = [(i, i + step) for i in range(count) if 0 <= i + step < count]
    return lax.ppermute(block, axis, pairs)


def lists_of(partners, vector_ids, pair_count):
    used = jnp.arange(partners.shape[1])[None, :] < pair_count[:, None]
    names = jnp.where(used, partners, NOWHERE)
    return jnp.stack([names, vector_ids], axis=2).reshape(-1, 2)


def parent_bands(spread, shares):
    axes = ("box", "theta", "phi") if shares == lax.axis_size("box") else ("theta", "phi")
    return lax.all_to_all(spread, axes, split_axis=0, concat_axis=0, tiled=True)


def staged_bands(incoming, shares):
    axes = ("box", "theta") if shares == lax.axis_size("box") else ("theta",)
    phi_size = lax.axis_size("phi")
    phi = lax.axis_index("phi")
    bands = incoming.reshape(-1, phi_size, *incoming.shape[1:])
    bands = lax.all_to_all(bands, axes, split_axis=0, concat_axis=0, tiled=True)
    received = []
    for distance in range(1, phi_size):
        piece = lax.dynamic_index_in_dim(bands, (phi + distance) % phi_size, 1, keepdims=False)
        ring = [(place, (place + distance) % phi_size) for place in range(phi_size)]
        received.append(lax.ppermute(piece, "phi", ring))
    return phi.astype(jnp.int32).reshape(1), bands, received


def translation_lines(lists, translation, shares, per_group):
    operator_total, _, theta_band, phi_band = translation.shape
    rank = lax.axis_index("box")
    if shares < lax.axis_size("box"):
        table = translation.reshape(operator_total, -1)
        base = ((rank - 1) * per_group).astype(jnp.int32).reshape(1)
        return couplings(lists, base, table, per_group, 3 * per_group)
    if shares == 2:
        other = lax.ppermute(lists, "box", [(0, 1), (1, 0)])
        lists = jnp.where(
            rank == 0, jnp.concatenate([lists, other]), jnp.concatenate([other, lists])
        )
    part = theta_band // shares
    table = lax.dynamic_slice_in_dim(translation, rank * part, part, axis=2)
    table = table.reshape(operator_total, -1)
    total = shares * per_group
    return couplings(lists, jnp.zeros((1,), jnp.int32), table, total, total)


def per_device(
    shares,
    up_weights,
    down_weights,
    coeffs,
    near_blocks,
    near_ids,
    near_count,
    radiation,
    partners,
    vector_ids,
    pair_count,
    translation,
):
    every = ("box", "theta", "phi")
    per_group = lax.axis_size("theta") * lax.axis_size("phi")
    rank = lax.axis_index(every).astype(jnp.int32).reshape(1)
    low = shift(coeffs, every, 1)
    spread = upward(coeffs, radiation, up_weights, shares * per_group)
    radiation_adjoint = adjoint(radiation)
    lists = lists_of(partners, vector_ids, pair_count)
    spread, lists = lax.optimization_barrier((spread, lists))
    lines = translation_lines(lists, translation, shares, per_group)
    spread, lines, radiation_adjoint = lax.optimization_barrier((spread, lines, radiation_adjoint))
    parents = parent_bands(spread, shares)
    slots = (near_ids, near_count, rank, near_blocks)
    near = near_field(*slots, low, 0)
    near, late = lax.optimization_barrier((near, coeffs))
    high = shift(late, every, -1)
    parents, near = lax.optimization_barrier((parents, near))
    sources = [parents]
    if shares < lax.axis_size("box"):
        sources = [shift(parents, "box", 1), parents, shift(parents, "box", -1)]
    incoming = translate(lines, sources)
    incoming, near = lax.optimization_barrier((incoming, near))
    phi, bands, received = staged_bands(incoming, shares)
    near = near_field(*slots, coeffs, 1, near)
    ready = near_field(*slots, high, 2, near, keep=(down_weights, radiation_adjoint))
    return downward(phi, bands, received, *ready)


def solution(mesh):
    box_size, theta_size, phi_size = (mesh.shape[axis] for axis in ("box", "theta", "phi"))
    shares = box_size if box_size <= 2 and TU // theta_size % box_size == 0 else 1
    up_weights, down_weights = operators(shares, theta_size, phi_size)
    in_specs = (
        P(),
        P(),
        P(("box", "theta", "phi"), None, None, None),
        P(("box", "theta", "phi"), None, None, None, None),
        P(("box", "theta", "phi"), None),
        P(("box", "theta", "phi")),
        P(("box", "theta", "phi"), None, None, None),
        P("box", None),
        P("box", None),
        P("box"),
        P(None, None, "theta", "phi"),
    )
    out_specs = P(("box", "theta", "phi"), None, None, None)
    mapped = jax.shard_map(
        functools.partial(per_device, shares),
        mesh=mesh,
        in_specs=in_specs,
        out_specs=out_specs,
        check_vma=False,
    )

    def product(*arrays):
        return mapped(jnp.asarray(up_weights), jnp.asarray(down_weights), *arrays)

    return product
```

```python
import functools
import math

import jax
import jax.numpy as jnp
import ml_dtypes
import numpy as np
from jax import lax
from jax.experimental import pallas as pl
from jax.experimental.pallas import tpu as pltpu
from jax.sharding import PartitionSpec as P

TL = 8
PL = 16
TU = 16
PU = 32

WEIGHT_UP = (-0.0546875, 0.8203125, 0.2734375, -0.0390625)
WEIGHT_DOWN = (-0.0390625, 0.2734375, 0.8203125, -0.0546875)
PHASE_SCALE = 1.3

F32 = jnp.float32
BF16 = jnp.bfloat16
MIB = 2**20
GROUP = 2
NOWHERE = -(2**20)


def lagrange(rows, columns, wrap):
    matrix = np.zeros((rows, columns))
    for row in range(rows):
        weights = WEIGHT_UP if row % 2 else WEIGHT_DOWN
        for order in range(4):
            node = row // 2 + row % 2 - 2 + order
            node = node % columns if wrap else min(max(node, 0), columns - 1)
            matrix[row, node] += weights[order]
    return matrix


def split_weights(matrix):
    high = matrix.astype(ml_dtypes.bfloat16)
    low = (matrix - high.astype(np.float64)).astype(ml_dtypes.bfloat16)
    return high, low


def operators(shares, theta_size, phi_size):
    theta_part = TU // theta_size // shares
    order = np.arange(TU * PU).reshape(theta_size, shares, theta_part, phi_size, PU // phi_size)
    order = order.transpose(1, 0, 3, 2, 4).reshape(-1)
    interp = np.kron(lagrange(TU, TL, False), lagrange(PU, PL, True))
    theta = math.pi * (np.arange(TU) + 0.5) / TU
    azimuth = 2.0 * math.pi * (np.arange(PU) + 0.5) / PU
    up, down = [], []
    for octant in range(4):
        sign_x = 2 * (octant % 2) - 1
        sign_y = 2 * (octant // 2 % 2) - 1
        sign_z = 2 * (octant // 4) - 1
        angle = PHASE_SCALE * (
            sign_x * np.sin(theta)[:, None] * np.cos(azimuth)[None]
            + sign_y * np.sin(theta)[:, None] * np.sin(azimuth)[None]
            + sign_z * np.cos(theta)[:, None]
        ).reshape(-1, 1)
        cos_high, cos_low = split_weights((np.cos(angle) * interp)[order])
        sin_high, sin_low = split_weights((np.sin(angle) * interp)[order])
        high = np.concatenate([cos_high, sin_high], axis=1)
        low = np.concatenate([cos_low, sin_low], axis=1)
        up.append(np.concatenate([high, low], axis=0))
        down += [cos_high.T, sin_high.T]
    return np.concatenate(up, axis=1), np.concatenate(down, axis=0)


def in_hbm(*arrays):
    return [pltpu.with_memory_space_constraint(array, pltpu.HBM) for array in arrays]


def dot(a, b):
    return jnp.dot(a, b, preferred_element_type=F32)


def side_by_side(real, imag):
    return jnp.concatenate([real, imag], axis=1)


def complex_columns(real, imag):
    return jnp.concatenate([side_by_side(real, imag), side_by_side(-imag, real)], axis=0)


def up_kernel(phi_ref, x_hbm, rad_hbm, w_hbm, *refs):
    pieces_hbm, (x_ref, rad_ref, w_ref, right, result, sems) = refs[:-6], refs[-6:]
    boxes, _, _, rhs = x_ref.shape
    points = rad_ref.shape[2]
    copies = [
        pltpu.make_async_copy(source, target, sems.at[place])
        for place, (source, target) in enumerate(
            ((x_hbm, x_ref), (rad_hbm, rad_ref), (w_hbm, w_ref))
        )
    ]
    for copy in copies:
        copy.start()
    copies[0].wait()
    copies[1].wait()
    half = boxes // 2
    for octant in range(boxes):
        left = side_by_side(rad_ref[octant, 0], rad_ref[octant, 1])
        straight = dot(left, complex_columns(x_ref[octant, 0], x_ref[octant, 1])).astype(BF16)
        real, imag = straight[:, :rhs], straight[:, rhs:]
        if octant < half:
            swapped = side_by_side(-imag, real)
        else:
            swapped = side_by_side(imag, -real)
        place = octant if octant < half else boxes - 1 - octant
        start = 2 * place * points
        right[octant // half, start : start + points] = straight
        right[octant // half, start + points : start + 2 * points] = swapped
    copies[2].wait()
    total = dot(w_ref[...], right[0]) + dot(w_ref[...], right[1])
    samples = total.shape[0] // 2
    total = total[:samples] + total[samples:]
    result[...] = total.astype(BF16).reshape(result.shape)
    phi_size = len(pieces_hbm)
    copies = []
    for distance, piece in enumerate(pieces_hbm):
        place = lax.rem(phi_ref[0] + distance, phi_size)
        copies.append(pltpu.make_async_copy(result.at[:, place], piece, sems.at[3 + distance]))
        copies[-1].start()
    for copy in copies:
        copy.wait()


def upward(phi, coeffs, radiation, weights, shape):
    boxes, _, basis, rhs = coeffs.shape
    rows, columns = weights.shape
    samples = rows // 2
    shape = (*shape, samples // math.prod(shape), 2 * rhs)
    piece = (shape[0], *shape[2:])
    hbm = pl.BlockSpec(memory_space=pltpu.HBM)
    return pl.pallas_call(
        up_kernel,
        in_specs=[pl.BlockSpec(memory_space=pltpu.SMEM)] + [hbm] * 3,
        out_specs=[hbm] * shape[1],
        out_shape=[pltpu.HBM(piece, BF16)] * shape[1],
        scratch_shapes=[
            pltpu.VMEM(coeffs.shape, BF16),
            pltpu.VMEM(radiation.shape, BF16),
            pltpu.VMEM(weights.shape, BF16),
            pltpu.VMEM((2, columns, 2 * rhs), BF16),
            pltpu.VMEM(shape, BF16),
            pltpu.SemaphoreType.DMA((3 + shape[1],)),
        ],
        compiler_params=pltpu.CompilerParams(vmem_limit_bytes=32 * MIB),
        cost_estimate=pl.CostEstimate(
            flops=2 * 10**9, bytes_accessed=4 * MIB, transcendentals=0
        ),
        name="upward",
    )(phi, *in_hbm(coeffs, radiation, weights))


def coupling_kernel(lists_ref, base_ref, table_ref, out_ref):
    rows = lists_ref.shape[0]
    samples = table_ref.shape[1] // 2
    _, targets, columns = out_ref.shape
    slots = rows // targets
    selector = (
        lax.broadcasted_iota(jnp.int32, (rows, table_ref.shape[0]), 1) == lists_ref[:, 1:2]
    )
    chosen = dot(selector.astype(BF16), table_ref[...]).astype(BF16)
    wide = lax.broadcasted_iota(jnp.int32, (rows, columns), 1) // samples
    match = wide + base_ref[0] == lists_ref[:, 0:1]
    spread = lax.broadcasted_iota(jnp.int32, (samples, columns), 0) == (
        lax.broadcasted_iota(jnp.int32, (samples, columns), 1) % samples
    )
    gather = (
        lax.broadcasted_iota(jnp.int32, (targets, rows), 1) // slots
        == lax.broadcasted_iota(jnp.int32, (targets, rows), 0)
    ).astype(BF16)
    tile = spread.astype(BF16)
    for part in range(2):
        lines = dot(chosen[:, part * samples : (part + 1) * samples], tile)
        out_ref[part] = dot(gather, jnp.where(match, lines, 0.0).astype(BF16))


def couplings(lists, base, table, targets, names):
    shape = (2, targets, names * (table.shape[1] // 2))
    vmem = pl.BlockSpec(memory_space=pltpu.VMEM)
    return pl.pallas_call(
        coupling_kernel,
        in_specs=[vmem, pl.BlockSpec(memory_space=pltpu.SMEM), vmem],
        out_specs=vmem,
        out_shape=jax.ShapeDtypeStruct(shape, F32),
        compiler_params=pltpu.CompilerParams(vmem_limit_bytes=16 * MIB),
        cost_estimate=pl.CostEstimate(
            flops=2 * 10**8, bytes_accessed=2 * 2**20, transcendentals=0
        ),
        name="coupling",
    )(lists, base, table)


def translate_kernel(phi_ref, lines_hbm, *refs):
    count = (len(refs) - 5) // 2
    sources, out_hbm = refs[:count], refs[count]
    phi = phi_ref[0]
    phi_size = sources[0].shape[1]
    held, lines, matrix, result, sems = refs[count + 1 :][:count], *refs[2 * count + 1 :]
    targets, samples, width = result.shape
    rhs = width // 2
    pairs = [(lines_hbm, lines)]
    for source, target in zip(sources, held):
        for distance in range(phi_size):
            place = lax.rem(phi + phi_size - distance, phi_size)
            pairs.append((source.at[:, distance], target.at[:, place]))
    copies = [
        pltpu.make_async_copy(source, target, sems.at[place])
        for place, (source, target) in enumerate(pairs)
    ]
    for copy in copies:
        copy.start()
    copies[0].wait()
    columns = matrix.shape[1]
    row = lax.broadcasted_iota(jnp.int32, (samples, columns), 0)
    diagonal = row == lax.broadcasted_iota(jnp.int32, (samples, columns), 1) % samples
    for part in range(2):
        for target in range(targets):
            line = jnp.broadcast_to(lines[part, target : target + 1], diagonal.shape)
            start = (part * targets + target) * samples
            matrix[start : start + samples] = jnp.where(diagonal, line, 0.0).astype(BF16)
    total = None
    start = 0
    for place, source in enumerate(held):
        for copy in copies[1 + place * phi_size : 1 + (place + 1) * phi_size]:
            copy.wait()
        stop = start + source.shape[0] * phi_size * samples
        part = dot(matrix[:, start:stop], source[...].reshape(stop - start, width))
        total = part if total is None else total + part
        start = stop
    half = targets * samples
    real = total[:half, :rhs] - total[half:, rhs:]
    imag = total[:half, rhs:] + total[half:, :rhs]
    result[...] = jnp.concatenate([real, imag], axis=1).astype(BF16).reshape(result.shape)
    pltpu.sync_copy(result, out_hbm)


def translate(phi, lines, sources):
    _, phi_size, samples, width = sources[0].shape
    _, targets, columns = lines.shape
    shape = (targets, samples, width)
    hbm = pl.BlockSpec(memory_space=pltpu.HBM)
    anywhere = pl.BlockSpec(memory_space=pl.ANY)
    return pl.pallas_call(
        translate_kernel,
        in_specs=[pl.BlockSpec(memory_space=pltpu.SMEM), hbm] + [anywhere] * len(sources),
        out_specs=hbm,
        out_shape=pltpu.HBM(shape, BF16),
        scratch_shapes=[
            *[pltpu.VMEM(source.shape, BF16) for source in sources],
            pltpu.VMEM(lines.shape, F32),
            pltpu.VMEM((2 * targets * samples, columns), BF16),
            pltpu.VMEM(shape, BF16),
            pltpu.SemaphoreType.DMA((1 + phi_size * len(sources),)),
        ],
        compiler_params=pltpu.CompilerParams(vmem_limit_bytes=24 * MIB),
        cost_estimate=pl.CostEstimate(
            flops=10**9, bytes_accessed=2 * MIB, transcendentals=0
        ),
        name="translate",
    )(phi, *in_hbm(lines), *sources)


def near_kernel(first, begun, kept, *refs):
    refs = list(refs)
    listed, starts_ref, blocks_hbm, source_hbm = refs[:4]
    before_hbm = refs[4] if begun else None
    kept_hbm = refs[4 + begun : 4 + begun + kept]
    out_ref = refs[4 + begun + kept]
    kept_refs = refs[5 + begun + kept : 5 + begun + 2 * kept]
    blocks, held, wide, total_ref, sems = refs[5 + begun + 2 * kept :]
    boxes, _, basis, rhs = held.shape
    most = blocks_hbm.shape[0]
    starts = [starts_ref[first, box] for box in range(boxes + 1)]

    def by_box(source, target, turn):
        return [
            pltpu.make_async_copy(
                source.at[box], target.at[box], sems.at[most + turn * boxes + box]
            )
            for box in range(boxes)
        ]

    source_copies = by_box(source_hbm, held, 0)
    before_copies = by_box(before_hbm, total_ref, 1) if begun else []
    out_copies = [] if kept else by_box(total_ref, out_ref, 2)
    kept_copies = [
        pltpu.make_async_copy(kept_hbm[place], kept_refs[place], sems.at[most + 3 * boxes + place])
        for place in range(kept)
    ]
    for copy in source_copies:
        copy.start()

    def block_copy(place):
        block = listed[first, place] // boxes
        return pltpu.make_async_copy(blocks_hbm.at[block], blocks.at[place], sems.at[place])

    def fetch(place, carry):
        block_copy(place).start()
        return carry

    lax.fori_loop(0, starts[boxes], fetch, 0)
    for copy in before_copies + kept_copies:
        copy.start()
    for copy in source_copies:
        copy.wait()
    for place in range(boxes):
        wide[place] = complex_columns(held[place, 0], held[place, 1])

    def landed(place, carry):
        block_copy(place).wait()
        return carry

    lax.fori_loop(0, starts[boxes], landed, 0)
    for copy in before_copies:
        copy.wait()

    def group(box, begin, size):
        left, right = [], []
        for step in range(size):
            place = starts[box] + begin + step
            valid = place < starts[box + 1]
            place = jnp.where(valid, place, 0)
            real, imag = blocks[place, 0], blocks[place, 1]
            real = jnp.where(valid, real, jnp.zeros_like(real))
            imag = jnp.where(valid, imag, jnp.zeros_like(imag))
            left.append(side_by_side(real, imag))
            right.append(wide[jnp.where(valid, listed[first, place] % boxes, 0)])
        return dot(jnp.concatenate(left, axis=1), jnp.concatenate(right, axis=0))

    possible = [(boxes - box, boxes, box + 1)[first] for box in range(boxes)]
    sizes = [min(count, 3 if count < 7 else 4) for count in possible]
    for box in range(boxes):
        part = group(box, 0, sizes[box])
        if begun:
            total_ref[box, 0] += part[:, :rhs]
            total_ref[box, 1] += part[:, rhs:]
        else:
            total_ref[box, 0] = part[:, :rhs]
            total_ref[box, 1] = part[:, rhs:]
    for box in range(boxes):

        def more(index, carry, box=box):
            part = group(box, sizes[box] + GROUP * index, GROUP)
            total_ref[box, 0] += part[:, :rhs]
            total_ref[box, 1] += part[:, rhs:]
            return carry

        rest = starts[box + 1] - starts[box] - sizes[box]
        lax.fori_loop(0, (jnp.maximum(rest, 0) + GROUP - 1) // GROUP, more, 0)
        if out_copies:
            out_copies[box].start()
    for copy in out_copies + kept_copies:
        copy.wait()


def near_slots(ids, used, rank):
    boxes, slots = ids.shape
    total = boxes * slots
    source = ids - (rank - 1) * boxes
    source = jnp.where(jnp.arange(slots) < used[:, None], source, -1).reshape(-1)
    wanted = (source >= 0) & (source // boxes == jnp.arange(3)[:, None])
    earlier = jnp.arange(total)[None, :] < jnp.arange(total)[:, None]
    place = jnp.sum((wanted[:, None, :] & earlier).astype(jnp.int32), axis=2)
    code = jnp.arange(total) * boxes + source % boxes
    chosen = wanted[:, None, :] & (place[:, None, :] == jnp.arange(total)[:, None])
    listed = jnp.sum(jnp.where(chosen, code, 0), axis=2)
    before = jnp.arange(total) // slots < jnp.arange(boxes + 1)[:, None]
    starts = jnp.sum((wanted[:, None, :] & before).astype(jnp.int32), axis=2)
    return listed.astype(jnp.int32), starts.astype(jnp.int32)


def near_field(listed, starts, blocks, source, first, before=None, keep=()):
    boxes, slots, _, basis, _ = blocks.shape
    blocks = blocks.reshape(boxes * slots, *blocks.shape[2:])
    rhs = source.shape[3]
    begun, kept = before is not None, len(keep)
    hbm = pl.BlockSpec(memory_space=pltpu.HBM)
    smem = pl.BlockSpec(memory_space=pltpu.SMEM)
    vmem = pl.BlockSpec(memory_space=pltpu.VMEM)
    shape = (boxes, 2, basis, rhs)
    scratch = [
        pltpu.VMEM(blocks.shape, BF16),
        pltpu.VMEM(source.shape, BF16),
        pltpu.VMEM((boxes, 2 * basis, 2 * rhs), BF16),
        pltpu.VMEM(shape, F32),
        pltpu.SemaphoreType.DMA((boxes * slots + 3 * boxes + kept,)),
    ]
    kernel = functools.partial(near_kernel, first, begun, kept)
    if kept:
        del scratch[3]
        inner = kernel

        def kernel(*refs):
            place = 4 + begun + kept
            inner(*refs[:-1], refs[place], refs[-1])

    return pl.pallas_call(
        kernel,
        in_specs=[smem] * 2 + [hbm] * (2 + begun + kept),
        out_specs=[vmem] * (1 + kept) if kept else hbm,
        out_shape=[
            pltpu.VMEM(shape, F32),
            *[pltpu.VMEM(array.shape, array.dtype) for array in keep],
        ]
        if kept
        else pltpu.HBM(shape, F32),
        scratch_shapes=scratch,
        compiler_params=pltpu.CompilerParams(vmem_limit_bytes=32 * MIB),
        cost_estimate=pl.CostEstimate(
            flops=10**11 if first == 2 else 2 * 10**9, bytes_accessed=8 * MIB, transcendentals=0
        ),
        name=("near_low", "near_own", "near_high")[first],
    )(listed, starts, *in_hbm(blocks, source, *([before] if begun else []), *keep))


def adjoint_kernel(rad_ref, out_hbm, held):
    for box in range(rad_ref.shape[0]):
        held[box] = side_by_side(rad_ref[box, 0].T, rad_ref[box, 1].T)
    pltpu.sync_copy(held, out_hbm)


def adjoint(radiation):
    boxes, _, points, basis = radiation.shape
    return pl.pallas_call(
        adjoint_kernel,
        in_specs=[pl.BlockSpec(memory_space=pltpu.VMEM)],
        out_specs=pl.BlockSpec(memory_space=pltpu.HBM),
        scratch_shapes=[pltpu.VMEM((boxes, basis, 2 * points), BF16)],
        out_shape=pltpu.HBM((boxes, basis, 2 * points), BF16),
        cost_estimate=pl.CostEstimate(
            flops=10**6, bytes_accessed=2 * MIB, transcendentals=0
        ),
        name="adjoint",
    )(radiation)


def down_kernel(phi_ref, near_ref, w_ref, adjoint_ref, *refs):
    bands_ref, received = refs[0], refs[1:-4]
    out_hbm, field, held, sems = refs[-4:]
    boxes, _, width = adjoint_ref.shape
    points = width // 2
    rhs = held.shape[3]
    phi = phi_ref[0]
    phi_size = field.shape[1]
    pairs = [(bands_ref.at[:, phi], field.at[:, phi])]
    for distance, piece in enumerate(received, 1):
        pairs.append((piece, field.at[:, lax.rem(phi + phi_size - distance, phi_size)]))
    copies = [
        pltpu.make_async_copy(source, target, sems.at[boxes + place])
        for place, (source, target) in enumerate(pairs)
    ]
    out_copies = [
        pltpu.make_async_copy(held.at[box], out_hbm.at[box], sems.at[box]) for box in range(boxes)
    ]
    for copy in copies:
        copy.start()
    for copy in copies:
        copy.wait()
    mixed = dot(w_ref[...], field[...].reshape(w_ref.shape[1], 2 * rhs))
    for octant in range(boxes // 2):
        start = 2 * octant * points
        cos_part = mixed[start : start + points]
        sin_part = mixed[start + points : start + 2 * points]
        cos_re, cos_im = cos_part[:, :rhs], cos_part[:, rhs:]
        sin_re, sin_im = sin_part[:, :rhs], sin_part[:, rhs:]
        leaves = (
            (octant, cos_re + sin_im, cos_im - sin_re),
            (boxes - 1 - octant, cos_re - sin_im, cos_im + sin_re),
        )
        for box, real, imag in leaves:
            real, imag = real.astype(BF16), imag.astype(BF16)
            right = jnp.concatenate([side_by_side(real, imag), side_by_side(imag, -real)], axis=0)
            far = dot(adjoint_ref[box], right)
            held[box, 0] = near_ref[box, 0] + far[:, :rhs]
            held[box, 1] = near_ref[box, 1] + far[:, rhs:]
            out_copies[box].start()
    for copy in out_copies:
        copy.wait()


def downward(phi, bands, received, near, weights, radiation_adjoint):
    boxes = near.shape[0]
    anywhere = pl.BlockSpec(memory_space=pl.ANY)
    ready = [
        pltpu.with_memory_space_constraint(array, pltpu.VMEM)
        for array in (near, weights, radiation_adjoint)
    ]
    return pl.pallas_call(
        down_kernel,
        in_specs=[pl.BlockSpec(memory_space=pltpu.SMEM)]
        + [pl.BlockSpec(memory_space=pltpu.VMEM)] * 3
        + [anywhere] * (1 + len(received)),
        out_specs=pl.BlockSpec(memory_space=pltpu.HBM),
        out_shape=jax.ShapeDtypeStruct(near.shape, F32),
        scratch_shapes=[
            pltpu.VMEM(bands.shape, BF16),
            pltpu.VMEM(near.shape, F32),
            pltpu.SemaphoreType.DMA((boxes + 1 + len(received),)),
        ],
        compiler_params=pltpu.CompilerParams(vmem_limit_bytes=32 * MIB),
        cost_estimate=pl.CostEstimate(
            flops=2 * 10**9, bytes_accessed=7 * MIB, transcendentals=0
        ),
        name="downward",
    )(phi, *ready, bands, *received)


def shift(block, axis, step):
    count = lax.axis_size(axis)
    pairs = [(i, i + step) for i in range(count) if 0 <= i + step < count]
    return lax.ppermute(block, axis, pairs)


def lists_of(partners, vector_ids, pair_count):
    used = jnp.arange(partners.shape[1])[None, :] < pair_count[:, None]
    names = jnp.where(used, partners, NOWHERE)
    return jnp.stack([names, vector_ids], axis=2).reshape(-1, 2)


def along_phi(pieces):
    size = len(pieces)
    received = [pieces[0]]
    for distance in range(1, size):
        ring = [(place, (place + distance) % size) for place in range(size)]
        received.append(lax.ppermute(pieces[distance], "phi", ring))
    return received


def across(bands, shares):
    axes = ("box", "theta") if shares == lax.axis_size("box") else ("theta",)
    return lax.all_to_all(bands, axes, split_axis=0, concat_axis=0, tiled=True)


def translation_lines(lists, translation, shares, per_group):
    operator_total, _, theta_band, phi_band = translation.shape
    rank = lax.axis_index("box")
    if shares < lax.axis_size("box"):
        table = translation.reshape(operator_total, -1)
        base = ((rank - 1) * per_group).astype(jnp.int32).reshape(1)
        return couplings(lists, base, table, per_group, 3 * per_group)
    if shares == 2:
        other = lax.ppermute(lists, "box", [(0, 1), (1, 0)])
        lists = jnp.where(
            rank == 0, jnp.concatenate([lists, other]), jnp.concatenate([other, lists])
        )
    part = theta_band // shares
    table = lax.dynamic_slice_in_dim(translation, rank * part, part, axis=2)
    table = table.reshape(operator_total, -1)
    total = shares * per_group
    return couplings(lists, jnp.zeros((1,), jnp.int32), table, total, total)


def per_device(
    shares,
    up_weights,
    down_weights,
    coeffs,
    near_blocks,
    near_ids,
    near_count,
    radiation,
    partners,
    vector_ids,
    pair_count,
    translation,
):
    every = ("box", "theta", "phi")
    phi_size = lax.axis_size("phi")
    per_group = lax.axis_size("theta") * phi_size
    groups = shares * per_group
    phi = lax.axis_index("phi")
    phi_ref = phi.astype(jnp.int32).reshape(1)
    low = shift(coeffs, every, 1)
    pieces = upward(phi_ref, coeffs, radiation, up_weights, (groups // phi_size, phi_size))
    lists = lists_of(partners, vector_ids, pair_count)
    pieces, lists = lax.optimization_barrier((pieces, lists))
    received = along_phi(pieces)
    radiation_adjoint = adjoint(radiation)
    lines = translation_lines(lists, translation, shares, per_group)
    slots = (*near_slots(near_ids, near_count, lax.axis_index(every)), near_blocks)
    near = near_field(*slots, coeffs, 1)
    received, lines, radiation_adjoint, near, late = lax.optimization_barrier(
        (received, lines, radiation_adjoint, near, coeffs)
    )
    high = shift(late, every, -1)
    parents = across(jnp.stack(received, axis=1), shares)
    sources = [parents]
    if shares < lax.axis_size("box"):
        sources = [shift(parents, "box", 1), parents, shift(parents, "box", -1)]
    incoming = translate(phi_ref, lines, sources)
    incoming, low = lax.optimization_barrier((incoming, low))
    bands = across(incoming.reshape(-1, phi_size, *incoming.shape[1:]), shares)
    pieces = [
        lax.dynamic_index_in_dim(bands, (phi + distance) % phi_size, 1, keepdims=False)
        for distance in range(phi_size)
    ]
    received = along_phi(pieces)[1:]
    near = near_field(*slots, low, 0, near)
    ready = near_field(*slots, high, 2, near, keep=(down_weights, radiation_adjoint))
    return downward(phi_ref, bands, received, *ready)


def solution(mesh):
    box_size, theta_size, phi_size = (mesh.shape[axis] for axis in ("box", "theta", "phi"))
    shares = box_size if box_size <= 2 and TU // theta_size % box_size == 0 else 1
    up_weights, down_weights = operators(shares, theta_size, phi_size)
    in_specs = (
        P(),
        P(),
        P(("box", "theta", "phi"), None, None, None),
        P(("box", "theta", "phi"), None, None, None, None),
        P(("box", "theta", "phi"), None),
        P(("box", "theta", "phi")),
        P(("box", "theta", "phi"), None, None, None),
        P("box", None),
        P("box", None),
        P("box"),
        P(None, None, "theta", "phi"),
    )
    out_specs = P(("box", "theta", "phi"), None, None, None)
    mapped = jax.shard_map(
        functools.partial(per_device, shares),
        mesh=mesh,
        in_specs=in_specs,
        out_specs=out_specs,
        check_vma=False,
    )

    def product(*arrays):
        return mapped(jnp.asarray(up_weights), jnp.asarray(down_weights), *arrays)

    return product
```

```python
import functools
import math

import jax
import jax.numpy as jnp
import ml_dtypes
import numpy as np
from jax import lax
from jax.experimental import pallas as pl
from jax.experimental.pallas import tpu as pltpu
from jax.sharding import PartitionSpec as P

TL = 8
PL = 16
TU = 16
PU = 32

WEIGHT_UP = (-0.0546875, 0.8203125, 0.2734375, -0.0390625)
WEIGHT_DOWN = (-0.0390625, 0.2734375, 0.8203125, -0.0546875)
PHASE_SCALE = 1.3

F32 = jnp.float32
BF16 = jnp.bfloat16
MIB = 2**20
GROUP = 2
NOWHERE = -(2**20)


def lagrange(rows, columns, wrap):
    matrix = np.zeros((rows, columns))
    for row in range(rows):
        weights = WEIGHT_UP if row % 2 else WEIGHT_DOWN
        for order in range(4):
            node = row // 2 + row % 2 - 2 + order
            node = node % columns if wrap else min(max(node, 0), columns - 1)
            matrix[row, node] += weights[order]
    return matrix


def split_weights(matrix):
    high = matrix.astype(ml_dtypes.bfloat16)
    low = (matrix - high.astype(np.float64)).astype(ml_dtypes.bfloat16)
    return high, low


def operators(shares, theta_size, phi_size):
    theta_part = TU // theta_size // shares
    order = np.arange(TU * PU).reshape(theta_size, shares, theta_part, phi_size, PU // phi_size)
    order = order.transpose(1, 0, 3, 2, 4).reshape(-1)
    interp = np.kron(lagrange(TU, TL, False), lagrange(PU, PL, True))
    theta = math.pi * (np.arange(TU) + 0.5) / TU
    azimuth = 2.0 * math.pi * (np.arange(PU) + 0.5) / PU
    up, down = [], []
    for octant in range(4):
        sign_x = 2 * (octant % 2) - 1
        sign_y = 2 * (octant // 2 % 2) - 1
        sign_z = 2 * (octant // 4) - 1
        angle = PHASE_SCALE * (
            sign_x * np.sin(theta)[:, None] * np.cos(azimuth)[None]
            + sign_y * np.sin(theta)[:, None] * np.sin(azimuth)[None]
            + sign_z * np.cos(theta)[:, None]
        ).reshape(-1, 1)
        cos_high, cos_low = split_weights((np.cos(angle) * interp)[order])
        sin_high, sin_low = split_weights((np.sin(angle) * interp)[order])
        high = np.concatenate([cos_high, sin_high], axis=1)
        low = np.concatenate([cos_low, sin_low], axis=1)
        up.append(np.concatenate([high, low], axis=0))
        down += [cos_high.T, sin_high.T]
    return np.concatenate(up, axis=1), np.concatenate(down, axis=0)


def in_hbm(*arrays):
    return [pltpu.with_memory_space_constraint(array, pltpu.HBM) for array in arrays]


def dot(a, b):
    return jnp.dot(a, b, preferred_element_type=F32)


def side_by_side(real, imag):
    return jnp.concatenate([real, imag], axis=1)


def complex_columns(real, imag):
    return jnp.concatenate([side_by_side(real, imag), side_by_side(-imag, real)], axis=0)


def up_kernel(x_hbm, rad_hbm, w_hbm, out_hbm, x_ref, rad_ref, w_ref, right, result, sems):
    boxes, _, _, rhs = x_ref.shape
    points = rad_ref.shape[2]
    copies = [
        pltpu.make_async_copy(source, target, sems.at[place])
        for place, (source, target) in enumerate(
            ((x_hbm, x_ref), (rad_hbm, rad_ref), (w_hbm, w_ref))
        )
    ]
    for copy in copies:
        copy.start()
    copies[0].wait()
    copies[1].wait()
    half = boxes // 2
    for octant in range(boxes):
        left = side_by_side(rad_ref[octant, 0], rad_ref[octant, 1])
        straight = dot(left, complex_columns(x_ref[octant, 0], x_ref[octant, 1])).astype(BF16)
        real, imag = straight[:, :rhs], straight[:, rhs:]
        if octant < half:
            swapped = side_by_side(-imag, real)
        else:
            swapped = side_by_side(imag, -real)
        place = octant if octant < half else boxes - 1 - octant
        start = 2 * place * points
        right[octant // half, start : start + points] = straight
        right[octant // half, start + points : start + 2 * points] = swapped
    copies[2].wait()
    total = dot(w_ref[...], right[0]) + dot(w_ref[...], right[1])
    samples = total.shape[0] // 2
    total = total[:samples] + total[samples:]
    result[...] = total.astype(BF16).reshape(result.shape)
    pltpu.sync_copy(result, out_hbm)


def upward(coeffs, radiation, weights, groups):
    boxes, _, basis, rhs = coeffs.shape
    rows, columns = weights.shape
    samples = rows // 2
    hbm = pl.BlockSpec(memory_space=pltpu.HBM)
    return pl.pallas_call(
        up_kernel,
        in_specs=[hbm] * 3,
        out_specs=hbm,
        out_shape=pltpu.HBM((groups, samples // groups, 2 * rhs), BF16),
        scratch_shapes=[
            pltpu.VMEM(coeffs.shape, BF16),
            pltpu.VMEM(radiation.shape, BF16),
            pltpu.VMEM(weights.shape, BF16),
            pltpu.VMEM((2, columns, 2 * rhs), BF16),
            pltpu.VMEM((groups, samples // groups, 2 * rhs), BF16),
            pltpu.SemaphoreType.DMA((3,)),
        ],
        compiler_params=pltpu.CompilerParams(vmem_limit_bytes=32 * MIB),
        cost_estimate=pl.CostEstimate(
            flops=2 * 10**9, bytes_accessed=4 * MIB, transcendentals=0
        ),
        name="upward",
    )(*in_hbm(coeffs, radiation, weights))


def coupling_kernel(lists_ref, base_ref, table_ref, out_ref):
    rows = lists_ref.shape[0]
    samples = table_ref.shape[1] // 2
    _, targets, columns = out_ref.shape
    slots = rows // targets
    selector = (
        lax.broadcasted_iota(jnp.int32, (rows, table_ref.shape[0]), 1) == lists_ref[:, 1:2]
    )
    chosen = dot(selector.astype(BF16), table_ref[...]).astype(BF16)
    wide = lax.broadcasted_iota(jnp.int32, (rows, columns), 1) // samples
    match = wide + base_ref[0] == lists_ref[:, 0:1]
    spread = lax.broadcasted_iota(jnp.int32, (samples, columns), 0) == (
        lax.broadcasted_iota(jnp.int32, (samples, columns), 1) % samples
    )
    gather = (
        lax.broadcasted_iota(jnp.int32, (targets, rows), 1) // slots
        == lax.broadcasted_iota(jnp.int32, (targets, rows), 0)
    ).astype(BF16)
    tile = spread.astype(BF16)
    for part in range(2):
        lines = dot(chosen[:, part * samples : (part + 1) * samples], tile)
        out_ref[part] = dot(gather, jnp.where(match, lines, 0.0).astype(BF16))


def couplings(lists, base, table, targets, names):
    shape = (2, targets, names * (table.shape[1] // 2))
    vmem = pl.BlockSpec(memory_space=pltpu.VMEM)
    return pl.pallas_call(
        coupling_kernel,
        in_specs=[vmem, pl.BlockSpec(memory_space=pltpu.SMEM), vmem],
        out_specs=vmem,
        out_shape=jax.ShapeDtypeStruct(shape, F32),
        compiler_params=pltpu.CompilerParams(vmem_limit_bytes=16 * MIB),
        cost_estimate=pl.CostEstimate(
            flops=2 * 10**8, bytes_accessed=2 * 2**20, transcendentals=0
        ),
        name="coupling",
    )(lists, base, table)


def translate_kernel(lines_hbm, *refs):
    count = (len(refs) - 5) // 2
    sources, out_hbm = refs[:count], refs[count]
    held, lines, matrix, result, sems = refs[count + 1 :][:count], *refs[2 * count + 1 :]
    targets, samples, width = result.shape
    rhs = width // 2
    copies = [
        pltpu.make_async_copy(source, target, sems.at[place])
        for place, (source, target) in enumerate(zip((lines_hbm, *sources), (lines, *held)))
    ]
    for copy in copies:
        copy.start()
    copies[0].wait()
    columns = matrix.shape[1]
    row = lax.broadcasted_iota(jnp.int32, (samples, columns), 0)
    diagonal = row == lax.broadcasted_iota(jnp.int32, (samples, columns), 1) % samples
    for part in range(2):
        for target in range(targets):
            line = jnp.broadcast_to(lines[part, target : target + 1], diagonal.shape)
            start = (part * targets + target) * samples
            matrix[start : start + samples] = jnp.where(diagonal, line, 0.0).astype(BF16)
    total = None
    start = 0
    for place, source in enumerate(held):
        copies[1 + place].wait()
        stop = start + source.shape[0] * samples
        part = dot(matrix[:, start:stop], source[...].reshape(stop - start, width))
        total = part if total is None else total + part
        start = stop
    half = targets * samples
    real = total[:half, :rhs] - total[half:, rhs:]
    imag = total[:half, rhs:] + total[half:, :rhs]
    result[...] = jnp.concatenate([real, imag], axis=1).astype(BF16).reshape(result.shape)
    pltpu.sync_copy(result, out_hbm)


def translate(lines, sources):
    _, samples, width = sources[0].shape
    _, targets, columns = lines.shape
    shape = (targets, samples, width)
    hbm = pl.BlockSpec(memory_space=pltpu.HBM)
    anywhere = pl.BlockSpec(memory_space=pl.ANY)
    return pl.pallas_call(
        translate_kernel,
        in_specs=[hbm] + [anywhere] * len(sources),
        out_specs=hbm,
        out_shape=pltpu.HBM(shape, BF16),
        scratch_shapes=[
            *[pltpu.VMEM(source.shape, BF16) for source in sources],
            pltpu.VMEM(lines.shape, F32),
            pltpu.VMEM((2 * targets * samples, columns), BF16),
            pltpu.VMEM(shape, BF16),
            pltpu.SemaphoreType.DMA((1 + len(sources),)),
        ],
        compiler_params=pltpu.CompilerParams(vmem_limit_bytes=24 * MIB),
        cost_estimate=pl.CostEstimate(
            flops=10**9, bytes_accessed=2 * MIB, transcendentals=0
        ),
        name="translate",
    )(*in_hbm(lines), *sources)


def near_kernel(first, begun, kept, *refs):
    refs = list(refs)
    listed, starts_ref, blocks_hbm, source_hbm = refs[:4]
    before_hbm = refs[4] if begun else None
    kept_hbm = refs[4 + begun : 4 + begun + kept]
    out_ref = refs[4 + begun + kept]
    kept_refs = refs[5 + begun + kept : 5 + begun + 2 * kept]
    blocks, held, wide, total_ref, sems = refs[5 + begun + 2 * kept :]
    boxes, _, basis, rhs = held.shape
    most = blocks_hbm.shape[0]
    starts = [starts_ref[first, box] for box in range(boxes + 1)]

    def by_box(source, target, turn):
        return [
            pltpu.make_async_copy(
                source.at[box], target.at[box], sems.at[most + turn * boxes + box]
            )
            for box in range(boxes)
        ]

    source_copies = by_box(source_hbm, held, 0)
    before_copies = by_box(before_hbm, total_ref, 1) if begun else []
    out_copies = [] if kept else by_box(total_ref, out_ref, 2)
    kept_copies = [
        pltpu.make_async_copy(kept_hbm[place], kept_refs[place], sems.at[most + 3 * boxes + place])
        for place in range(kept)
    ]
    for copy in source_copies:
        copy.start()

    def block_copy(place):
        block = listed[first, place] // boxes
        return pltpu.make_async_copy(blocks_hbm.at[block], blocks.at[place], sems.at[place])

    def fetch(place, carry):
        block_copy(place).start()
        return carry

    lax.fori_loop(0, starts[boxes], fetch, 0)
    for copy in before_copies + kept_copies:
        copy.start()
    for copy in source_copies:
        copy.wait()
    for place in range(boxes):
        wide[place] = complex_columns(held[place, 0], held[place, 1])

    def landed(place, carry):
        block_copy(place).wait()
        return carry

    lax.fori_loop(0, starts[boxes], landed, 0)
    for copy in before_copies:
        copy.wait()

    def group(box, begin, size):
        left, right = [], []
        for step in range(size):
            place = starts[box] + begin + step
            valid = place < starts[box + 1]
            place = jnp.where(valid, place, 0)
            real, imag = blocks[place, 0], blocks[place, 1]
            real = jnp.where(valid, real, jnp.zeros_like(real))
            imag = jnp.where(valid, imag, jnp.zeros_like(imag))
            left.append(side_by_side(real, imag))
            right.append(wide[jnp.where(valid, listed[first, place] % boxes, 0)])
        return dot(jnp.concatenate(left, axis=1), jnp.concatenate(right, axis=0))

    possible = [(boxes - box, boxes, box + 1)[first] for box in range(boxes)]
    sizes = [min(count, 3 if count < 7 else 4) for count in possible]
    for box in range(boxes):
        part = group(box, 0, sizes[box])
        if begun:
            total_ref[box, 0] += part[:, :rhs]
            total_ref[box, 1] += part[:, rhs:]
        else:
            total_ref[box, 0] = part[:, :rhs]
            total_ref[box, 1] = part[:, rhs:]
    for box in range(boxes):

        def more(index, carry, box=box):
            part = group(box, sizes[box] + GROUP * index, GROUP)
            total_ref[box, 0] += part[:, :rhs]
            total_ref[box, 1] += part[:, rhs:]
            return carry

        rest = starts[box + 1] - starts[box] - sizes[box]
        lax.fori_loop(0, (jnp.maximum(rest, 0) + GROUP - 1) // GROUP, more, 0)
        if out_copies:
            out_copies[box].start()
    for copy in out_copies + kept_copies:
        copy.wait()


def near_slots(ids, used, rank):
    boxes, slots = ids.shape
    total = boxes * slots
    source = ids - (rank - 1) * boxes
    source = jnp.where(jnp.arange(slots) < used[:, None], source, -1).reshape(-1)
    wanted = (source >= 0) & (source // boxes == jnp.arange(3)[:, None])
    earlier = jnp.arange(total)[None, :] < jnp.arange(total)[:, None]
    place = jnp.sum((wanted[:, None, :] & earlier).astype(jnp.int32), axis=2)
    code = jnp.arange(total) * boxes + source % boxes
    chosen = wanted[:, None, :] & (place[:, None, :] == jnp.arange(total)[:, None])
    listed = jnp.sum(jnp.where(chosen, code, 0), axis=2)
    before = jnp.arange(total) // slots < jnp.arange(boxes + 1)[:, None]
    starts = jnp.sum((wanted[:, None, :] & before).astype(jnp.int32), axis=2)
    return listed.astype(jnp.int32), starts.astype(jnp.int32)


def near_field(listed, starts, blocks, source, first, before=None, keep=()):
    boxes, slots, _, basis, _ = blocks.shape
    blocks = blocks.reshape(boxes * slots, *blocks.shape[2:])
    rhs = source.shape[3]
    begun, kept = before is not None, len(keep)
    hbm = pl.BlockSpec(memory_space=pltpu.HBM)
    smem = pl.BlockSpec(memory_space=pltpu.SMEM)
    vmem = pl.BlockSpec(memory_space=pltpu.VMEM)
    shape = (boxes, 2, basis, rhs)
    scratch = [
        pltpu.VMEM(blocks.shape, BF16),
        pltpu.VMEM(source.shape, BF16),
        pltpu.VMEM((boxes, 2 * basis, 2 * rhs), BF16),
        pltpu.VMEM(shape, F32),
        pltpu.SemaphoreType.DMA((boxes * slots + 3 * boxes + kept,)),
    ]
    kernel = functools.partial(near_kernel, first, begun, kept)
    if kept:
        del scratch[3]
        inner = kernel

        def kernel(*refs):
            place = 4 + begun + kept
            inner(*refs[:-1], refs[place], refs[-1])

    return pl.pallas_call(
        kernel,
        in_specs=[smem] * 2
        + [hbm, pl.BlockSpec(memory_space=pl.ANY)]
        + [hbm] * (begun + kept),
        out_specs=[vmem] * (1 + kept) if kept else hbm,
        out_shape=[
            pltpu.VMEM(shape, F32),
            *[pltpu.VMEM(array.shape, array.dtype) for array in keep],
        ]
        if kept
        else pltpu.HBM(shape, F32),
        scratch_shapes=scratch,
        compiler_params=pltpu.CompilerParams(vmem_limit_bytes=32 * MIB),
        cost_estimate=pl.CostEstimate(
            flops=10**11 if first == 2 else 2 * 10**9, bytes_accessed=8 * MIB, transcendentals=0
        ),
        name=("near_low", "near_own", "near_high")[first],
    )(
        listed,
        starts,
        *in_hbm(blocks),
        source if first != 1 else in_hbm(source)[0],
        *in_hbm(*([before] if begun else []), *keep),
    )


def adjoint_kernel(rad_ref, out_hbm, held):
    for box in range(rad_ref.shape[0]):
        held[box] = side_by_side(rad_ref[box, 0].T, rad_ref[box, 1].T)
    pltpu.sync_copy(held, out_hbm)


def adjoint(radiation):
    boxes, _, points, basis = radiation.shape
    return pl.pallas_call(
        adjoint_kernel,
        in_specs=[pl.BlockSpec(memory_space=pltpu.VMEM)],
        out_specs=pl.BlockSpec(memory_space=pltpu.HBM),
        scratch_shapes=[pltpu.VMEM((boxes, basis, 2 * points), BF16)],
        out_shape=pltpu.HBM((boxes, basis, 2 * points), BF16),
        cost_estimate=pl.CostEstimate(
            flops=10**6, bytes_accessed=2 * MIB, transcendentals=0
        ),
        name="adjoint",
    )(radiation)


def down_kernel(phi_ref, near_ref, w_ref, adjoint_ref, *refs):
    bands_ref, received = refs[0], refs[1:-4]
    out_hbm, field, held, sems = refs[-4:]
    boxes, _, width = adjoint_ref.shape
    points = width // 2
    rhs = held.shape[3]
    phi = phi_ref[0]
    phi_size = field.shape[1]
    pairs = [(bands_ref.at[:, phi], field.at[:, phi])]
    for distance, piece in enumerate(received, 1):
        pairs.append((piece, field.at[:, lax.rem(phi + phi_size - distance, phi_size)]))
    copies = [
        pltpu.make_async_copy(source, target, sems.at[boxes + place])
        for place, (source, target) in enumerate(pairs)
    ]
    out_copies = [
        pltpu.make_async_copy(held.at[box], out_hbm.at[box], sems.at[box]) for box in range(boxes)
    ]
    for copy in copies:
        copy.start()
    for copy in copies:
        copy.wait()
    mixed = dot(w_ref[...], field[...].reshape(w_ref.shape[1], 2 * rhs))
    for octant in range(boxes // 2):
        start = 2 * octant * points
        cos_part = mixed[start : start + points]
        sin_part = mixed[start + points : start + 2 * points]
        cos_re, cos_im = cos_part[:, :rhs], cos_part[:, rhs:]
        sin_re, sin_im = sin_part[:, :rhs], sin_part[:, rhs:]
        leaves = (
            (octant, cos_re + sin_im, cos_im - sin_re),
            (boxes - 1 - octant, cos_re - sin_im, cos_im + sin_re),
        )
        for box, real, imag in leaves:
            real, imag = real.astype(BF16), imag.astype(BF16)
            right = jnp.concatenate([side_by_side(real, imag), side_by_side(imag, -real)], axis=0)
            far = dot(adjoint_ref[box], right)
            held[box, 0] = near_ref[box, 0] + far[:, :rhs]
            held[box, 1] = near_ref[box, 1] + far[:, rhs:]
            out_copies[box].start()
    for copy in out_copies:
        copy.wait()


def downward(phi, bands, received, near, weights, radiation_adjoint):
    boxes = near.shape[0]
    anywhere = pl.BlockSpec(memory_space=pl.ANY)
    ready = [
        pltpu.with_memory_space_constraint(array, pltpu.VMEM)
        for array in (near, weights, radiation_adjoint)
    ]
    return pl.pallas_call(
        down_kernel,
        in_specs=[pl.BlockSpec(memory_space=pltpu.SMEM)]
        + [pl.BlockSpec(memory_space=pltpu.VMEM)] * 3
        + [anywhere] * (1 + len(received)),
        out_specs=pl.BlockSpec(memory_space=pltpu.HBM),
        out_shape=jax.ShapeDtypeStruct(near.shape, F32),
        scratch_shapes=[
            pltpu.VMEM(bands.shape, BF16),
            pltpu.VMEM(near.shape, F32),
            pltpu.SemaphoreType.DMA((boxes + 1 + len(received),)),
        ],
        compiler_params=pltpu.CompilerParams(vmem_limit_bytes=32 * MIB),
        cost_estimate=pl.CostEstimate(
            flops=2 * 10**9, bytes_accessed=7 * MIB, transcendentals=0
        ),
        name="downward",
    )(phi, *ready, bands, *received)


def shift(block, axis, step):
    count = lax.axis_size(axis)
    pairs = [(i, i + step) for i in range(count) if 0 <= i + step < count]
    return lax.ppermute(block, axis, pairs)


def lists_of(partners, vector_ids, pair_count):
    used = jnp.arange(partners.shape[1])[None, :] < pair_count[:, None]
    names = jnp.where(used, partners, NOWHERE)
    return jnp.stack([names, vector_ids], axis=2).reshape(-1, 2)


def parent_bands(spread, shares):
    axes = ("box", "theta", "phi") if shares == lax.axis_size("box") else ("theta", "phi")
    return lax.all_to_all(spread, axes, split_axis=0, concat_axis=0, tiled=True)


def staged_bands(incoming, shares):
    axes = ("box", "theta") if shares == lax.axis_size("box") else ("theta",)
    phi_size = lax.axis_size("phi")
    phi = lax.axis_index("phi")
    bands = incoming.reshape(-1, phi_size, *incoming.shape[1:])
    bands = lax.all_to_all(bands, axes, split_axis=0, concat_axis=0, tiled=True)
    received = []
    for distance in range(1, phi_size):
        piece = lax.dynamic_index_in_dim(bands, (phi + distance) % phi_size, 1, keepdims=False)
        ring = [(place, (place + distance) % phi_size) for place in range(phi_size)]
        received.append(lax.ppermute(piece, "phi", ring))
    return phi.astype(jnp.int32).reshape(1), bands, received


def translation_lines(lists, translation, shares, per_group):
    operator_total, _, theta_band, phi_band = translation.shape
    rank = lax.axis_index("box")
    if shares < lax.axis_size("box"):
        table = translation.reshape(operator_total, -1)
        base = ((rank - 1) * per_group).astype(jnp.int32).reshape(1)
        return couplings(lists, base, table, per_group, 3 * per_group)
    if shares == 2:
        other = lax.ppermute(lists, "box", [(0, 1), (1, 0)])
        lists = jnp.where(
            rank == 0, jnp.concatenate([lists, other]), jnp.concatenate([other, lists])
        )
    part = theta_band // shares
    table = lax.dynamic_slice_in_dim(translation, rank * part, part, axis=2)
    table = table.reshape(operator_total, -1)
    total = shares * per_group
    return couplings(lists, jnp.zeros((1,), jnp.int32), table, total, total)


def per_device(
    shares,
    up_weights,
    down_weights,
    coeffs,
    near_blocks,
    near_ids,
    near_count,
    radiation,
    partners,
    vector_ids,
    pair_count,
    translation,
):
    every = ("box", "theta", "phi")
    per_group = lax.axis_size("theta") * lax.axis_size("phi")
    low = shift(coeffs, every, 1)
    spread = upward(coeffs, radiation, up_weights, shares * per_group)
    radiation_adjoint = adjoint(radiation)
    lists = lists_of(partners, vector_ids, pair_count)
    spread, lists = lax.optimization_barrier((spread, lists))
    lines = translation_lines(lists, translation, shares, per_group)
    listed, starts = near_slots(near_ids, near_count, lax.axis_index(every))
    spread, lines, radiation_adjoint, listed, starts = lax.optimization_barrier(
        (spread, lines, radiation_adjoint, listed, starts)
    )
    parents = parent_bands(spread, shares)
    near = near_field(listed, starts, near_blocks, low, 0)
    near, late = lax.optimization_barrier((near, coeffs))
    high = shift(late, every, -1)
    parents, near = lax.optimization_barrier((parents, near))
    sources = [parents]
    if shares < lax.axis_size("box"):
        sources = [shift(parents, "box", 1), parents, shift(parents, "box", -1)]
    incoming = translate(lines, sources)
    incoming, near = lax.optimization_barrier((incoming, near))
    phi, bands, received = staged_bands(incoming, shares)
    near = near_field(listed, starts, near_blocks, coeffs, 1, near)
    ready = near_field(
        listed, starts, near_blocks, high, 2, near, keep=(down_weights, radiation_adjoint)
    )
    return downward(phi, bands, received, *ready)


def solution(mesh):
    box_size, theta_size, phi_size = (mesh.shape[axis] for axis in ("box", "theta", "phi"))
    shares = box_size if box_size <= 2 and TU // theta_size % box_size == 0 else 1
    up_weights, down_weights = operators(shares, theta_size, phi_size)
    in_specs = (
        P(),
        P(),
        P(("box", "theta", "phi"), None, None, None),
        P(("box", "theta", "phi"), None, None, None, None),
        P(("box", "theta", "phi"), None),
        P(("box", "theta", "phi")),
        P(("box", "theta", "phi"), None, None, None),
        P("box", None),
        P("box", None),
        P("box"),
        P(None, None, "theta", "phi"),
    )
    out_specs = P(("box", "theta", "phi"), None, None, None)
    mapped = jax.shard_map(
        functools.partial(per_device, shares),
        mesh=mesh,
        in_specs=in_specs,
        out_specs=out_specs,
        check_vma=False,
    )

    def product(*arrays):
        return mapped(jnp.asarray(up_weights), jnp.asarray(down_weights), *arrays)

    return product
```

```python
import functools
import math

import jax
import jax.numpy as jnp
import ml_dtypes
import numpy as np
from jax import lax
from jax.experimental import pallas as pl
from jax.experimental.pallas import tpu as pltpu
from jax.sharding import PartitionSpec as P

TL = 8
PL = 16
TU = 16
PU = 32

WEIGHT_UP = (-0.0546875, 0.8203125, 0.2734375, -0.0390625)
WEIGHT_DOWN = (-0.0390625, 0.2734375, 0.8203125, -0.0546875)
PHASE_SCALE = 1.3

F32 = jnp.float32
BF16 = jnp.bfloat16
MIB = 2**20
GROUP = 2
NOWHERE = -(2**20)


def lagrange(rows, columns, wrap):
    matrix = np.zeros((rows, columns))
    for row in range(rows):
        weights = WEIGHT_UP if row % 2 else WEIGHT_DOWN
        for order in range(4):
            node = row // 2 + row % 2 - 2 + order
            node = node % columns if wrap else min(max(node, 0), columns - 1)
            matrix[row, node] += weights[order]
    return matrix


def split_weights(matrix):
    high = matrix.astype(ml_dtypes.bfloat16)
    low = (matrix - high.astype(np.float64)).astype(ml_dtypes.bfloat16)
    return high, low


def operators(shares, theta_size, phi_size):
    theta_part = TU // theta_size // shares
    order = np.arange(TU * PU).reshape(theta_size, shares, theta_part, phi_size, PU // phi_size)
    order = order.transpose(1, 0, 3, 2, 4).reshape(-1)
    interp = np.kron(lagrange(TU, TL, False), lagrange(PU, PL, True))
    theta = math.pi * (np.arange(TU) + 0.5) / TU
    azimuth = 2.0 * math.pi * (np.arange(PU) + 0.5) / PU
    up, down = [], []
    for octant in range(4):
        sign_x = 2 * (octant % 2) - 1
        sign_y = 2 * (octant // 2 % 2) - 1
        sign_z = 2 * (octant // 4) - 1
        angle = PHASE_SCALE * (
            sign_x * np.sin(theta)[:, None] * np.cos(azimuth)[None]
            + sign_y * np.sin(theta)[:, None] * np.sin(azimuth)[None]
            + sign_z * np.cos(theta)[:, None]
        ).reshape(-1, 1)
        cos_high, cos_low = split_weights((np.cos(angle) * interp)[order])
        sin_high, sin_low = split_weights((np.sin(angle) * interp)[order])
        high = np.concatenate([cos_high, sin_high], axis=1)
        low = np.concatenate([cos_low, sin_low], axis=1)
        up.append(np.concatenate([high, low], axis=0))
        down += [cos_high.T, sin_high.T]
    return np.concatenate(up, axis=1), np.concatenate(down, axis=0)


def in_hbm(*arrays):
    return [pltpu.with_memory_space_constraint(array, pltpu.HBM) for array in arrays]


def dot(a, b):
    return jnp.dot(a, b, preferred_element_type=F32)


def side_by_side(real, imag):
    return jnp.concatenate([real, imag], axis=1)


def complex_columns(real, imag):
    return jnp.concatenate([side_by_side(real, imag), side_by_side(-imag, real)], axis=0)


def up_kernel(x_hbm, rad_hbm, w_hbm, out_hbm, x_ref, rad_ref, w_ref, right, result, sems):
    boxes, _, _, rhs = x_ref.shape
    points = rad_ref.shape[2]
    copies = [
        pltpu.make_async_copy(source, target, sems.at[place])
        for place, (source, target) in enumerate(
            ((x_hbm, x_ref), (rad_hbm, rad_ref), (w_hbm, w_ref))
        )
    ]
    for copy in copies:
        copy.start()
    copies[0].wait()
    copies[1].wait()
    half = boxes // 2
    for octant in range(boxes):
        left = side_by_side(rad_ref[octant, 0], rad_ref[octant, 1])
        straight = dot(left, complex_columns(x_ref[octant, 0], x_ref[octant, 1])).astype(BF16)
        real, imag = straight[:, :rhs], straight[:, rhs:]
        if octant < half:
            swapped = side_by_side(-imag, real)
        else:
            swapped = side_by_side(imag, -real)
        place = octant if octant < half else boxes - 1 - octant
        start = 2 * place * points
        right[octant // half, start : start + points] = straight
        right[octant // half, start + points : start + 2 * points] = swapped
    copies[2].wait()
    total = dot(w_ref[...], right[0]) + dot(w_ref[...], right[1])
    samples = total.shape[0] // 2
    total = total[:samples] + total[samples:]
    result[...] = total.astype(BF16).reshape(result.shape)
    pltpu.sync_copy(result, out_hbm)


def upward(coeffs, radiation, weights, groups):
    boxes, _, basis, rhs = coeffs.shape
    rows, columns = weights.shape
    samples = rows // 2
    hbm = pl.BlockSpec(memory_space=pltpu.HBM)
    return pl.pallas_call(
        up_kernel,
        in_specs=[hbm] * 3,
        out_specs=hbm,
        out_shape=pltpu.HBM((groups, samples // groups, 2 * rhs), BF16),
        scratch_shapes=[
            pltpu.VMEM(coeffs.shape, BF16),
            pltpu.VMEM(radiation.shape, BF16),
            pltpu.VMEM(weights.shape, BF16),
            pltpu.VMEM((2, columns, 2 * rhs), BF16),
            pltpu.VMEM((groups, samples // groups, 2 * rhs), BF16),
            pltpu.SemaphoreType.DMA((3,)),
        ],
        compiler_params=pltpu.CompilerParams(vmem_limit_bytes=32 * MIB),
        cost_estimate=pl.CostEstimate(
            flops=2 * 10**9, bytes_accessed=4 * MIB, transcendentals=0
        ),
        name="upward",
    )(*in_hbm(coeffs, radiation, weights))


def coupling_kernel(lists_ref, base_ref, table_ref, out_ref):
    rows = lists_ref.shape[0]
    samples = table_ref.shape[1] // 2
    _, targets, columns = out_ref.shape
    slots = rows // targets
    selector = (
        lax.broadcasted_iota(jnp.int32, (rows, table_ref.shape[0]), 1) == lists_ref[:, 1:2]
    )
    chosen = dot(selector.astype(BF16), table_ref[...]).astype(BF16)
    wide = lax.broadcasted_iota(jnp.int32, (rows, columns), 1) // samples
    match = wide + base_ref[0] == lists_ref[:, 0:1]
    spread = lax.broadcasted_iota(jnp.int32, (samples, columns), 0) == (
        lax.broadcasted_iota(jnp.int32, (samples, columns), 1) % samples
    )
    gather = (
        lax.broadcasted_iota(jnp.int32, (targets, rows), 1) // slots
        == lax.broadcasted_iota(jnp.int32, (targets, rows), 0)
    ).astype(BF16)
    tile = spread.astype(BF16)
    for part in range(2):
        lines = dot(chosen[:, part * samples : (part + 1) * samples], tile)
        out_ref[part] = dot(gather, jnp.where(match, lines, 0.0).astype(BF16))


def couplings(lists, base, table, targets, names):
    shape = (2, targets, names * (table.shape[1] // 2))
    vmem = pl.BlockSpec(memory_space=pltpu.VMEM)
    return pl.pallas_call(
        coupling_kernel,
        in_specs=[vmem, pl.BlockSpec(memory_space=pltpu.SMEM), vmem],
        out_specs=vmem,
        out_shape=jax.ShapeDtypeStruct(shape, F32),
        compiler_params=pltpu.CompilerParams(vmem_limit_bytes=16 * MIB),
        cost_estimate=pl.CostEstimate(
            flops=2 * 10**8, bytes_accessed=2 * 2**20, transcendentals=0
        ),
        name="coupling",
    )(lists, base, table)


def translate_kernel(lines_hbm, *refs):
    count = (len(refs) - 5) // 2
    sources, out_hbm = refs[:count], refs[count]
    held, lines, matrix, result, sems = refs[count + 1 :][:count], *refs[2 * count + 1 :]
    targets, samples, width = result.shape
    rhs = width // 2
    copies = [
        pltpu.make_async_copy(source, target, sems.at[place])
        for place, (source, target) in enumerate(zip((lines_hbm, *sources), (lines, *held)))
    ]
    for copy in copies:
        copy.start()
    copies[0].wait()
    columns = matrix.shape[1]
    row = lax.broadcasted_iota(jnp.int32, (samples, columns), 0)
    diagonal = row == lax.broadcasted_iota(jnp.int32, (samples, columns), 1) % samples
    for part in range(2):
        for target in range(targets):
            line = jnp.broadcast_to(lines[part, target : target + 1], diagonal.shape)
            start = (part * targets + target) * samples
            matrix[start : start + samples] = jnp.where(diagonal, line, 0.0).astype(BF16)
    total = None
    start = 0
    for place, source in enumerate(held):
        copies[1 + place].wait()
        stop = start + source.shape[0] * samples
        part = dot(matrix[:, start:stop], source[...].reshape(stop - start, width))
        total = part if total is None else total + part
        start = stop
    half = targets * samples
    real = total[:half, :rhs] - total[half:, rhs:]
    imag = total[:half, rhs:] + total[half:, :rhs]
    result[...] = jnp.concatenate([real, imag], axis=1).astype(BF16).reshape(result.shape)
    pltpu.sync_copy(result, out_hbm)


def translate(lines, sources):
    _, samples, width = sources[0].shape
    _, targets, columns = lines.shape
    shape = (targets, samples, width)
    hbm = pl.BlockSpec(memory_space=pltpu.HBM)
    anywhere = pl.BlockSpec(memory_space=pl.ANY)
    return pl.pallas_call(
        translate_kernel,
        in_specs=[hbm] + [anywhere] * len(sources),
        out_specs=hbm,
        out_shape=pltpu.HBM(shape, BF16),
        scratch_shapes=[
            *[pltpu.VMEM(source.shape, BF16) for source in sources],
            pltpu.VMEM(lines.shape, F32),
            pltpu.VMEM((2 * targets * samples, columns), BF16),
            pltpu.VMEM(shape, BF16),
            pltpu.SemaphoreType.DMA((1 + len(sources),)),
        ],
        compiler_params=pltpu.CompilerParams(vmem_limit_bytes=24 * MIB),
        cost_estimate=pl.CostEstimate(
            flops=10**9, bytes_accessed=2 * MIB, transcendentals=0
        ),
        name="translate",
    )(*in_hbm(lines), *sources)


def near_kernel(first, begun, kept, *refs):
    count = 1 if first == 1 else 2
    listed, starts_ref, blocks_hbm = refs[:3]
    source_refs, refs = refs[3 : 3 + count], refs[3 + count :]
    before_hbm = refs[0] if begun else None
    kept_hbm = refs[begun : begun + kept]
    out_ref = refs[begun + kept]
    kept_refs = refs[1 + begun + kept : 1 + begun + 2 * kept]
    blocks, held, wide, total_ref, sems = refs[1 + begun + 2 * kept :]
    boxes, _, basis, rhs = held.shape
    most = blocks_hbm.shape[0]
    starts = [starts_ref[first, box] for box in range(boxes + 1)]

    def by_box(source, target, turn):
        return [
            pltpu.make_async_copy(
                source.at[box], target.at[box], sems.at[most + turn * boxes + box]
            )
            for box in range(boxes)
        ]

    part = boxes // count
    source_copies = [
        pltpu.make_async_copy(
            source_refs[box // part].at[box % part], held.at[box], sems.at[most + box]
        )
        for box in range(boxes)
    ]
    before_copies = by_box(before_hbm, total_ref, 1) if begun else []
    out_copies = [] if kept else by_box(total_ref, out_ref, 2)
    kept_copies = [
        pltpu.make_async_copy(kept_hbm[place], kept_refs[place], sems.at[most + 3 * boxes + place])
        for place in range(kept)
    ]
    for copy in source_copies:
        copy.start()

    def block_copy(place):
        block = listed[first, place] // boxes
        return pltpu.make_async_copy(blocks_hbm.at[block], blocks.at[place], sems.at[place])

    def fetch(place, carry):
        block_copy(place).start()
        return carry

    lax.fori_loop(0, starts[boxes], fetch, 0)
    for copy in before_copies + kept_copies:
        copy.start()
    for copy in source_copies:
        copy.wait()
    for place in range(boxes):
        wide[place] = complex_columns(held[place, 0], held[place, 1])

    def landed(place, carry):
        block_copy(place).wait()
        return carry

    lax.fori_loop(0, starts[boxes], landed, 0)
    for copy in before_copies:
        copy.wait()

    def group(box, begin, size):
        left, right = [], []
        for step in range(size):
            place = starts[box] + begin + step
            valid = place < starts[box + 1]
            place = jnp.where(valid, place, 0)
            real, imag = blocks[place, 0], blocks[place, 1]
            real = jnp.where(valid, real, jnp.zeros_like(real))
            imag = jnp.where(valid, imag, jnp.zeros_like(imag))
            left.append(side_by_side(real, imag))
            right.append(wide[jnp.where(valid, listed[first, place] % boxes, 0)])
        return dot(jnp.concatenate(left, axis=1), jnp.concatenate(right, axis=0))

    half = boxes // 2
    possible = [
        (
            min(half, boxes - box) + min(half, box + 1),
            boxes,
            max(half - box, 0) + max(box + 1 - half, 0),
        )[first]
        for box in range(boxes)
    ]
    sizes = [min(most_sources, 3 if most_sources < 7 else 4) for most_sources in possible]
    for box in range(boxes):
        part = group(box, 0, sizes[box])
        if begun:
            total_ref[box, 0] += part[:, :rhs]
            total_ref[box, 1] += part[:, rhs:]
        else:
            total_ref[box, 0] = part[:, :rhs]
            total_ref[box, 1] = part[:, rhs:]
    for box in range(boxes):

        def more(index, carry, box=box):
            part = group(box, sizes[box] + GROUP * index, GROUP)
            total_ref[box, 0] += part[:, :rhs]
            total_ref[box, 1] += part[:, rhs:]
            return carry

        rest = starts[box + 1] - starts[box] - sizes[box]
        lax.fori_loop(0, (jnp.maximum(rest, 0) + GROUP - 1) // GROUP, more, 0)
        if out_copies:
            out_copies[box].start()
    for copy in out_copies + kept_copies:
        copy.wait()


def near_slots(ids, used, rank):
    boxes, slots = ids.shape
    total = boxes * slots
    source = ids - (rank - 1) * boxes
    source = jnp.where(jnp.arange(slots) < used[:, None], source, -1).reshape(-1)
    half = boxes // 2
    side, inside = source // boxes, source % boxes
    near = ((side == 0) & (inside >= half)) | ((side == 2) & (inside < half))
    far = ((side == 0) & (inside < half)) | ((side == 2) & (inside >= half))
    wanted = (source >= 0) & jnp.stack([near, side == 1, far])
    inside = jnp.where(near, (inside + half) % boxes, inside)
    earlier = jnp.arange(total)[None, :] < jnp.arange(total)[:, None]
    place = jnp.sum((wanted[:, None, :] & earlier).astype(jnp.int32), axis=2)
    code = jnp.arange(total) * boxes + inside
    chosen = wanted[:, None, :] & (place[:, None, :] == jnp.arange(total)[:, None])
    listed = jnp.sum(jnp.where(chosen, code, 0), axis=2)
    before = jnp.arange(total) // slots < jnp.arange(boxes + 1)[:, None]
    starts = jnp.sum((wanted[:, None, :] & before).astype(jnp.int32), axis=2)
    return listed.astype(jnp.int32), starts.astype(jnp.int32)


def near_field(listed, starts, blocks, sources, first, before=None, keep=()):
    boxes, slots, _, basis, _ = blocks.shape
    blocks = blocks.reshape(boxes * slots, *blocks.shape[2:])
    rhs = sources[0].shape[3]
    begun, kept = before is not None, len(keep)
    hbm = pl.BlockSpec(memory_space=pltpu.HBM)
    smem = pl.BlockSpec(memory_space=pltpu.SMEM)
    vmem = pl.BlockSpec(memory_space=pltpu.VMEM)
    shape = (boxes, 2, basis, rhs)
    scratch = [
        pltpu.VMEM(blocks.shape, BF16),
        pltpu.VMEM(shape, BF16),
        pltpu.VMEM((boxes, 2 * basis, 2 * rhs), BF16),
        pltpu.VMEM(shape, F32),
        pltpu.SemaphoreType.DMA((boxes * slots + 3 * boxes + kept,)),
    ]
    kernel = functools.partial(near_kernel, first, begun, kept)
    if kept:
        del scratch[3]
        inner = kernel

        def kernel(*refs):
            place = 3 + len(sources) + begun + kept
            inner(*refs[:-1], refs[place], refs[-1])

    return pl.pallas_call(
        kernel,
        in_specs=[smem] * 2
        + [hbm]
        + [pl.BlockSpec(memory_space=pl.ANY)] * len(sources)
        + [hbm] * (begun + kept),
        out_specs=[vmem] * (1 + kept) if kept else hbm,
        out_shape=[
            pltpu.VMEM(shape, F32),
            *[pltpu.VMEM(array.shape, array.dtype) for array in keep],
        ]
        if kept
        else pltpu.HBM(shape, F32),
        scratch_shapes=scratch,
        compiler_params=pltpu.CompilerParams(vmem_limit_bytes=32 * MIB),
        cost_estimate=pl.CostEstimate(
            flops=10**11 if first == 2 else 2 * 10**9, bytes_accessed=8 * MIB, transcendentals=0
        ),
        name=("near_nearer", "near_own", "near_farther")[first],
    )(
        listed,
        starts,
        *in_hbm(blocks),
        *(sources if first != 1 else in_hbm(*sources)),
        *in_hbm(*([before] if begun else []), *keep),
    )


def adjoint_kernel(rad_ref, out_hbm, held):
    for box in range(rad_ref.shape[0]):
        held[box] = side_by_side(rad_ref[box, 0].T, rad_ref[box, 1].T)
    pltpu.sync_copy(held, out_hbm)


def adjoint(radiation):
    boxes, _, points, basis = radiation.shape
    return pl.pallas_call(
        adjoint_kernel,
        in_specs=[pl.BlockSpec(memory_space=pltpu.VMEM)],
        out_specs=pl.BlockSpec(memory_space=pltpu.HBM),
        scratch_shapes=[pltpu.VMEM((boxes, basis, 2 * points), BF16)],
        out_shape=pltpu.HBM((boxes, basis, 2 * points), BF16),
        cost_estimate=pl.CostEstimate(
            flops=10**6, bytes_accessed=2 * MIB, transcendentals=0
        ),
        name="adjoint",
    )(radiation)


def down_kernel(phi_ref, near_ref, w_ref, adjoint_ref, *refs):
    bands_ref, received = refs[0], refs[1:-4]
    out_hbm, field, held, sems = refs[-4:]
    boxes, _, width = adjoint_ref.shape
    points = width // 2
    rhs = held.shape[3]
    phi = phi_ref[0]
    phi_size = field.shape[1]
    pairs = [(bands_ref.at[:, phi], field.at[:, phi])]
    for distance, piece in enumerate(received, 1):
        pairs.append((piece, field.at[:, lax.rem(phi + phi_size - distance, phi_size)]))
    copies = [
        pltpu.make_async_copy(source, target, sems.at[boxes + place])
        for place, (source, target) in enumerate(pairs)
    ]
    out_copies = [
        pltpu.make_async_copy(held.at[box], out_hbm.at[box], sems.at[box]) for box in range(boxes)
    ]
    for copy in copies:
        copy.start()
    for copy in copies:
        copy.wait()
    mixed = dot(w_ref[...], field[...].reshape(w_ref.shape[1], 2 * rhs))
    for octant in range(boxes // 2):
        start = 2 * octant * points
        cos_part = mixed[start : start + points]
        sin_part = mixed[start + points : start + 2 * points]
        cos_re, cos_im = cos_part[:, :rhs], cos_part[:, rhs:]
        sin_re, sin_im = sin_part[:, :rhs], sin_part[:, rhs:]
        leaves = (
            (octant, cos_re + sin_im, cos_im - sin_re),
            (boxes - 1 - octant, cos_re - sin_im, cos_im + sin_re),
        )
        for box, real, imag in leaves:
            real, imag = real.astype(BF16), imag.astype(BF16)
            right = jnp.concatenate([side_by_side(real, imag), side_by_side(imag, -real)], axis=0)
            far = dot(adjoint_ref[box], right)
            held[box, 0] = near_ref[box, 0] + far[:, :rhs]
            held[box, 1] = near_ref[box, 1] + far[:, rhs:]
            out_copies[box].start()
    for copy in out_copies:
        copy.wait()


def downward(phi, bands, received, near, weights, radiation_adjoint):
    boxes = near.shape[0]
    anywhere = pl.BlockSpec(memory_space=pl.ANY)
    ready = [
        pltpu.with_memory_space_constraint(array, pltpu.VMEM)
        for array in (near, weights, radiation_adjoint)
    ]
    return pl.pallas_call(
        down_kernel,
        in_specs=[pl.BlockSpec(memory_space=pltpu.SMEM)]
        + [pl.BlockSpec(memory_space=pltpu.VMEM)] * 3
        + [anywhere] * (1 + len(received)),
        out_specs=pl.BlockSpec(memory_space=pltpu.HBM),
        out_shape=jax.ShapeDtypeStruct(near.shape, F32),
        scratch_shapes=[
            pltpu.VMEM(bands.shape, BF16),
            pltpu.VMEM(near.shape, F32),
            pltpu.SemaphoreType.DMA((boxes + 1 + len(received),)),
        ],
        compiler_params=pltpu.CompilerParams(vmem_limit_bytes=32 * MIB),
        cost_estimate=pl.CostEstimate(
            flops=2 * 10**9, bytes_accessed=7 * MIB, transcendentals=0
        ),
        name="downward",
    )(phi, *ready, bands, *received)


def shift(block, axis, step):
    count = lax.axis_size(axis)
    pairs = [(i, i + step) for i in range(count) if 0 <= i + step < count]
    return lax.ppermute(block, axis, pairs)


def lists_of(partners, vector_ids, pair_count):
    used = jnp.arange(partners.shape[1])[None, :] < pair_count[:, None]
    names = jnp.where(used, partners, NOWHERE)
    return jnp.stack([names, vector_ids], axis=2).reshape(-1, 2)


def parent_bands(spread, shares):
    axes = ("box", "theta", "phi") if shares == lax.axis_size("box") else ("theta", "phi")
    return lax.all_to_all(spread, axes, split_axis=0, concat_axis=0, tiled=True)


def staged_bands(incoming, shares):
    axes = ("box", "theta") if shares == lax.axis_size("box") else ("theta",)
    phi_size = lax.axis_size("phi")
    phi = lax.axis_index("phi")
    bands = incoming.reshape(-1, phi_size, *incoming.shape[1:])
    bands = lax.all_to_all(bands, axes, split_axis=0, concat_axis=0, tiled=True)
    received = []
    for distance in range(1, phi_size):
        piece = lax.dynamic_index_in_dim(bands, (phi + distance) % phi_size, 1, keepdims=False)
        ring = [(place, (place + distance) % phi_size) for place in range(phi_size)]
        received.append(lax.ppermute(piece, "phi", ring))
    return phi.astype(jnp.int32).reshape(1), bands, received


def translation_lines(lists, translation, shares, per_group):
    operator_total, _, theta_band, phi_band = translation.shape
    rank = lax.axis_index("box")
    if shares < lax.axis_size("box"):
        table = translation.reshape(operator_total, -1)
        base = ((rank - 1) * per_group).astype(jnp.int32).reshape(1)
        return couplings(lists, base, table, per_group, 3 * per_group)
    if shares == 2:
        other = lax.ppermute(lists, "box", [(0, 1), (1, 0)])
        lists = jnp.where(
            rank == 0, jnp.concatenate([lists, other]), jnp.concatenate([other, lists])
        )
    part = theta_band // shares
    table = lax.dynamic_slice_in_dim(translation, rank * part, part, axis=2)
    table = table.reshape(operator_total, -1)
    total = shares * per_group
    return couplings(lists, jnp.zeros((1,), jnp.int32), table, total, total)


def per_device(
    shares,
    up_weights,
    down_weights,
    coeffs,
    near_blocks,
    near_ids,
    near_count,
    radiation,
    partners,
    vector_ids,
    pair_count,
    translation,
):
    every = ("box", "theta", "phi")
    per_group = lax.axis_size("theta") * lax.axis_size("phi")
    half = coeffs.shape[0] // 2
    front, back = coeffs[:half], coeffs[half:]
    nearer = (shift(back, every, 1), shift(front, every, -1))
    spread = upward(coeffs, radiation, up_weights, shares * per_group)
    radiation_adjoint = adjoint(radiation)
    lists = lists_of(partners, vector_ids, pair_count)
    spread, lists = lax.optimization_barrier((spread, lists))
    lines = translation_lines(lists, translation, shares, per_group)
    listed, starts = near_slots(near_ids, near_count, lax.axis_index(every))
    spread, lines, radiation_adjoint, listed, starts = lax.optimization_barrier(
        (spread, lines, radiation_adjoint, listed, starts)
    )
    parents = parent_bands(spread, shares)
    near = near_field(listed, starts, near_blocks, nearer, 0)
    near, front, back = lax.optimization_barrier((near, front, back))
    farther = (shift(front, every, 1), shift(back, every, -1))
    parents, near = lax.optimization_barrier((parents, near))
    sources = [parents]
    if shares < lax.axis_size("box"):
        sources = [shift(parents, "box", 1), parents, shift(parents, "box", -1)]
    incoming = translate(lines, sources)
    incoming, near = lax.optimization_barrier((incoming, near))
    phi, bands, received = staged_bands(incoming, shares)
    near = near_field(listed, starts, near_blocks, (coeffs,), 1, near)
    ready = near_field(
        listed, starts, near_blocks, farther, 2, near, keep=(down_weights, radiation_adjoint)
    )
    return downward(phi, bands, received, *ready)


def solution(mesh):
    box_size, theta_size, phi_size = (mesh.shape[axis] for axis in ("box", "theta", "phi"))
    shares = box_size if box_size <= 2 and TU // theta_size % box_size == 0 else 1
    up_weights, down_weights = operators(shares, theta_size, phi_size)
    in_specs = (
        P(),
        P(),
        P(("box", "theta", "phi"), None, None, None),
        P(("box", "theta", "phi"), None, None, None, None),
        P(("box", "theta", "phi"), None),
        P(("box", "theta", "phi")),
        P(("box", "theta", "phi"), None, None, None),
        P("box", None),
        P("box", None),
        P("box"),
        P(None, None, "theta", "phi"),
    )
    out_specs = P(("box", "theta", "phi"), None, None, None)
    mapped = jax.shard_map(
        functools.partial(per_device, shares),
        mesh=mesh,
        in_specs=in_specs,
        out_specs=out_specs,
        check_vma=False,
    )

    def product(*arrays):
        return mapped(jnp.asarray(up_weights), jnp.asarray(down_weights), *arrays)

    return product
```

```python
import functools
import math

import jax
import jax.numpy as jnp
import ml_dtypes
import numpy as np
from jax import lax
from jax.experimental import pallas as pl
from jax.experimental.pallas import tpu as pltpu
from jax.sharding import PartitionSpec as P

TL = 8
PL = 16
TU = 16
PU = 32

WEIGHT_UP = (-0.0546875, 0.8203125, 0.2734375, -0.0390625)
WEIGHT_DOWN = (-0.0390625, 0.2734375, 0.8203125, -0.0546875)
PHASE_SCALE = 1.3

F32 = jnp.float32
BF16 = jnp.bfloat16
MIB = 2**20
GROUP = 2
NOWHERE = -(2**20)


def lagrange(rows, columns, wrap):
    matrix = np.zeros((rows, columns))
    for row in range(rows):
        weights = WEIGHT_UP if row % 2 else WEIGHT_DOWN
        for order in range(4):
            node = row // 2 + row % 2 - 2 + order
            node = node % columns if wrap else min(max(node, 0), columns - 1)
            matrix[row, node] += weights[order]
    return matrix


def split_weights(matrix):
    high = matrix.astype(ml_dtypes.bfloat16)
    low = (matrix - high.astype(np.float64)).astype(ml_dtypes.bfloat16)
    return high, low


def operators(shares, theta_size, phi_size):
    theta_part = TU // theta_size // shares
    order = np.arange(TU * PU).reshape(theta_size, shares, theta_part, phi_size, PU // phi_size)
    order = order.transpose(1, 0, 3, 2, 4).reshape(-1)
    interp = np.kron(lagrange(TU, TL, False), lagrange(PU, PL, True))
    theta = math.pi * (np.arange(TU) + 0.5) / TU
    azimuth = 2.0 * math.pi * (np.arange(PU) + 0.5) / PU
    up, down = [], []
    for octant in range(4):
        sign_x = 2 * (octant % 2) - 1
        sign_y = 2 * (octant // 2 % 2) - 1
        sign_z = 2 * (octant // 4) - 1
        angle = PHASE_SCALE * (
            sign_x * np.sin(theta)[:, None] * np.cos(azimuth)[None]
            + sign_y * np.sin(theta)[:, None] * np.sin(azimuth)[None]
            + sign_z * np.cos(theta)[:, None]
        ).reshape(-1, 1)
        cos_high, cos_low = split_weights((np.cos(angle) * interp)[order])
        sin_high, sin_low = split_weights((np.sin(angle) * interp)[order])
        high = np.concatenate([cos_high, sin_high], axis=1)
        low = np.concatenate([cos_low, sin_low], axis=1)
        up.append(np.concatenate([high, low], axis=0))
        down += [cos_high.T, sin_high.T]
    return np.concatenate(up, axis=1), np.concatenate(down, axis=0)


def in_hbm(*arrays):
    return [pltpu.with_memory_space_constraint(array, pltpu.HBM) for array in arrays]


def dot(a, b):
    return jnp.dot(a, b, preferred_element_type=F32)


def side_by_side(real, imag):
    return jnp.concatenate([real, imag], axis=1)


def complex_columns(real, imag):
    return jnp.concatenate([side_by_side(real, imag), side_by_side(-imag, real)], axis=0)


def up_kernel(x_hbm, rad_hbm, w_hbm, out_hbm, x_ref, rad_ref, w_ref, right, result, sems):
    boxes, _, _, rhs = x_ref.shape
    points = rad_ref.shape[2]
    copies = [
        pltpu.make_async_copy(source, target, sems.at[place])
        for place, (source, target) in enumerate(
            ((x_hbm, x_ref), (rad_hbm, rad_ref), (w_hbm, w_ref))
        )
    ]
    for copy in copies:
        copy.start()
    copies[0].wait()
    copies[1].wait()
    half = boxes // 2
    for octant in range(boxes):
        left = side_by_side(rad_ref[octant, 0], rad_ref[octant, 1])
        straight = dot(left, complex_columns(x_ref[octant, 0], x_ref[octant, 1])).astype(BF16)
        real, imag = straight[:, :rhs], straight[:, rhs:]
        if octant < half:
            swapped = side_by_side(-imag, real)
        else:
            swapped = side_by_side(imag, -real)
        place = octant if octant < half else boxes - 1 - octant
        start = 2 * place * points
        right[octant // half, start : start + points] = straight
        right[octant // half, start + points : start + 2 * points] = swapped
    copies[2].wait()
    total = dot(w_ref[...], right[0]) + dot(w_ref[...], right[1])
    samples = total.shape[0] // 2
    total = total[:samples] + total[samples:]
    result[...] = total.astype(BF16).reshape(result.shape)
    pltpu.sync_copy(result, out_hbm)


def upward(coeffs, radiation, weights, groups):
    boxes, _, basis, rhs = coeffs.shape
    rows, columns = weights.shape
    samples = rows // 2
    hbm = pl.BlockSpec(memory_space=pltpu.HBM)
    return pl.pallas_call(
        up_kernel,
        in_specs=[hbm] * 3,
        out_specs=hbm,
        out_shape=pltpu.HBM((groups, samples // groups, 2 * rhs), BF16),
        scratch_shapes=[
            pltpu.VMEM(coeffs.shape, BF16),
            pltpu.VMEM(radiation.shape, BF16),
            pltpu.VMEM(weights.shape, BF16),
            pltpu.VMEM((2, columns, 2 * rhs), BF16),
            pltpu.VMEM((groups, samples // groups, 2 * rhs), BF16),
            pltpu.SemaphoreType.DMA((3,)),
        ],
        compiler_params=pltpu.CompilerParams(vmem_limit_bytes=32 * MIB),
        cost_estimate=pl.CostEstimate(
            flops=10**6, bytes_accessed=2**10, transcendentals=0
        ),
        name="upward",
    )(*in_hbm(coeffs, radiation, weights))


def coupling_kernel(lists_ref, base_ref, table_ref, out_ref):
    rows = lists_ref.shape[0]
    samples = table_ref.shape[1] // 2
    _, targets, columns = out_ref.shape
    slots = rows // targets
    selector = (
        lax.broadcasted_iota(jnp.int32, (rows, table_ref.shape[0]), 1) == lists_ref[:, 1:2]
    )
    chosen = dot(selector.astype(BF16), table_ref[...]).astype(BF16)
    wide = lax.broadcasted_iota(jnp.int32, (rows, columns), 1) // samples
    match = wide + base_ref[0] == lists_ref[:, 0:1]
    spread = lax.broadcasted_iota(jnp.int32, (samples, columns), 0) == (
        lax.broadcasted_iota(jnp.int32, (samples, columns), 1) % samples
    )
    gather = (
        lax.broadcasted_iota(jnp.int32, (targets, rows), 1) // slots
        == lax.broadcasted_iota(jnp.int32, (targets, rows), 0)
    ).astype(BF16)
    tile = spread.astype(BF16)
    for part in range(2):
        lines = dot(chosen[:, part * samples : (part + 1) * samples], tile)
        out_ref[part] = dot(gather, jnp.where(match, lines, 0.0).astype(BF16))


def couplings(lists, base, table, targets, names):
    shape = (2, targets, names * (table.shape[1] // 2))
    vmem = pl.BlockSpec(memory_space=pltpu.VMEM)
    return pl.pallas_call(
        coupling_kernel,
        in_specs=[vmem, pl.BlockSpec(memory_space=pltpu.SMEM), vmem],
        out_specs=vmem,
        out_shape=jax.ShapeDtypeStruct(shape, F32),
        compiler_params=pltpu.CompilerParams(vmem_limit_bytes=16 * MIB),
        cost_estimate=pl.CostEstimate(
            flops=2 * 10**8, bytes_accessed=2 * 2**20, transcendentals=0
        ),
        name="coupling",
    )(lists, base, table)


def translate_kernel(lines_hbm, *refs):
    count = (len(refs) - 5) // 2
    sources, out_hbm = refs[:count], refs[count]
    held, lines, matrix, result, sems = refs[count + 1 :][:count], *refs[2 * count + 1 :]
    targets, samples, width = result.shape
    rhs = width // 2
    copies = [
        pltpu.make_async_copy(source, target, sems.at[place])
        for place, (source, target) in enumerate(zip((lines_hbm, *sources), (lines, *held)))
    ]
    for copy in copies:
        copy.start()
    copies[0].wait()
    columns = matrix.shape[1]
    row = lax.broadcasted_iota(jnp.int32, (samples, columns), 0)
    diagonal = row == lax.broadcasted_iota(jnp.int32, (samples, columns), 1) % samples
    for part in range(2):
        for target in range(targets):
            line = jnp.broadcast_to(lines[part, target : target + 1], diagonal.shape)
            start = (part * targets + target) * samples
            matrix[start : start + samples] = jnp.where(diagonal, line, 0.0).astype(BF16)
    total = None
    start = 0
    for place, source in enumerate(held):
        copies[1 + place].wait()
        stop = start + source.shape[0] * samples
        part = dot(matrix[:, start:stop], source[...].reshape(stop - start, width))
        total = part if total is None else total + part
        start = stop
    half = targets * samples
    real = total[:half, :rhs] - total[half:, rhs:]
    imag = total[:half, rhs:] + total[half:, :rhs]
    result[...] = jnp.concatenate([real, imag], axis=1).astype(BF16).reshape(result.shape)
    pltpu.sync_copy(result, out_hbm)


def translate(lines, sources):
    _, samples, width = sources[0].shape
    _, targets, columns = lines.shape
    shape = (targets, samples, width)
    hbm = pl.BlockSpec(memory_space=pltpu.HBM)
    anywhere = pl.BlockSpec(memory_space=pl.ANY)
    return pl.pallas_call(
        translate_kernel,
        in_specs=[hbm] + [anywhere] * len(sources),
        out_specs=hbm,
        out_shape=pltpu.HBM(shape, BF16),
        scratch_shapes=[
            *[pltpu.VMEM(source.shape, BF16) for source in sources],
            pltpu.VMEM(lines.shape, F32),
            pltpu.VMEM((2 * targets * samples, columns), BF16),
            pltpu.VMEM(shape, BF16),
            pltpu.SemaphoreType.DMA((1 + len(sources),)),
        ],
        compiler_params=pltpu.CompilerParams(vmem_limit_bytes=24 * MIB),
        cost_estimate=pl.CostEstimate(
            flops=10**6, bytes_accessed=2**10, transcendentals=0
        ),
        name="translate",
    )(*in_hbm(lines), *sources)


def near_kernel(first, begun, kept, *refs):
    count = 1 if first == 1 else 2
    listed, starts_ref, blocks_hbm = refs[:3]
    source_refs, refs = refs[3 : 3 + count], refs[3 + count :]
    before_hbm = refs[0] if begun else None
    kept_hbm = refs[begun : begun + kept]
    out_ref = refs[begun + kept]
    kept_refs = refs[1 + begun + kept : 1 + begun + 2 * kept]
    blocks, held, wide, total_ref, sems = refs[1 + begun + 2 * kept :]
    boxes, _, basis, rhs = held.shape
    most = blocks_hbm.shape[0]
    starts = [starts_ref[first, box] for box in range(boxes + 1)]

    def by_box(source, target, turn):
        return [
            pltpu.make_async_copy(
                source.at[box], target.at[box], sems.at[most + turn * boxes + box]
            )
            for box in range(boxes)
        ]

    part = boxes // count
    source_copies = [
        pltpu.make_async_copy(
            source_refs[box // part].at[box % part], held.at[box], sems.at[most + box]
        )
        for box in range(boxes)
    ]
    before_copies = by_box(before_hbm, total_ref, 1) if begun else []
    out_copies = [] if kept else by_box(total_ref, out_ref, 2)
    kept_copies = [
        pltpu.make_async_copy(kept_hbm[place], kept_refs[place], sems.at[most + 3 * boxes + place])
        for place in range(kept)
    ]
    for copy in source_copies:
        copy.start()

    def block_copy(place):
        block = listed[first, place] // boxes
        return pltpu.make_async_copy(blocks_hbm.at[block], blocks.at[place], sems.at[place])

    def fetch(place, carry):
        block_copy(place).start()
        return carry

    lax.fori_loop(0, starts[boxes], fetch, 0)
    for copy in before_copies + kept_copies:
        copy.start()
    for copy in source_copies:
        copy.wait()
    for place in range(boxes):
        wide[place] = complex_columns(held[place, 0], held[place, 1])

    def landed(place, carry):
        block_copy(place).wait()
        return carry

    lax.fori_loop(0, starts[boxes], landed, 0)
    for copy in before_copies:
        copy.wait()

    def group(box, begin, size):
        left, right = [], []
        for step in range(size):
            place = starts[box] + begin + step
            valid = place < starts[box + 1]
            place = jnp.where(valid, place, 0)
            real, imag = blocks[place, 0], blocks[place, 1]
            real = jnp.where(valid, real, jnp.zeros_like(real))
            imag = jnp.where(valid, imag, jnp.zeros_like(imag))
            left.append(side_by_side(real, imag))
            right.append(wide[jnp.where(valid, listed[first, place] % boxes, 0)])
        return dot(jnp.concatenate(left, axis=1), jnp.concatenate(right, axis=0))

    half = boxes // 2
    possible = [
        (
            min(half, boxes - box) + min(half, box + 1),
            boxes,
            max(half - box, 0) + max(box + 1 - half, 0),
        )[first]
        for box in range(boxes)
    ]
    sizes = [min(most_sources, 3 if most_sources < 7 else 4) for most_sources in possible]
    for box in range(boxes):
        part = group(box, 0, sizes[box])
        if begun:
            total_ref[box, 0] += part[:, :rhs]
            total_ref[box, 1] += part[:, rhs:]
        else:
            total_ref[box, 0] = part[:, :rhs]
            total_ref[box, 1] = part[:, rhs:]
    for box in range(boxes):

        def more(index, carry, box=box):
            part = group(box, sizes[box] + GROUP * index, GROUP)
            total_ref[box, 0] += part[:, :rhs]
            total_ref[box, 1] += part[:, rhs:]
            return carry

        rest = starts[box + 1] - starts[box] - sizes[box]
        lax.fori_loop(0, (jnp.maximum(rest, 0) + GROUP - 1) // GROUP, more, 0)
        if out_copies:
            out_copies[box].start()
    for copy in out_copies + kept_copies:
        copy.wait()


def near_slots(ids, used, rank):
    boxes, slots = ids.shape
    total = boxes * slots
    source = ids - (rank - 1) * boxes
    source = jnp.where(jnp.arange(slots) < used[:, None], source, -1).reshape(-1)
    half = boxes // 2
    side, inside = source // boxes, source % boxes
    near = ((side == 0) & (inside >= half)) | ((side == 2) & (inside < half))
    far = ((side == 0) & (inside < half)) | ((side == 2) & (inside >= half))
    wanted = (source >= 0) & jnp.stack([near, side == 1, far])
    inside = jnp.where(near, (inside + half) % boxes, inside)
    earlier = jnp.arange(total)[None, :] < jnp.arange(total)[:, None]
    place = jnp.sum((wanted[:, None, :] & earlier).astype(jnp.int32), axis=2)
    code = jnp.arange(total) * boxes + inside
    chosen = wanted[:, None, :] & (place[:, None, :] == jnp.arange(total)[:, None])
    listed = jnp.sum(jnp.where(chosen, code, 0), axis=2)
    before = jnp.arange(total) // slots < jnp.arange(boxes + 1)[:, None]
    starts = jnp.sum((wanted[:, None, :] & before).astype(jnp.int32), axis=2)
    return listed.astype(jnp.int32), starts.astype(jnp.int32)


def near_field(listed, starts, blocks, sources, first, before=None, keep=()):
    boxes, slots, _, basis, _ = blocks.shape
    blocks = blocks.reshape(boxes * slots, *blocks.shape[2:])
    rhs = sources[0].shape[3]
    begun, kept = before is not None, len(keep)
    hbm = pl.BlockSpec(memory_space=pltpu.HBM)
    smem = pl.BlockSpec(memory_space=pltpu.SMEM)
    vmem = pl.BlockSpec(memory_space=pltpu.VMEM)
    shape = (boxes, 2, basis, rhs)
    scratch = [
        pltpu.VMEM(blocks.shape, BF16),
        pltpu.VMEM(shape, BF16),
        pltpu.VMEM((boxes, 2 * basis, 2 * rhs), BF16),
        pltpu.VMEM(shape, F32),
        pltpu.SemaphoreType.DMA((boxes * slots + 3 * boxes + kept,)),
    ]
    kernel = functools.partial(near_kernel, first, begun, kept)
    if kept:
        del scratch[3]
        inner = kernel

        def kernel(*refs):
            place = 3 + len(sources) + begun + kept
            inner(*refs[:-1], refs[place], refs[-1])

    return pl.pallas_call(
        kernel,
        in_specs=[smem] * 2
        + [hbm]
        + [pl.BlockSpec(memory_space=pl.ANY)] * len(sources)
        + [hbm] * (begun + kept),
        out_specs=[vmem] * (1 + kept) if kept else hbm,
        out_shape=[
            pltpu.VMEM(shape, F32),
            *[pltpu.VMEM(array.shape, array.dtype) for array in keep],
        ]
        if kept
        else pltpu.HBM(shape, F32),
        scratch_shapes=scratch,
        compiler_params=pltpu.CompilerParams(vmem_limit_bytes=32 * MIB),
        cost_estimate=pl.CostEstimate(
            flops=10**6 if first == 1 else 10**11, bytes_accessed=2**10, transcendentals=0
        ),
        name=("near_nearer", "near_own", "near_farther")[first],
    )(
        listed,
        starts,
        *in_hbm(blocks),
        *(sources if first != 1 else in_hbm(*sources)),
        *in_hbm(*([before] if begun else []), *keep),
    )


def adjoint_kernel(rad_ref, out_hbm, held):
    for box in range(rad_ref.shape[0]):
        held[box] = side_by_side(rad_ref[box, 0].T, rad_ref[box, 1].T)
    pltpu.sync_copy(held, out_hbm)


def adjoint(radiation):
    boxes, _, points, basis = radiation.shape
    return pl.pallas_call(
        adjoint_kernel,
        in_specs=[pl.BlockSpec(memory_space=pltpu.VMEM)],
        out_specs=pl.BlockSpec(memory_space=pltpu.HBM),
        scratch_shapes=[pltpu.VMEM((boxes, basis, 2 * points), BF16)],
        out_shape=pltpu.HBM((boxes, basis, 2 * points), BF16),
        cost_estimate=pl.CostEstimate(
            flops=10**6, bytes_accessed=2**10, transcendentals=0
        ),
        name="adjoint",
    )(radiation)


def down_kernel(near_ref, w_ref, adjoint_ref, field_ref, out_hbm, field, held, sems):
    boxes, _, width = adjoint_ref.shape
    points = width // 2
    rhs = held.shape[3]
    field_copy = pltpu.make_async_copy(field_ref, field, sems.at[boxes])
    field_copy.start()
    out_copies = [
        pltpu.make_async_copy(held.at[box], out_hbm.at[box], sems.at[box]) for box in range(boxes)
    ]
    field_copy.wait()
    mixed = dot(w_ref[...], field[...].reshape(w_ref.shape[1], 2 * rhs))
    for octant in range(boxes // 2):
        start = 2 * octant * points
        cos_part = mixed[start : start + points]
        sin_part = mixed[start + points : start + 2 * points]
        cos_re, cos_im = cos_part[:, :rhs], cos_part[:, rhs:]
        sin_re, sin_im = sin_part[:, :rhs], sin_part[:, rhs:]
        leaves = (
            (octant, cos_re + sin_im, cos_im - sin_re),
            (boxes - 1 - octant, cos_re - sin_im, cos_im + sin_re),
        )
        for box, real, imag in leaves:
            real, imag = real.astype(BF16), imag.astype(BF16)
            right = jnp.concatenate([side_by_side(real, imag), side_by_side(imag, -real)], axis=0)
            far = dot(adjoint_ref[box], right)
            held[box, 0] = near_ref[box, 0] + far[:, :rhs]
            held[box, 1] = near_ref[box, 1] + far[:, rhs:]
            out_copies[box].start()
    for copy in out_copies:
        copy.wait()


def downward(field, near, weights, radiation_adjoint):
    boxes = near.shape[0]
    ready = [
        pltpu.with_memory_space_constraint(array, pltpu.VMEM)
        for array in (near, weights, radiation_adjoint)
    ]
    return pl.pallas_call(
        down_kernel,
        in_specs=[pl.BlockSpec(memory_space=pltpu.VMEM)] * 3
        + [pl.BlockSpec(memory_space=pl.ANY)],
        out_specs=pl.BlockSpec(memory_space=pltpu.HBM),
        out_shape=jax.ShapeDtypeStruct(near.shape, F32),
        scratch_shapes=[
            pltpu.VMEM(field.shape, BF16),
            pltpu.VMEM(near.shape, F32),
            pltpu.SemaphoreType.DMA((boxes + 1,)),
        ],
        compiler_params=pltpu.CompilerParams(vmem_limit_bytes=32 * MIB),
        cost_estimate=pl.CostEstimate(
            flops=10**6, bytes_accessed=2**10, transcendentals=0
        ),
        name="downward",
    )(*ready, field)


def shift(block, axis, step):
    count = lax.axis_size(axis)
    pairs = [(i, i + step) for i in range(count) if 0 <= i + step < count]
    return lax.ppermute(block, axis, pairs)


def lists_of(partners, vector_ids, pair_count):
    used = jnp.arange(partners.shape[1])[None, :] < pair_count[:, None]
    names = jnp.where(used, partners, NOWHERE)
    return jnp.stack([names, vector_ids], axis=2).reshape(-1, 2)


def parent_bands(spread, shares):
    axes = ("box", "theta", "phi") if shares == lax.axis_size("box") else ("theta", "phi")
    return lax.all_to_all(spread, axes, split_axis=0, concat_axis=0, tiled=True)


def translation_lines(lists, translation, shares, per_group):
    operator_total, _, theta_band, phi_band = translation.shape
    rank = lax.axis_index("box")
    if shares < lax.axis_size("box"):
        table = translation.reshape(operator_total, -1)
        base = ((rank - 1) * per_group).astype(jnp.int32).reshape(1)
        return couplings(lists, base, table, per_group, 3 * per_group)
    if shares == 2:
        other = lax.ppermute(lists, "box", [(0, 1), (1, 0)])
        lists = jnp.where(
            rank == 0, jnp.concatenate([lists, other]), jnp.concatenate([other, lists])
        )
    part = theta_band // shares
    table = lax.dynamic_slice_in_dim(translation, rank * part, part, axis=2)
    table = table.reshape(operator_total, -1)
    total = shares * per_group
    return couplings(lists, jnp.zeros((1,), jnp.int32), table, total, total)


def per_device(
    shares,
    up_weights,
    down_weights,
    coeffs,
    near_blocks,
    near_ids,
    near_count,
    radiation,
    partners,
    vector_ids,
    pair_count,
    translation,
):
    every = ("box", "theta", "phi")
    per_group = lax.axis_size("theta") * lax.axis_size("phi")
    half = coeffs.shape[0] // 2
    front, back = coeffs[:half], coeffs[half:]
    nearer = (shift(back, every, 1), shift(front, every, -1))
    spread = upward(coeffs, radiation, up_weights, shares * per_group)
    radiation_adjoint = adjoint(radiation)
    lists = lists_of(partners, vector_ids, pair_count)
    spread, lists = lax.optimization_barrier((spread, lists))
    lines = translation_lines(lists, translation, shares, per_group)
    listed, starts = near_slots(near_ids, near_count, lax.axis_index(every))
    spread, lines, radiation_adjoint, listed, starts = lax.optimization_barrier(
        (spread, lines, radiation_adjoint, listed, starts)
    )
    parents = parent_bands(spread, shares)
    near = near_field(listed, starts, near_blocks, nearer, 0)
    near, front, back = lax.optimization_barrier((near, front, back))
    farther = (shift(front, every, 1), shift(back, every, -1))
    parents, near = lax.optimization_barrier((parents, near))
    sources = [parents]
    if shares < lax.axis_size("box"):
        sources = [shift(parents, "box", 1), parents, shift(parents, "box", -1)]
    incoming = translate(lines, sources)
    incoming, near = lax.optimization_barrier((incoming, near))
    field = parent_bands(incoming, shares)
    near = near_field(listed, starts, near_blocks, (coeffs,), 1, near)
    ready = near_field(
        listed, starts, near_blocks, farther, 2, near, keep=(down_weights, radiation_adjoint)
    )
    return downward(field, *ready)


def solution(mesh):
    box_size, theta_size, phi_size = (mesh.shape[axis] for axis in ("box", "theta", "phi"))
    shares = box_size if box_size <= 2 and TU // theta_size % box_size == 0 else 1
    up_weights, down_weights = operators(shares, theta_size, phi_size)
    in_specs = (
        P(),
        P(),
        P(("box", "theta", "phi"), None, None, None),
        P(("box", "theta", "phi"), None, None, None, None),
        P(("box", "theta", "phi"), None),
        P(("box", "theta", "phi")),
        P(("box", "theta", "phi"), None, None, None),
        P("box", None),
        P("box", None),
        P("box"),
        P(None, None, "theta", "phi"),
    )
    out_specs = P(("box", "theta", "phi"), None, None, None)
    mapped = jax.shard_map(
        functools.partial(per_device, shares),
        mesh=mesh,
        in_specs=in_specs,
        out_specs=out_specs,
        check_vma=False,
    )

    def product(*arrays):
        return mapped(jnp.asarray(up_weights), jnp.asarray(down_weights), *arrays)

    return product
```

```python
import functools
import math

import jax
import jax.numpy as jnp
import ml_dtypes
import numpy as np
from jax import lax
from jax.experimental import pallas as pl
from jax.experimental.pallas import tpu as pltpu
from jax.sharding import PartitionSpec as P

TL = 8
PL = 16
TU = 16
PU = 32

WEIGHT_UP = (-0.0546875, 0.8203125, 0.2734375, -0.0390625)
WEIGHT_DOWN = (-0.0390625, 0.2734375, 0.8203125, -0.0546875)
PHASE_SCALE = 1.3

F32 = jnp.float32
BF16 = jnp.bfloat16
MIB = 2**20
GROUP = 2
NOWHERE = -(2**20)


def lagrange(rows, columns, wrap):
    matrix = np.zeros((rows, columns))
    for row in range(rows):
        weights = WEIGHT_UP if row % 2 else WEIGHT_DOWN
        for order in range(4):
            node = row // 2 + row % 2 - 2 + order
            node = node % columns if wrap else min(max(node, 0), columns - 1)
            matrix[row, node] += weights[order]
    return matrix


def split_weights(matrix):
    high = matrix.astype(ml_dtypes.bfloat16)
    low = (matrix - high.astype(np.float64)).astype(ml_dtypes.bfloat16)
    return high, low


def operators(shares, theta_size, phi_size):
    theta_part = TU // theta_size // shares
    order = np.arange(TU * PU).reshape(theta_size, shares, theta_part, phi_size, PU // phi_size)
    order = order.transpose(1, 0, 3, 2, 4).reshape(-1)
    interp = np.kron(lagrange(TU, TL, False), lagrange(PU, PL, True))
    theta = math.pi * (np.arange(TU) + 0.5) / TU
    azimuth = 2.0 * math.pi * (np.arange(PU) + 0.5) / PU
    up, down = [], []
    for octant in range(4):
        sign_x = 2 * (octant % 2) - 1
        sign_y = 2 * (octant // 2 % 2) - 1
        sign_z = 2 * (octant // 4) - 1
        angle = PHASE_SCALE * (
            sign_x * np.sin(theta)[:, None] * np.cos(azimuth)[None]
            + sign_y * np.sin(theta)[:, None] * np.sin(azimuth)[None]
            + sign_z * np.cos(theta)[:, None]
        ).reshape(-1, 1)
        cos_high, cos_low = split_weights((np.cos(angle) * interp)[order])
        sin_high, sin_low = split_weights((np.sin(angle) * interp)[order])
        high = np.concatenate([cos_high, sin_high], axis=1)
        low = np.concatenate([cos_low, sin_low], axis=1)
        up.append(np.concatenate([high, low], axis=0))
        down += [cos_high.T, sin_high.T]
    return np.concatenate(up, axis=1), np.concatenate(down, axis=0)


def in_hbm(*arrays):
    return [pltpu.with_memory_space_constraint(array, pltpu.HBM) for array in arrays]


def dot(a, b):
    return jnp.dot(a, b, preferred_element_type=F32)


def side_by_side(real, imag):
    return jnp.concatenate([real, imag], axis=1)


def complex_columns(real, imag):
    return jnp.concatenate([side_by_side(real, imag), side_by_side(-imag, real)], axis=0)


def up_kernel(x_hbm, rad_hbm, w_hbm, out_hbm, x_ref, rad_ref, w_ref, right, result, sems):
    boxes, _, _, rhs = x_ref.shape
    points = rad_ref.shape[2]
    copies = [
        pltpu.make_async_copy(source, target, sems.at[place])
        for place, (source, target) in enumerate(
            ((x_hbm, x_ref), (rad_hbm, rad_ref), (w_hbm, w_ref))
        )
    ]
    for copy in copies:
        copy.start()
    copies[0].wait()
    copies[1].wait()
    half = boxes // 2
    for octant in range(boxes):
        left = side_by_side(rad_ref[octant, 0], rad_ref[octant, 1])
        straight = dot(left, complex_columns(x_ref[octant, 0], x_ref[octant, 1])).astype(BF16)
        real, imag = straight[:, :rhs], straight[:, rhs:]
        if octant < half:
            swapped = side_by_side(-imag, real)
        else:
            swapped = side_by_side(imag, -real)
        place = octant if octant < half else boxes - 1 - octant
        start = 2 * place * points
        right[octant // half, start : start + points] = straight
        right[octant // half, start + points : start + 2 * points] = swapped
    copies[2].wait()
    total = dot(w_ref[...], right[0]) + dot(w_ref[...], right[1])
    samples = total.shape[0] // 2
    total = total[:samples] + total[samples:]
    result[...] = total.astype(BF16).reshape(result.shape)
    pltpu.sync_copy(result, out_hbm)


def upward(coeffs, radiation, weights, groups):
    boxes, _, basis, rhs = coeffs.shape
    rows, columns = weights.shape
    samples = rows // 2
    hbm = pl.BlockSpec(memory_space=pltpu.HBM)
    return pl.pallas_call(
        up_kernel,
        in_specs=[hbm] * 3,
        out_specs=hbm,
        out_shape=pltpu.HBM((groups, samples // groups, 2 * rhs), BF16),
        scratch_shapes=[
            pltpu.VMEM(coeffs.shape, BF16),
            pltpu.VMEM(radiation.shape, BF16),
            pltpu.VMEM(weights.shape, BF16),
            pltpu.VMEM((2, columns, 2 * rhs), BF16),
            pltpu.VMEM((groups, samples // groups, 2 * rhs), BF16),
            pltpu.SemaphoreType.DMA((3,)),
        ],
        compiler_params=pltpu.CompilerParams(vmem_limit_bytes=32 * MIB),
        cost_estimate=pl.CostEstimate(
            flops=10**6, bytes_accessed=2**10, transcendentals=0
        ),
        name="upward",
    )(*in_hbm(coeffs, radiation, weights))


def coupling_kernel(lists_ref, base_ref, table_ref, out_ref):
    rows = lists_ref.shape[0]
    samples = table_ref.shape[1] // 2
    _, targets, columns = out_ref.shape
    slots = rows // targets
    selector = (
        lax.broadcasted_iota(jnp.int32, (rows, table_ref.shape[0]), 1) == lists_ref[:, 1:2]
    )
    chosen = dot(selector.astype(BF16), table_ref[...]).astype(BF16)
    wide = lax.broadcasted_iota(jnp.int32, (rows, columns), 1) // samples
    match = wide + base_ref[0] == lists_ref[:, 0:1]
    spread = lax.broadcasted_iota(jnp.int32, (samples, columns), 0) == (
        lax.broadcasted_iota(jnp.int32, (samples, columns), 1) % samples
    )
    gather = (
        lax.broadcasted_iota(jnp.int32, (targets, rows), 1) // slots
        == lax.broadcasted_iota(jnp.int32, (targets, rows), 0)
    ).astype(BF16)
    tile = spread.astype(BF16)
    for part in range(2):
        lines = dot(chosen[:, part * samples : (part + 1) * samples], tile)
        out_ref[part] = dot(gather, jnp.where(match, lines, 0.0).astype(BF16))


def couplings(lists, base, table, targets, names):
    shape = (2, targets, names * (table.shape[1] // 2))
    vmem = pl.BlockSpec(memory_space=pltpu.VMEM)
    return pl.pallas_call(
        coupling_kernel,
        in_specs=[vmem, pl.BlockSpec(memory_space=pltpu.SMEM), vmem],
        out_specs=vmem,
        out_shape=jax.ShapeDtypeStruct(shape, F32),
        compiler_params=pltpu.CompilerParams(vmem_limit_bytes=16 * MIB),
        cost_estimate=pl.CostEstimate(
            flops=2 * 10**8, bytes_accessed=2 * 2**20, transcendentals=0
        ),
        name="coupling",
    )(lists, base, table)


def translate_kernel(lines_hbm, *refs):
    count = (len(refs) - 5) // 2
    sources, out_hbm = refs[:count], refs[count]
    held, lines, matrix, result, sems = refs[count + 1 :][:count], *refs[2 * count + 1 :]
    targets, samples, width = result.shape
    rhs = width // 2
    copies = [
        pltpu.make_async_copy(source, target, sems.at[place])
        for place, (source, target) in enumerate(zip((lines_hbm, *sources), (lines, *held)))
    ]
    for copy in copies:
        copy.start()
    copies[0].wait()
    columns = matrix.shape[1]
    row = lax.broadcasted_iota(jnp.int32, (samples, columns), 0)
    diagonal = row == lax.broadcasted_iota(jnp.int32, (samples, columns), 1) % samples
    for part in range(2):
        for target in range(targets):
            line = jnp.broadcast_to(lines[part, target : target + 1], diagonal.shape)
            start = (part * targets + target) * samples
            matrix[start : start + samples] = jnp.where(diagonal, line, 0.0).astype(BF16)
    total = None
    start = 0
    for place, source in enumerate(held):
        copies[1 + place].wait()
        stop = start + source.shape[0] * samples
        part = dot(matrix[:, start:stop], source[...].reshape(stop - start, width))
        total = part if total is None else total + part
        start = stop
    half = targets * samples
    real = total[:half, :rhs] - total[half:, rhs:]
    imag = total[:half, rhs:] + total[half:, :rhs]
    result[...] = jnp.concatenate([real, imag], axis=1).astype(BF16).reshape(result.shape)
    pltpu.sync_copy(result, out_hbm)


def translate(lines, sources):
    _, samples, width = sources[0].shape
    _, targets, columns = lines.shape
    shape = (targets, samples, width)
    hbm = pl.BlockSpec(memory_space=pltpu.HBM)
    anywhere = pl.BlockSpec(memory_space=pl.ANY)
    return pl.pallas_call(
        translate_kernel,
        in_specs=[hbm] + [anywhere] * len(sources),
        out_specs=hbm,
        out_shape=pltpu.HBM(shape, BF16),
        scratch_shapes=[
            *[pltpu.VMEM(source.shape, BF16) for source in sources],
            pltpu.VMEM(lines.shape, F32),
            pltpu.VMEM((2 * targets * samples, columns), BF16),
            pltpu.VMEM(shape, BF16),
            pltpu.SemaphoreType.DMA((1 + len(sources),)),
        ],
        compiler_params=pltpu.CompilerParams(vmem_limit_bytes=24 * MIB),
        cost_estimate=pl.CostEstimate(
            flops=10**6, bytes_accessed=2**10, transcendentals=0
        ),
        name="translate",
    )(*in_hbm(lines), *sources)


def near_kernel(first, begun, kept, *refs):
    count = 1 if first == 1 else 2
    listed, starts_ref, blocks_hbm = refs[:3]
    source_refs, refs = refs[3 : 3 + count], refs[3 + count :]
    before_hbm = refs[0] if begun else None
    kept_hbm = refs[begun : begun + kept]
    out_ref = refs[begun + kept]
    kept_refs = refs[1 + begun + kept : 1 + begun + 2 * kept]
    blocks, held, wide, total_ref, sems = refs[1 + begun + 2 * kept :]
    boxes, _, basis, rhs = held.shape
    most = blocks_hbm.shape[0]
    starts = [starts_ref[first, box] for box in range(boxes + 1)]

    def by_box(source, target, turn):
        return [
            pltpu.make_async_copy(
                source.at[box], target.at[box], sems.at[most + turn * boxes + box]
            )
            for box in range(boxes)
        ]

    part = boxes // count
    source_copies = [
        pltpu.make_async_copy(
            source_refs[box // part].at[box % part], held.at[box], sems.at[most + box]
        )
        for box in range(boxes)
    ]
    before_copies = by_box(before_hbm, total_ref, 1) if begun else []
    out_copies = [] if kept else by_box(total_ref, out_ref, 2)
    kept_copies = [
        pltpu.make_async_copy(kept_hbm[place], kept_refs[place], sems.at[most + 3 * boxes + place])
        for place in range(kept)
    ]
    for copy in source_copies:
        copy.start()

    def block_copy(place):
        block = listed[first, place] // boxes
        return pltpu.make_async_copy(blocks_hbm.at[block], blocks.at[place], sems.at[place])

    def fetch(place, carry):
        block_copy(place).start()
        return carry

    lax.fori_loop(0, starts[boxes], fetch, 0)
    for copy in before_copies + kept_copies:
        copy.start()
    for copy in source_copies:
        copy.wait()
    for place in range(boxes):
        wide[place] = complex_columns(held[place, 0], held[place, 1])

    def landed(place, carry):
        block_copy(place).wait()
        return carry

    lax.fori_loop(0, starts[boxes], landed, 0)
    for copy in before_copies:
        copy.wait()

    def group(box, begin, size):
        left, right = [], []
        for step in range(size):
            place = starts[box] + begin + step
            valid = place < starts[box + 1]
            place = jnp.where(valid, place, 0)
            real, imag = blocks[place, 0], blocks[place, 1]
            real = jnp.where(valid, real, jnp.zeros_like(real))
            imag = jnp.where(valid, imag, jnp.zeros_like(imag))
            left.append(side_by_side(real, imag))
            right.append(wide[jnp.where(valid, listed[first, place] % boxes, 0)])
        return dot(jnp.concatenate(left, axis=1), jnp.concatenate(right, axis=0))

    half = boxes // 2
    possible = [
        (
            min(half, boxes - box) + min(half, box + 1),
            boxes,
            max(half - box, 0) + max(box + 1 - half, 0),
        )[first]
        for box in range(boxes)
    ]
    sizes = [min(most_sources, 3 if most_sources < 7 else 4) for most_sources in possible]
    for box in range(boxes):
        part = group(box, 0, sizes[box])
        if begun:
            total_ref[box, 0] += part[:, :rhs]
            total_ref[box, 1] += part[:, rhs:]
        else:
            total_ref[box, 0] = part[:, :rhs]
            total_ref[box, 1] = part[:, rhs:]
    for box in range(boxes):

        def more(index, carry, box=box):
            part = group(box, sizes[box] + GROUP * index, GROUP)
            total_ref[box, 0] += part[:, :rhs]
            total_ref[box, 1] += part[:, rhs:]
            return carry

        rest = starts[box + 1] - starts[box] - sizes[box]
        lax.fori_loop(0, (jnp.maximum(rest, 0) + GROUP - 1) // GROUP, more, 0)
        if out_copies:
            out_copies[box].start()
    for copy in out_copies + kept_copies:
        copy.wait()


def near_slots(ids, used, rank):
    boxes, slots = ids.shape
    total = boxes * slots
    source = ids - (rank - 1) * boxes
    source = jnp.where(jnp.arange(slots) < used[:, None], source, -1).reshape(-1)
    half = boxes // 2
    side, inside = source // boxes, source % boxes
    near = ((side == 0) & (inside >= half)) | ((side == 2) & (inside < half))
    far = ((side == 0) & (inside < half)) | ((side == 2) & (inside >= half))
    wanted = (source >= 0) & jnp.stack([near, side == 1, far])
    inside = jnp.where(near, (inside + half) % boxes, inside)
    earlier = jnp.arange(total)[None, :] < jnp.arange(total)[:, None]
    place = jnp.sum((wanted[:, None, :] & earlier).astype(jnp.int32), axis=2)
    code = jnp.arange(total) * boxes + inside
    chosen = wanted[:, None, :] & (place[:, None, :] == jnp.arange(total)[:, None])
    listed = jnp.sum(jnp.where(chosen, code, 0), axis=2)
    before = jnp.arange(total) // slots < jnp.arange(boxes + 1)[:, None]
    starts = jnp.sum((wanted[:, None, :] & before).astype(jnp.int32), axis=2)
    return listed.astype(jnp.int32), starts.astype(jnp.int32)


def near_field(listed, starts, blocks, sources, first, before=None, keep=()):
    boxes, slots, _, basis, _ = blocks.shape
    blocks = blocks.reshape(boxes * slots, *blocks.shape[2:])
    rhs = sources[0].shape[3]
    begun, kept = before is not None, len(keep)
    hbm = pl.BlockSpec(memory_space=pltpu.HBM)
    smem = pl.BlockSpec(memory_space=pltpu.SMEM)
    vmem = pl.BlockSpec(memory_space=pltpu.VMEM)
    shape = (boxes, 2, basis, rhs)
    scratch = [
        pltpu.VMEM(blocks.shape, BF16),
        pltpu.VMEM(shape, BF16),
        pltpu.VMEM((boxes, 2 * basis, 2 * rhs), BF16),
        pltpu.VMEM(shape, F32),
        pltpu.SemaphoreType.DMA((boxes * slots + 3 * boxes + kept,)),
    ]
    kernel = functools.partial(near_kernel, first, begun, kept)
    if kept:
        del scratch[3]
        inner = kernel

        def kernel(*refs):
            place = 3 + len(sources) + begun + kept
            inner(*refs[:-1], refs[place], refs[-1])

    return pl.pallas_call(
        kernel,
        in_specs=[smem] * 2
        + [hbm]
        + [pl.BlockSpec(memory_space=pl.ANY)] * len(sources)
        + [hbm] * (begun + kept),
        out_specs=[vmem] * (1 + kept) if kept else hbm,
        out_shape=[
            pltpu.VMEM(shape, F32),
            *[pltpu.VMEM(array.shape, array.dtype) for array in keep],
        ]
        if kept
        else pltpu.HBM(shape, F32),
        scratch_shapes=scratch,
        compiler_params=pltpu.CompilerParams(vmem_limit_bytes=32 * MIB),
        cost_estimate=pl.CostEstimate(
            flops=10**6 if first == 1 else 10**11, bytes_accessed=2**10, transcendentals=0
        ),
        name=("near_nearer", "near_own", "near_farther")[first],
    )(
        listed,
        starts,
        *in_hbm(blocks),
        *(sources if first != 1 else in_hbm(*sources)),
        *in_hbm(*([before] if begun else []), *keep),
    )


def adjoint_kernel(rad_ref, out_hbm, held):
    for box in range(rad_ref.shape[0]):
        held[box] = side_by_side(rad_ref[box, 0].T, rad_ref[box, 1].T)
    pltpu.sync_copy(held, out_hbm)


def adjoint(radiation):
    boxes, _, points, basis = radiation.shape
    return pl.pallas_call(
        adjoint_kernel,
        in_specs=[pl.BlockSpec(memory_space=pltpu.VMEM)],
        out_specs=pl.BlockSpec(memory_space=pltpu.HBM),
        scratch_shapes=[pltpu.VMEM((boxes, basis, 2 * points), BF16)],
        out_shape=pltpu.HBM((boxes, basis, 2 * points), BF16),
        cost_estimate=pl.CostEstimate(
            flops=10**6, bytes_accessed=2**10, transcendentals=0
        ),
        name="adjoint",
    )(radiation)


def down_kernel(w_hbm, adjoint_hbm, near_hbm, field_ref, out_hbm, *scratch):
    w_ref, adjoint_ref, field, held, sems = scratch
    boxes, _, width = adjoint_ref.shape
    points = width // 2
    rhs = held.shape[3]
    rows = w_ref.shape[0] // boxes

    def by_box(source, target, turn):
        return [
            pltpu.make_async_copy(source(box), target(box), sems.at[turn * boxes + box])
            for box in range(boxes)
        ]

    w_copies = by_box(
        lambda box: w_hbm.at[pl.ds(box * rows, rows)],
        lambda box: w_ref.at[pl.ds(box * rows, rows)],
        0,
    )
    adjoint_copies = by_box(lambda box: adjoint_hbm.at[box], lambda box: adjoint_ref.at[box], 1)
    near_copies = by_box(lambda box: near_hbm.at[box], lambda box: held.at[box], 2)
    out_copies = by_box(lambda box: held.at[box], lambda box: out_hbm.at[box], 3)
    field_copy = pltpu.make_async_copy(field_ref, field, sems.at[4 * boxes])
    field_copy.start()
    for copy in w_copies + adjoint_copies + near_copies:
        copy.start()
    field_copy.wait()
    for copy in w_copies:
        copy.wait()
    mixed = dot(w_ref[...], field[...].reshape(w_ref.shape[1], 2 * rhs))
    for copy in adjoint_copies + near_copies:
        copy.wait()
    for octant in range(boxes // 2):
        start = 2 * octant * points
        cos_part = mixed[start : start + points]
        sin_part = mixed[start + points : start + 2 * points]
        cos_re, cos_im = cos_part[:, :rhs], cos_part[:, rhs:]
        sin_re, sin_im = sin_part[:, :rhs], sin_part[:, rhs:]
        leaves = (
            (octant, cos_re + sin_im, cos_im - sin_re),
            (boxes - 1 - octant, cos_re - sin_im, cos_im + sin_re),
        )
        for box, real, imag in leaves:
            real, imag = real.astype(BF16), imag.astype(BF16)
            right = jnp.concatenate([side_by_side(real, imag), side_by_side(imag, -real)], axis=0)
            far = dot(adjoint_ref[box], right)
            held[box, 0] += far[:, :rhs]
            held[box, 1] += far[:, rhs:]
            out_copies[box].start()
    for copy in out_copies:
        copy.wait()


def downward(field, near, weights, radiation_adjoint):
    boxes = near.shape[0]
    hbm = pl.BlockSpec(memory_space=pltpu.HBM)
    return pl.pallas_call(
        down_kernel,
        in_specs=[hbm] * 3 + [pl.BlockSpec(memory_space=pl.ANY)],
        out_specs=hbm,
        out_shape=jax.ShapeDtypeStruct(near.shape, F32),
        scratch_shapes=[
            pltpu.VMEM(weights.shape, BF16),
            pltpu.VMEM(radiation_adjoint.shape, BF16),
            pltpu.VMEM(field.shape, BF16),
            pltpu.VMEM(near.shape, F32),
            pltpu.SemaphoreType.DMA((4 * boxes + 1,)),
        ],
        compiler_params=pltpu.CompilerParams(vmem_limit_bytes=32 * MIB),
        cost_estimate=pl.CostEstimate(
            flops=10**6, bytes_accessed=2**10, transcendentals=0
        ),
        name="downward",
    )(*in_hbm(weights, radiation_adjoint, near), field)


def shift(block, axis, step):
    count = lax.axis_size(axis)
    pairs = [(i, i + step) for i in range(count) if 0 <= i + step < count]
    return lax.ppermute(block, axis, pairs)


def lists_of(partners, vector_ids, pair_count):
    used = jnp.arange(partners.shape[1])[None, :] < pair_count[:, None]
    names = jnp.where(used, partners, NOWHERE)
    return jnp.stack([names, vector_ids], axis=2).reshape(-1, 2)


def parent_bands(spread, shares):
    axes = ("box", "theta", "phi") if shares == lax.axis_size("box") else ("theta", "phi")
    return lax.all_to_all(spread, axes, split_axis=0, concat_axis=0, tiled=True)


def translation_lines(lists, translation, shares, per_group):
    operator_total, _, theta_band, phi_band = translation.shape
    rank = lax.axis_index("box")
    if shares < lax.axis_size("box"):
        table = translation.reshape(operator_total, -1)
        base = ((rank - 1) * per_group).astype(jnp.int32).reshape(1)
        return couplings(lists, base, table, per_group, 3 * per_group)
    if shares == 2:
        other = lax.ppermute(lists, "box", [(0, 1), (1, 0)])
        lists = jnp.where(
            rank == 0, jnp.concatenate([lists, other]), jnp.concatenate([other, lists])
        )
    part = theta_band // shares
    table = lax.dynamic_slice_in_dim(translation, rank * part, part, axis=2)
    table = table.reshape(operator_total, -1)
    total = shares * per_group
    return couplings(lists, jnp.zeros((1,), jnp.int32), table, total, total)


def per_device(
    shares,
    up_weights,
    down_weights,
    coeffs,
    near_blocks,
    near_ids,
    near_count,
    radiation,
    partners,
    vector_ids,
    pair_count,
    translation,
):
    every = ("box", "theta", "phi")
    per_group = lax.axis_size("theta") * lax.axis_size("phi")
    half = coeffs.shape[0] // 2
    front, back = coeffs[:half], coeffs[half:]
    nearer = (shift(back, every, 1), shift(front, every, -1))
    spread = upward(coeffs, radiation, up_weights, shares * per_group)
    radiation_adjoint = adjoint(radiation)
    spread, radiation_adjoint = lax.optimization_barrier((spread, radiation_adjoint))
    parents = parent_bands(spread, shares)
    lists = lists_of(partners, vector_ids, pair_count)
    lines = translation_lines(lists, translation, shares, per_group)
    listed, starts = near_slots(near_ids, near_count, lax.axis_index(every))
    lines, listed, starts = lax.optimization_barrier((lines, listed, starts))
    near = near_field(listed, starts, near_blocks, nearer, 0)
    near, front, back = lax.optimization_barrier((near, front, back))
    farther = (shift(front, every, 1), shift(back, every, -1))
    parents, near = lax.optimization_barrier((parents, near))
    sources = [parents]
    if shares < lax.axis_size("box"):
        sources = [shift(parents, "box", 1), parents, shift(parents, "box", -1)]
    incoming = translate(lines, sources)
    incoming, near = lax.optimization_barrier((incoming, near))
    field = parent_bands(incoming, shares)
    near = near_field(listed, starts, near_blocks, (coeffs,), 1, near)
    near = near_field(listed, starts, near_blocks, farther, 2, near)
    return downward(field, near, down_weights, radiation_adjoint)


def solution(mesh):
    box_size, theta_size, phi_size = (mesh.shape[axis] for axis in ("box", "theta", "phi"))
    shares = box_size if box_size <= 2 and TU // theta_size % box_size == 0 else 1
    up_weights, down_weights = operators(shares, theta_size, phi_size)
    in_specs = (
        P(),
        P(),
        P(("box", "theta", "phi"), None, None, None),
        P(("box", "theta", "phi"), None, None, None, None),
        P(("box", "theta", "phi"), None),
        P(("box", "theta", "phi")),
        P(("box", "theta", "phi"), None, None, None),
        P("box", None),
        P("box", None),
        P("box"),
        P(None, None, "theta", "phi"),
    )
    out_specs = P(("box", "theta", "phi"), None, None, None)
    mapped = jax.shard_map(
        functools.partial(per_device, shares),
        mesh=mesh,
        in_specs=in_specs,
        out_specs=out_specs,
        check_vma=False,
    )

    def product(*arrays):
        return mapped(jnp.asarray(up_weights), jnp.asarray(down_weights), *arrays)

    return product
```

```python
import functools
import math

import jax
import jax.numpy as jnp
import ml_dtypes
import numpy as np
from jax import lax
from jax.experimental import pallas as pl
from jax.experimental.pallas import tpu as pltpu
from jax.sharding import PartitionSpec as P

TL = 8
PL = 16
TU = 16
PU = 32

WEIGHT_UP = (-0.0546875, 0.8203125, 0.2734375, -0.0390625)
WEIGHT_DOWN = (-0.0390625, 0.2734375, 0.8203125, -0.0546875)
PHASE_SCALE = 1.3

F32 = jnp.float32
BF16 = jnp.bfloat16
MIB = 2**20
GROUP = 2
NOWHERE = -(2**20)


def lagrange(rows, columns, wrap):
    matrix = np.zeros((rows, columns))
    for row in range(rows):
        weights = WEIGHT_UP if row % 2 else WEIGHT_DOWN
        for order in range(4):
            node = row // 2 + row % 2 - 2 + order
            node = node % columns if wrap else min(max(node, 0), columns - 1)
            matrix[row, node] += weights[order]
    return matrix


def split_weights(matrix):
    high = matrix.astype(ml_dtypes.bfloat16)
    low = (matrix - high.astype(np.float64)).astype(ml_dtypes.bfloat16)
    return high, low


def operators(shares, theta_size, phi_size):
    theta_part = TU // theta_size // shares
    order = np.arange(TU * PU).reshape(theta_size, shares, theta_part, phi_size, PU // phi_size)
    order = order.transpose(1, 0, 3, 2, 4).reshape(-1)
    interp = np.kron(lagrange(TU, TL, False), lagrange(PU, PL, True))
    theta = math.pi * (np.arange(TU) + 0.5) / TU
    azimuth = 2.0 * math.pi * (np.arange(PU) + 0.5) / PU
    up, down = [], []
    for octant in range(4):
        sign_x = 2 * (octant % 2) - 1
        sign_y = 2 * (octant // 2 % 2) - 1
        sign_z = 2 * (octant // 4) - 1
        angle = PHASE_SCALE * (
            sign_x * np.sin(theta)[:, None] * np.cos(azimuth)[None]
            + sign_y * np.sin(theta)[:, None] * np.sin(azimuth)[None]
            + sign_z * np.cos(theta)[:, None]
        ).reshape(-1, 1)
        cos_high, cos_low = split_weights((np.cos(angle) * interp)[order])
        sin_high, sin_low = split_weights((np.sin(angle) * interp)[order])
        high = np.concatenate([cos_high, sin_high], axis=1)
        low = np.concatenate([cos_low, sin_low], axis=1)
        up.append(np.concatenate([high, low], axis=0))
        down += [cos_high.T, sin_high.T]
    return np.concatenate(up, axis=1), np.concatenate(down, axis=0)


def in_hbm(*arrays):
    return [pltpu.with_memory_space_constraint(array, pltpu.HBM) for array in arrays]


def dot(a, b):
    return jnp.dot(a, b, preferred_element_type=F32)


def side_by_side(real, imag):
    return jnp.concatenate([real, imag], axis=1)


def complex_columns(real, imag):
    return jnp.concatenate([side_by_side(real, imag), side_by_side(-imag, real)], axis=0)


def up_kernel(x_hbm, rad_hbm, w_hbm, out_hbm, x_ref, rad_ref, w_ref, right, result, sems):
    boxes, _, _, rhs = x_ref.shape
    points = rad_ref.shape[2]
    copies = [
        pltpu.make_async_copy(source, target, sems.at[place])
        for place, (source, target) in enumerate(
            ((x_hbm, x_ref), (rad_hbm, rad_ref), (w_hbm, w_ref))
        )
    ]
    for copy in copies:
        copy.start()
    copies[0].wait()
    copies[1].wait()
    half = boxes // 2
    for octant in range(boxes):
        left = side_by_side(rad_ref[octant, 0], rad_ref[octant, 1])
        straight = dot(left, complex_columns(x_ref[octant, 0], x_ref[octant, 1])).astype(BF16)
        real, imag = straight[:, :rhs], straight[:, rhs:]
        if octant < half:
            swapped = side_by_side(-imag, real)
        else:
            swapped = side_by_side(imag, -real)
        place = octant if octant < half else boxes - 1 - octant
        start = 2 * place * points
        right[octant // half, start : start + points] = straight
        right[octant // half, start + points : start + 2 * points] = swapped
    copies[2].wait()
    total = dot(w_ref[...], right[0]) + dot(w_ref[...], right[1])
    samples = total.shape[0] // 2
    total = total[:samples] + total[samples:]
    result[...] = total.astype(BF16).reshape(result.shape)
    pltpu.sync_copy(result, out_hbm)


def upward(coeffs, radiation, weights, groups):
    boxes, _, basis, rhs = coeffs.shape
    rows, columns = weights.shape
    samples = rows // 2
    hbm = pl.BlockSpec(memory_space=pltpu.HBM)
    return pl.pallas_call(
        up_kernel,
        in_specs=[hbm] * 3,
        out_specs=hbm,
        out_shape=pltpu.HBM((groups, samples // groups, 2 * rhs), BF16),
        scratch_shapes=[
            pltpu.VMEM(coeffs.shape, BF16),
            pltpu.VMEM(radiation.shape, BF16),
            pltpu.VMEM(weights.shape, BF16),
            pltpu.VMEM((2, columns, 2 * rhs), BF16),
            pltpu.VMEM((groups, samples // groups, 2 * rhs), BF16),
            pltpu.SemaphoreType.DMA((3,)),
        ],
        compiler_params=pltpu.CompilerParams(vmem_limit_bytes=32 * MIB),
        cost_estimate=pl.CostEstimate(
            flops=2 * 10**9, bytes_accessed=4 * MIB, transcendentals=0
        ),
        name="upward",
    )(*in_hbm(coeffs, radiation, weights))


def coupling_kernel(lists_ref, base_ref, table_ref, out_ref):
    rows = lists_ref.shape[0]
    samples = table_ref.shape[1] // 2
    _, targets, columns = out_ref.shape
    slots = rows // targets
    selector = (
        lax.broadcasted_iota(jnp.int32, (rows, table_ref.shape[0]), 1) == lists_ref[:, 1:2]
    )
    chosen = dot(selector.astype(BF16), table_ref[...]).astype(BF16)
    wide = lax.broadcasted_iota(jnp.int32, (rows, columns), 1) // samples
    match = wide + base_ref[0] == lists_ref[:, 0:1]
    spread = lax.broadcasted_iota(jnp.int32, (samples, columns), 0) == (
        lax.broadcasted_iota(jnp.int32, (samples, columns), 1) % samples
    )
    gather = (
        lax.broadcasted_iota(jnp.int32, (targets, rows), 1) // slots
        == lax.broadcasted_iota(jnp.int32, (targets, rows), 0)
    ).astype(BF16)
    tile = spread.astype(BF16)
    for part in range(2):
        lines = dot(chosen[:, part * samples : (part + 1) * samples], tile)
        out_ref[part] = dot(gather, jnp.where(match, lines, 0.0).astype(BF16))


def couplings(lists, base, table, targets, names):
    shape = (2, targets, names * (table.shape[1] // 2))
    vmem = pl.BlockSpec(memory_space=pltpu.VMEM)
    return pl.pallas_call(
        coupling_kernel,
        in_specs=[vmem, pl.BlockSpec(memory_space=pltpu.SMEM), vmem],
        out_specs=vmem,
        out_shape=jax.ShapeDtypeStruct(shape, F32),
        compiler_params=pltpu.CompilerParams(vmem_limit_bytes=16 * MIB),
        cost_estimate=pl.CostEstimate(
            flops=2 * 10**8, bytes_accessed=2 * 2**20, transcendentals=0
        ),
        name="coupling",
    )(lists, base, table)


def translate_kernel(lines_hbm, *refs):
    count = (len(refs) - 5) // 2
    sources, out_hbm = refs[:count], refs[count]
    held, lines, matrix, result, sems = refs[count + 1 :][:count], *refs[2 * count + 1 :]
    targets, samples, width = result.shape
    rhs = width // 2
    copies = [
        pltpu.make_async_copy(source, target, sems.at[place])
        for place, (source, target) in enumerate(zip((lines_hbm, *sources), (lines, *held)))
    ]
    for copy in copies:
        copy.start()
    copies[0].wait()
    columns = matrix.shape[1]
    row = lax.broadcasted_iota(jnp.int32, (samples, columns), 0)
    diagonal = row == lax.broadcasted_iota(jnp.int32, (samples, columns), 1) % samples
    for part in range(2):
        for target in range(targets):
            line = jnp.broadcast_to(lines[part, target : target + 1], diagonal.shape)
            start = (part * targets + target) * samples
            matrix[start : start + samples] = jnp.where(diagonal, line, 0.0).astype(BF16)
    total = None
    start = 0
    for place, source in enumerate(held):
        copies[1 + place].wait()
        stop = start + source.shape[0] * samples
        part = dot(matrix[:, start:stop], source[...].reshape(stop - start, width))
        total = part if total is None else total + part
        start = stop
    half = targets * samples
    real = total[:half, :rhs] - total[half:, rhs:]
    imag = total[:half, rhs:] + total[half:, :rhs]
    result[...] = jnp.concatenate([real, imag], axis=1).astype(BF16).reshape(result.shape)
    pltpu.sync_copy(result, out_hbm)


def translate(lines, sources):
    _, samples, width = sources[0].shape
    _, targets, columns = lines.shape
    shape = (targets, samples, width)
    hbm = pl.BlockSpec(memory_space=pltpu.HBM)
    anywhere = pl.BlockSpec(memory_space=pl.ANY)
    return pl.pallas_call(
        translate_kernel,
        in_specs=[hbm] + [anywhere] * len(sources),
        out_specs=hbm,
        out_shape=pltpu.HBM(shape, BF16),
        scratch_shapes=[
            *[pltpu.VMEM(source.shape, BF16) for source in sources],
            pltpu.VMEM(lines.shape, F32),
            pltpu.VMEM((2 * targets * samples, columns), BF16),
            pltpu.VMEM(shape, BF16),
            pltpu.SemaphoreType.DMA((1 + len(sources),)),
        ],
        compiler_params=pltpu.CompilerParams(vmem_limit_bytes=24 * MIB),
        cost_estimate=pl.CostEstimate(
            flops=10**9, bytes_accessed=2 * MIB, transcendentals=0
        ),
        name="translate",
    )(*in_hbm(lines), *sources)


def near_kernel(first, begun, kept, *refs):
    refs = list(refs)
    listed, starts_ref, blocks_hbm, source_hbm = refs[:4]
    before_hbm = refs[4] if begun else None
    kept_hbm = refs[4 + begun : 4 + begun + kept]
    out_ref = refs[4 + begun + kept]
    kept_refs = refs[5 + begun + kept : 5 + begun + 2 * kept]
    blocks, held, wide, total_ref, sems = refs[5 + begun + 2 * kept :]
    boxes, _, basis, rhs = held.shape
    most = blocks_hbm.shape[0]
    starts = [starts_ref[first, box] for box in range(boxes + 1)]

    def by_box(source, target, turn):
        return [
            pltpu.make_async_copy(
                source.at[box], target.at[box], sems.at[most + turn * boxes + box]
            )
            for box in range(boxes)
        ]

    source_copies = by_box(source_hbm, held, 0)
    before_copies = by_box(before_hbm, total_ref, 1) if begun else []
    out_copies = [] if kept else by_box(total_ref, out_ref, 2)
    kept_copies = [
        pltpu.make_async_copy(kept_hbm[place], kept_refs[place], sems.at[most + 3 * boxes + place])
        for place in range(kept)
    ]
    for copy in source_copies:
        copy.start()

    def block_copy(place):
        block = listed[first, place] // boxes
        return pltpu.make_async_copy(blocks_hbm.at[block], blocks.at[place], sems.at[place])

    def fetch(place, carry):
        block_copy(place).start()
        return carry

    lax.fori_loop(0, starts[boxes], fetch, 0)
    for copy in before_copies + kept_copies:
        copy.start()
    for copy in source_copies:
        copy.wait()
    for place in range(boxes):
        wide[place] = complex_columns(held[place, 0], held[place, 1])

    def landed(place, carry):
        block_copy(place).wait()
        return carry

    lax.fori_loop(0, starts[boxes], landed, 0)
    for copy in before_copies:
        copy.wait()

    def group(box, begin, size):
        left, right = [], []
        for step in range(size):
            place = starts[box] + begin + step
            valid = place < starts[box + 1]
            place = jnp.where(valid, place, 0)
            real, imag = blocks[place, 0], blocks[place, 1]
            real = jnp.where(valid, real, jnp.zeros_like(real))
            imag = jnp.where(valid, imag, jnp.zeros_like(imag))
            left.append(side_by_side(real, imag))
            right.append(wide[jnp.where(valid, listed[first, place] % boxes, 0)])
        return dot(jnp.concatenate(left, axis=1), jnp.concatenate(right, axis=0))

    possible = [(boxes - box, boxes, box + 1)[first] for box in range(boxes)]
    sizes = [min(count, 3 if count < 7 else 4) for count in possible]
    for box in range(boxes):
        part = group(box, 0, sizes[box])
        if begun:
            total_ref[box, 0] += part[:, :rhs]
            total_ref[box, 1] += part[:, rhs:]
        else:
            total_ref[box, 0] = part[:, :rhs]
            total_ref[box, 1] = part[:, rhs:]
    for box in range(boxes):

        def more(index, carry, box=box):
            part = group(box, sizes[box] + GROUP * index, GROUP)
            total_ref[box, 0] += part[:, :rhs]
            total_ref[box, 1] += part[:, rhs:]
            return carry

        rest = starts[box + 1] - starts[box] - sizes[box]
        lax.fori_loop(0, (jnp.maximum(rest, 0) + GROUP - 1) // GROUP, more, 0)
        if out_copies:
            out_copies[box].start()
    for copy in out_copies + kept_copies:
        copy.wait()


def near_slots(ids, used, rank):
    boxes, slots = ids.shape
    total = boxes * slots
    source = ids - (rank - 1) * boxes
    source = jnp.where(jnp.arange(slots) < used[:, None], source, -1).reshape(-1)
    wanted = (source >= 0) & (source // boxes == jnp.arange(3)[:, None])
    earlier = jnp.arange(total)[None, :] < jnp.arange(total)[:, None]
    place = jnp.sum((wanted[:, None, :] & earlier).astype(jnp.int32), axis=2)
    code = jnp.arange(total) * boxes + source % boxes
    chosen = wanted[:, None, :] & (place[:, None, :] == jnp.arange(total)[:, None])
    listed = jnp.sum(jnp.where(chosen, code, 0), axis=2)
    before = jnp.arange(total) // slots < jnp.arange(boxes + 1)[:, None]
    starts = jnp.sum((wanted[:, None, :] & before).astype(jnp.int32), axis=2)
    return listed.astype(jnp.int32), starts.astype(jnp.int32)


def near_field(listed, starts, blocks, source, first, before=None, keep=()):
    boxes, slots, _, basis, _ = blocks.shape
    blocks = blocks.reshape(boxes * slots, *blocks.shape[2:])
    rhs = source.shape[3]
    begun, kept = before is not None, len(keep)
    hbm = pl.BlockSpec(memory_space=pltpu.HBM)
    smem = pl.BlockSpec(memory_space=pltpu.SMEM)
    vmem = pl.BlockSpec(memory_space=pltpu.VMEM)
    shape = (boxes, 2, basis, rhs)
    scratch = [
        pltpu.VMEM(blocks.shape, BF16),
        pltpu.VMEM(source.shape, BF16),
        pltpu.VMEM((boxes, 2 * basis, 2 * rhs), BF16),
        pltpu.VMEM(shape, F32),
        pltpu.SemaphoreType.DMA((boxes * slots + 3 * boxes + kept,)),
    ]
    kernel = functools.partial(near_kernel, first, begun, kept)
    if kept:
        del scratch[3]
        inner = kernel

        def kernel(*refs):
            place = 4 + begun + kept
            inner(*refs[:-1], refs[place], refs[-1])

    return pl.pallas_call(
        kernel,
        in_specs=[smem] * 2
        + [hbm, pl.BlockSpec(memory_space=pl.ANY)]
        + [hbm] * (begun + kept),
        out_specs=[vmem] * (1 + kept) if kept else hbm,
        out_shape=[
            pltpu.VMEM(shape, F32),
            *[pltpu.VMEM(array.shape, array.dtype) for array in keep],
        ]
        if kept
        else pltpu.HBM(shape, F32),
        scratch_shapes=scratch,
        compiler_params=pltpu.CompilerParams(vmem_limit_bytes=32 * MIB),
        cost_estimate=pl.CostEstimate(
            flops=10**11 if first == 2 else 2 * 10**9, bytes_accessed=8 * MIB, transcendentals=0
        ),
        name=("near_low", "near_own", "near_high")[first],
    )(
        listed,
        starts,
        *in_hbm(blocks),
        source if first != 1 else in_hbm(source)[0],
        *in_hbm(*([before] if begun else []), *keep),
    )


def adjoint_kernel(rad_ref, out_hbm, held):
    for box in range(rad_ref.shape[0]):
        held[box] = side_by_side(rad_ref[box, 0].T, rad_ref[box, 1].T)
    pltpu.sync_copy(held, out_hbm)


def adjoint(radiation):
    boxes, _, points, basis = radiation.shape
    return pl.pallas_call(
        adjoint_kernel,
        in_specs=[pl.BlockSpec(memory_space=pltpu.VMEM)],
        out_specs=pl.BlockSpec(memory_space=pltpu.HBM),
        scratch_shapes=[pltpu.VMEM((boxes, basis, 2 * points), BF16)],
        out_shape=pltpu.HBM((boxes, basis, 2 * points), BF16),
        cost_estimate=pl.CostEstimate(
            flops=10**6, bytes_accessed=2 * MIB, transcendentals=0
        ),
        name="adjoint",
    )(radiation)


def down_kernel(phi_ref, near_ref, w_ref, adjoint_ref, *refs):
    bands_ref, received = refs[0], refs[1:-4]
    out_hbm, field, held, sems = refs[-4:]
    boxes, _, width = adjoint_ref.shape
    points = width // 2
    rhs = held.shape[3]
    phi = phi_ref[0]
    phi_size = field.shape[1]
    pairs = [(bands_ref.at[:, phi], field.at[:, phi])]
    for distance, piece in enumerate(received, 1):
        pairs.append((piece, field.at[:, lax.rem(phi + phi_size - distance, phi_size)]))
    copies = [
        pltpu.make_async_copy(source, target, sems.at[boxes + place])
        for place, (source, target) in enumerate(pairs)
    ]
    out_copies = [
        pltpu.make_async_copy(held.at[box], out_hbm.at[box], sems.at[box]) for box in range(boxes)
    ]
    for copy in copies:
        copy.start()
    for copy in copies:
        copy.wait()
    mixed = dot(w_ref[...], field[...].reshape(w_ref.shape[1], 2 * rhs))
    for octant in range(boxes // 2):
        start = 2 * octant * points
        cos_part = mixed[start : start + points]
        sin_part = mixed[start + points : start + 2 * points]
        cos_re, cos_im = cos_part[:, :rhs], cos_part[:, rhs:]
        sin_re, sin_im = sin_part[:, :rhs], sin_part[:, rhs:]
        leaves = (
            (octant, cos_re + sin_im, cos_im - sin_re),
            (boxes - 1 - octant, cos_re - sin_im, cos_im + sin_re),
        )
        for box, real, imag in leaves:
            real, imag = real.astype(BF16), imag.astype(BF16)
            right = jnp.concatenate([side_by_side(real, imag), side_by_side(imag, -real)], axis=0)
            far = dot(adjoint_ref[box], right)
            held[box, 0] = near_ref[box, 0] + far[:, :rhs]
            held[box, 1] = near_ref[box, 1] + far[:, rhs:]
            out_copies[box].start()
    for copy in out_copies:
        copy.wait()


def downward(phi, bands, received, near, weights, radiation_adjoint):
    boxes = near.shape[0]
    anywhere = pl.BlockSpec(memory_space=pl.ANY)
    ready = [
        pltpu.with_memory_space_constraint(array, pltpu.VMEM)
        for array in (near, weights, radiation_adjoint)
    ]
    return pl.pallas_call(
        down_kernel,
        in_specs=[pl.BlockSpec(memory_space=pltpu.SMEM)]
        + [pl.BlockSpec(memory_space=pltpu.VMEM)] * 3
        + [anywhere] * (1 + len(received)),
        out_specs=pl.BlockSpec(memory_space=pltpu.HBM),
        out_shape=jax.ShapeDtypeStruct(near.shape, F32),
        scratch_shapes=[
            pltpu.VMEM(bands.shape, BF16),
            pltpu.VMEM(near.shape, F32),
            pltpu.SemaphoreType.DMA((boxes + 1 + len(received),)),
        ],
        compiler_params=pltpu.CompilerParams(vmem_limit_bytes=32 * MIB),
        cost_estimate=pl.CostEstimate(
            flops=2 * 10**9, bytes_accessed=7 * MIB, transcendentals=0
        ),
        name="downward",
    )(phi, *ready, bands, *received)


def shift(block, axis, step):
    count = lax.axis_size(axis)
    pairs = [(i, i + step) for i in range(count) if 0 <= i + step < count]
    return lax.ppermute(block, axis, pairs)


def lists_of(partners, vector_ids, pair_count):
    used = jnp.arange(partners.shape[1])[None, :] < pair_count[:, None]
    names = jnp.where(used, partners, NOWHERE)
    return jnp.stack([names, vector_ids], axis=2).reshape(-1, 2)


def cross_lines(block):
    every = ("box", "theta", "phi")
    size = lax.axis_size("phi")
    lines = lax.axis_size("box") * lax.axis_size("theta")
    pairs = [(line * size, (line - 1) * size) for line in range(1, lines)]
    crossed = lax.ppermute(block, every, pairs)
    return jnp.where(lax.axis_index("phi") == 0, crossed, block)


def parent_bands(spread, shares):
    axes = ("box", "theta", "phi") if shares == lax.axis_size("box") else ("theta", "phi")
    return lax.all_to_all(spread, axes, split_axis=0, concat_axis=0, tiled=True)


def staged_bands(incoming, shares):
    axes = ("box", "theta") if shares == lax.axis_size("box") else ("theta",)
    phi_size = lax.axis_size("phi")
    phi = lax.axis_index("phi")
    bands = incoming.reshape(-1, phi_size, *incoming.shape[1:])
    bands = lax.all_to_all(bands, axes, split_axis=0, concat_axis=0, tiled=True)
    received = []
    for distance in range(1, phi_size):
        piece = lax.dynamic_index_in_dim(bands, (phi + distance) % phi_size, 1, keepdims=False)
        ring = [(place, (place + distance) % phi_size) for place in range(phi_size)]
        received.append(lax.ppermute(piece, "phi", ring))
    return phi.astype(jnp.int32).reshape(1), bands, received


def translation_lines(lists, translation, shares, per_group):
    operator_total, _, theta_band, phi_band = translation.shape
    rank = lax.axis_index("box")
    if shares < lax.axis_size("box"):
        table = translation.reshape(operator_total, -1)
        base = ((rank - 1) * per_group).astype(jnp.int32).reshape(1)
        return couplings(lists, base, table, per_group, 3 * per_group)
    if shares == 2:
        other = lax.ppermute(lists, "box", [(0, 1), (1, 0)])
        lists = jnp.where(
            rank == 0, jnp.concatenate([lists, other]), jnp.concatenate([other, lists])
        )
    part = theta_band // shares
    table = lax.dynamic_slice_in_dim(translation, rank * part, part, axis=2)
    table = table.reshape(operator_total, -1)
    total = shares * per_group
    return couplings(lists, jnp.zeros((1,), jnp.int32), table, total, total)


def per_device(
    shares,
    up_weights,
    down_weights,
    coeffs,
    near_blocks,
    near_ids,
    near_count,
    radiation,
    partners,
    vector_ids,
    pair_count,
    translation,
):
    every = ("box", "theta", "phi")
    per_group = lax.axis_size("theta") * lax.axis_size("phi")
    low = shift(coeffs, every, 1)
    ahead = cross_lines(coeffs)
    spread = upward(coeffs, radiation, up_weights, shares * per_group)
    radiation_adjoint = adjoint(radiation)
    lists = lists_of(partners, vector_ids, pair_count)
    spread, lists = lax.optimization_barrier((spread, lists))
    lines = translation_lines(lists, translation, shares, per_group)
    listed, starts = near_slots(near_ids, near_count, lax.axis_index(every))
    spread, lines, radiation_adjoint, listed, starts, ahead = lax.optimization_barrier(
        (spread, lines, radiation_adjoint, listed, starts, ahead)
    )
    parents = parent_bands(spread, shares)
    near = near_field(listed, starts, near_blocks, low, 0)
    near, ahead = lax.optimization_barrier((near, ahead))
    phi_size = lax.axis_size("phi")
    high = lax.ppermute(ahead, "phi", [(i, (i - 1) % phi_size) for i in range(phi_size)])
    parents, near = lax.optimization_barrier((parents, near))
    sources = [parents]
    if shares < lax.axis_size("box"):
        sources = [shift(parents, "box", 1), parents, shift(parents, "box", -1)]
    incoming = translate(lines, sources)
    incoming, near = lax.optimization_barrier((incoming, near))
    phi, bands, received = staged_bands(incoming, shares)
    near = near_field(listed, starts, near_blocks, coeffs, 1, near)
    ready = near_field(
        listed, starts, near_blocks, high, 2, near, keep=(down_weights, radiation_adjoint)
    )
    return downward(phi, bands, received, *ready)


def solution(mesh):
    box_size, theta_size, phi_size = (mesh.shape[axis] for axis in ("box", "theta", "phi"))
    shares = box_size if box_size <= 2 and TU // theta_size % box_size == 0 else 1
    up_weights, down_weights = operators(shares, theta_size, phi_size)
    in_specs = (
        P(),
        P(),
        P(("box", "theta", "phi"), None, None, None),
        P(("box", "theta", "phi"), None, None, None, None),
        P(("box", "theta", "phi"), None),
        P(("box", "theta", "phi")),
        P(("box", "theta", "phi"), None, None, None),
        P("box", None),
        P("box", None),
        P("box"),
        P(None, None, "theta", "phi"),
    )
    out_specs = P(("box", "theta", "phi"), None, None, None)
    mapped = jax.shard_map(
        functools.partial(per_device, shares),
        mesh=mesh,
        in_specs=in_specs,
        out_specs=out_specs,
        check_vma=False,
    )

    def product(*arrays):
        return mapped(jnp.asarray(up_weights), jnp.asarray(down_weights), *arrays)

    return product
```

```python
import functools
import math

import jax
import jax.numpy as jnp
import ml_dtypes
import numpy as np
from jax import lax
from jax.experimental import pallas as pl
from jax.experimental.pallas import tpu as pltpu
from jax.sharding import PartitionSpec as P

TL = 8
PL = 16
TU = 16
PU = 32

WEIGHT_UP = (-0.0546875, 0.8203125, 0.2734375, -0.0390625)
WEIGHT_DOWN = (-0.0390625, 0.2734375, 0.8203125, -0.0546875)
PHASE_SCALE = 1.3

F32 = jnp.float32
BF16 = jnp.bfloat16
MIB = 2**20
GROUP = 2
NOWHERE = -(2**20)


def lagrange(rows, columns, wrap):
    matrix = np.zeros((rows, columns))
    for row in range(rows):
        weights = WEIGHT_UP if row % 2 else WEIGHT_DOWN
        for order in range(4):
            node = row // 2 + row % 2 - 2 + order
            node = node % columns if wrap else min(max(node, 0), columns - 1)
            matrix[row, node] += weights[order]
    return matrix


def split_weights(matrix):
    high = matrix.astype(ml_dtypes.bfloat16)
    low = (matrix - high.astype(np.float64)).astype(ml_dtypes.bfloat16)
    return high, low


def operators(shares, theta_size, phi_size):
    theta_part = TU // theta_size // shares
    order = np.arange(TU * PU).reshape(theta_size, shares, theta_part, phi_size, PU // phi_size)
    order = order.transpose(1, 0, 3, 2, 4).reshape(-1)
    interp = np.kron(lagrange(TU, TL, False), lagrange(PU, PL, True))
    theta = math.pi * (np.arange(TU) + 0.5) / TU
    azimuth = 2.0 * math.pi * (np.arange(PU) + 0.5) / PU
    up, down = [], []
    for octant in range(4):
        sign_x = 2 * (octant % 2) - 1
        sign_y = 2 * (octant // 2 % 2) - 1
        sign_z = 2 * (octant // 4) - 1
        angle = PHASE_SCALE * (
            sign_x * np.sin(theta)[:, None] * np.cos(azimuth)[None]
            + sign_y * np.sin(theta)[:, None] * np.sin(azimuth)[None]
            + sign_z * np.cos(theta)[:, None]
        ).reshape(-1, 1)
        cos_high, cos_low = split_weights((np.cos(angle) * interp)[order])
        sin_high, sin_low = split_weights((np.sin(angle) * interp)[order])
        high = np.concatenate([cos_high, sin_high], axis=1)
        low = np.concatenate([cos_low, sin_low], axis=1)
        up.append(np.concatenate([high, low], axis=0))
        down += [cos_high.T, sin_high.T]
    return np.concatenate(up, axis=1), np.concatenate(down, axis=0)


def in_hbm(*arrays):
    return [pltpu.with_memory_space_constraint(array, pltpu.HBM) for array in arrays]


def dot(a, b):
    return jnp.dot(a, b, preferred_element_type=F32)


def side_by_side(real, imag):
    return jnp.concatenate([real, imag], axis=1)


def complex_columns(real, imag):
    return jnp.concatenate([side_by_side(real, imag), side_by_side(-imag, real)], axis=0)


def up_kernel(x_hbm, rad_hbm, w_hbm, out_hbm, x_ref, rad_ref, w_ref, right, result, sems):
    boxes, _, _, rhs = x_ref.shape
    points = rad_ref.shape[2]
    copies = [
        pltpu.make_async_copy(source, target, sems.at[place])
        for place, (source, target) in enumerate(
            ((x_hbm, x_ref), (rad_hbm, rad_ref), (w_hbm, w_ref))
        )
    ]
    for copy in copies:
        copy.start()
    copies[0].wait()
    copies[1].wait()
    half = boxes // 2
    for octant in range(boxes):
        left = side_by_side(rad_ref[octant, 0], rad_ref[octant, 1])
        straight = dot(left, complex_columns(x_ref[octant, 0], x_ref[octant, 1])).astype(BF16)
        real, imag = straight[:, :rhs], straight[:, rhs:]
        if octant < half:
            swapped = side_by_side(-imag, real)
        else:
            swapped = side_by_side(imag, -real)
        place = octant if octant < half else boxes - 1 - octant
        start = 2 * place * points
        right[octant // half, start : start + points] = straight
        right[octant // half, start + points : start + 2 * points] = swapped
    copies[2].wait()
    total = dot(w_ref[...], right[0]) + dot(w_ref[...], right[1])
    samples = total.shape[0] // 2
    total = total[:samples] + total[samples:]
    result[...] = total.astype(BF16).reshape(result.shape)
    pltpu.sync_copy(result, out_hbm)


def upward(coeffs, radiation, weights, groups):
    boxes, _, basis, rhs = coeffs.shape
    rows, columns = weights.shape
    samples = rows // 2
    hbm = pl.BlockSpec(memory_space=pltpu.HBM)
    return pl.pallas_call(
        up_kernel,
        in_specs=[hbm] * 3,
        out_specs=hbm,
        out_shape=pltpu.HBM((groups, samples // groups, 2 * rhs), BF16),
        scratch_shapes=[
            pltpu.VMEM(coeffs.shape, BF16),
            pltpu.VMEM(radiation.shape, BF16),
            pltpu.VMEM(weights.shape, BF16),
            pltpu.VMEM((2, columns, 2 * rhs), BF16),
            pltpu.VMEM((groups, samples // groups, 2 * rhs), BF16),
            pltpu.SemaphoreType.DMA((3,)),
        ],
        compiler_params=pltpu.CompilerParams(vmem_limit_bytes=32 * MIB),
        cost_estimate=pl.CostEstimate(
            flops=2 * 10**9, bytes_accessed=4 * MIB, transcendentals=0
        ),
        name="upward",
    )(*in_hbm(coeffs, radiation, weights))


def coupling_kernel(lists_ref, base_ref, table_ref, out_ref):
    rows = lists_ref.shape[0]
    samples = table_ref.shape[1] // 2
    _, targets, columns = out_ref.shape
    slots = rows // targets
    selector = (
        lax.broadcasted_iota(jnp.int32, (rows, table_ref.shape[0]), 1) == lists_ref[:, 1:2]
    )
    chosen = dot(selector.astype(BF16), table_ref[...]).astype(BF16)
    wide = lax.broadcasted_iota(jnp.int32, (rows, columns), 1) // samples
    match = wide + base_ref[0] == lists_ref[:, 0:1]
    spread = lax.broadcasted_iota(jnp.int32, (samples, columns), 0) == (
        lax.broadcasted_iota(jnp.int32, (samples, columns), 1) % samples
    )
    gather = (
        lax.broadcasted_iota(jnp.int32, (targets, rows), 1) // slots
        == lax.broadcasted_iota(jnp.int32, (targets, rows), 0)
    ).astype(BF16)
    tile = spread.astype(BF16)
    for part in range(2):
        lines = dot(chosen[:, part * samples : (part + 1) * samples], tile)
        out_ref[part] = dot(gather, jnp.where(match, lines, 0.0).astype(BF16))


def couplings(lists, base, table, targets, names):
    shape = (2, targets, names * (table.shape[1] // 2))
    vmem = pl.BlockSpec(memory_space=pltpu.VMEM)
    return pl.pallas_call(
        coupling_kernel,
        in_specs=[vmem, pl.BlockSpec(memory_space=pltpu.SMEM), vmem],
        out_specs=vmem,
        out_shape=jax.ShapeDtypeStruct(shape, F32),
        compiler_params=pltpu.CompilerParams(vmem_limit_bytes=16 * MIB),
        cost_estimate=pl.CostEstimate(
            flops=2 * 10**8, bytes_accessed=2 * 2**20, transcendentals=0
        ),
        name="coupling",
    )(lists, base, table)


def translate_kernel(lines_hbm, *refs):
    count = (len(refs) - 5) // 2
    sources, out_hbm = refs[:count], refs[count]
    held, lines, matrix, result, sems = refs[count + 1 :][:count], *refs[2 * count + 1 :]
    targets, samples, width = result.shape
    rhs = width // 2
    copies = [
        pltpu.make_async_copy(source, target, sems.at[place])
        for place, (source, target) in enumerate(zip((lines_hbm, *sources), (lines, *held)))
    ]
    for copy in copies:
        copy.start()
    copies[0].wait()
    columns = matrix.shape[1]
    row = lax.broadcasted_iota(jnp.int32, (samples, columns), 0)
    diagonal = row == lax.broadcasted_iota(jnp.int32, (samples, columns), 1) % samples
    for part in range(2):
        for target in range(targets):
            line = jnp.broadcast_to(lines[part, target : target + 1], diagonal.shape)
            start = (part * targets + target) * samples
            matrix[start : start + samples] = jnp.where(diagonal, line, 0.0).astype(BF16)
    total = None
    start = 0
    for place, source in enumerate(held):
        copies[1 + place].wait()
        stop = start + source.shape[0] * samples
        part = dot(matrix[:, start:stop], source[...].reshape(stop - start, width))
        total = part if total is None else total + part
        start = stop
    half = targets * samples
    real = total[:half, :rhs] - total[half:, rhs:]
    imag = total[:half, rhs:] + total[half:, :rhs]
    result[...] = jnp.concatenate([real, imag], axis=1).astype(BF16).reshape(result.shape)
    pltpu.sync_copy(result, out_hbm)


def translate(lines, sources):
    _, samples, width = sources[0].shape
    _, targets, columns = lines.shape
    shape = (targets, samples, width)
    hbm = pl.BlockSpec(memory_space=pltpu.HBM)
    anywhere = pl.BlockSpec(memory_space=pl.ANY)
    return pl.pallas_call(
        translate_kernel,
        in_specs=[hbm] + [anywhere] * len(sources),
        out_specs=hbm,
        out_shape=pltpu.HBM(shape, BF16),
        scratch_shapes=[
            *[pltpu.VMEM(source.shape, BF16) for source in sources],
            pltpu.VMEM(lines.shape, F32),
            pltpu.VMEM((2 * targets * samples, columns), BF16),
            pltpu.VMEM(shape, BF16),
            pltpu.SemaphoreType.DMA((1 + len(sources),)),
        ],
        compiler_params=pltpu.CompilerParams(vmem_limit_bytes=24 * MIB),
        cost_estimate=pl.CostEstimate(
            flops=10**9, bytes_accessed=2 * MIB, transcendentals=0
        ),
        name="translate",
    )(*in_hbm(lines), *sources)


def near_kernel(first, begun, kept, *refs):
    refs = list(refs)
    listed, starts_ref, blocks_hbm, source_hbm = refs[:4]
    before_hbm = refs[4] if begun else None
    kept_hbm = refs[4 + begun : 4 + begun + kept]
    out_ref = refs[4 + begun + kept]
    kept_refs = refs[5 + begun + kept : 5 + begun + 2 * kept]
    blocks, held, wide, total_ref, sems = refs[5 + begun + 2 * kept :]
    boxes, _, basis, rhs = held.shape
    most = blocks_hbm.shape[0]
    starts = [starts_ref[first, box] for box in range(boxes + 1)]

    def by_box(source, target, turn):
        return [
            pltpu.make_async_copy(
                source.at[box], target.at[box], sems.at[most + turn * boxes + box]
            )
            for box in range(boxes)
        ]

    source_copies = by_box(source_hbm, held, 0)
    before_copies = by_box(before_hbm, total_ref, 1) if begun else []
    out_copies = [] if kept else by_box(total_ref, out_ref, 2)
    kept_copies = [
        pltpu.make_async_copy(kept_hbm[place], kept_refs[place], sems.at[most + 3 * boxes + place])
        for place in range(kept)
    ]
    for copy in source_copies:
        copy.start()

    def block_copy(place):
        block = listed[first, place] // boxes
        return pltpu.make_async_copy(blocks_hbm.at[block], blocks.at[place], sems.at[place])

    def fetch(place, carry):
        block_copy(place).start()
        return carry

    lax.fori_loop(0, starts[boxes], fetch, 0)
    for copy in before_copies + kept_copies:
        copy.start()
    for copy in source_copies:
        copy.wait()
    for place in range(boxes):
        wide[place] = complex_columns(held[place, 0], held[place, 1])

    def landed(place, carry):
        block_copy(place).wait()
        return carry

    lax.fori_loop(0, starts[boxes], landed, 0)
    for copy in before_copies:
        copy.wait()

    def group(box, begin, size):
        left, right = [], []
        for step in range(size):
            place = starts[box] + begin + step
            valid = place < starts[box + 1]
            place = jnp.where(valid, place, 0)
            real, imag = blocks[place, 0], blocks[place, 1]
            real = jnp.where(valid, real, jnp.zeros_like(real))
            imag = jnp.where(valid, imag, jnp.zeros_like(imag))
            left.append(side_by_side(real, imag))
            right.append(wide[jnp.where(valid, listed[first, place] % boxes, 0)])
        return dot(jnp.concatenate(left, axis=1), jnp.concatenate(right, axis=0))

    possible = [(boxes - box, boxes, box + 1)[first] for box in range(boxes)]
    sizes = [min(count, 3 if count < 7 else 4) for count in possible]
    for box in range(boxes):
        part = group(box, 0, sizes[box])
        if begun:
            total_ref[box, 0] += part[:, :rhs]
            total_ref[box, 1] += part[:, rhs:]
        else:
            total_ref[box, 0] = part[:, :rhs]
            total_ref[box, 1] = part[:, rhs:]
    for box in range(boxes):

        def more(index, carry, box=box):
            part = group(box, sizes[box] + GROUP * index, GROUP)
            total_ref[box, 0] += part[:, :rhs]
            total_ref[box, 1] += part[:, rhs:]
            return carry

        rest = starts[box + 1] - starts[box] - sizes[box]
        lax.fori_loop(0, (jnp.maximum(rest, 0) + GROUP - 1) // GROUP, more, 0)
        if out_copies:
            out_copies[box].start()
    for copy in out_copies + kept_copies:
        copy.wait()


def near_slots(ids, used, rank):
    boxes, slots = ids.shape
    total = boxes * slots
    source = ids - (rank - 1) * boxes
    source = jnp.where(jnp.arange(slots) < used[:, None], source, -1).reshape(-1)
    wanted = (source >= 0) & (source // boxes == jnp.arange(3)[:, None])
    earlier = jnp.arange(total)[None, :] < jnp.arange(total)[:, None]
    place = jnp.sum((wanted[:, None, :] & earlier).astype(jnp.int32), axis=2)
    code = jnp.arange(total) * boxes + source % boxes
    chosen = wanted[:, None, :] & (place[:, None, :] == jnp.arange(total)[:, None])
    listed = jnp.sum(jnp.where(chosen, code, 0), axis=2)
    before = jnp.arange(total) // slots < jnp.arange(boxes + 1)[:, None]
    starts = jnp.sum((wanted[:, None, :] & before).astype(jnp.int32), axis=2)
    return listed.astype(jnp.int32), starts.astype(jnp.int32)


def near_field(listed, starts, blocks, source, first, before=None, keep=()):
    boxes, slots, _, basis, _ = blocks.shape
    blocks = blocks.reshape(boxes * slots, *blocks.shape[2:])
    rhs = source.shape[3]
    begun, kept = before is not None, len(keep)
    hbm = pl.BlockSpec(memory_space=pltpu.HBM)
    smem = pl.BlockSpec(memory_space=pltpu.SMEM)
    vmem = pl.BlockSpec(memory_space=pltpu.VMEM)
    shape = (boxes, 2, basis, rhs)
    scratch = [
        pltpu.VMEM(blocks.shape, BF16),
        pltpu.VMEM(source.shape, BF16),
        pltpu.VMEM((boxes, 2 * basis, 2 * rhs), BF16),
        pltpu.VMEM(shape, F32),
        pltpu.SemaphoreType.DMA((boxes * slots + 3 * boxes + kept,)),
    ]
    kernel = functools.partial(near_kernel, first, begun, kept)
    if kept:
        del scratch[3]
        inner = kernel

        def kernel(*refs):
            place = 4 + begun + kept
            inner(*refs[:-1], refs[place], refs[-1])

    return pl.pallas_call(
        kernel,
        in_specs=[smem] * 2
        + [hbm, pl.BlockSpec(memory_space=pl.ANY)]
        + [hbm] * (begun + kept),
        out_specs=[vmem] * (1 + kept) if kept else hbm,
        out_shape=[
            pltpu.VMEM(shape, F32),
            *[pltpu.VMEM(array.shape, array.dtype) for array in keep],
        ]
        if kept
        else pltpu.HBM(shape, F32),
        scratch_shapes=scratch,
        compiler_params=pltpu.CompilerParams(vmem_limit_bytes=32 * MIB),
        cost_estimate=pl.CostEstimate(
            flops=10**11 if first == 2 else 2 * 10**9, bytes_accessed=8 * MIB, transcendentals=0
        ),
        name=("near_low", "near_own", "near_high")[first],
    )(
        listed,
        starts,
        *in_hbm(blocks),
        source if first != 1 else in_hbm(source)[0],
        *in_hbm(*([before] if begun else []), *keep),
    )


def adjoint_kernel(rad_ref, out_hbm, held):
    for box in range(rad_ref.shape[0]):
        held[box] = side_by_side(rad_ref[box, 0].T, rad_ref[box, 1].T)
    pltpu.sync_copy(held, out_hbm)


def adjoint(radiation):
    boxes, _, points, basis = radiation.shape
    return pl.pallas_call(
        adjoint_kernel,
        in_specs=[pl.BlockSpec(memory_space=pltpu.VMEM)],
        out_specs=pl.BlockSpec(memory_space=pltpu.HBM),
        scratch_shapes=[pltpu.VMEM((boxes, basis, 2 * points), BF16)],
        out_shape=pltpu.HBM((boxes, basis, 2 * points), BF16),
        cost_estimate=pl.CostEstimate(
            flops=10**6, bytes_accessed=2 * MIB, transcendentals=0
        ),
        name="adjoint",
    )(radiation)


def down_kernel(phi_ref, near_ref, w_ref, adjoint_ref, *refs):
    bands_ref, received = refs[0], refs[1:-4]
    out_hbm, field, held, sems = refs[-4:]
    boxes, _, width = adjoint_ref.shape
    points = width // 2
    rhs = held.shape[3]
    phi = phi_ref[0]
    phi_size = field.shape[1]
    pairs = [(bands_ref.at[:, phi], field.at[:, phi])]
    for distance, piece in enumerate(received, 1):
        pairs.append((piece, field.at[:, lax.rem(phi + phi_size - distance, phi_size)]))
    copies = [
        pltpu.make_async_copy(source, target, sems.at[boxes + place])
        for place, (source, target) in enumerate(pairs)
    ]
    out_copies = [
        pltpu.make_async_copy(held.at[box], out_hbm.at[box], sems.at[box]) for box in range(boxes)
    ]
    for copy in copies:
        copy.start()
    for copy in copies:
        copy.wait()
    mixed = dot(w_ref[...], field[...].reshape(w_ref.shape[1], 2 * rhs))
    for octant in range(boxes // 2):
        start = 2 * octant * points
        cos_part = mixed[start : start + points]
        sin_part = mixed[start + points : start + 2 * points]
        cos_re, cos_im = cos_part[:, :rhs], cos_part[:, rhs:]
        sin_re, sin_im = sin_part[:, :rhs], sin_part[:, rhs:]
        leaves = (
            (octant, cos_re + sin_im, cos_im - sin_re),
            (boxes - 1 - octant, cos_re - sin_im, cos_im + sin_re),
        )
        for box, real, imag in leaves:
            real, imag = real.astype(BF16), imag.astype(BF16)
            right = jnp.concatenate([side_by_side(real, imag), side_by_side(imag, -real)], axis=0)
            far = dot(adjoint_ref[box], right)
            held[box, 0] = near_ref[box, 0] + far[:, :rhs]
            held[box, 1] = near_ref[box, 1] + far[:, rhs:]
            out_copies[box].start()
    for copy in out_copies:
        copy.wait()


def downward(phi, bands, received, near, weights, radiation_adjoint):
    boxes = near.shape[0]
    anywhere = pl.BlockSpec(memory_space=pl.ANY)
    ready = [
        pltpu.with_memory_space_constraint(array, pltpu.VMEM)
        for array in (near, weights, radiation_adjoint)
    ]
    return pl.pallas_call(
        down_kernel,
        in_specs=[pl.BlockSpec(memory_space=pltpu.SMEM)]
        + [pl.BlockSpec(memory_space=pltpu.VMEM)] * 3
        + [anywhere] * (1 + len(received)),
        out_specs=pl.BlockSpec(memory_space=pltpu.HBM),
        out_shape=jax.ShapeDtypeStruct(near.shape, F32),
        scratch_shapes=[
            pltpu.VMEM(bands.shape, BF16),
            pltpu.VMEM(near.shape, F32),
            pltpu.SemaphoreType.DMA((boxes + 1 + len(received),)),
        ],
        compiler_params=pltpu.CompilerParams(vmem_limit_bytes=32 * MIB),
        cost_estimate=pl.CostEstimate(
            flops=2 * 10**9, bytes_accessed=7 * MIB, transcendentals=0
        ),
        name="downward",
    )(phi, *ready, bands, *received)


def shift(block, axis, step):
    count = lax.axis_size(axis)
    pairs = [(i, i + step) for i in range(count) if 0 <= i + step < count]
    return lax.ppermute(block, axis, pairs)


def lists_of(partners, vector_ids, pair_count):
    used = jnp.arange(partners.shape[1])[None, :] < pair_count[:, None]
    names = jnp.where(used, partners, NOWHERE)
    return jnp.stack([names, vector_ids], axis=2).reshape(-1, 2)


def cross_lines(block):
    every = ("box", "theta", "phi")
    size = lax.axis_size("phi")
    lines = lax.axis_size("box") * lax.axis_size("theta")
    pairs = [(line * size, (line - 1) * size) for line in range(1, lines)]
    crossed = lax.ppermute(block, every, pairs)
    return jnp.where(lax.axis_index("phi") == 0, crossed, block)


def parent_bands(spread, shares):
    axes = ("box", "theta", "phi") if shares == lax.axis_size("box") else ("theta", "phi")
    return lax.all_to_all(spread, axes, split_axis=0, concat_axis=0, tiled=True)


def staged_bands(incoming, shares):
    axes = ("box", "theta") if shares == lax.axis_size("box") else ("theta",)
    phi_size = lax.axis_size("phi")
    phi = lax.axis_index("phi")
    bands = incoming.reshape(-1, phi_size, *incoming.shape[1:])
    bands = lax.all_to_all(bands, axes, split_axis=0, concat_axis=0, tiled=True)
    received = []
    for distance in range(1, phi_size):
        piece = lax.dynamic_index_in_dim(bands, (phi + distance) % phi_size, 1, keepdims=False)
        ring = [(place, (place + distance) % phi_size) for place in range(phi_size)]
        received.append(lax.ppermute(piece, "phi", ring))
    return phi.astype(jnp.int32).reshape(1), bands, received


def translation_lines(lists, translation, shares, per_group):
    operator_total, _, theta_band, phi_band = translation.shape
    rank = lax.axis_index("box")
    if shares < lax.axis_size("box"):
        table = translation.reshape(operator_total, -1)
        base = ((rank - 1) * per_group).astype(jnp.int32).reshape(1)
        return couplings(lists, base, table, per_group, 3 * per_group)
    if shares == 2:
        other = lax.ppermute(lists, "box", [(0, 1), (1, 0)])
        lists = jnp.where(
            rank == 0, jnp.concatenate([lists, other]), jnp.concatenate([other, lists])
        )
    part = theta_band // shares
    table = lax.dynamic_slice_in_dim(translation, rank * part, part, axis=2)
    table = table.reshape(operator_total, -1)
    total = shares * per_group
    return couplings(lists, jnp.zeros((1,), jnp.int32), table, total, total)


def per_device(
    shares,
    up_weights,
    down_weights,
    coeffs,
    near_blocks,
    near_ids,
    near_count,
    radiation,
    partners,
    vector_ids,
    pair_count,
    translation,
):
    every = ("box", "theta", "phi")
    per_group = lax.axis_size("theta") * lax.axis_size("phi")
    low = shift(coeffs, every, 1)
    ahead = cross_lines(coeffs)
    spread = upward(coeffs, radiation, up_weights, shares * per_group)
    radiation_adjoint = adjoint(radiation)
    lists = lists_of(partners, vector_ids, pair_count)
    lines = translation_lines(lists, translation, shares, per_group)
    listed, starts = near_slots(near_ids, near_count, lax.axis_index(every))
    spread, radiation_adjoint = lax.optimization_barrier((spread, radiation_adjoint))
    parents = parent_bands(spread, shares)
    lines, listed, starts, ahead = lax.optimization_barrier((lines, listed, starts, ahead))
    near = near_field(listed, starts, near_blocks, low, 0)
    near, ahead = lax.optimization_barrier((near, ahead))
    phi_size = lax.axis_size("phi")
    high = lax.ppermute(ahead, "phi", [(i, (i - 1) % phi_size) for i in range(phi_size)])
    parents, near = lax.optimization_barrier((parents, near))
    sources = [parents]
    if shares < lax.axis_size("box"):
        sources = [shift(parents, "box", 1), parents, shift(parents, "box", -1)]
    incoming = translate(lines, sources)
    incoming, near = lax.optimization_barrier((incoming, near))
    phi, bands, received = staged_bands(incoming, shares)
    near = near_field(listed, starts, near_blocks, coeffs, 1, near)
    ready = near_field(
        listed, starts, near_blocks, high, 2, near, keep=(down_weights, radiation_adjoint)
    )
    return downward(phi, bands, received, *ready)


def solution(mesh):
    box_size, theta_size, phi_size = (mesh.shape[axis] for axis in ("box", "theta", "phi"))
    shares = box_size if box_size <= 2 and TU // theta_size % box_size == 0 else 1
    up_weights, down_weights = operators(shares, theta_size, phi_size)
    in_specs = (
        P(),
        P(),
        P(("box", "theta", "phi"), None, None, None),
        P(("box", "theta", "phi"), None, None, None, None),
        P(("box", "theta", "phi"), None),
        P(("box", "theta", "phi")),
        P(("box", "theta", "phi"), None, None, None),
        P("box", None),
        P("box", None),
        P("box"),
        P(None, None, "theta", "phi"),
    )
    out_specs = P(("box", "theta", "phi"), None, None, None)
    mapped = jax.shard_map(
        functools.partial(per_device, shares),
        mesh=mesh,
        in_specs=in_specs,
        out_specs=out_specs,
        check_vma=False,
    )

    def product(*arrays):
        return mapped(jnp.asarray(up_weights), jnp.asarray(down_weights), *arrays)

    return product
```

```python
import functools
import math

import jax
import jax.numpy as jnp
import ml_dtypes
import numpy as np
from jax import lax
from jax.experimental import pallas as pl
from jax.experimental.pallas import tpu as pltpu
from jax.sharding import PartitionSpec as P

TL = 8
PL = 16
TU = 16
PU = 32

WEIGHT_UP = (-0.0546875, 0.8203125, 0.2734375, -0.0390625)
WEIGHT_DOWN = (-0.0390625, 0.2734375, 0.8203125, -0.0546875)
PHASE_SCALE = 1.3

F32 = jnp.float32
BF16 = jnp.bfloat16
MIB = 2**20
GROUP = 2
NOWHERE = -(2**20)


def lagrange(rows, columns, wrap):
    matrix = np.zeros((rows, columns))
    for row in range(rows):
        weights = WEIGHT_UP if row % 2 else WEIGHT_DOWN
        for order in range(4):
            node = row // 2 + row % 2 - 2 + order
            node = node % columns if wrap else min(max(node, 0), columns - 1)
            matrix[row, node] += weights[order]
    return matrix


def split_weights(matrix):
    high = matrix.astype(ml_dtypes.bfloat16)
    low = (matrix - high.astype(np.float64)).astype(ml_dtypes.bfloat16)
    return high, low


def operators(shares, theta_size, phi_size):
    theta_part = TU // theta_size // shares
    order = np.arange(TU * PU).reshape(theta_size, shares, theta_part, phi_size, PU // phi_size)
    order = order.transpose(1, 0, 3, 2, 4).reshape(-1)
    interp = np.kron(lagrange(TU, TL, False), lagrange(PU, PL, True))
    theta = math.pi * (np.arange(TU) + 0.5) / TU
    azimuth = 2.0 * math.pi * (np.arange(PU) + 0.5) / PU
    up, down = [], []
    for octant in range(4):
        sign_x = 2 * (octant % 2) - 1
        sign_y = 2 * (octant // 2 % 2) - 1
        sign_z = 2 * (octant // 4) - 1
        angle = PHASE_SCALE * (
            sign_x * np.sin(theta)[:, None] * np.cos(azimuth)[None]
            + sign_y * np.sin(theta)[:, None] * np.sin(azimuth)[None]
            + sign_z * np.cos(theta)[:, None]
        ).reshape(-1, 1)
        cos_high, cos_low = split_weights((np.cos(angle) * interp)[order])
        sin_high, sin_low = split_weights((np.sin(angle) * interp)[order])
        high = np.concatenate([cos_high, sin_high], axis=1)
        low = np.concatenate([cos_low, sin_low], axis=1)
        up.append(np.concatenate([high, low], axis=0))
        down += [cos_high.T, sin_high.T]
    return np.concatenate(up, axis=1), np.concatenate(down, axis=0)


def in_hbm(*arrays):
    return [pltpu.with_memory_space_constraint(array, pltpu.HBM) for array in arrays]


def dot(a, b):
    return jnp.dot(a, b, preferred_element_type=F32)


def side_by_side(real, imag):
    return jnp.concatenate([real, imag], axis=1)


def complex_columns(real, imag):
    return jnp.concatenate([side_by_side(real, imag), side_by_side(-imag, real)], axis=0)


def up_kernel(x_hbm, rad_hbm, w_hbm, out_hbm, x_ref, rad_ref, w_ref, right, result, sems):
    boxes, _, _, rhs = x_ref.shape
    points = rad_ref.shape[2]
    copies = [
        pltpu.make_async_copy(source, target, sems.at[place])
        for place, (source, target) in enumerate(
            ((x_hbm, x_ref), (rad_hbm, rad_ref), (w_hbm, w_ref))
        )
    ]
    for copy in copies:
        copy.start()
    copies[0].wait()
    copies[1].wait()
    half = boxes // 2
    for octant in range(boxes):
        left = side_by_side(rad_ref[octant, 0], rad_ref[octant, 1])
        straight = dot(left, complex_columns(x_ref[octant, 0], x_ref[octant, 1])).astype(BF16)
        real, imag = straight[:, :rhs], straight[:, rhs:]
        if octant < half:
            swapped = side_by_side(-imag, real)
        else:
            swapped = side_by_side(imag, -real)
        place = octant if octant < half else boxes - 1 - octant
        start = 2 * place * points
        right[octant // half, start : start + points] = straight
        right[octant // half, start + points : start + 2 * points] = swapped
    copies[2].wait()
    total = dot(w_ref[...], right[0]) + dot(w_ref[...], right[1])
    samples = total.shape[0] // 2
    total = total[:samples] + total[samples:]
    result[...] = total.astype(BF16).reshape(result.shape)
    pltpu.sync_copy(result, out_hbm)


def upward(coeffs, radiation, weights, groups):
    boxes, _, basis, rhs = coeffs.shape
    rows, columns = weights.shape
    samples = rows // 2
    hbm = pl.BlockSpec(memory_space=pltpu.HBM)
    return pl.pallas_call(
        up_kernel,
        in_specs=[hbm] * 3,
        out_specs=hbm,
        out_shape=pltpu.HBM((groups, samples // groups, 2 * rhs), BF16),
        scratch_shapes=[
            pltpu.VMEM(coeffs.shape, BF16),
            pltpu.VMEM(radiation.shape, BF16),
            pltpu.VMEM(weights.shape, BF16),
            pltpu.VMEM((2, columns, 2 * rhs), BF16),
            pltpu.VMEM((groups, samples // groups, 2 * rhs), BF16),
            pltpu.SemaphoreType.DMA((3,)),
        ],
        compiler_params=pltpu.CompilerParams(vmem_limit_bytes=32 * MIB),
        cost_estimate=pl.CostEstimate(
            flops=2 * 10**9, bytes_accessed=4 * MIB, transcendentals=0
        ),
        name="upward",
    )(*in_hbm(coeffs, radiation, weights))


def coupling_kernel(lists_ref, base_ref, table_ref, out_ref):
    rows = lists_ref.shape[0]
    samples = table_ref.shape[1] // 2
    _, targets, columns = out_ref.shape
    slots = rows // targets
    selector = (
        lax.broadcasted_iota(jnp.int32, (rows, table_ref.shape[0]), 1) == lists_ref[:, 1:2]
    )
    chosen = dot(selector.astype(BF16), table_ref[...]).astype(BF16)
    wide = lax.broadcasted_iota(jnp.int32, (rows, columns), 1) // samples
    match = wide + base_ref[0] == lists_ref[:, 0:1]
    spread = lax.broadcasted_iota(jnp.int32, (samples, columns), 0) == (
        lax.broadcasted_iota(jnp.int32, (samples, columns), 1) % samples
    )
    gather = (
        lax.broadcasted_iota(jnp.int32, (targets, rows), 1) // slots
        == lax.broadcasted_iota(jnp.int32, (targets, rows), 0)
    ).astype(BF16)
    tile = spread.astype(BF16)
    for part in range(2):
        lines = dot(chosen[:, part * samples : (part + 1) * samples], tile)
        out_ref[part] = dot(gather, jnp.where(match, lines, 0.0).astype(BF16))


def couplings(lists, base, table, targets, names):
    shape = (2, targets, names * (table.shape[1] // 2))
    vmem = pl.BlockSpec(memory_space=pltpu.VMEM)
    return pl.pallas_call(
        coupling_kernel,
        in_specs=[vmem, pl.BlockSpec(memory_space=pltpu.SMEM), vmem],
        out_specs=vmem,
        out_shape=jax.ShapeDtypeStruct(shape, F32),
        compiler_params=pltpu.CompilerParams(vmem_limit_bytes=16 * MIB),
        cost_estimate=pl.CostEstimate(
            flops=2 * 10**8, bytes_accessed=2 * 2**20, transcendentals=0
        ),
        name="coupling",
    )(lists, base, table)


def translate_kernel(lines_hbm, *refs):
    count = (len(refs) - 5) // 2
    sources, out_hbm = refs[:count], refs[count]
    held, lines, matrix, result, sems = refs[count + 1 :][:count], *refs[2 * count + 1 :]
    targets, samples, width = result.shape
    rhs = width // 2
    copies = [
        pltpu.make_async_copy(source, target, sems.at[place])
        for place, (source, target) in enumerate(zip((lines_hbm, *sources), (lines, *held)))
    ]
    for copy in copies:
        copy.start()
    copies[0].wait()
    columns = matrix.shape[1]
    row = lax.broadcasted_iota(jnp.int32, (samples, columns), 0)
    diagonal = row == lax.broadcasted_iota(jnp.int32, (samples, columns), 1) % samples
    for part in range(2):
        for target in range(targets):
            line = jnp.broadcast_to(lines[part, target : target + 1], diagonal.shape)
            start = (part * targets + target) * samples
            matrix[start : start + samples] = jnp.where(diagonal, line, 0.0).astype(BF16)
    total = None
    start = 0
    for place, source in enumerate(held):
        copies[1 + place].wait()
        stop = start + source.shape[0] * samples
        part = dot(matrix[:, start:stop], source[...].reshape(stop - start, width))
        total = part if total is None else total + part
        start = stop
    half = targets * samples
    real = total[:half, :rhs] - total[half:, rhs:]
    imag = total[:half, rhs:] + total[half:, :rhs]
    result[...] = jnp.concatenate([real, imag], axis=1).astype(BF16).reshape(result.shape)
    pltpu.sync_copy(result, out_hbm)


def translate(lines, sources):
    _, samples, width = sources[0].shape
    _, targets, columns = lines.shape
    shape = (targets, samples, width)
    hbm = pl.BlockSpec(memory_space=pltpu.HBM)
    anywhere = pl.BlockSpec(memory_space=pl.ANY)
    return pl.pallas_call(
        translate_kernel,
        in_specs=[hbm] + [anywhere] * len(sources),
        out_specs=hbm,
        out_shape=pltpu.HBM(shape, BF16),
        scratch_shapes=[
            *[pltpu.VMEM(source.shape, BF16) for source in sources],
            pltpu.VMEM(lines.shape, F32),
            pltpu.VMEM((2 * targets * samples, columns), BF16),
            pltpu.VMEM(shape, BF16),
            pltpu.SemaphoreType.DMA((1 + len(sources),)),
        ],
        compiler_params=pltpu.CompilerParams(vmem_limit_bytes=24 * MIB),
        cost_estimate=pl.CostEstimate(
            flops=10**9, bytes_accessed=2 * MIB, transcendentals=0
        ),
        name="translate",
    )(*in_hbm(lines), *sources)


def near_kernel(first, begun, kept, *refs):
    refs = list(refs)
    listed, starts_ref, blocks_hbm, source_hbm = refs[:4]
    before_hbm = refs[4] if begun else None
    kept_hbm = refs[4 + begun : 4 + begun + kept]
    out_ref = refs[4 + begun + kept]
    kept_refs = refs[5 + begun + kept : 5 + begun + 2 * kept]
    blocks, held, wide, total_ref, sems = refs[5 + begun + 2 * kept :]
    boxes, _, basis, rhs = held.shape
    most = blocks_hbm.shape[0]
    starts = [starts_ref[first, box] for box in range(boxes + 1)]

    def by_box(source, target, turn):
        return [
            pltpu.make_async_copy(
                source.at[box], target.at[box], sems.at[most + turn * boxes + box]
            )
            for box in range(boxes)
        ]

    source_copies = by_box(source_hbm, held, 0)
    before_copies = by_box(before_hbm, total_ref, 1) if begun else []
    out_copies = [] if kept else by_box(total_ref, out_ref, 2)
    kept_copies = [
        pltpu.make_async_copy(kept_hbm[place], kept_refs[place], sems.at[most + 3 * boxes + place])
        for place in range(kept)
    ]
    for copy in source_copies:
        copy.start()

    def block_copy(place):
        block = listed[first, place] // boxes
        return pltpu.make_async_copy(blocks_hbm.at[block], blocks.at[place], sems.at[place])

    def fetch(place, carry):
        block_copy(place).start()
        return carry

    lax.fori_loop(0, starts[boxes], fetch, 0)
    for copy in before_copies + kept_copies:
        copy.start()
    for copy in source_copies:
        copy.wait()
    for place in range(boxes):
        wide[place] = complex_columns(held[place, 0], held[place, 1])

    def landed(place, carry):
        block_copy(place).wait()
        return carry

    lax.fori_loop(0, starts[boxes], landed, 0)
    for copy in before_copies:
        copy.wait()

    def group(box, begin, size):
        left, right = [], []
        for step in range(size):
            place = starts[box] + begin + step
            valid = place < starts[box + 1]
            place = jnp.where(valid, place, 0)
            real, imag = blocks[place, 0], blocks[place, 1]
            real = jnp.where(valid, real, jnp.zeros_like(real))
            imag = jnp.where(valid, imag, jnp.zeros_like(imag))
            left.append(side_by_side(real, imag))
            right.append(wide[jnp.where(valid, listed[first, place] % boxes, 0)])
        return dot(jnp.concatenate(left, axis=1), jnp.concatenate(right, axis=0))

    possible = [(boxes - box, boxes, box + 1)[first] for box in range(boxes)]
    sizes = [min(count, 3 if count < 7 else 4) for count in possible]
    for box in range(boxes):
        part = group(box, 0, sizes[box])
        if begun:
            total_ref[box, 0] += part[:, :rhs]
            total_ref[box, 1] += part[:, rhs:]
        else:
            total_ref[box, 0] = part[:, :rhs]
            total_ref[box, 1] = part[:, rhs:]
    for box in range(boxes):

        def more(index, carry, box=box):
            part = group(box, sizes[box] + GROUP * index, GROUP)
            total_ref[box, 0] += part[:, :rhs]
            total_ref[box, 1] += part[:, rhs:]
            return carry

        rest = starts[box + 1] - starts[box] - sizes[box]
        lax.fori_loop(0, (jnp.maximum(rest, 0) + GROUP - 1) // GROUP, more, 0)
        if out_copies:
            out_copies[box].start()
    for copy in out_copies + kept_copies:
        copy.wait()


def near_slots(ids, used, rank):
    boxes, slots = ids.shape
    total = boxes * slots
    source = ids - (rank - 1) * boxes
    source = jnp.where(jnp.arange(slots) < used[:, None], source, -1).reshape(-1)
    wanted = (source >= 0) & (source // boxes == jnp.arange(3)[:, None])
    earlier = jnp.arange(total)[None, :] < jnp.arange(total)[:, None]
    place = jnp.sum((wanted[:, None, :] & earlier).astype(jnp.int32), axis=2)
    code = jnp.arange(total) * boxes + source % boxes
    chosen = wanted[:, None, :] & (place[:, None, :] == jnp.arange(total)[:, None])
    listed = jnp.sum(jnp.where(chosen, code, 0), axis=2)
    before = jnp.arange(total) // slots < jnp.arange(boxes + 1)[:, None]
    starts = jnp.sum((wanted[:, None, :] & before).astype(jnp.int32), axis=2)
    return listed.astype(jnp.int32), starts.astype(jnp.int32)


def near_field(listed, starts, blocks, source, first, before=None, keep=()):
    boxes, slots, _, basis, _ = blocks.shape
    blocks = blocks.reshape(boxes * slots, *blocks.shape[2:])
    rhs = source.shape[3]
    begun, kept = before is not None, len(keep)
    hbm = pl.BlockSpec(memory_space=pltpu.HBM)
    smem = pl.BlockSpec(memory_space=pltpu.SMEM)
    vmem = pl.BlockSpec(memory_space=pltpu.VMEM)
    shape = (boxes, 2, basis, rhs)
    scratch = [
        pltpu.VMEM(blocks.shape, BF16),
        pltpu.VMEM(source.shape, BF16),
        pltpu.VMEM((boxes, 2 * basis, 2 * rhs), BF16),
        pltpu.VMEM(shape, F32),
        pltpu.SemaphoreType.DMA((boxes * slots + 3 * boxes + kept,)),
    ]
    kernel = functools.partial(near_kernel, first, begun, kept)
    if kept:
        del scratch[3]
        inner = kernel

        def kernel(*refs):
            place = 4 + begun + kept
            inner(*refs[:-1], refs[place], refs[-1])

    return pl.pallas_call(
        kernel,
        in_specs=[smem] * 2
        + [hbm, pl.BlockSpec(memory_space=pl.ANY)]
        + [hbm] * (begun + kept),
        out_specs=[vmem] * (1 + kept) if kept else hbm,
        out_shape=[
            pltpu.VMEM(shape, F32),
            *[pltpu.VMEM(array.shape, array.dtype) for array in keep],
        ]
        if kept
        else pltpu.HBM(shape, F32),
        scratch_shapes=scratch,
        compiler_params=pltpu.CompilerParams(vmem_limit_bytes=32 * MIB),
        cost_estimate=pl.CostEstimate(
            flops=10**11 if first == 2 else 2 * 10**9, bytes_accessed=8 * MIB, transcendentals=0
        ),
        name=("near_low", "near_own", "near_high")[first],
    )(
        listed,
        starts,
        *in_hbm(blocks),
        source if first != 1 else in_hbm(source)[0],
        *in_hbm(*([before] if begun else []), *keep),
    )


def adjoint_kernel(rad_ref, out_hbm, held):
    for box in range(rad_ref.shape[0]):
        held[box] = side_by_side(rad_ref[box, 0].T, rad_ref[box, 1].T)
    pltpu.sync_copy(held, out_hbm)


def adjoint(radiation):
    boxes, _, points, basis = radiation.shape
    return pl.pallas_call(
        adjoint_kernel,
        in_specs=[pl.BlockSpec(memory_space=pltpu.VMEM)],
        out_specs=pl.BlockSpec(memory_space=pltpu.HBM),
        scratch_shapes=[pltpu.VMEM((boxes, basis, 2 * points), BF16)],
        out_shape=pltpu.HBM((boxes, basis, 2 * points), BF16),
        cost_estimate=pl.CostEstimate(
            flops=10**6, bytes_accessed=2 * MIB, transcendentals=0
        ),
        name="adjoint",
    )(radiation)


def down_kernel(phi_ref, near_ref, w_ref, adjoint_ref, *refs):
    bands_ref, received = refs[0], refs[1:-4]
    out_hbm, field, held, sems = refs[-4:]
    boxes, _, width = adjoint_ref.shape
    points = width // 2
    rhs = held.shape[3]
    phi = phi_ref[0]
    phi_size = field.shape[1]
    pairs = [(bands_ref.at[:, phi], field.at[:, phi])]
    for distance, piece in enumerate(received, 1):
        pairs.append((piece, field.at[:, lax.rem(phi + phi_size - distance, phi_size)]))
    copies = [
        pltpu.make_async_copy(source, target, sems.at[boxes + place])
        for place, (source, target) in enumerate(pairs)
    ]
    out_copies = [
        pltpu.make_async_copy(held.at[box], out_hbm.at[box], sems.at[box]) for box in range(boxes)
    ]
    for copy in copies:
        copy.start()
    for copy in copies:
        copy.wait()
    mixed = dot(w_ref[...], field[...].reshape(w_ref.shape[1], 2 * rhs))
    for octant in range(boxes // 2):
        start = 2 * octant * points
        cos_part = mixed[start : start + points]
        sin_part = mixed[start + points : start + 2 * points]
        cos_re, cos_im = cos_part[:, :rhs], cos_part[:, rhs:]
        sin_re, sin_im = sin_part[:, :rhs], sin_part[:, rhs:]
        leaves = (
            (octant, cos_re + sin_im, cos_im - sin_re),
            (boxes - 1 - octant, cos_re - sin_im, cos_im + sin_re),
        )
        for box, real, imag in leaves:
            real, imag = real.astype(BF16), imag.astype(BF16)
            right = jnp.concatenate([side_by_side(real, imag), side_by_side(imag, -real)], axis=0)
            far = dot(adjoint_ref[box], right)
            held[box, 0] = near_ref[box, 0] + far[:, :rhs]
            held[box, 1] = near_ref[box, 1] + far[:, rhs:]
            out_copies[box].start()
    for copy in out_copies:
        copy.wait()


def downward(phi, bands, received, near, weights, radiation_adjoint):
    boxes = near.shape[0]
    anywhere = pl.BlockSpec(memory_space=pl.ANY)
    ready = [
        pltpu.with_memory_space_constraint(array, pltpu.VMEM)
        for array in (near, weights, radiation_adjoint)
    ]
    return pl.pallas_call(
        down_kernel,
        in_specs=[pl.BlockSpec(memory_space=pltpu.SMEM)]
        + [pl.BlockSpec(memory_space=pltpu.VMEM)] * 3
        + [anywhere] * (1 + len(received)),
        out_specs=pl.BlockSpec(memory_space=pltpu.HBM),
        out_shape=jax.ShapeDtypeStruct(near.shape, F32),
        scratch_shapes=[
            pltpu.VMEM(bands.shape, BF16),
            pltpu.VMEM(near.shape, F32),
            pltpu.SemaphoreType.DMA((boxes + 1 + len(received),)),
        ],
        compiler_params=pltpu.CompilerParams(vmem_limit_bytes=32 * MIB),
        cost_estimate=pl.CostEstimate(
            flops=2 * 10**9, bytes_accessed=7 * MIB, transcendentals=0
        ),
        name="downward",
    )(phi, *ready, bands, *received)


def shift(block, axis, step):
    count = lax.axis_size(axis)
    pairs = [(i, i + step) for i in range(count) if 0 <= i + step < count]
    return lax.ppermute(block, axis, pairs)


def lists_of(partners, vector_ids, pair_count):
    used = jnp.arange(partners.shape[1])[None, :] < pair_count[:, None]
    names = jnp.where(used, partners, NOWHERE)
    return jnp.stack([names, vector_ids], axis=2).reshape(-1, 2)


def cross_lines(block):
    every = ("box", "theta", "phi")
    size = lax.axis_size("phi")
    lines = lax.axis_size("box") * lax.axis_size("theta")
    pairs = [(line * size, (line - 1) * size) for line in range(1, lines)]
    crossed = lax.ppermute(block, every, pairs)
    return jnp.where(lax.axis_index("phi") == 0, crossed, block)


def parent_bands(spread, shares):
    axes = ("box", "theta", "phi") if shares == lax.axis_size("box") else ("theta", "phi")
    return lax.all_to_all(spread, axes, split_axis=0, concat_axis=0, tiled=True)


def staged_bands(incoming, shares):
    axes = ("box", "theta") if shares == lax.axis_size("box") else ("theta",)
    phi_size = lax.axis_size("phi")
    phi = lax.axis_index("phi")
    bands = incoming.reshape(-1, phi_size, *incoming.shape[1:])
    bands = lax.all_to_all(bands, axes, split_axis=0, concat_axis=0, tiled=True)
    received = []
    for distance in range(1, phi_size):
        piece = lax.dynamic_index_in_dim(bands, (phi + distance) % phi_size, 1, keepdims=False)
        ring = [(place, (place + distance) % phi_size) for place in range(phi_size)]
        received.append(lax.ppermute(piece, "phi", ring))
    return phi.astype(jnp.int32).reshape(1), bands, received


def translation_lines(lists, translation, shares, per_group):
    operator_total, _, theta_band, phi_band = translation.shape
    rank = lax.axis_index("box")
    if shares < lax.axis_size("box"):
        table = translation.reshape(operator_total, -1)
        base = ((rank - 1) * per_group).astype(jnp.int32).reshape(1)
        return couplings(lists, base, table, per_group, 3 * per_group)
    if shares == 2:
        other = lax.ppermute(lists, "box", [(0, 1), (1, 0)])
        lists = jnp.where(
            rank == 0, jnp.concatenate([lists, other]), jnp.concatenate([other, lists])
        )
    part = theta_band // shares
    table = lax.dynamic_slice_in_dim(translation, rank * part, part, axis=2)
    table = table.reshape(operator_total, -1)
    total = shares * per_group
    return couplings(lists, jnp.zeros((1,), jnp.int32), table, total, total)


def per_device(
    shares,
    up_weights,
    down_weights,
    coeffs,
    near_blocks,
    near_ids,
    near_count,
    radiation,
    partners,
    vector_ids,
    pair_count,
    translation,
):
    every = ("box", "theta", "phi")
    per_group = lax.axis_size("theta") * lax.axis_size("phi")
    low = shift(coeffs, every, 1)
    ahead = cross_lines(coeffs)
    spread = upward(coeffs, radiation, up_weights, shares * per_group)
    radiation_adjoint = adjoint(radiation)
    lists = lists_of(partners, vector_ids, pair_count)
    lines = translation_lines(lists, translation, shares, per_group)
    listed, starts = near_slots(near_ids, near_count, lax.axis_index(every))
    spread, radiation_adjoint = lax.optimization_barrier((spread, radiation_adjoint))
    parents = parent_bands(spread, shares)
    lines, listed, starts, ahead = lax.optimization_barrier((lines, listed, starts, ahead))
    near = near_field(listed, starts, near_blocks, low, 0)
    parents, near, ahead = lax.optimization_barrier((parents, near, ahead))
    phi_size = lax.axis_size("phi")
    high = lax.ppermute(ahead, "phi", [(i, (i - 1) % phi_size) for i in range(phi_size)])
    sources = [parents]
    if shares < lax.axis_size("box"):
        sources = [shift(parents, "box", 1), parents, shift(parents, "box", -1)]
    incoming = translate(lines, sources)
    incoming, near = lax.optimization_barrier((incoming, near))
    phi, bands, received = staged_bands(incoming, shares)
    near = near_field(listed, starts, near_blocks, coeffs, 1, near)
    ready = near_field(
        listed, starts, near_blocks, high, 2, near, keep=(down_weights, radiation_adjoint)
    )
    return downward(phi, bands, received, *ready)


def solution(mesh):
    box_size, theta_size, phi_size = (mesh.shape[axis] for axis in ("box", "theta", "phi"))
    shares = box_size if box_size <= 2 and TU // theta_size % box_size == 0 else 1
    up_weights, down_weights = operators(shares, theta_size, phi_size)
    in_specs = (
        P(),
        P(),
        P(("box", "theta", "phi"), None, None, None),
        P(("box", "theta", "phi"), None, None, None, None),
        P(("box", "theta", "phi"), None),
        P(("box", "theta", "phi")),
        P(("box", "theta", "phi"), None, None, None),
        P("box", None),
        P("box", None),
        P("box"),
        P(None, None, "theta", "phi"),
    )
    out_specs = P(("box", "theta", "phi"), None, None, None)
    mapped = jax.shard_map(
        functools.partial(per_device, shares),
        mesh=mesh,
        in_specs=in_specs,
        out_specs=out_specs,
        check_vma=False,
    )

    def product(*arrays):
        return mapped(jnp.asarray(up_weights), jnp.asarray(down_weights), *arrays)

    return product
```

```python
import functools
import math

import jax
import jax.numpy as jnp
import ml_dtypes
import numpy as np
from jax import lax
from jax.experimental import pallas as pl
from jax.experimental.pallas import tpu as pltpu
from jax.sharding import PartitionSpec as P

TL = 8
PL = 16
TU = 16
PU = 32

WEIGHT_UP = (-0.0546875, 0.8203125, 0.2734375, -0.0390625)
WEIGHT_DOWN = (-0.0390625, 0.2734375, 0.8203125, -0.0546875)
PHASE_SCALE = 1.3

F32 = jnp.float32
BF16 = jnp.bfloat16
MIB = 2**20
GROUP = 2
NOWHERE = -(2**20)


def lagrange(rows, columns, wrap):
    matrix = np.zeros((rows, columns))
    for row in range(rows):
        weights = WEIGHT_UP if row % 2 else WEIGHT_DOWN
        for order in range(4):
            node = row // 2 + row % 2 - 2 + order
            node = node % columns if wrap else min(max(node, 0), columns - 1)
            matrix[row, node] += weights[order]
    return matrix


def split_weights(matrix):
    high = matrix.astype(ml_dtypes.bfloat16)
    low = (matrix - high.astype(np.float64)).astype(ml_dtypes.bfloat16)
    return high, low


def operators(shares, theta_size, phi_size):
    theta_part = TU // theta_size // shares
    order = np.arange(TU * PU).reshape(theta_size, shares, theta_part, phi_size, PU // phi_size)
    order = order.transpose(1, 0, 3, 2, 4).reshape(-1)
    interp = np.kron(lagrange(TU, TL, False), lagrange(PU, PL, True))
    theta = math.pi * (np.arange(TU) + 0.5) / TU
    azimuth = 2.0 * math.pi * (np.arange(PU) + 0.5) / PU
    up, down = [], []
    for octant in range(4):
        sign_x = 2 * (octant % 2) - 1
        sign_y = 2 * (octant // 2 % 2) - 1
        sign_z = 2 * (octant // 4) - 1
        angle = PHASE_SCALE * (
            sign_x * np.sin(theta)[:, None] * np.cos(azimuth)[None]
            + sign_y * np.sin(theta)[:, None] * np.sin(azimuth)[None]
            + sign_z * np.cos(theta)[:, None]
        ).reshape(-1, 1)
        cos_high, cos_low = split_weights((np.cos(angle) * interp)[order])
        sin_high, sin_low = split_weights((np.sin(angle) * interp)[order])
        high = np.concatenate([cos_high, sin_high], axis=1)
        low = np.concatenate([cos_low, sin_low], axis=1)
        up.append(np.concatenate([high, low], axis=0))
        down += [cos_high.T, sin_high.T]
    return np.concatenate(up, axis=1), np.concatenate(down, axis=0)


def in_hbm(*arrays):
    return [pltpu.with_memory_space_constraint(array, pltpu.HBM) for array in arrays]


def dot(a, b):
    return jnp.dot(a, b, preferred_element_type=F32)


def side_by_side(real, imag):
    return jnp.concatenate([real, imag], axis=1)


def complex_columns(real, imag):
    return jnp.concatenate([side_by_side(real, imag), side_by_side(-imag, real)], axis=0)


def up_kernel(x_hbm, rad_hbm, w_hbm, out_hbm, x_ref, rad_ref, w_ref, right, result, sems):
    boxes, _, _, rhs = x_ref.shape
    points = rad_ref.shape[2]
    copies = [
        pltpu.make_async_copy(source, target, sems.at[place])
        for place, (source, target) in enumerate(
            ((x_hbm, x_ref), (rad_hbm, rad_ref), (w_hbm, w_ref))
        )
    ]
    for copy in copies:
        copy.start()
    copies[0].wait()
    copies[1].wait()
    half = boxes // 2
    for octant in range(boxes):
        left = side_by_side(rad_ref[octant, 0], rad_ref[octant, 1])
        straight = dot(left, complex_columns(x_ref[octant, 0], x_ref[octant, 1])).astype(BF16)
        real, imag = straight[:, :rhs], straight[:, rhs:]
        if octant < half:
            swapped = side_by_side(-imag, real)
        else:
            swapped = side_by_side(imag, -real)
        place = octant if octant < half else boxes - 1 - octant
        start = 2 * place * points
        right[octant // half, start : start + points] = straight
        right[octant // half, start + points : start + 2 * points] = swapped
    copies[2].wait()
    total = dot(w_ref[...], right[0]) + dot(w_ref[...], right[1])
    samples = total.shape[0] // 2
    total = total[:samples] + total[samples:]
    result[...] = total.astype(BF16).reshape(result.shape)
    pltpu.sync_copy(result, out_hbm)


def upward(coeffs, radiation, weights, groups):
    boxes, _, basis, rhs = coeffs.shape
    rows, columns = weights.shape
    samples = rows // 2
    hbm = pl.BlockSpec(memory_space=pltpu.HBM)
    return pl.pallas_call(
        up_kernel,
        in_specs=[hbm] * 3,
        out_specs=hbm,
        out_shape=pltpu.HBM((groups, samples // groups, 2 * rhs), BF16),
        scratch_shapes=[
            pltpu.VMEM(coeffs.shape, BF16),
            pltpu.VMEM(radiation.shape, BF16),
            pltpu.VMEM(weights.shape, BF16),
            pltpu.VMEM((2, columns, 2 * rhs), BF16),
            pltpu.VMEM((groups, samples // groups, 2 * rhs), BF16),
            pltpu.SemaphoreType.DMA((3,)),
        ],
        compiler_params=pltpu.CompilerParams(vmem_limit_bytes=32 * MIB),
        cost_estimate=pl.CostEstimate(
            flops=2 * 10**9, bytes_accessed=4 * MIB, transcendentals=0
        ),
        name="upward",
    )(*in_hbm(coeffs, radiation, weights))


def coupling_kernel(lists_ref, base_ref, table_ref, out_ref):
    rows = lists_ref.shape[0]
    samples = table_ref.shape[1] // 2
    _, targets, columns = out_ref.shape
    slots = rows // targets
    selector = (
        lax.broadcasted_iota(jnp.int32, (rows, table_ref.shape[0]), 1) == lists_ref[:, 1:2]
    )
    chosen = dot(selector.astype(BF16), table_ref[...]).astype(BF16)
    wide = lax.broadcasted_iota(jnp.int32, (rows, columns), 1) // samples
    match = wide + base_ref[0] == lists_ref[:, 0:1]
    spread = lax.broadcasted_iota(jnp.int32, (samples, columns), 0) == (
        lax.broadcasted_iota(jnp.int32, (samples, columns), 1) % samples
    )
    gather = (
        lax.broadcasted_iota(jnp.int32, (targets, rows), 1) // slots
        == lax.broadcasted_iota(jnp.int32, (targets, rows), 0)
    ).astype(BF16)
    tile = spread.astype(BF16)
    for part in range(2):
        lines = dot(chosen[:, part * samples : (part + 1) * samples], tile)
        out_ref[part] = dot(gather, jnp.where(match, lines, 0.0).astype(BF16))


def couplings(lists, base, table, targets, names):
    shape = (2, targets, names * (table.shape[1] // 2))
    vmem = pl.BlockSpec(memory_space=pltpu.VMEM)
    return pl.pallas_call(
        coupling_kernel,
        in_specs=[vmem, pl.BlockSpec(memory_space=pltpu.SMEM), vmem],
        out_specs=vmem,
        out_shape=jax.ShapeDtypeStruct(shape, F32),
        compiler_params=pltpu.CompilerParams(vmem_limit_bytes=16 * MIB),
        cost_estimate=pl.CostEstimate(
            flops=2 * 10**8, bytes_accessed=2 * 2**20, transcendentals=0
        ),
        name="coupling",
    )(lists, base, table)


def translate_kernel(lines_hbm, *refs):
    count = (len(refs) - 5) // 2
    sources, out_hbm = refs[:count], refs[count]
    held, lines, matrix, result, sems = refs[count + 1 :][:count], *refs[2 * count + 1 :]
    targets, samples, width = result.shape
    rhs = width // 2
    copies = [
        pltpu.make_async_copy(source, target, sems.at[place])
        for place, (source, target) in enumerate(zip((lines_hbm, *sources), (lines, *held)))
    ]
    for copy in copies:
        copy.start()
    copies[0].wait()
    columns = matrix.shape[1]
    row = lax.broadcasted_iota(jnp.int32, (samples, columns), 0)
    diagonal = row == lax.broadcasted_iota(jnp.int32, (samples, columns), 1) % samples
    for part in range(2):
        for target in range(targets):
            line = jnp.broadcast_to(lines[part, target : target + 1], diagonal.shape)
            start = (part * targets + target) * samples
            matrix[start : start + samples] = jnp.where(diagonal, line, 0.0).astype(BF16)
    total = None
    start = 0
    for place, source in enumerate(held):
        copies[1 + place].wait()
        stop = start + source.shape[0] * samples
        part = dot(matrix[:, start:stop], source[...].reshape(stop - start, width))
        total = part if total is None else total + part
        start = stop
    half = targets * samples
    real = total[:half, :rhs] - total[half:, rhs:]
    imag = total[:half, rhs:] + total[half:, :rhs]
    result[...] = jnp.concatenate([real, imag], axis=1).astype(BF16).reshape(result.shape)
    pltpu.sync_copy(result, out_hbm)


def translate(lines, sources):
    _, samples, width = sources[0].shape
    _, targets, columns = lines.shape
    shape = (targets, samples, width)
    hbm = pl.BlockSpec(memory_space=pltpu.HBM)
    anywhere = pl.BlockSpec(memory_space=pl.ANY)
    return pl.pallas_call(
        translate_kernel,
        in_specs=[hbm] + [anywhere] * len(sources),
        out_specs=hbm,
        out_shape=pltpu.HBM(shape, BF16),
        scratch_shapes=[
            *[pltpu.VMEM(source.shape, BF16) for source in sources],
            pltpu.VMEM(lines.shape, F32),
            pltpu.VMEM((2 * targets * samples, columns), BF16),
            pltpu.VMEM(shape, BF16),
            pltpu.SemaphoreType.DMA((1 + len(sources),)),
        ],
        compiler_params=pltpu.CompilerParams(vmem_limit_bytes=24 * MIB),
        cost_estimate=pl.CostEstimate(
            flops=10**9, bytes_accessed=2 * MIB, transcendentals=0
        ),
        name="translate",
    )(*in_hbm(lines), *sources)


def near_kernel(first, begun, kept, *refs):
    refs = list(refs)
    listed, blocks_hbm, held = refs[:3]
    before_hbm = refs[3] if begun else None
    kept_hbm = refs[3 + begun : 3 + begun + kept]
    out_ref = refs[3 + begun + kept]
    kept_refs = refs[4 + begun + kept : 4 + begun + 2 * kept]
    blocks, wide, total_ref, sems = refs[4 + begun + 2 * kept :]
    boxes, _, basis, rhs = held.shape
    most = blocks_hbm.shape[0]
    starts = [listed[first, most + box] for box in range(boxes + 1)]

    def by_box(source, target, turn):
        return [
            pltpu.make_async_copy(
                source.at[box], target.at[box], sems.at[most + turn * boxes + box]
            )
            for box in range(boxes)
        ]

    before_copies = by_box(before_hbm, total_ref, 0) if begun else []
    out_copies = [] if kept else by_box(total_ref, out_ref, 1)
    kept_copies = [
        pltpu.make_async_copy(kept_hbm[place], kept_refs[place], sems.at[most + 2 * boxes + place])
        for place in range(kept)
    ]

    def block_copy(place):
        block = listed[first, place] // boxes
        return pltpu.make_async_copy(blocks_hbm.at[block], blocks.at[place], sems.at[place])

    def fetch(place, carry):
        block_copy(place).start()
        return carry

    lax.fori_loop(0, starts[boxes], fetch, 0)
    for copy in before_copies + kept_copies:
        copy.start()
    for place in range(boxes):
        wide[place] = complex_columns(held[place, 0], held[place, 1])

    def landed(place, carry):
        block_copy(place).wait()
        return carry

    lax.fori_loop(0, starts[boxes], landed, 0)
    for copy in before_copies:
        copy.wait()

    def group(box, begin, size):
        left, right = [], []
        for step in range(size):
            place = starts[box] + begin + step
            valid = place < starts[box + 1]
            place = jnp.where(valid, place, 0)
            real, imag = blocks[place, 0], blocks[place, 1]
            real = jnp.where(valid, real, jnp.zeros_like(real))
            imag = jnp.where(valid, imag, jnp.zeros_like(imag))
            left.append(side_by_side(real, imag))
            right.append(wide[jnp.where(valid, listed[first, place] % boxes, 0)])
        return dot(jnp.concatenate(left, axis=1), jnp.concatenate(right, axis=0))

    possible = [(boxes - box, boxes, box + 1)[first] for box in range(boxes)]
    sizes = [min(count, 3 if count < 7 else 4) for count in possible]
    for box in range(boxes):
        part = group(box, 0, sizes[box])
        if begun:
            total_ref[box, 0] += part[:, :rhs]
            total_ref[box, 1] += part[:, rhs:]
        else:
            total_ref[box, 0] = part[:, :rhs]
            total_ref[box, 1] = part[:, rhs:]
    for box in range(boxes):

        def more(index, carry, box=box):
            part = group(box, sizes[box] + GROUP * index, GROUP)
            total_ref[box, 0] += part[:, :rhs]
            total_ref[box, 1] += part[:, rhs:]
            return carry

        rest = starts[box + 1] - starts[box] - sizes[box]
        lax.fori_loop(0, (jnp.maximum(rest, 0) + GROUP - 1) // GROUP, more, 0)
        if out_copies:
            out_copies[box].start()
    for copy in out_copies + kept_copies:
        copy.wait()


def near_slots(ids, used, rank):
    boxes, slots = ids.shape
    total = boxes * slots
    source = ids - (rank - 1) * boxes
    source = jnp.where(jnp.arange(slots) < used[:, None], source, -1).reshape(-1)
    wanted = (source >= 0) & (source // boxes == jnp.arange(3)[:, None])
    earlier = jnp.arange(total)[None, :] < jnp.arange(total)[:, None]
    place = jnp.sum((wanted[:, None, :] & earlier).astype(jnp.int32), axis=2)
    code = jnp.arange(total) * boxes + source % boxes
    chosen = wanted[:, None, :] & (place[:, None, :] == jnp.arange(total)[:, None])
    listed = jnp.sum(jnp.where(chosen, code, 0), axis=2)
    before = jnp.arange(total) // slots < jnp.arange(boxes + 1)[:, None]
    starts = jnp.sum((wanted[:, None, :] & before).astype(jnp.int32), axis=2)
    return jnp.concatenate([listed, starts], axis=1).astype(jnp.int32)


def near_field(listed, blocks, source, first, before=None, keep=()):
    boxes, slots, _, basis, _ = blocks.shape
    blocks = blocks.reshape(boxes * slots, *blocks.shape[2:])
    rhs = source.shape[3]
    begun, kept = before is not None, len(keep)
    hbm = pl.BlockSpec(memory_space=pltpu.HBM)
    smem = pl.BlockSpec(memory_space=pltpu.SMEM)
    vmem = pl.BlockSpec(memory_space=pltpu.VMEM)
    shape = (boxes, 2, basis, rhs)
    scratch = [
        pltpu.VMEM(blocks.shape, BF16),
        pltpu.VMEM((boxes, 2 * basis, 2 * rhs), BF16),
        pltpu.VMEM(shape, F32),
        pltpu.SemaphoreType.DMA((boxes * slots + 2 * boxes + kept,)),
    ]
    kernel = functools.partial(near_kernel, first, begun, kept)
    if kept:
        del scratch[2]
        inner = kernel

        def kernel(*refs):
            place = 3 + begun + kept
            inner(*refs[:-1], refs[place], refs[-1])

    return pl.pallas_call(
        kernel,
        in_specs=[smem, hbm, vmem] + [hbm] * (begun + kept),
        out_specs=[vmem] * (1 + kept) if kept else hbm,
        out_shape=[
            pltpu.VMEM(shape, F32),
            *[pltpu.VMEM(array.shape, array.dtype) for array in keep],
        ]
        if kept
        else pltpu.HBM(shape, F32),
        scratch_shapes=scratch,
        compiler_params=pltpu.CompilerParams(vmem_limit_bytes=32 * MIB),
        cost_estimate=pl.CostEstimate(
            flops=10**11 if first == 2 else 2 * 10**9, bytes_accessed=8 * MIB, transcendentals=0
        ),
        name=("near_low", "near_own", "near_high")[first],
    )(
        listed,
        *in_hbm(blocks),
        source,
        *in_hbm(*([before] if begun else []), *keep),
    )


def adjoint_kernel(rad_ref, out_hbm, held):
    for box in range(rad_ref.shape[0]):
        held[box] = side_by_side(rad_ref[box, 0].T, rad_ref[box, 1].T)
    pltpu.sync_copy(held, out_hbm)


def adjoint(radiation):
    boxes, _, points, basis = radiation.shape
    return pl.pallas_call(
        adjoint_kernel,
        in_specs=[pl.BlockSpec(memory_space=pltpu.VMEM)],
        out_specs=pl.BlockSpec(memory_space=pltpu.HBM),
        scratch_shapes=[pltpu.VMEM((boxes, basis, 2 * points), BF16)],
        out_shape=pltpu.HBM((boxes, basis, 2 * points), BF16),
        cost_estimate=pl.CostEstimate(
            flops=10**6, bytes_accessed=2 * MIB, transcendentals=0
        ),
        name="adjoint",
    )(radiation)


def down_kernel(phi_ref, near_ref, before_ref, w_ref, adjoint_ref, *refs):
    bands_ref, received = refs[0], refs[1:-4]
    out_hbm, field, held, sems = refs[-4:]
    boxes, _, width = adjoint_ref.shape
    points = width // 2
    rhs = held.shape[3]
    phi = phi_ref[0]
    phi_size = field.shape[1]
    pairs = [(bands_ref.at[:, phi], field.at[:, phi])]
    for distance, piece in enumerate(received, 1):
        pairs.append((piece, field.at[:, lax.rem(phi + phi_size - distance, phi_size)]))
    copies = [
        pltpu.make_async_copy(source, target, sems.at[boxes + place])
        for place, (source, target) in enumerate(pairs)
    ]
    out_copies = [
        pltpu.make_async_copy(held.at[box], out_hbm.at[box], sems.at[box]) for box in range(boxes)
    ]
    for copy in copies:
        copy.start()
    for copy in copies:
        copy.wait()
    mixed = dot(w_ref[...], field[...].reshape(w_ref.shape[1], 2 * rhs))
    for octant in range(boxes // 2):
        start = 2 * octant * points
        cos_part = mixed[start : start + points]
        sin_part = mixed[start + points : start + 2 * points]
        cos_re, cos_im = cos_part[:, :rhs], cos_part[:, rhs:]
        sin_re, sin_im = sin_part[:, :rhs], sin_part[:, rhs:]
        leaves = (
            (octant, cos_re + sin_im, cos_im - sin_re),
            (boxes - 1 - octant, cos_re - sin_im, cos_im + sin_re),
        )
        for box, real, imag in leaves:
            real, imag = real.astype(BF16), imag.astype(BF16)
            right = jnp.concatenate([side_by_side(real, imag), side_by_side(imag, -real)], axis=0)
            far = dot(adjoint_ref[box], right)
            held[box, 0] = near_ref[box, 0] + before_ref[box, 0] + far[:, :rhs]
            held[box, 1] = near_ref[box, 1] + before_ref[box, 1] + far[:, rhs:]
            out_copies[box].start()
    for copy in out_copies:
        copy.wait()


def downward(phi, bands, received, near, before, weights, radiation_adjoint):
    boxes = near.shape[0]
    anywhere = pl.BlockSpec(memory_space=pl.ANY)
    ready = [
        pltpu.with_memory_space_constraint(array, pltpu.VMEM)
        for array in (near, before, weights, radiation_adjoint)
    ]
    return pl.pallas_call(
        down_kernel,
        in_specs=[pl.BlockSpec(memory_space=pltpu.SMEM)]
        + [pl.BlockSpec(memory_space=pltpu.VMEM)] * 4
        + [anywhere] * (1 + len(received)),
        out_specs=pl.BlockSpec(memory_space=pltpu.HBM),
        out_shape=jax.ShapeDtypeStruct(near.shape, F32),
        scratch_shapes=[
            pltpu.VMEM(bands.shape, BF16),
            pltpu.VMEM(near.shape, F32),
            pltpu.SemaphoreType.DMA((boxes + 1 + len(received),)),
        ],
        compiler_params=pltpu.CompilerParams(vmem_limit_bytes=32 * MIB),
        cost_estimate=pl.CostEstimate(
            flops=2 * 10**9, bytes_accessed=7 * MIB, transcendentals=0
        ),
        name="downward",
    )(phi, *ready, bands, *received)


def shift(block, axis, step):
    count = lax.axis_size(axis)
    pairs = [(i, i + step) for i in range(count) if 0 <= i + step < count]
    return lax.ppermute(block, axis, pairs)


def lists_of(partners, vector_ids, pair_count):
    used = jnp.arange(partners.shape[1])[None, :] < pair_count[:, None]
    names = jnp.where(used, partners, NOWHERE)
    return jnp.stack([names, vector_ids], axis=2).reshape(-1, 2)


def parent_bands(spread, shares):
    axes = ("box", "theta", "phi") if shares == lax.axis_size("box") else ("theta", "phi")
    return lax.all_to_all(spread, axes, split_axis=0, concat_axis=0, tiled=True)


def staged_bands(incoming, shares):
    axes = ("box", "theta") if shares == lax.axis_size("box") else ("theta",)
    phi_size = lax.axis_size("phi")
    phi = lax.axis_index("phi")
    bands = incoming.reshape(-1, phi_size, *incoming.shape[1:])
    bands = lax.all_to_all(bands, axes, split_axis=0, concat_axis=0, tiled=True)
    received = []
    for distance in range(1, phi_size):
        piece = lax.dynamic_index_in_dim(bands, (phi + distance) % phi_size, 1, keepdims=False)
        ring = [(place, (place + distance) % phi_size) for place in range(phi_size)]
        received.append(lax.ppermute(piece, "phi", ring))
    return phi.astype(jnp.int32).reshape(1), bands, received


def translation_lines(lists, translation, shares, per_group):
    operator_total, _, theta_band, phi_band = translation.shape
    rank = lax.axis_index("box")
    if shares < lax.axis_size("box"):
        table = translation.reshape(operator_total, -1)
        base = ((rank - 1) * per_group).astype(jnp.int32).reshape(1)
        return couplings(lists, base, table, per_group, 3 * per_group)
    if shares == 2:
        other = lax.ppermute(lists, "box", [(0, 1), (1, 0)])
        lists = jnp.where(
            rank == 0, jnp.concatenate([lists, other]), jnp.concatenate([other, lists])
        )
    part = theta_band // shares
    table = lax.dynamic_slice_in_dim(translation, rank * part, part, axis=2)
    table = table.reshape(operator_total, -1)
    total = shares * per_group
    return couplings(lists, jnp.zeros((1,), jnp.int32), table, total, total)


def per_device(
    shares,
    up_weights,
    down_weights,
    coeffs,
    near_blocks,
    near_ids,
    near_count,
    radiation,
    partners,
    vector_ids,
    pair_count,
    translation,
):
    every = ("box", "theta", "phi")
    per_group = lax.axis_size("theta") * lax.axis_size("phi")
    low = shift(coeffs, every, 1)
    spread = upward(coeffs, radiation, up_weights, shares * per_group)
    radiation_adjoint = adjoint(radiation)
    lists = lists_of(partners, vector_ids, pair_count)
    spread, lists = lax.optimization_barrier((spread, lists))
    lines = translation_lines(lists, translation, shares, per_group)
    listed = near_slots(near_ids, near_count, lax.axis_index(every))
    spread, lines, radiation_adjoint, listed = lax.optimization_barrier(
        (spread, lines, radiation_adjoint, listed)
    )
    parents = parent_bands(spread, shares)
    near = near_field(listed, near_blocks, low, 0)
    near, late = lax.optimization_barrier((near, coeffs))
    high = shift(late, every, -1)
    parents, near = lax.optimization_barrier((parents, near))
    sources = [parents]
    if shares < lax.axis_size("box"):
        sources = [shift(parents, "box", 1), parents, shift(parents, "box", -1)]
    incoming = translate(lines, sources)
    incoming, near = lax.optimization_barrier((incoming, near))
    phi, bands, received = staged_bands(incoming, shares)
    near = near_field(listed, near_blocks, coeffs, 1, near)
    ready = near_field(
        listed, near_blocks, high, 2, keep=(near, down_weights, radiation_adjoint)
    )
    return downward(phi, bands, received, *ready)


def solution(mesh):
    box_size, theta_size, phi_size = (mesh.shape[axis] for axis in ("box", "theta", "phi"))
    shares = box_size if box_size <= 2 and TU // theta_size % box_size == 0 else 1
    up_weights, down_weights = operators(shares, theta_size, phi_size)
    in_specs = (
        P(),
        P(),
        P(("box", "theta", "phi"), None, None, None),
        P(("box", "theta", "phi"), None, None, None, None),
        P(("box", "theta", "phi"), None),
        P(("box", "theta", "phi")),
        P(("box", "theta", "phi"), None, None, None),
        P("box", None),
        P("box", None),
        P("box"),
        P(None, None, "theta", "phi"),
    )
    out_specs = P(("box", "theta", "phi"), None, None, None)
    mapped = jax.shard_map(
        functools.partial(per_device, shares),
        mesh=mesh,
        in_specs=in_specs,
        out_specs=out_specs,
        check_vma=False,
    )

    def product(*arrays):
        return mapped(jnp.asarray(up_weights), jnp.asarray(down_weights), *arrays)

    return product
```

```python
import functools
import math

import jax
import jax.numpy as jnp
import ml_dtypes
import numpy as np
from jax import lax
from jax.experimental import pallas as pl
from jax.experimental.pallas import tpu as pltpu
from jax.sharding import PartitionSpec as P

TL = 8
PL = 16
TU = 16
PU = 32

WEIGHT_UP = (-0.0546875, 0.8203125, 0.2734375, -0.0390625)
WEIGHT_DOWN = (-0.0390625, 0.2734375, 0.8203125, -0.0546875)
PHASE_SCALE = 1.3

F32 = jnp.float32
BF16 = jnp.bfloat16
MIB = 2**20
GROUP = 2
NOWHERE = -(2**20)


def lagrange(rows, columns, wrap):
    matrix = np.zeros((rows, columns))
    for row in range(rows):
        weights = WEIGHT_UP if row % 2 else WEIGHT_DOWN
        for order in range(4):
            node = row // 2 + row % 2 - 2 + order
            node = node % columns if wrap else min(max(node, 0), columns - 1)
            matrix[row, node] += weights[order]
    return matrix


def split_weights(matrix):
    high = matrix.astype(ml_dtypes.bfloat16)
    low = (matrix - high.astype(np.float64)).astype(ml_dtypes.bfloat16)
    return high, low


def operators(shares, theta_size, phi_size):
    theta_part = TU // theta_size // shares
    order = np.arange(TU * PU).reshape(theta_size, shares, theta_part, phi_size, PU // phi_size)
    order = order.transpose(1, 0, 3, 2, 4).reshape(-1)
    interp = np.kron(lagrange(TU, TL, False), lagrange(PU, PL, True))
    theta = math.pi * (np.arange(TU) + 0.5) / TU
    azimuth = 2.0 * math.pi * (np.arange(PU) + 0.5) / PU
    up, down = [], []
    for octant in range(4):
        sign_x = 2 * (octant % 2) - 1
        sign_y = 2 * (octant // 2 % 2) - 1
        sign_z = 2 * (octant // 4) - 1
        angle = PHASE_SCALE * (
            sign_x * np.sin(theta)[:, None] * np.cos(azimuth)[None]
            + sign_y * np.sin(theta)[:, None] * np.sin(azimuth)[None]
            + sign_z * np.cos(theta)[:, None]
        ).reshape(-1, 1)
        cos_high, cos_low = split_weights((np.cos(angle) * interp)[order])
        sin_high, sin_low = split_weights((np.sin(angle) * interp)[order])
        high = np.concatenate([cos_high, sin_high], axis=1)
        low = np.concatenate([cos_low, sin_low], axis=1)
        up.append(np.concatenate([high, low], axis=0))
        down += [cos_high.T, sin_high.T]
    down = np.concatenate(down, axis=0)
    down = down.reshape(down.shape[0], shares * theta_size, phi_size, -1).transpose(2, 0, 1, 3)
    return np.concatenate(up, axis=1), down.reshape(phi_size, down.shape[1], -1)


def in_hbm(*arrays):
    return [pltpu.with_memory_space_constraint(array, pltpu.HBM) for array in arrays]


def dot(a, b):
    return jnp.dot(a, b, preferred_element_type=F32)


def side_by_side(real, imag):
    return jnp.concatenate([real, imag], axis=1)


def complex_columns(real, imag):
    return jnp.concatenate([side_by_side(real, imag), side_by_side(-imag, real)], axis=0)


def up_kernel(x_hbm, rad_hbm, w_hbm, out_hbm, x_ref, rad_ref, w_ref, right, result, sems):
    boxes, _, _, rhs = x_ref.shape
    points = rad_ref.shape[2]
    copies = [
        pltpu.make_async_copy(source, target, sems.at[place])
        for place, (source, target) in enumerate(
            ((x_hbm, x_ref), (rad_hbm, rad_ref), (w_hbm, w_ref))
        )
    ]
    for copy in copies:
        copy.start()
    copies[0].wait()
    copies[1].wait()
    half = boxes // 2
    for octant in range(boxes):
        left = side_by_side(rad_ref[octant, 0], rad_ref[octant, 1])
        straight = dot(left, complex_columns(x_ref[octant, 0], x_ref[octant, 1])).astype(BF16)
        real, imag = straight[:, :rhs], straight[:, rhs:]
        if octant < half:
            swapped = side_by_side(-imag, real)
        else:
            swapped = side_by_side(imag, -real)
        place = octant if octant < half else boxes - 1 - octant
        start = 2 * place * points
        right[octant // half, start : start + points] = straight
        right[octant // half, start + points : start + 2 * points] = swapped
    copies[2].wait()
    total = dot(w_ref[...], right[0]) + dot(w_ref[...], right[1])
    samples = total.shape[0] // 2
    total = total[:samples] + total[samples:]
    result[...] = total.astype(BF16).reshape(result.shape)
    pltpu.sync_copy(result, out_hbm)


def upward(coeffs, radiation, weights, groups):
    boxes, _, basis, rhs = coeffs.shape
    rows, columns = weights.shape
    samples = rows // 2
    hbm = pl.BlockSpec(memory_space=pltpu.HBM)
    return pl.pallas_call(
        up_kernel,
        in_specs=[hbm] * 3,
        out_specs=hbm,
        out_shape=pltpu.HBM((groups, samples // groups, 2 * rhs), BF16),
        scratch_shapes=[
            pltpu.VMEM(coeffs.shape, BF16),
            pltpu.VMEM(radiation.shape, BF16),
            pltpu.VMEM(weights.shape, BF16),
            pltpu.VMEM((2, columns, 2 * rhs), BF16),
            pltpu.VMEM((groups, samples // groups, 2 * rhs), BF16),
            pltpu.SemaphoreType.DMA((3,)),
        ],
        compiler_params=pltpu.CompilerParams(vmem_limit_bytes=32 * MIB),
        cost_estimate=pl.CostEstimate(
            flops=2 * 10**9, bytes_accessed=4 * MIB, transcendentals=0
        ),
        name="upward",
    )(*in_hbm(coeffs, radiation, weights))


def coupling_kernel(lists_ref, base_ref, table_ref, out_ref):
    rows = lists_ref.shape[0]
    samples = table_ref.shape[1] // 2
    _, targets, columns = out_ref.shape
    slots = rows // targets
    selector = (
        lax.broadcasted_iota(jnp.int32, (rows, table_ref.shape[0]), 1) == lists_ref[:, 1:2]
    )
    chosen = dot(selector.astype(BF16), table_ref[...]).astype(BF16)
    wide = lax.broadcasted_iota(jnp.int32, (rows, columns), 1) // samples
    match = wide + base_ref[0] == lists_ref[:, 0:1]
    spread = lax.broadcasted_iota(jnp.int32, (samples, columns), 0) == (
        lax.broadcasted_iota(jnp.int32, (samples, columns), 1) % samples
    )
    gather = (
        lax.broadcasted_iota(jnp.int32, (targets, rows), 1) // slots
        == lax.broadcasted_iota(jnp.int32, (targets, rows), 0)
    ).astype(BF16)
    tile = spread.astype(BF16)
    for part in range(2):
        lines = dot(chosen[:, part * samples : (part + 1) * samples], tile)
        out_ref[part] = dot(gather, jnp.where(match, lines, 0.0).astype(BF16))


def couplings(lists, base, table, targets, names):
    shape = (2, targets, names * (table.shape[1] // 2))
    vmem = pl.BlockSpec(memory_space=pltpu.VMEM)
    return pl.pallas_call(
        coupling_kernel,
        in_specs=[vmem, pl.BlockSpec(memory_space=pltpu.SMEM), vmem],
        out_specs=vmem,
        out_shape=jax.ShapeDtypeStruct(shape, F32),
        compiler_params=pltpu.CompilerParams(vmem_limit_bytes=16 * MIB),
        cost_estimate=pl.CostEstimate(
            flops=2 * 10**8, bytes_accessed=2 * 2**20, transcendentals=0
        ),
        name="coupling",
    )(lists, base, table)


def translate_kernel(lines_hbm, *refs):
    count = (len(refs) - 5) // 2
    sources, out_hbm = refs[:count], refs[count]
    held, lines, matrix, result, sems = refs[count + 1 :][:count], *refs[2 * count + 1 :]
    targets, samples, width = result.shape
    rhs = width // 2
    copies = [
        pltpu.make_async_copy(source, target, sems.at[place])
        for place, (source, target) in enumerate(zip((lines_hbm, *sources), (lines, *held)))
    ]
    for copy in copies:
        copy.start()
    copies[0].wait()
    columns = matrix.shape[1]
    row = lax.broadcasted_iota(jnp.int32, (samples, columns), 0)
    diagonal = row == lax.broadcasted_iota(jnp.int32, (samples, columns), 1) % samples
    for part in range(2):
        for target in range(targets):
            line = jnp.broadcast_to(lines[part, target : target + 1], diagonal.shape)
            start = (part * targets + target) * samples
            matrix[start : start + samples] = jnp.where(diagonal, line, 0.0).astype(BF16)
    total = None
    start = 0
    for place, source in enumerate(held):
        copies[1 + place].wait()
        stop = start + source.shape[0] * samples
        part = dot(matrix[:, start:stop], source[...].reshape(stop - start, width))
        total = part if total is None else total + part
        start = stop
    half = targets * samples
    real = total[:half, :rhs] - total[half:, rhs:]
    imag = total[:half, rhs:] + total[half:, :rhs]
    result[...] = jnp.concatenate([real, imag], axis=1).astype(BF16).reshape(result.shape)
    pltpu.sync_copy(result, out_hbm)


def translate(lines, sources):
    _, samples, width = sources[0].shape
    _, targets, columns = lines.shape
    shape = (targets, samples, width)
    hbm = pl.BlockSpec(memory_space=pltpu.HBM)
    anywhere = pl.BlockSpec(memory_space=pl.ANY)
    return pl.pallas_call(
        translate_kernel,
        in_specs=[hbm] + [anywhere] * len(sources),
        out_specs=hbm,
        out_shape=pltpu.HBM(shape, BF16),
        scratch_shapes=[
            *[pltpu.VMEM(source.shape, BF16) for source in sources],
            pltpu.VMEM(lines.shape, F32),
            pltpu.VMEM((2 * targets * samples, columns), BF16),
            pltpu.VMEM(shape, BF16),
            pltpu.SemaphoreType.DMA((1 + len(sources),)),
        ],
        compiler_params=pltpu.CompilerParams(vmem_limit_bytes=24 * MIB),
        cost_estimate=pl.CostEstimate(
            flops=10**9, bytes_accessed=2 * MIB, transcendentals=0
        ),
        name="translate",
    )(*in_hbm(lines), *sources)


def near_kernel(first, begun, kept, *refs):
    refs = list(refs)
    listed, blocks_hbm, held = refs[:3]
    before_hbm = refs[3] if begun else None
    kept_hbm = refs[3 + begun : 3 + begun + kept]
    out_ref = refs[3 + begun + kept]
    kept_refs = refs[4 + begun + kept : 4 + begun + 2 * kept]
    blocks, wide, total_ref, *earlier, sems = refs[4 + begun + 2 * kept :]
    held_back = begun and kept
    boxes, _, basis, rhs = held.shape
    most = blocks_hbm.shape[0]
    starts = [listed[first, most + box] for box in range(boxes + 1)]

    def by_box(source, target, turn):
        return [
            pltpu.make_async_copy(
                source.at[box], target.at[box], sems.at[most + turn * boxes + box]
            )
            for box in range(boxes)
        ]

    before_copies = by_box(before_hbm, earlier[0] if held_back else total_ref, 0) if begun else []
    out_copies = [] if kept else by_box(total_ref, out_ref, 1)
    kept_copies = [
        pltpu.make_async_copy(kept_hbm[place], kept_refs[place], sems.at[most + 2 * boxes + place])
        for place in range(kept)
    ]

    def block_copy(place):
        block = listed[first, place] // boxes
        return pltpu.make_async_copy(blocks_hbm.at[block], blocks.at[place], sems.at[place])

    def fetch(place, carry):
        block_copy(place).start()
        return carry

    lax.fori_loop(0, starts[boxes], fetch, 0)
    for copy in before_copies + kept_copies:
        copy.start()
    for place in range(boxes):
        wide[place] = complex_columns(held[place, 0], held[place, 1])

    def landed(place, carry):
        block_copy(place).wait()
        return carry

    lax.fori_loop(0, starts[boxes], landed, 0)
    if not held_back:
        for copy in before_copies:
            copy.wait()

    def group(box, begin, size):
        left, right = [], []
        for step in range(size):
            place = starts[box] + begin + step
            valid = place < starts[box + 1]
            place = jnp.where(valid, place, 0)
            real, imag = blocks[place, 0], blocks[place, 1]
            real = jnp.where(valid, real, jnp.zeros_like(real))
            imag = jnp.where(valid, imag, jnp.zeros_like(imag))
            left.append(side_by_side(real, imag))
            right.append(wide[jnp.where(valid, listed[first, place] % boxes, 0)])
        return dot(jnp.concatenate(left, axis=1), jnp.concatenate(right, axis=0))

    possible = [(boxes - box, boxes, box + 1)[first] for box in range(boxes)]
    sizes = [min(count, 3 if count < 7 else 4) for count in possible]
    for box in range(boxes):
        part = group(box, 0, sizes[box])
        if begun and not held_back:
            total_ref[box, 0] += part[:, :rhs]
            total_ref[box, 1] += part[:, rhs:]
        else:
            total_ref[box, 0] = part[:, :rhs]
            total_ref[box, 1] = part[:, rhs:]
    for box in range(boxes):

        def more(index, carry, box=box):
            part = group(box, sizes[box] + GROUP * index, GROUP)
            total_ref[box, 0] += part[:, :rhs]
            total_ref[box, 1] += part[:, rhs:]
            return carry

        rest = starts[box + 1] - starts[box] - sizes[box]
        lax.fori_loop(0, (jnp.maximum(rest, 0) + GROUP - 1) // GROUP, more, 0)
        if out_copies:
            out_copies[box].start()
    for copy in out_copies + kept_copies:
        copy.wait()
    if held_back:
        for box in range(boxes):
            before_copies[box].wait()
            total_ref[box] += earlier[0][box]


def near_slots(ids, used, rank):
    boxes, slots = ids.shape
    total = boxes * slots
    source = ids - (rank - 1) * boxes
    source = jnp.where(jnp.arange(slots) < used[:, None], source, -1).reshape(-1)
    wanted = (source >= 0) & (source // boxes == jnp.arange(3)[:, None])
    earlier = jnp.arange(total)[None, :] < jnp.arange(total)[:, None]
    place = jnp.sum((wanted[:, None, :] & earlier).astype(jnp.int32), axis=2)
    code = jnp.arange(total) * boxes + source % boxes
    chosen = wanted[:, None, :] & (place[:, None, :] == jnp.arange(total)[:, None])
    listed = jnp.sum(jnp.where(chosen, code, 0), axis=2)
    before = jnp.arange(total) // slots < jnp.arange(boxes + 1)[:, None]
    starts = jnp.sum((wanted[:, None, :] & before).astype(jnp.int32), axis=2)
    return jnp.concatenate([listed, starts], axis=1).astype(jnp.int32)


def near_field(listed, blocks, source, first, before=None, keep=()):
    boxes, slots, _, basis, _ = blocks.shape
    blocks = blocks.reshape(boxes * slots, *blocks.shape[2:])
    rhs = source.shape[3]
    begun, kept = before is not None, len(keep)
    hbm = pl.BlockSpec(memory_space=pltpu.HBM)
    smem = pl.BlockSpec(memory_space=pltpu.SMEM)
    vmem = pl.BlockSpec(memory_space=pltpu.VMEM)
    shape = (boxes, 2, basis, rhs)
    scratch = [
        pltpu.VMEM(blocks.shape, BF16),
        pltpu.VMEM((boxes, 2 * basis, 2 * rhs), BF16),
        pltpu.VMEM(shape, F32),
        pltpu.SemaphoreType.DMA((boxes * slots + 2 * boxes + kept,)),
    ]
    kernel = functools.partial(near_kernel, first, begun, kept)
    if kept:
        del scratch[2]
        if begun:
            scratch.insert(2, pltpu.VMEM(shape, F32))
        inner = kernel

        def kernel(*refs):
            place, tail = 3 + begun + kept, 1 + begun
            inner(*refs[:-tail], refs[place], *refs[-tail:])

    return pl.pallas_call(
        kernel,
        in_specs=[smem, hbm, vmem] + [hbm] * (begun + kept),
        out_specs=[vmem] * (1 + kept) if kept else hbm,
        out_shape=[
            pltpu.VMEM(shape, F32),
            *[pltpu.VMEM(array.shape, array.dtype) for array in keep],
        ]
        if kept
        else pltpu.HBM(shape, F32),
        scratch_shapes=scratch,
        compiler_params=pltpu.CompilerParams(vmem_limit_bytes=32 * MIB),
        cost_estimate=pl.CostEstimate(
            flops=10**11 if first == 2 else 2 * 10**9, bytes_accessed=8 * MIB, transcendentals=0
        ),
        name=("near_low", "near_own", "near_high")[first],
    )(
        listed,
        *in_hbm(blocks),
        source,
        *in_hbm(*([before] if begun else []), *keep),
    )


def adjoint_kernel(rad_ref, out_hbm, held):
    for box in range(rad_ref.shape[0]):
        held[box] = side_by_side(rad_ref[box, 0].T, rad_ref[box, 1].T)
    pltpu.sync_copy(held, out_hbm)


def adjoint(radiation):
    boxes, _, points, basis = radiation.shape
    return pl.pallas_call(
        adjoint_kernel,
        in_specs=[pl.BlockSpec(memory_space=pltpu.VMEM)],
        out_specs=pl.BlockSpec(memory_space=pltpu.HBM),
        scratch_shapes=[pltpu.VMEM((boxes, basis, 2 * points), BF16)],
        out_shape=pltpu.HBM((boxes, basis, 2 * points), BF16),
        cost_estimate=pl.CostEstimate(
            flops=10**6, bytes_accessed=2 * MIB, transcendentals=0
        ),
        name="adjoint",
    )(radiation)


def down_kernel(phi_ref, near_ref, w_ref, adjoint_ref, *refs):
    pieces, (out_hbm, held, sems) = refs[:-3], refs[-3:]
    boxes, _, width = adjoint_ref.shape
    points = width // 2
    rhs = held.shape[3]
    phi = phi_ref[0]
    phi_size = len(pieces)
    out_copies = [
        pltpu.make_async_copy(held.at[box], out_hbm.at[box], sems.at[box]) for box in range(boxes)
    ]
    places = [lax.rem(phi + phi_size - distance, phi_size) for distance in range(phi_size)]
    left = jnp.concatenate([w_ref[place] for place in places], axis=1)
    right = jnp.concatenate([piece[...].reshape(-1, 2 * rhs) for piece in pieces], axis=0)
    mixed = dot(left, right)
    for octant in range(boxes // 2):
        start = 2 * octant * points
        cos_part = mixed[start : start + points]
        sin_part = mixed[start + points : start + 2 * points]
        cos_re, cos_im = cos_part[:, :rhs], cos_part[:, rhs:]
        sin_re, sin_im = sin_part[:, :rhs], sin_part[:, rhs:]
        leaves = (
            (octant, cos_re + sin_im, cos_im - sin_re),
            (boxes - 1 - octant, cos_re - sin_im, cos_im + sin_re),
        )
        for box, real, imag in leaves:
            real, imag = real.astype(BF16), imag.astype(BF16)
            right = jnp.concatenate([side_by_side(real, imag), side_by_side(imag, -real)], axis=0)
            far = dot(adjoint_ref[box], right)
            held[box, 0] = near_ref[box, 0] + far[:, :rhs]
            held[box, 1] = near_ref[box, 1] + far[:, rhs:]
            out_copies[box].start()
    for copy in out_copies:
        copy.wait()


def downward(phi, pieces, near, weights, radiation_adjoint):
    boxes = near.shape[0]
    vmem = pl.BlockSpec(memory_space=pltpu.VMEM)
    ready = [
        pltpu.with_memory_space_constraint(array, pltpu.VMEM)
        for array in (near, weights, radiation_adjoint)
    ]
    return pl.pallas_call(
        down_kernel,
        in_specs=[pl.BlockSpec(memory_space=pltpu.SMEM)] + [vmem] * (3 + len(pieces)),
        out_specs=pl.BlockSpec(memory_space=pltpu.HBM),
        out_shape=jax.ShapeDtypeStruct(near.shape, F32),
        scratch_shapes=[
            pltpu.VMEM(near.shape, F32),
            pltpu.SemaphoreType.DMA((boxes,)),
        ],
        compiler_params=pltpu.CompilerParams(vmem_limit_bytes=32 * MIB),
        cost_estimate=pl.CostEstimate(
            flops=2 * 10**9, bytes_accessed=7 * MIB, transcendentals=0
        ),
        name="downward",
    )(phi, *ready, *pieces)


def shift(block, axis, step):
    count = lax.axis_size(axis)
    pairs = [(i, i + step) for i in range(count) if 0 <= i + step < count]
    return lax.ppermute(block, axis, pairs)


def lists_of(partners, vector_ids, pair_count):
    used = jnp.arange(partners.shape[1])[None, :] < pair_count[:, None]
    names = jnp.where(used, partners, NOWHERE)
    return jnp.stack([names, vector_ids], axis=2).reshape(-1, 2)


def parent_bands(spread, shares):
    axes = ("box", "theta", "phi") if shares == lax.axis_size("box") else ("theta", "phi")
    return lax.all_to_all(spread, axes, split_axis=0, concat_axis=0, tiled=True)


def staged_bands(incoming, shares):
    axes = ("box", "theta") if shares == lax.axis_size("box") else ("theta",)
    phi_size = lax.axis_size("phi")
    phi = lax.axis_index("phi")
    bands = incoming.reshape(-1, phi_size, *incoming.shape[1:])
    bands = lax.all_to_all(bands, axes, split_axis=0, concat_axis=0, tiled=True)
    received = []
    for distance in range(phi_size):
        piece = lax.dynamic_index_in_dim(bands, (phi + distance) % phi_size, 1, keepdims=False)
        if distance:
            ring = [(place, (place + distance) % phi_size) for place in range(phi_size)]
            piece = lax.ppermute(piece, "phi", ring)
        received.append(piece)
    return phi.astype(jnp.int32).reshape(1), received


def translation_lines(lists, translation, shares, per_group):
    operator_total, _, theta_band, phi_band = translation.shape
    rank = lax.axis_index("box")
    if shares < lax.axis_size("box"):
        table = translation.reshape(operator_total, -1)
        base = ((rank - 1) * per_group).astype(jnp.int32).reshape(1)
        return couplings(lists, base, table, per_group, 3 * per_group)
    if shares == 2:
        other = lax.ppermute(lists, "box", [(0, 1), (1, 0)])
        lists = jnp.where(
            rank == 0, jnp.concatenate([lists, other]), jnp.concatenate([other, lists])
        )
    part = theta_band // shares
    table = lax.dynamic_slice_in_dim(translation, rank * part, part, axis=2)
    table = table.reshape(operator_total, -1)
    total = shares * per_group
    return couplings(lists, jnp.zeros((1,), jnp.int32), table, total, total)


def per_device(
    shares,
    up_weights,
    down_weights,
    coeffs,
    near_blocks,
    near_ids,
    near_count,
    radiation,
    partners,
    vector_ids,
    pair_count,
    translation,
):
    every = ("box", "theta", "phi")
    per_group = lax.axis_size("theta") * lax.axis_size("phi")
    low = shift(coeffs, every, 1)
    spread = upward(coeffs, radiation, up_weights, shares * per_group)
    radiation_adjoint = adjoint(radiation)
    lists = lists_of(partners, vector_ids, pair_count)
    spread, lists = lax.optimization_barrier((spread, lists))
    lines = translation_lines(lists, translation, shares, per_group)
    listed = near_slots(near_ids, near_count, lax.axis_index(every))
    spread, lines, radiation_adjoint, listed = lax.optimization_barrier(
        (spread, lines, radiation_adjoint, listed)
    )
    parents = parent_bands(spread, shares)
    near = near_field(listed, near_blocks, low, 0)
    near, late = lax.optimization_barrier((near, coeffs))
    high = shift(late, every, -1)
    parents, near = lax.optimization_barrier((parents, near))
    sources = [parents]
    if shares < lax.axis_size("box"):
        sources = [shift(parents, "box", 1), parents, shift(parents, "box", -1)]
    incoming = translate(lines, sources)
    incoming, near = lax.optimization_barrier((incoming, near))
    phi, pieces = staged_bands(incoming, shares)
    near = near_field(listed, near_blocks, coeffs, 1, near)
    ready = near_field(
        listed, near_blocks, high, 2, near, keep=(down_weights, radiation_adjoint)
    )
    return downward(phi, pieces, *ready)


def solution(mesh):
    box_size, theta_size, phi_size = (mesh.shape[axis] for axis in ("box", "theta", "phi"))
    shares = box_size if box_size <= 2 and TU // theta_size % box_size == 0 else 1
    up_weights, down_weights = operators(shares, theta_size, phi_size)
    in_specs = (
        P(),
        P(),
        P(("box", "theta", "phi"), None, None, None),
        P(("box", "theta", "phi"), None, None, None, None),
        P(("box", "theta", "phi"), None),
        P(("box", "theta", "phi")),
        P(("box", "theta", "phi"), None, None, None),
        P("box", None),
        P("box", None),
        P("box"),
        P(None, None, "theta", "phi"),
    )
    out_specs = P(("box", "theta", "phi"), None, None, None)
    mapped = jax.shard_map(
        functools.partial(per_device, shares),
        mesh=mesh,
        in_specs=in_specs,
        out_specs=out_specs,
        check_vma=False,
    )

    def product(*arrays):
        return mapped(jnp.asarray(up_weights), jnp.asarray(down_weights), *arrays)

    return product
```

```python
import functools
import math

import jax
import jax.numpy as jnp
import ml_dtypes
import numpy as np
from jax import lax
from jax.experimental import pallas as pl
from jax.experimental.pallas import tpu as pltpu
from jax.sharding import PartitionSpec as P

TL = 8
PL = 16
TU = 16
PU = 32

WEIGHT_UP = (-0.0546875, 0.8203125, 0.2734375, -0.0390625)
WEIGHT_DOWN = (-0.0390625, 0.2734375, 0.8203125, -0.0546875)
PHASE_SCALE = 1.3

F32 = jnp.float32
BF16 = jnp.bfloat16
MIB = 2**20
GROUP = 2
NOWHERE = -(2**20)


def lagrange(rows, columns, wrap):
    matrix = np.zeros((rows, columns))
    for row in range(rows):
        weights = WEIGHT_UP if row % 2 else WEIGHT_DOWN
        for order in range(4):
            node = row // 2 + row % 2 - 2 + order
            node = node % columns if wrap else min(max(node, 0), columns - 1)
            matrix[row, node] += weights[order]
    return matrix


def split_weights(matrix):
    high = matrix.astype(ml_dtypes.bfloat16)
    low = (matrix - high.astype(np.float64)).astype(ml_dtypes.bfloat16)
    return high, low


def operators(shares, theta_size, phi_size):
    theta_part = TU // theta_size // shares
    order = np.arange(TU * PU).reshape(theta_size, shares, theta_part, phi_size, PU // phi_size)
    order = order.transpose(1, 0, 3, 2, 4).reshape(-1)
    interp = np.kron(lagrange(TU, TL, False), lagrange(PU, PL, True))
    theta = math.pi * (np.arange(TU) + 0.5) / TU
    azimuth = 2.0 * math.pi * (np.arange(PU) + 0.5) / PU
    up, down = [], []
    for octant in range(4):
        sign_x = 2 * (octant % 2) - 1
        sign_y = 2 * (octant // 2 % 2) - 1
        sign_z = 2 * (octant // 4) - 1
        angle = PHASE_SCALE * (
            sign_x * np.sin(theta)[:, None] * np.cos(azimuth)[None]
            + sign_y * np.sin(theta)[:, None] * np.sin(azimuth)[None]
            + sign_z * np.cos(theta)[:, None]
        ).reshape(-1, 1)
        cos_high, cos_low = split_weights((np.cos(angle) * interp)[order])
        sin_high, sin_low = split_weights((np.sin(angle) * interp)[order])
        high = np.concatenate([cos_high, sin_high], axis=1)
        low = np.concatenate([cos_low, sin_low], axis=1)
        up.append(np.concatenate([high, low], axis=0))
        down += [cos_high.T, sin_high.T]
    return np.concatenate(up, axis=1), np.concatenate(down, axis=0)


def in_hbm(*arrays):
    return [pltpu.with_memory_space_constraint(array, pltpu.HBM) for array in arrays]


def dot(a, b):
    return jnp.dot(a, b, preferred_element_type=F32)


def side_by_side(real, imag):
    return jnp.concatenate([real, imag], axis=1)


def complex_columns(real, imag):
    return jnp.concatenate([side_by_side(real, imag), side_by_side(-imag, real)], axis=0)


def up_kernel(x_hbm, rad_hbm, w_hbm, out_hbm, x_ref, rad_ref, w_ref, right, result, sems):
    boxes, _, _, rhs = x_ref.shape
    points = rad_ref.shape[2]
    copies = [
        pltpu.make_async_copy(source, target, sems.at[place])
        for place, (source, target) in enumerate(
            ((x_hbm, x_ref), (rad_hbm, rad_ref), (w_hbm, w_ref))
        )
    ]
    for copy in copies:
        copy.start()
    copies[0].wait()
    copies[1].wait()
    half = boxes // 2
    for octant in range(boxes):
        left = side_by_side(rad_ref[octant, 0], rad_ref[octant, 1])
        straight = dot(left, complex_columns(x_ref[octant, 0], x_ref[octant, 1])).astype(BF16)
        real, imag = straight[:, :rhs], straight[:, rhs:]
        if octant < half:
            swapped = side_by_side(-imag, real)
        else:
            swapped = side_by_side(imag, -real)
        place = octant if octant < half else boxes - 1 - octant
        start = 2 * place * points
        right[octant // half, start : start + points] = straight
        right[octant // half, start + points : start + 2 * points] = swapped
    copies[2].wait()
    total = dot(w_ref[...], right[0]) + dot(w_ref[...], right[1])
    samples = total.shape[0] // 2
    total = total[:samples] + total[samples:]
    result[...] = total.astype(BF16).reshape(result.shape)
    pltpu.sync_copy(result, out_hbm)


def upward(coeffs, radiation, weights, groups):
    boxes, _, basis, rhs = coeffs.shape
    rows, columns = weights.shape
    samples = rows // 2
    hbm = pl.BlockSpec(memory_space=pltpu.HBM)
    return pl.pallas_call(
        up_kernel,
        in_specs=[hbm] * 3,
        out_specs=hbm,
        out_shape=pltpu.HBM((groups, samples // groups, 2 * rhs), BF16),
        scratch_shapes=[
            pltpu.VMEM(coeffs.shape, BF16),
            pltpu.VMEM(radiation.shape, BF16),
            pltpu.VMEM(weights.shape, BF16),
            pltpu.VMEM((2, columns, 2 * rhs), BF16),
            pltpu.VMEM((groups, samples // groups, 2 * rhs), BF16),
            pltpu.SemaphoreType.DMA((3,)),
        ],
        compiler_params=pltpu.CompilerParams(vmem_limit_bytes=32 * MIB),
        cost_estimate=pl.CostEstimate(
            flops=2 * 10**9, bytes_accessed=4 * MIB, transcendentals=0
        ),
        name="upward",
    )(*in_hbm(coeffs, radiation, weights))


def coupling_kernel(lists_ref, base_ref, table_ref, out_ref):
    rows = lists_ref.shape[0]
    samples = table_ref.shape[1] // 2
    _, targets, columns = out_ref.shape
    slots = rows // targets
    selector = (
        lax.broadcasted_iota(jnp.int32, (rows, table_ref.shape[0]), 1) == lists_ref[:, 1:2]
    )
    chosen = dot(selector.astype(BF16), table_ref[...]).astype(BF16)
    wide = lax.broadcasted_iota(jnp.int32, (rows, columns), 1) // samples
    match = wide + base_ref[0] == lists_ref[:, 0:1]
    spread = lax.broadcasted_iota(jnp.int32, (samples, columns), 0) == (
        lax.broadcasted_iota(jnp.int32, (samples, columns), 1) % samples
    )
    gather = (
        lax.broadcasted_iota(jnp.int32, (targets, rows), 1) // slots
        == lax.broadcasted_iota(jnp.int32, (targets, rows), 0)
    ).astype(BF16)
    tile = spread.astype(BF16)
    for part in range(2):
        lines = dot(chosen[:, part * samples : (part + 1) * samples], tile)
        out_ref[part] = dot(gather, jnp.where(match, lines, 0.0).astype(BF16))


def couplings(lists, base, table, targets, names):
    shape = (2, targets, names * (table.shape[1] // 2))
    vmem = pl.BlockSpec(memory_space=pltpu.VMEM)
    return pl.pallas_call(
        coupling_kernel,
        in_specs=[vmem, pl.BlockSpec(memory_space=pltpu.SMEM), vmem],
        out_specs=vmem,
        out_shape=jax.ShapeDtypeStruct(shape, F32),
        compiler_params=pltpu.CompilerParams(vmem_limit_bytes=16 * MIB),
        cost_estimate=pl.CostEstimate(
            flops=2 * 10**8, bytes_accessed=2 * 2**20, transcendentals=0
        ),
        name="coupling",
    )(lists, base, table)


def translate_kernel(lines_hbm, *refs):
    count = (len(refs) - 5) // 2
    sources, out_hbm = refs[:count], refs[count]
    held, lines, matrix, result, sems = refs[count + 1 :][:count], *refs[2 * count + 1 :]
    targets, samples, width = result.shape
    rhs = width // 2
    copies = [
        pltpu.make_async_copy(source, target, sems.at[place])
        for place, (source, target) in enumerate(zip((lines_hbm, *sources), (lines, *held)))
    ]
    for copy in copies:
        copy.start()
    copies[0].wait()
    columns = matrix.shape[1]
    row = lax.broadcasted_iota(jnp.int32, (samples, columns), 0)
    diagonal = row == lax.broadcasted_iota(jnp.int32, (samples, columns), 1) % samples
    for part in range(2):
        for target in range(targets):
            line = jnp.broadcast_to(lines[part, target : target + 1], diagonal.shape)
            start = (part * targets + target) * samples
            matrix[start : start + samples] = jnp.where(diagonal, line, 0.0).astype(BF16)
    total = None
    start = 0
    for place, source in enumerate(held):
        copies[1 + place].wait()
        stop = start + source.shape[0] * samples
        part = dot(matrix[:, start:stop], source[...].reshape(stop - start, width))
        total = part if total is None else total + part
        start = stop
    half = targets * samples
    real = total[:half, :rhs] - total[half:, rhs:]
    imag = total[:half, rhs:] + total[half:, :rhs]
    result[...] = jnp.concatenate([real, imag], axis=1).astype(BF16).reshape(result.shape)
    pltpu.sync_copy(result, out_hbm)


def translate(lines, sources):
    _, samples, width = sources[0].shape
    _, targets, columns = lines.shape
    shape = (targets, samples, width)
    hbm = pl.BlockSpec(memory_space=pltpu.HBM)
    anywhere = pl.BlockSpec(memory_space=pl.ANY)
    return pl.pallas_call(
        translate_kernel,
        in_specs=[hbm] + [anywhere] * len(sources),
        out_specs=hbm,
        out_shape=pltpu.HBM(shape, BF16),
        scratch_shapes=[
            *[pltpu.VMEM(source.shape, BF16) for source in sources],
            pltpu.VMEM(lines.shape, F32),
            pltpu.VMEM((2 * targets * samples, columns), BF16),
            pltpu.VMEM(shape, BF16),
            pltpu.SemaphoreType.DMA((1 + len(sources),)),
        ],
        compiler_params=pltpu.CompilerParams(vmem_limit_bytes=24 * MIB),
        cost_estimate=pl.CostEstimate(
            flops=10**9, bytes_accessed=2 * MIB, transcendentals=0
        ),
        name="translate",
    )(*in_hbm(lines), *sources)


def near_kernel(first, begun, kept, *refs):
    refs = list(refs)
    listed, blocks_hbm, held = refs[:3]
    before_hbm = refs[3] if begun else None
    kept_hbm = refs[3 + begun : 3 + begun + kept]
    out_ref = refs[3 + begun + kept]
    kept_refs = refs[4 + begun + kept : 4 + begun + 2 * kept]
    blocks, wide, total_ref, sems = refs[4 + begun + 2 * kept :]
    boxes, _, basis, rhs = held.shape
    most = blocks_hbm.shape[0]
    starts = [listed[first, most + box] for box in range(boxes + 1)]

    def by_box(source, target, turn):
        return [
            pltpu.make_async_copy(
                source.at[box], target.at[box], sems.at[most + turn * boxes + box]
            )
            for box in range(boxes)
        ]

    before_copies = by_box(before_hbm, total_ref, 0) if begun else []
    out_copies = [] if kept else by_box(total_ref, out_ref, 1)
    kept_copies = [
        pltpu.make_async_copy(kept_hbm[place], kept_refs[place], sems.at[most + 2 * boxes + place])
        for place in range(kept)
    ]

    def block_copy(place):
        block = listed[first, place] // boxes
        return pltpu.make_async_copy(blocks_hbm.at[block], blocks.at[place], sems.at[place])

    def fetch(place, carry):
        block_copy(place).start()
        return carry

    lax.fori_loop(0, starts[boxes], fetch, 0)
    for copy in before_copies + kept_copies:
        copy.start()
    for place in range(boxes):
        wide[place] = complex_columns(held[place, 0], held[place, 1])

    def landed(place, carry):
        block_copy(place).wait()
        return carry

    lax.fori_loop(0, starts[boxes], landed, 0)
    for copy in before_copies:
        copy.wait()

    def group(box, begin, size):
        left, right = [], []
        for step in range(size):
            place = starts[box] + begin + step
            valid = place < starts[box + 1]
            place = jnp.where(valid, place, 0)
            real, imag = blocks[place, 0], blocks[place, 1]
            real = jnp.where(valid, real, jnp.zeros_like(real))
            imag = jnp.where(valid, imag, jnp.zeros_like(imag))
            left.append(side_by_side(real, imag))
            right.append(wide[jnp.where(valid, listed[first, place] % boxes, 0)])
        return dot(jnp.concatenate(left, axis=1), jnp.concatenate(right, axis=0))

    possible = [(boxes - box, boxes, box + 1)[first] for box in range(boxes)]
    sizes = [min(count, 3 if count < 7 else 4) for count in possible]
    for box in range(boxes):
        part = group(box, 0, sizes[box])
        if begun:
            total_ref[box, 0] += part[:, :rhs]
            total_ref[box, 1] += part[:, rhs:]
        else:
            total_ref[box, 0] = part[:, :rhs]
            total_ref[box, 1] = part[:, rhs:]
    for box in range(boxes):

        def more(index, carry, box=box):
            part = group(box, sizes[box] + GROUP * index, GROUP)
            total_ref[box, 0] += part[:, :rhs]
            total_ref[box, 1] += part[:, rhs:]
            return carry

        rest = starts[box + 1] - starts[box] - sizes[box]
        lax.fori_loop(0, (jnp.maximum(rest, 0) + GROUP - 1) // GROUP, more, 0)
        if out_copies:
            out_copies[box].start()
    for copy in out_copies + kept_copies:
        copy.wait()


def near_slots(ids, used, rank):
    boxes, slots = ids.shape
    total = boxes * slots
    source = ids - (rank - 1) * boxes
    source = jnp.where(jnp.arange(slots) < used[:, None], source, -1).reshape(-1)
    wanted = (source >= 0) & (source // boxes == jnp.arange(3)[:, None])
    earlier = jnp.arange(total)[None, :] < jnp.arange(total)[:, None]
    place = jnp.sum((wanted[:, None, :] & earlier).astype(jnp.int32), axis=2)
    code = jnp.arange(total) * boxes + source % boxes
    chosen = wanted[:, None, :] & (place[:, None, :] == jnp.arange(total)[:, None])
    listed = jnp.sum(jnp.where(chosen, code, 0), axis=2)
    before = jnp.arange(total) // slots < jnp.arange(boxes + 1)[:, None]
    starts = jnp.sum((wanted[:, None, :] & before).astype(jnp.int32), axis=2)
    return jnp.concatenate([listed, starts], axis=1).astype(jnp.int32)


def near_field(listed, blocks, source, first, before=None, keep=()):
    boxes, slots, _, basis, _ = blocks.shape
    blocks = blocks.reshape(boxes * slots, *blocks.shape[2:])
    rhs = source.shape[3]
    begun, kept = before is not None, len(keep)
    hbm = pl.BlockSpec(memory_space=pltpu.HBM)
    smem = pl.BlockSpec(memory_space=pltpu.SMEM)
    vmem = pl.BlockSpec(memory_space=pltpu.VMEM)
    shape = (boxes, 2, basis, rhs)
    scratch = [
        pltpu.VMEM(blocks.shape, BF16),
        pltpu.VMEM((boxes, 2 * basis, 2 * rhs), BF16),
        pltpu.VMEM(shape, F32),
        pltpu.SemaphoreType.DMA((boxes * slots + 2 * boxes + kept,)),
    ]
    kernel = functools.partial(near_kernel, first, begun, kept)
    if kept:
        del scratch[2]
        inner = kernel

        def kernel(*refs):
            place = 3 + begun + kept
            inner(*refs[:-1], refs[place], refs[-1])

    return pl.pallas_call(
        kernel,
        in_specs=[smem, hbm, vmem] + [hbm] * (begun + kept),
        out_specs=[vmem] * (1 + kept) if kept else hbm,
        out_shape=[
            pltpu.VMEM(shape, F32),
            *[pltpu.VMEM(array.shape, array.dtype) for array in keep],
        ]
        if kept
        else pltpu.HBM(shape, F32),
        scratch_shapes=scratch,
        compiler_params=pltpu.CompilerParams(vmem_limit_bytes=32 * MIB),
        cost_estimate=pl.CostEstimate(
            flops=10**11 if first == 2 else 2 * 10**9, bytes_accessed=8 * MIB, transcendentals=0
        ),
        name=("near_low", "near_own", "near_high")[first],
    )(
        listed,
        *in_hbm(blocks),
        source,
        *in_hbm(*([before] if begun else []), *keep),
    )


def adjoint_kernel(rad_ref, out_hbm, held):
    for box in range(rad_ref.shape[0]):
        held[box] = side_by_side(rad_ref[box, 0].T, rad_ref[box, 1].T)
    pltpu.sync_copy(held, out_hbm)


def adjoint(radiation):
    boxes, _, points, basis = radiation.shape
    return pl.pallas_call(
        adjoint_kernel,
        in_specs=[pl.BlockSpec(memory_space=pltpu.VMEM)],
        out_specs=pl.BlockSpec(memory_space=pltpu.HBM),
        scratch_shapes=[pltpu.VMEM((boxes, basis, 2 * points), BF16)],
        out_shape=pltpu.HBM((boxes, basis, 2 * points), BF16),
        cost_estimate=pl.CostEstimate(
            flops=10**6, bytes_accessed=2 * MIB, transcendentals=0
        ),
        name="adjoint",
    )(radiation)


def down_kernel(phi_ref, near_ref, before_ref, w_ref, adjoint_ref, *refs):
    bands_ref, received = refs[0], refs[1:-4]
    out_hbm, field, held, sems = refs[-4:]
    boxes, _, width = adjoint_ref.shape
    points = width // 2
    rhs = held.shape[3]
    phi = phi_ref[0]
    phi_size = field.shape[1]
    pairs = [(bands_ref.at[:, phi], field.at[:, phi])]
    for distance, piece in zip(phi_distances(phi_size), received):
        pairs.append((piece, field.at[:, lax.rem(phi + phi_size - distance, phi_size)]))
    copies = [
        pltpu.make_async_copy(source, target, sems.at[boxes + place])
        for place, (source, target) in enumerate(pairs)
    ]
    out_copies = [
        pltpu.make_async_copy(held.at[box], out_hbm.at[box], sems.at[box]) for box in range(boxes)
    ]
    for copy in copies:
        copy.start()
    for copy in copies:
        copy.wait()
    mixed = dot(w_ref[...], field[...].reshape(w_ref.shape[1], 2 * rhs))
    for octant in range(boxes // 2):
        start = 2 * octant * points
        cos_part = mixed[start : start + points]
        sin_part = mixed[start + points : start + 2 * points]
        cos_re, cos_im = cos_part[:, :rhs], cos_part[:, rhs:]
        sin_re, sin_im = sin_part[:, :rhs], sin_part[:, rhs:]
        leaves = (
            (octant, cos_re + sin_im, cos_im - sin_re),
            (boxes - 1 - octant, cos_re - sin_im, cos_im + sin_re),
        )
        for box, real, imag in leaves:
            real, imag = real.astype(BF16), imag.astype(BF16)
            right = jnp.concatenate([side_by_side(real, imag), side_by_side(imag, -real)], axis=0)
            far = dot(adjoint_ref[box], right)
            held[box, 0] = near_ref[box, 0] + before_ref[box, 0] + far[:, :rhs]
            held[box, 1] = near_ref[box, 1] + before_ref[box, 1] + far[:, rhs:]
            out_copies[box].start()
    for copy in out_copies:
        copy.wait()


def downward(phi, bands, received, near, before, weights, radiation_adjoint):
    boxes = near.shape[0]
    anywhere = pl.BlockSpec(memory_space=pl.ANY)
    ready = [
        pltpu.with_memory_space_constraint(array, pltpu.VMEM)
        for array in (near, before, weights, radiation_adjoint)
    ]
    return pl.pallas_call(
        down_kernel,
        in_specs=[pl.BlockSpec(memory_space=pltpu.SMEM)]
        + [pl.BlockSpec(memory_space=pltpu.VMEM)] * 4
        + [anywhere] * (1 + len(received)),
        out_specs=pl.BlockSpec(memory_space=pltpu.HBM),
        out_shape=jax.ShapeDtypeStruct(near.shape, F32),
        scratch_shapes=[
            pltpu.VMEM(bands.shape, BF16),
            pltpu.VMEM(near.shape, F32),
            pltpu.SemaphoreType.DMA((boxes + 1 + len(received),)),
        ],
        compiler_params=pltpu.CompilerParams(vmem_limit_bytes=32 * MIB),
        cost_estimate=pl.CostEstimate(
            flops=2 * 10**9, bytes_accessed=7 * MIB, transcendentals=0
        ),
        name="downward",
    )(phi, *ready, bands, *received)


def shift(block, axis, step):
    count = lax.axis_size(axis)
    pairs = [(i, i + step) for i in range(count) if 0 <= i + step < count]
    return lax.ppermute(block, axis, pairs)


def lists_of(partners, vector_ids, pair_count):
    used = jnp.arange(partners.shape[1])[None, :] < pair_count[:, None]
    names = jnp.where(used, partners, NOWHERE)
    return jnp.stack([names, vector_ids], axis=2).reshape(-1, 2)


def parent_bands(spread, shares):
    axes = ("box", "theta", "phi") if shares == lax.axis_size("box") else ("theta", "phi")
    return lax.all_to_all(spread, axes, split_axis=0, concat_axis=0, tiled=True)


def phi_distances(size):
    return sorted(range(1, size), key=lambda distance: min(distance, size - distance))


def staged_bands(incoming, shares):
    axes = ("box", "theta") if shares == lax.axis_size("box") else ("theta",)
    phi_size = lax.axis_size("phi")
    phi = lax.axis_index("phi")
    bands = incoming.reshape(-1, phi_size, *incoming.shape[1:])
    bands = lax.all_to_all(bands, axes, split_axis=0, concat_axis=0, tiled=True)
    received = []
    for distance in phi_distances(phi_size):
        piece = lax.dynamic_index_in_dim(bands, (phi + distance) % phi_size, 1, keepdims=False)
        ring = [(place, (place + distance) % phi_size) for place in range(phi_size)]
        received.append(lax.ppermute(piece, "phi", ring))
    return phi.astype(jnp.int32).reshape(1), bands, received


def translation_lines(lists, translation, shares, per_group):
    operator_total, _, theta_band, phi_band = translation.shape
    rank = lax.axis_index("box")
    if shares < lax.axis_size("box"):
        table = translation.reshape(operator_total, -1)
        base = ((rank - 1) * per_group).astype(jnp.int32).reshape(1)
        return couplings(lists, base, table, per_group, 3 * per_group)
    if shares == 2:
        other = lax.ppermute(lists, "box", [(0, 1), (1, 0)])
        lists = jnp.where(
            rank == 0, jnp.concatenate([lists, other]), jnp.concatenate([other, lists])
        )
    part = theta_band // shares
    table = lax.dynamic_slice_in_dim(translation, rank * part, part, axis=2)
    table = table.reshape(operator_total, -1)
    total = shares * per_group
    return couplings(lists, jnp.zeros((1,), jnp.int32), table, total, total)


def per_device(
    shares,
    up_weights,
    down_weights,
    coeffs,
    near_blocks,
    near_ids,
    near_count,
    radiation,
    partners,
    vector_ids,
    pair_count,
    translation,
):
    every = ("box", "theta", "phi")
    per_group = lax.axis_size("theta") * lax.axis_size("phi")
    low = shift(coeffs, every, 1)
    spread = upward(coeffs, radiation, up_weights, shares * per_group)
    radiation_adjoint = adjoint(radiation)
    lists = lists_of(partners, vector_ids, pair_count)
    spread, lists = lax.optimization_barrier((spread, lists))
    lines = translation_lines(lists, translation, shares, per_group)
    listed = near_slots(near_ids, near_count, lax.axis_index(every))
    spread, lines, radiation_adjoint, listed = lax.optimization_barrier(
        (spread, lines, radiation_adjoint, listed)
    )
    parents = parent_bands(spread, shares)
    near = near_field(listed, near_blocks, low, 0)
    near, late = lax.optimization_barrier((near, coeffs))
    high = shift(late, every, -1)
    parents, near = lax.optimization_barrier((parents, near))
    sources = [parents]
    if shares < lax.axis_size("box"):
        sources = [shift(parents, "box", 1), parents, shift(parents, "box", -1)]
    incoming = translate(lines, sources)
    incoming, near = lax.optimization_barrier((incoming, near))
    phi, bands, received = staged_bands(incoming, shares)
    near = near_field(listed, near_blocks, coeffs, 1, near)
    ready = near_field(
        listed, near_blocks, high, 2, keep=(near, down_weights, radiation_adjoint)
    )
    return downward(phi, bands, received, *ready)


def solution(mesh):
    box_size, theta_size, phi_size = (mesh.shape[axis] for axis in ("box", "theta", "phi"))
    shares = box_size if box_size <= 2 and TU // theta_size % box_size == 0 else 1
    up_weights, down_weights = operators(shares, theta_size, phi_size)
    in_specs = (
        P(),
        P(),
        P(("box", "theta", "phi"), None, None, None),
        P(("box", "theta", "phi"), None, None, None, None),
        P(("box", "theta", "phi"), None),
        P(("box", "theta", "phi")),
        P(("box", "theta", "phi"), None, None, None),
        P("box", None),
        P("box", None),
        P("box"),
        P(None, None, "theta", "phi"),
    )
    out_specs = P(("box", "theta", "phi"), None, None, None)
    mapped = jax.shard_map(
        functools.partial(per_device, shares),
        mesh=mesh,
        in_specs=in_specs,
        out_specs=out_specs,
        check_vma=False,
    )

    def product(*arrays):
        return mapped(jnp.asarray(up_weights), jnp.asarray(down_weights), *arrays)

    return product
```

```python
import functools
import math

import jax
import jax.numpy as jnp
import ml_dtypes
import numpy as np
from jax import lax
from jax.experimental import pallas as pl
from jax.experimental.pallas import tpu as pltpu
from jax.sharding import PartitionSpec as P

TL = 8
PL = 16
TU = 16
PU = 32

WEIGHT_UP = (-0.0546875, 0.8203125, 0.2734375, -0.0390625)
WEIGHT_DOWN = (-0.0390625, 0.2734375, 0.8203125, -0.0546875)
PHASE_SCALE = 1.3

F32 = jnp.float32
BF16 = jnp.bfloat16
MIB = 2**20
GROUP = 2
NOWHERE = -(2**20)


def lagrange(rows, columns, wrap):
    matrix = np.zeros((rows, columns))
    for row in range(rows):
        weights = WEIGHT_UP if row % 2 else WEIGHT_DOWN
        for order in range(4):
            node = row // 2 + row % 2 - 2 + order
            node = node % columns if wrap else min(max(node, 0), columns - 1)
            matrix[row, node] += weights[order]
    return matrix


def split_weights(matrix):
    high = matrix.astype(ml_dtypes.bfloat16)
    low = (matrix - high.astype(np.float64)).astype(ml_dtypes.bfloat16)
    return high, low


def operators(shares, theta_size, phi_size):
    theta_part = TU // theta_size // shares
    order = np.arange(TU * PU).reshape(theta_size, shares, theta_part, phi_size, PU // phi_size)
    order = order.transpose(1, 0, 3, 2, 4).reshape(-1)
    interp = np.kron(lagrange(TU, TL, False), lagrange(PU, PL, True))
    theta = math.pi * (np.arange(TU) + 0.5) / TU
    azimuth = 2.0 * math.pi * (np.arange(PU) + 0.5) / PU
    up, down = [], []
    for octant in range(4):
        sign_x = 2 * (octant % 2) - 1
        sign_y = 2 * (octant // 2 % 2) - 1
        sign_z = 2 * (octant // 4) - 1
        angle = PHASE_SCALE * (
            sign_x * np.sin(theta)[:, None] * np.cos(azimuth)[None]
            + sign_y * np.sin(theta)[:, None] * np.sin(azimuth)[None]
            + sign_z * np.cos(theta)[:, None]
        ).reshape(-1, 1)
        cos_high, cos_low = split_weights((np.cos(angle) * interp)[order])
        sin_high, sin_low = split_weights((np.sin(angle) * interp)[order])
        high = np.concatenate([cos_high, sin_high], axis=1)
        low = np.concatenate([cos_low, sin_low], axis=1)
        up.append(np.concatenate([high, low], axis=0))
        down += [cos_high.T, sin_high.T]
    return np.concatenate(up, axis=1), np.concatenate(down, axis=0)


def in_hbm(*arrays):
    return [pltpu.with_memory_space_constraint(array, pltpu.HBM) for array in arrays]


def dot(a, b):
    return jnp.dot(a, b, preferred_element_type=F32)


def side_by_side(real, imag):
    return jnp.concatenate([real, imag], axis=1)


def complex_columns(real, imag):
    return jnp.concatenate([side_by_side(real, imag), side_by_side(-imag, real)], axis=0)


def up_kernel(x_hbm, rad_hbm, w_hbm, out_hbm, x_ref, rad_ref, w_ref, right, result, sems):
    boxes, _, _, rhs = x_ref.shape
    points = rad_ref.shape[2]
    copies = [
        pltpu.make_async_copy(source, target, sems.at[place])
        for place, (source, target) in enumerate(
            ((x_hbm, x_ref), (rad_hbm, rad_ref), (w_hbm, w_ref))
        )
    ]
    for copy in copies:
        copy.start()
    copies[0].wait()
    copies[1].wait()
    half = boxes // 2
    for octant in range(boxes):
        left = side_by_side(rad_ref[octant, 0], rad_ref[octant, 1])
        straight = dot(left, complex_columns(x_ref[octant, 0], x_ref[octant, 1])).astype(BF16)
        real, imag = straight[:, :rhs], straight[:, rhs:]
        if octant < half:
            swapped = side_by_side(-imag, real)
        else:
            swapped = side_by_side(imag, -real)
        place = octant if octant < half else boxes - 1 - octant
        start = 2 * place * points
        right[octant // half, start : start + points] = straight
        right[octant // half, start + points : start + 2 * points] = swapped
    copies[2].wait()
    total = dot(w_ref[...], right[0]) + dot(w_ref[...], right[1])
    samples = total.shape[0] // 2
    total = total[:samples] + total[samples:]
    result[...] = total.astype(BF16).reshape(result.shape)
    pltpu.sync_copy(result, out_hbm)


def upward(coeffs, radiation, weights, groups):
    boxes, _, basis, rhs = coeffs.shape
    rows, columns = weights.shape
    samples = rows // 2
    hbm = pl.BlockSpec(memory_space=pltpu.HBM)
    return pl.pallas_call(
        up_kernel,
        in_specs=[hbm] * 3,
        out_specs=hbm,
        out_shape=pltpu.HBM((groups, samples // groups, 2 * rhs), BF16),
        scratch_shapes=[
            pltpu.VMEM(coeffs.shape, BF16),
            pltpu.VMEM(radiation.shape, BF16),
            pltpu.VMEM(weights.shape, BF16),
            pltpu.VMEM((2, columns, 2 * rhs), BF16),
            pltpu.VMEM((groups, samples // groups, 2 * rhs), BF16),
            pltpu.SemaphoreType.DMA((3,)),
        ],
        compiler_params=pltpu.CompilerParams(vmem_limit_bytes=32 * MIB),
        cost_estimate=pl.CostEstimate(
            flops=2 * 10**9, bytes_accessed=4 * MIB, transcendentals=0
        ),
        name="upward",
    )(*in_hbm(coeffs, radiation, weights))


def coupling_kernel(lists_ref, base_ref, table_ref, out_ref):
    rows = lists_ref.shape[0]
    samples = table_ref.shape[1] // 2
    _, targets, columns = out_ref.shape
    slots = rows // targets
    selector = (
        lax.broadcasted_iota(jnp.int32, (rows, table_ref.shape[0]), 1) == lists_ref[:, 1:2]
    )
    chosen = dot(selector.astype(BF16), table_ref[...]).astype(BF16)
    wide = lax.broadcasted_iota(jnp.int32, (rows, columns), 1) // samples
    match = wide + base_ref[0] == lists_ref[:, 0:1]
    spread = lax.broadcasted_iota(jnp.int32, (samples, columns), 0) == (
        lax.broadcasted_iota(jnp.int32, (samples, columns), 1) % samples
    )
    gather = (
        lax.broadcasted_iota(jnp.int32, (targets, rows), 1) // slots
        == lax.broadcasted_iota(jnp.int32, (targets, rows), 0)
    ).astype(BF16)
    tile = spread.astype(BF16)
    for part in range(2):
        lines = dot(chosen[:, part * samples : (part + 1) * samples], tile)
        out_ref[part] = dot(gather, jnp.where(match, lines, 0.0).astype(BF16))


def couplings(lists, base, table, targets, names):
    shape = (2, targets, names * (table.shape[1] // 2))
    vmem = pl.BlockSpec(memory_space=pltpu.VMEM)
    return pl.pallas_call(
        coupling_kernel,
        in_specs=[vmem, pl.BlockSpec(memory_space=pltpu.SMEM), vmem],
        out_specs=vmem,
        out_shape=jax.ShapeDtypeStruct(shape, F32),
        compiler_params=pltpu.CompilerParams(vmem_limit_bytes=16 * MIB),
        cost_estimate=pl.CostEstimate(
            flops=2 * 10**8, bytes_accessed=2 * 2**20, transcendentals=0
        ),
        name="coupling",
    )(lists, base, table)


def translate_kernel(lines_hbm, *refs):
    count = (len(refs) - 5) // 2
    sources, out_hbm = refs[:count], refs[count]
    held, lines, matrix, result, sems = refs[count + 1 :][:count], *refs[2 * count + 1 :]
    targets, samples, width = result.shape
    rhs = width // 2
    copies = [
        pltpu.make_async_copy(source, target, sems.at[place])
        for place, (source, target) in enumerate(zip((lines_hbm, *sources), (lines, *held)))
    ]
    for copy in copies:
        copy.start()
    copies[0].wait()
    columns = matrix.shape[1]
    row = lax.broadcasted_iota(jnp.int32, (samples, columns), 0)
    diagonal = row == lax.broadcasted_iota(jnp.int32, (samples, columns), 1) % samples
    for part in range(2):
        for target in range(targets):
            line = jnp.broadcast_to(lines[part, target : target + 1], diagonal.shape)
            start = (part * targets + target) * samples
            matrix[start : start + samples] = jnp.where(diagonal, line, 0.0).astype(BF16)
    total = None
    start = 0
    for place, source in enumerate(held):
        copies[1 + place].wait()
        stop = start + source.shape[0] * samples
        part = dot(matrix[:, start:stop], source[...].reshape(stop - start, width))
        total = part if total is None else total + part
        start = stop
    half = targets * samples
    real = total[:half, :rhs] - total[half:, rhs:]
    imag = total[:half, rhs:] + total[half:, :rhs]
    result[...] = jnp.concatenate([real, imag], axis=1).astype(BF16).reshape(result.shape)
    pltpu.sync_copy(result, out_hbm)


def translate(lines, sources):
    _, samples, width = sources[0].shape
    _, targets, columns = lines.shape
    shape = (targets, samples, width)
    hbm = pl.BlockSpec(memory_space=pltpu.HBM)
    anywhere = pl.BlockSpec(memory_space=pl.ANY)
    return pl.pallas_call(
        translate_kernel,
        in_specs=[hbm] + [anywhere] * len(sources),
        out_specs=hbm,
        out_shape=pltpu.HBM(shape, BF16),
        scratch_shapes=[
            *[pltpu.VMEM(source.shape, BF16) for source in sources],
            pltpu.VMEM(lines.shape, F32),
            pltpu.VMEM((2 * targets * samples, columns), BF16),
            pltpu.VMEM(shape, BF16),
            pltpu.SemaphoreType.DMA((1 + len(sources),)),
        ],
        compiler_params=pltpu.CompilerParams(vmem_limit_bytes=24 * MIB),
        cost_estimate=pl.CostEstimate(
            flops=10**9, bytes_accessed=2 * MIB, transcendentals=0
        ),
        name="translate",
    )(*in_hbm(lines), *sources)


def near_kernel(first, begun, kept, *refs):
    refs = list(refs)
    listed, blocks_hbm, held = refs[:3]
    before_hbm = refs[3] if begun else None
    kept_hbm = refs[3 + begun : 3 + begun + kept]
    out_ref = refs[3 + begun + kept]
    kept_refs = refs[4 + begun + kept : 4 + begun + 2 * kept]
    blocks, wide, total_ref, sems = refs[4 + begun + 2 * kept :]
    boxes, _, basis, rhs = held.shape
    most = blocks_hbm.shape[0]
    starts = [listed[first, most + box] for box in range(boxes + 1)]

    def by_box(source, target, turn):
        return [
            pltpu.make_async_copy(
                source.at[box], target.at[box], sems.at[most + turn * boxes + box]
            )
            for box in range(boxes)
        ]

    before_copies = by_box(before_hbm, total_ref, 0) if begun else []
    out_copies = [] if kept else by_box(total_ref, out_ref, 1)
    kept_copies = [
        pltpu.make_async_copy(kept_hbm[place], kept_refs[place], sems.at[most + 2 * boxes + place])
        for place in range(kept)
    ]

    def block_copy(place):
        block = listed[first, place] // boxes
        return pltpu.make_async_copy(blocks_hbm.at[block], blocks.at[place], sems.at[place])

    def fetch(place, carry):
        block_copy(place).start()
        return carry

    lax.fori_loop(0, starts[boxes], fetch, 0)
    for copy in before_copies + kept_copies:
        copy.start()
    for place in range(boxes):
        wide[place] = complex_columns(held[place, 0], held[place, 1])

    def landed(place, carry):
        block_copy(place).wait()
        return carry

    lax.fori_loop(0, starts[boxes], landed, 0)
    for copy in before_copies:
        copy.wait()

    def group(box, begin, size):
        left, right = [], []
        for step in range(size):
            place = starts[box] + begin + step
            valid = place < starts[box + 1]
            place = jnp.where(valid, place, 0)
            real, imag = blocks[place, 0], blocks[place, 1]
            real = jnp.where(valid, real, jnp.zeros_like(real))
            imag = jnp.where(valid, imag, jnp.zeros_like(imag))
            left.append(side_by_side(real, imag))
            right.append(wide[jnp.where(valid, listed[first, place] % boxes, 0)])
        return dot(jnp.concatenate(left, axis=1), jnp.concatenate(right, axis=0))

    possible = [(boxes - box, boxes, box + 1)[first] for box in range(boxes)]
    sizes = [min(count, 3 if count < 7 else 4) for count in possible]
    for box in range(boxes):
        part = group(box, 0, sizes[box])
        if begun:
            total_ref[box, 0] += part[:, :rhs]
            total_ref[box, 1] += part[:, rhs:]
        else:
            total_ref[box, 0] = part[:, :rhs]
            total_ref[box, 1] = part[:, rhs:]
    for box in range(boxes):

        def more(index, carry, box=box):
            part = group(box, sizes[box] + GROUP * index, GROUP)
            total_ref[box, 0] += part[:, :rhs]
            total_ref[box, 1] += part[:, rhs:]
            return carry

        rest = starts[box + 1] - starts[box] - sizes[box]
        lax.fori_loop(0, (jnp.maximum(rest, 0) + GROUP - 1) // GROUP, more, 0)
        if out_copies:
            out_copies[box].start()
    for copy in out_copies + kept_copies:
        copy.wait()


def near_slots(ids, used, rank):
    boxes, slots = ids.shape
    total = boxes * slots
    source = ids - (rank - 1) * boxes
    source = jnp.where(jnp.arange(slots) < used[:, None], source, -1).reshape(-1)
    wanted = (source >= 0) & (source // boxes == jnp.arange(3)[:, None])
    earlier = jnp.arange(total)[None, :] < jnp.arange(total)[:, None]
    place = jnp.sum((wanted[:, None, :] & earlier).astype(jnp.int32), axis=2)
    code = jnp.arange(total) * boxes + source % boxes
    chosen = wanted[:, None, :] & (place[:, None, :] == jnp.arange(total)[:, None])
    listed = jnp.sum(jnp.where(chosen, code, 0), axis=2)
    before = jnp.arange(total) // slots < jnp.arange(boxes + 1)[:, None]
    starts = jnp.sum((wanted[:, None, :] & before).astype(jnp.int32), axis=2)
    return jnp.concatenate([listed, starts], axis=1).astype(jnp.int32)


def near_field(listed, blocks, source, first, before=None, keep=()):
    boxes, slots, _, basis, _ = blocks.shape
    blocks = blocks.reshape(boxes * slots, *blocks.shape[2:])
    rhs = source.shape[3]
    begun, kept = before is not None, len(keep)
    hbm = pl.BlockSpec(memory_space=pltpu.HBM)
    smem = pl.BlockSpec(memory_space=pltpu.SMEM)
    vmem = pl.BlockSpec(memory_space=pltpu.VMEM)
    shape = (boxes, 2, basis, rhs)
    scratch = [
        pltpu.VMEM(blocks.shape, BF16),
        pltpu.VMEM((boxes, 2 * basis, 2 * rhs), BF16),
        pltpu.VMEM(shape, F32),
        pltpu.SemaphoreType.DMA((boxes * slots + 2 * boxes + kept,)),
    ]
    kernel = functools.partial(near_kernel, first, begun, kept)
    if kept:
        del scratch[2]
        inner = kernel

        def kernel(*refs):
            place = 3 + begun + kept
            inner(*refs[:-1], refs[place], refs[-1])

    return pl.pallas_call(
        kernel,
        in_specs=[smem, hbm, vmem] + [hbm] * (begun + kept),
        out_specs=[vmem] * (1 + kept) if kept else hbm,
        out_shape=[
            pltpu.VMEM(shape, F32),
            *[pltpu.VMEM(array.shape, array.dtype) for array in keep],
        ]
        if kept
        else pltpu.HBM(shape, F32),
        scratch_shapes=scratch,
        compiler_params=pltpu.CompilerParams(vmem_limit_bytes=32 * MIB),
        cost_estimate=pl.CostEstimate(
            flops=10**11 if first == 2 else 2 * 10**9, bytes_accessed=8 * MIB, transcendentals=0
        ),
        name=("near_low", "near_own", "near_high")[first],
    )(
        listed,
        *in_hbm(blocks),
        source,
        *in_hbm(*([before] if begun else []), *keep),
    )


def adjoint_kernel(rad_ref, out_hbm, held):
    for box in range(rad_ref.shape[0]):
        held[box] = side_by_side(rad_ref[box, 0].T, rad_ref[box, 1].T)
    pltpu.sync_copy(held, out_hbm)


def adjoint(radiation):
    boxes, _, points, basis = radiation.shape
    return pl.pallas_call(
        adjoint_kernel,
        in_specs=[pl.BlockSpec(memory_space=pltpu.VMEM)],
        out_specs=pl.BlockSpec(memory_space=pltpu.HBM),
        scratch_shapes=[pltpu.VMEM((boxes, basis, 2 * points), BF16)],
        out_shape=pltpu.HBM((boxes, basis, 2 * points), BF16),
        cost_estimate=pl.CostEstimate(
            flops=10**6, bytes_accessed=2 * MIB, transcendentals=0
        ),
        name="adjoint",
    )(radiation)


def down_kernel(phi_ref, near_ref, before_ref, w_ref, adjoint_ref, *refs):
    bands_ref, received = refs[0], refs[1:-4]
    out_hbm, field, held, sems = refs[-4:]
    boxes, _, width = adjoint_ref.shape
    points = width // 2
    rhs = held.shape[3]
    phi = phi_ref[0]
    phi_size = field.shape[1]
    pairs = [(bands_ref.at[:, phi], field.at[:, phi])]
    for distance, piece in zip(phi_distances(phi_size), received):
        pairs.append((piece, field.at[:, lax.rem(phi + phi_size - distance, phi_size)]))
    copies = [
        pltpu.make_async_copy(source, target, sems.at[boxes + place])
        for place, (source, target) in enumerate(pairs)
    ]
    out_copies = [
        pltpu.make_async_copy(held.at[box], out_hbm.at[box], sems.at[box]) for box in range(boxes)
    ]
    for copy in copies:
        copy.start()
    for copy in copies:
        copy.wait()
    mixed = dot(w_ref[...], field[...].reshape(w_ref.shape[1], 2 * rhs))
    for octant in range(boxes // 2):
        start = 2 * octant * points
        cos_part = mixed[start : start + points]
        sin_part = mixed[start + points : start + 2 * points]
        cos_re, cos_im = cos_part[:, :rhs], cos_part[:, rhs:]
        sin_re, sin_im = sin_part[:, :rhs], sin_part[:, rhs:]
        leaves = (
            (octant, cos_re + sin_im, cos_im - sin_re),
            (boxes - 1 - octant, cos_re - sin_im, cos_im + sin_re),
        )
        for box, real, imag in leaves:
            real, imag = real.astype(BF16), imag.astype(BF16)
            right = jnp.concatenate([side_by_side(real, imag), side_by_side(imag, -real)], axis=0)
            far = dot(adjoint_ref[box], right)
            held[box, 0] = near_ref[box, 0] + before_ref[box, 0] + far[:, :rhs]
            held[box, 1] = near_ref[box, 1] + before_ref[box, 1] + far[:, rhs:]
            out_copies[box].start()
    for copy in out_copies:
        copy.wait()


def downward(phi, bands, received, near, before, weights, radiation_adjoint):
    boxes = near.shape[0]
    anywhere = pl.BlockSpec(memory_space=pl.ANY)
    ready = [
        pltpu.with_memory_space_constraint(array, pltpu.VMEM)
        for array in (near, before, weights, radiation_adjoint)
    ]
    return pl.pallas_call(
        down_kernel,
        in_specs=[pl.BlockSpec(memory_space=pltpu.SMEM)]
        + [pl.BlockSpec(memory_space=pltpu.VMEM)] * 4
        + [anywhere] * (1 + len(received)),
        out_specs=pl.BlockSpec(memory_space=pltpu.HBM),
        out_shape=jax.ShapeDtypeStruct(near.shape, F32),
        scratch_shapes=[
            pltpu.VMEM(bands.shape, BF16),
            pltpu.VMEM(near.shape, F32),
            pltpu.SemaphoreType.DMA((boxes + 1 + len(received),)),
        ],
        compiler_params=pltpu.CompilerParams(vmem_limit_bytes=32 * MIB),
        cost_estimate=pl.CostEstimate(
            flops=2 * 10**9, bytes_accessed=7 * MIB, transcendentals=0
        ),
        name="downward",
    )(phi, *ready, bands, *received)


def shift(block, axis, step):
    count = lax.axis_size(axis)
    pairs = [(i, i + step) for i in range(count) if 0 <= i + step < count]
    return lax.ppermute(block, axis, pairs)


def lists_of(partners, vector_ids, pair_count):
    used = jnp.arange(partners.shape[1])[None, :] < pair_count[:, None]
    names = jnp.where(used, partners, NOWHERE)
    return jnp.stack([names, vector_ids], axis=2).reshape(-1, 2)


def parent_bands(spread, shares):
    axes = ("box", "theta", "phi") if shares == lax.axis_size("box") else ("theta", "phi")
    return lax.all_to_all(spread, axes, split_axis=0, concat_axis=0, tiled=True)


def phi_distances(size):
    return sorted(range(1, size), key=lambda distance: -min(distance, size - distance))


def staged_bands(incoming, shares):
    axes = ("box", "theta") if shares == lax.axis_size("box") else ("theta",)
    phi_size = lax.axis_size("phi")
    phi = lax.axis_index("phi")
    bands = incoming.reshape(-1, phi_size, *incoming.shape[1:])
    bands = lax.all_to_all(bands, axes, split_axis=0, concat_axis=0, tiled=True)
    received = []
    for distance in phi_distances(phi_size):
        piece = lax.dynamic_index_in_dim(bands, (phi + distance) % phi_size, 1, keepdims=False)
        ring = [(place, (place + distance) % phi_size) for place in range(phi_size)]
        received.append(lax.ppermute(piece, "phi", ring))
    return phi.astype(jnp.int32).reshape(1), bands, received


def translation_lines(lists, translation, shares, per_group):
    operator_total, _, theta_band, phi_band = translation.shape
    rank = lax.axis_index("box")
    if shares < lax.axis_size("box"):
        table = translation.reshape(operator_total, -1)
        base = ((rank - 1) * per_group).astype(jnp.int32).reshape(1)
        return couplings(lists, base, table, per_group, 3 * per_group)
    if shares == 2:
        other = lax.ppermute(lists, "box", [(0, 1), (1, 0)])
        lists = jnp.where(
            rank == 0, jnp.concatenate([lists, other]), jnp.concatenate([other, lists])
        )
    part = theta_band // shares
    table = lax.dynamic_slice_in_dim(translation, rank * part, part, axis=2)
    table = table.reshape(operator_total, -1)
    total = shares * per_group
    return couplings(lists, jnp.zeros((1,), jnp.int32), table, total, total)


def per_device(
    shares,
    up_weights,
    down_weights,
    coeffs,
    near_blocks,
    near_ids,
    near_count,
    radiation,
    partners,
    vector_ids,
    pair_count,
    translation,
):
    every = ("box", "theta", "phi")
    per_group = lax.axis_size("theta") * lax.axis_size("phi")
    low = shift(coeffs, every, 1)
    spread = upward(coeffs, radiation, up_weights, shares * per_group)
    radiation_adjoint = adjoint(radiation)
    lists = lists_of(partners, vector_ids, pair_count)
    spread, lists = lax.optimization_barrier((spread, lists))
    lines = translation_lines(lists, translation, shares, per_group)
    listed = near_slots(near_ids, near_count, lax.axis_index(every))
    spread, lines, radiation_adjoint, listed = lax.optimization_barrier(
        (spread, lines, radiation_adjoint, listed)
    )
    parents = parent_bands(spread, shares)
    near = near_field(listed, near_blocks, low, 0)
    near, late = lax.optimization_barrier((near, coeffs))
    high = shift(late, every, -1)
    parents, near = lax.optimization_barrier((parents, near))
    sources = [parents]
    if shares < lax.axis_size("box"):
        sources = [shift(parents, "box", 1), parents, shift(parents, "box", -1)]
    incoming = translate(lines, sources)
    incoming, near = lax.optimization_barrier((incoming, near))
    phi, bands, received = staged_bands(incoming, shares)
    near = near_field(listed, near_blocks, coeffs, 1, near)
    ready = near_field(
        listed, near_blocks, high, 2, keep=(near, down_weights, radiation_adjoint)
    )
    return downward(phi, bands, received, *ready)


def solution(mesh):
    box_size, theta_size, phi_size = (mesh.shape[axis] for axis in ("box", "theta", "phi"))
    shares = box_size if box_size <= 2 and TU // theta_size % box_size == 0 else 1
    up_weights, down_weights = operators(shares, theta_size, phi_size)
    in_specs = (
        P(),
        P(),
        P(("box", "theta", "phi"), None, None, None),
        P(("box", "theta", "phi"), None, None, None, None),
        P(("box", "theta", "phi"), None),
        P(("box", "theta", "phi")),
        P(("box", "theta", "phi"), None, None, None),
        P("box", None),
        P("box", None),
        P("box"),
        P(None, None, "theta", "phi"),
    )
    out_specs = P(("box", "theta", "phi"), None, None, None)
    mapped = jax.shard_map(
        functools.partial(per_device, shares),
        mesh=mesh,
        in_specs=in_specs,
        out_specs=out_specs,
        check_vma=False,
    )

    def product(*arrays):
        return mapped(jnp.asarray(up_weights), jnp.asarray(down_weights), *arrays)

    return product
```

```python
import functools
import math

import jax
import jax.numpy as jnp
import ml_dtypes
import numpy as np
from jax import lax
from jax.experimental import pallas as pl
from jax.experimental.pallas import tpu as pltpu
from jax.sharding import PartitionSpec as P

TL = 8
PL = 16
TU = 16
PU = 32

WEIGHT_UP = (-0.0546875, 0.8203125, 0.2734375, -0.0390625)
WEIGHT_DOWN = (-0.0390625, 0.2734375, 0.8203125, -0.0546875)
PHASE_SCALE = 1.3

F32 = jnp.float32
BF16 = jnp.bfloat16
MIB = 2**20
GROUP = 2
NOWHERE = -(2**20)


def lagrange(rows, columns, wrap):
    matrix = np.zeros((rows, columns))
    for row in range(rows):
        weights = WEIGHT_UP if row % 2 else WEIGHT_DOWN
        for order in range(4):
            node = row // 2 + row % 2 - 2 + order
            node = node % columns if wrap else min(max(node, 0), columns - 1)
            matrix[row, node] += weights[order]
    return matrix


def split_weights(matrix):
    high = matrix.astype(ml_dtypes.bfloat16)
    low = (matrix - high.astype(np.float64)).astype(ml_dtypes.bfloat16)
    return high, low


def operators(shares, theta_size, phi_size):
    theta_part = TU // theta_size // shares
    order = np.arange(TU * PU).reshape(theta_size, shares, theta_part, phi_size, PU // phi_size)
    order = order.transpose(1, 0, 3, 2, 4).reshape(-1)
    interp = np.kron(lagrange(TU, TL, False), lagrange(PU, PL, True))
    theta = math.pi * (np.arange(TU) + 0.5) / TU
    azimuth = 2.0 * math.pi * (np.arange(PU) + 0.5) / PU
    up, down = [], []
    for octant in range(4):
        sign_x = 2 * (octant % 2) - 1
        sign_y = 2 * (octant // 2 % 2) - 1
        sign_z = 2 * (octant // 4) - 1
        angle = PHASE_SCALE * (
            sign_x * np.sin(theta)[:, None] * np.cos(azimuth)[None]
            + sign_y * np.sin(theta)[:, None] * np.sin(azimuth)[None]
            + sign_z * np.cos(theta)[:, None]
        ).reshape(-1, 1)
        cos_high, cos_low = split_weights((np.cos(angle) * interp)[order])
        sin_high, sin_low = split_weights((np.sin(angle) * interp)[order])
        high = np.concatenate([cos_high, sin_high], axis=1)
        low = np.concatenate([cos_low, sin_low], axis=1)
        up.append(np.concatenate([high, low], axis=0))
        down += [cos_high.T, sin_high.T]
    return np.concatenate(up, axis=1), np.concatenate(down, axis=0)


def in_hbm(*arrays):
    return [pltpu.with_memory_space_constraint(array, pltpu.HBM) for array in arrays]


def dot(a, b):
    return jnp.dot(a, b, preferred_element_type=F32)


def side_by_side(real, imag):
    return jnp.concatenate([real, imag], axis=1)


def complex_columns(real, imag):
    return jnp.concatenate([side_by_side(real, imag), side_by_side(-imag, real)], axis=0)


def up_kernel(x_hbm, rad_hbm, w_hbm, out_hbm, x_ref, rad_ref, w_ref, right, result, sems):
    boxes, _, _, rhs = x_ref.shape
    points = rad_ref.shape[2]
    copies = [
        pltpu.make_async_copy(source, target, sems.at[place])
        for place, (source, target) in enumerate(
            ((x_hbm, x_ref), (rad_hbm, rad_ref), (w_hbm, w_ref))
        )
    ]
    for copy in copies:
        copy.start()
    copies[0].wait()
    copies[1].wait()
    half = boxes // 2
    for octant in range(boxes):
        left = side_by_side(rad_ref[octant, 0], rad_ref[octant, 1])
        straight = dot(left, complex_columns(x_ref[octant, 0], x_ref[octant, 1])).astype(BF16)
        real, imag = straight[:, :rhs], straight[:, rhs:]
        if octant < half:
            swapped = side_by_side(-imag, real)
        else:
            swapped = side_by_side(imag, -real)
        place = octant if octant < half else boxes - 1 - octant
        start = 2 * place * points
        right[octant // half, start : start + points] = straight
        right[octant // half, start + points : start + 2 * points] = swapped
    copies[2].wait()
    total = dot(w_ref[...], right[0]) + dot(w_ref[...], right[1])
    samples = total.shape[0] // 2
    total = total[:samples] + total[samples:]
    result[...] = total.astype(BF16).reshape(result.shape)
    pltpu.sync_copy(result, out_hbm)


def upward(coeffs, radiation, weights, groups):
    boxes, _, basis, rhs = coeffs.shape
    rows, columns = weights.shape
    samples = rows // 2
    hbm = pl.BlockSpec(memory_space=pltpu.HBM)
    return pl.pallas_call(
        up_kernel,
        in_specs=[hbm] * 3,
        out_specs=hbm,
        out_shape=pltpu.HBM((groups, samples // groups, 2 * rhs), BF16),
        scratch_shapes=[
            pltpu.VMEM(coeffs.shape, BF16),
            pltpu.VMEM(radiation.shape, BF16),
            pltpu.VMEM(weights.shape, BF16),
            pltpu.VMEM((2, columns, 2 * rhs), BF16),
            pltpu.VMEM((groups, samples // groups, 2 * rhs), BF16),
            pltpu.SemaphoreType.DMA((3,)),
        ],
        compiler_params=pltpu.CompilerParams(vmem_limit_bytes=32 * MIB),
        cost_estimate=pl.CostEstimate(
            flops=2 * 10**9, bytes_accessed=4 * MIB, transcendentals=0
        ),
        name="upward",
    )(*in_hbm(coeffs, radiation, weights))


def coupling_kernel(lists_ref, base_ref, table_ref, out_ref):
    rows = lists_ref.shape[0]
    samples = table_ref.shape[1] // 2
    _, targets, columns = out_ref.shape
    slots = rows // targets
    selector = (
        lax.broadcasted_iota(jnp.int32, (rows, table_ref.shape[0]), 1) == lists_ref[:, 1:2]
    )
    chosen = dot(selector.astype(BF16), table_ref[...]).astype(BF16)
    wide = lax.broadcasted_iota(jnp.int32, (rows, columns), 1) // samples
    match = wide + base_ref[0] == lists_ref[:, 0:1]
    spread = lax.broadcasted_iota(jnp.int32, (samples, columns), 0) == (
        lax.broadcasted_iota(jnp.int32, (samples, columns), 1) % samples
    )
    gather = (
        lax.broadcasted_iota(jnp.int32, (targets, rows), 1) // slots
        == lax.broadcasted_iota(jnp.int32, (targets, rows), 0)
    ).astype(BF16)
    tile = spread.astype(BF16)
    for part in range(2):
        lines = dot(chosen[:, part * samples : (part + 1) * samples], tile)
        out_ref[part] = dot(gather, jnp.where(match, lines, 0.0).astype(BF16))


def couplings(lists, base, table, targets, names):
    shape = (2, targets, names * (table.shape[1] // 2))
    vmem = pl.BlockSpec(memory_space=pltpu.VMEM)
    return pl.pallas_call(
        coupling_kernel,
        in_specs=[vmem, pl.BlockSpec(memory_space=pltpu.SMEM), vmem],
        out_specs=vmem,
        out_shape=jax.ShapeDtypeStruct(shape, F32),
        compiler_params=pltpu.CompilerParams(vmem_limit_bytes=16 * MIB),
        cost_estimate=pl.CostEstimate(
            flops=2 * 10**8, bytes_accessed=2 * 2**20, transcendentals=0
        ),
        name="coupling",
    )(lists, base, table)


def translate_kernel(lines_hbm, *refs):
    count = (len(refs) - 5) // 2
    sources, out_hbm = refs[:count], refs[count]
    held, lines, matrix, result, sems = refs[count + 1 :][:count], *refs[2 * count + 1 :]
    targets, samples, width = result.shape
    rhs = width // 2
    copies = [
        pltpu.make_async_copy(source, target, sems.at[place])
        for place, (source, target) in enumerate(zip((lines_hbm, *sources), (lines, *held)))
    ]
    for copy in copies:
        copy.start()
    copies[0].wait()
    columns = matrix.shape[1]
    row = lax.broadcasted_iota(jnp.int32, (samples, columns), 0)
    diagonal = row == lax.broadcasted_iota(jnp.int32, (samples, columns), 1) % samples
    for part in range(2):
        for target in range(targets):
            line = jnp.broadcast_to(lines[part, target : target + 1], diagonal.shape)
            start = (part * targets + target) * samples
            matrix[start : start + samples] = jnp.where(diagonal, line, 0.0).astype(BF16)
    total = None
    start = 0
    for place, source in enumerate(held):
        copies[1 + place].wait()
        stop = start + source.shape[0] * samples
        part = dot(matrix[:, start:stop], source[...].reshape(stop - start, width))
        total = part if total is None else total + part
        start = stop
    half = targets * samples
    real = total[:half, :rhs] - total[half:, rhs:]
    imag = total[:half, rhs:] + total[half:, :rhs]
    result[...] = jnp.concatenate([real, imag], axis=1).astype(BF16).reshape(result.shape)
    pltpu.sync_copy(result, out_hbm)


def translate(lines, sources):
    _, samples, width = sources[0].shape
    _, targets, columns = lines.shape
    shape = (targets, samples, width)
    hbm = pl.BlockSpec(memory_space=pltpu.HBM)
    anywhere = pl.BlockSpec(memory_space=pl.ANY)
    return pl.pallas_call(
        translate_kernel,
        in_specs=[hbm] + [anywhere] * len(sources),
        out_specs=hbm,
        out_shape=pltpu.HBM(shape, BF16),
        scratch_shapes=[
            *[pltpu.VMEM(source.shape, BF16) for source in sources],
            pltpu.VMEM(lines.shape, F32),
            pltpu.VMEM((2 * targets * samples, columns), BF16),
            pltpu.VMEM(shape, BF16),
            pltpu.SemaphoreType.DMA((1 + len(sources),)),
        ],
        compiler_params=pltpu.CompilerParams(vmem_limit_bytes=24 * MIB),
        cost_estimate=pl.CostEstimate(
            flops=10**9, bytes_accessed=2 * MIB, transcendentals=0
        ),
        name="translate",
    )(*in_hbm(lines), *sources)


def near_kernel(first, begun, kept, *refs):
    refs = list(refs)
    listed, blocks_hbm, held = refs[:3]
    before_hbm = refs[3] if begun else None
    kept_hbm = refs[3 + begun : 3 + begun + kept]
    out_ref = refs[3 + begun + kept]
    kept_refs = refs[4 + begun + kept : 4 + begun + 2 * kept]
    blocks, wide, total_ref, sems = refs[4 + begun + 2 * kept :]
    boxes, _, basis, rhs = held.shape
    most = blocks_hbm.shape[0]
    starts = [listed[first, most + box] for box in range(boxes + 1)]

    def by_box(source, target, turn):
        return [
            pltpu.make_async_copy(
                source.at[box], target.at[box], sems.at[most + turn * boxes + box]
            )
            for box in range(boxes)
        ]

    before_copies = by_box(before_hbm, total_ref, 0) if begun else []
    out_copies = [] if kept else by_box(total_ref, out_ref, 1)
    kept_copies = [
        pltpu.make_async_copy(kept_hbm[place], kept_refs[place], sems.at[most + 2 * boxes + place])
        for place in range(kept)
    ]

    def block_copy(place):
        block = listed[first, place] // boxes
        return pltpu.make_async_copy(blocks_hbm.at[block], blocks.at[place], sems.at[place])

    def fetch(place, carry):
        block_copy(place).start()
        return carry

    lax.fori_loop(0, starts[boxes], fetch, 0)
    for copy in before_copies + kept_copies:
        copy.start()
    for place in range(boxes):
        wide[place] = complex_columns(held[place, 0], held[place, 1])

    def landed(place, carry):
        block_copy(place).wait()
        return carry

    lax.fori_loop(0, starts[boxes], landed, 0)
    for copy in before_copies:
        copy.wait()

    def group(box, begin, size):
        left, right = [], []
        for step in range(size):
            place = starts[box] + begin + step
            valid = place < starts[box + 1]
            place = jnp.where(valid, place, 0)
            real, imag = blocks[place, 0], blocks[place, 1]
            real = jnp.where(valid, real, jnp.zeros_like(real))
            imag = jnp.where(valid, imag, jnp.zeros_like(imag))
            left.append(side_by_side(real, imag))
            right.append(wide[jnp.where(valid, listed[first, place] % boxes, 0)])
        return dot(jnp.concatenate(left, axis=1), jnp.concatenate(right, axis=0))

    possible = [(boxes - box, boxes, box + 1)[first] for box in range(boxes)]
    sizes = [min(count, 3 if count < 7 else 4) for count in possible]
    for box in range(boxes):
        part = group(box, 0, sizes[box])
        if begun:
            total_ref[box, 0] += part[:, :rhs]
            total_ref[box, 1] += part[:, rhs:]
        else:
            total_ref[box, 0] = part[:, :rhs]
            total_ref[box, 1] = part[:, rhs:]
    for box in range(boxes):

        def more(index, carry, box=box):
            part = group(box, sizes[box] + GROUP * index, GROUP)
            total_ref[box, 0] += part[:, :rhs]
            total_ref[box, 1] += part[:, rhs:]
            return carry

        rest = starts[box + 1] - starts[box] - sizes[box]
        lax.fori_loop(0, (jnp.maximum(rest, 0) + GROUP - 1) // GROUP, more, 0)
        if out_copies:
            out_copies[box].start()
    for copy in out_copies + kept_copies:
        copy.wait()


def near_slots(ids, used, rank):
    boxes, slots = ids.shape
    total = boxes * slots
    source = ids - (rank - 1) * boxes
    source = jnp.where(jnp.arange(slots) < used[:, None], source, -1).reshape(-1)
    wanted = (source >= 0) & (source // boxes == jnp.arange(3)[:, None])
    earlier = jnp.arange(total)[None, :] < jnp.arange(total)[:, None]
    place = jnp.sum((wanted[:, None, :] & earlier).astype(jnp.int32), axis=2)
    code = jnp.arange(total) * boxes + source % boxes
    chosen = wanted[:, None, :] & (place[:, None, :] == jnp.arange(total)[:, None])
    listed = jnp.sum(jnp.where(chosen, code, 0), axis=2)
    before = jnp.arange(total) // slots < jnp.arange(boxes + 1)[:, None]
    starts = jnp.sum((wanted[:, None, :] & before).astype(jnp.int32), axis=2)
    return jnp.concatenate([listed, starts], axis=1).astype(jnp.int32)


def near_field(listed, blocks, source, first, before=None, keep=()):
    boxes, slots, _, basis, _ = blocks.shape
    blocks = blocks.reshape(boxes * slots, *blocks.shape[2:])
    rhs = source.shape[3]
    begun, kept = before is not None, len(keep)
    hbm = pl.BlockSpec(memory_space=pltpu.HBM)
    smem = pl.BlockSpec(memory_space=pltpu.SMEM)
    vmem = pl.BlockSpec(memory_space=pltpu.VMEM)
    shape = (boxes, 2, basis, rhs)
    scratch = [
        pltpu.VMEM(blocks.shape, BF16),
        pltpu.VMEM((boxes, 2 * basis, 2 * rhs), BF16),
        pltpu.VMEM(shape, F32),
        pltpu.SemaphoreType.DMA((boxes * slots + 2 * boxes + kept,)),
    ]
    kernel = functools.partial(near_kernel, first, begun, kept)
    if kept:
        del scratch[2]
        inner = kernel

        def kernel(*refs):
            place = 3 + begun + kept
            inner(*refs[:-1], refs[place], refs[-1])

    return pl.pallas_call(
        kernel,
        in_specs=[smem, hbm, vmem] + [hbm] * (begun + kept),
        out_specs=[vmem] * (1 + kept) if kept else hbm,
        out_shape=[
            pltpu.VMEM(shape, F32),
            *[pltpu.VMEM(array.shape, array.dtype) for array in keep],
        ]
        if kept
        else pltpu.HBM(shape, F32),
        scratch_shapes=scratch,
        compiler_params=pltpu.CompilerParams(vmem_limit_bytes=32 * MIB),
        cost_estimate=pl.CostEstimate(
            flops=10**11 if first == 2 else 2 * 10**9, bytes_accessed=8 * MIB, transcendentals=0
        ),
        name=("near_low", "near_own", "near_high")[first],
    )(
        listed,
        *in_hbm(blocks),
        source,
        *in_hbm(*([before] if begun else []), *keep),
    )


def adjoint_kernel(rad_ref, out_hbm, held):
    for box in range(rad_ref.shape[0]):
        real, imag = rad_ref[box, 0].T, rad_ref[box, 1].T
        held[box] = jnp.concatenate([side_by_side(real, imag), side_by_side(-imag, real)], axis=0)
    pltpu.sync_copy(held, out_hbm)


def adjoint(radiation):
    boxes, _, points, basis = radiation.shape
    return pl.pallas_call(
        adjoint_kernel,
        in_specs=[pl.BlockSpec(memory_space=pltpu.VMEM)],
        out_specs=pl.BlockSpec(memory_space=pltpu.HBM),
        scratch_shapes=[pltpu.VMEM((boxes, 2 * basis, 2 * points), BF16)],
        out_shape=pltpu.HBM((boxes, 2 * basis, 2 * points), BF16),
        cost_estimate=pl.CostEstimate(
            flops=10**6, bytes_accessed=2 * MIB, transcendentals=0
        ),
        name="adjoint",
    )(radiation)


def down_kernel(phi_ref, near_ref, before_ref, w_ref, adjoint_ref, *refs):
    bands_ref, received = refs[0], refs[1:-4]
    out_hbm, field, held, sems = refs[-4:]
    boxes, _, width = adjoint_ref.shape
    points = width // 2
    rhs = held.shape[3]
    phi = phi_ref[0]
    phi_size = field.shape[1]
    pairs = [(bands_ref.at[:, phi], field.at[:, phi])]
    for distance, piece in enumerate(received, 1):
        pairs.append((piece, field.at[:, lax.rem(phi + phi_size - distance, phi_size)]))
    copies = [
        pltpu.make_async_copy(source, target, sems.at[boxes + place])
        for place, (source, target) in enumerate(pairs)
    ]
    out_copies = [
        pltpu.make_async_copy(held.at[box], out_hbm.at[box], sems.at[box]) for box in range(boxes)
    ]
    for copy in copies:
        copy.start()
    for copy in copies:
        copy.wait()
    mixed = dot(w_ref[...], field[...].reshape(w_ref.shape[1], 2 * rhs))
    for octant in range(boxes // 2):
        start = 2 * octant * points
        cos_part = mixed[start : start + points]
        sin_part = mixed[start + points : start + 2 * points]
        cos_re, cos_im = cos_part[:, :rhs], cos_part[:, rhs:]
        sin_re, sin_im = sin_part[:, :rhs], sin_part[:, rhs:]
        leaves = (
            (octant, cos_re + sin_im, cos_im - sin_re),
            (boxes - 1 - octant, cos_re - sin_im, cos_im + sin_re),
        )
        for box, real, imag in leaves:
            leaf = jnp.concatenate([real, imag], axis=0).astype(BF16)
            far = dot(adjoint_ref[box], leaf)
            held[box] = near_ref[box] + before_ref[box] + far.reshape(held.shape[1:])
            out_copies[box].start()
    for copy in out_copies:
        copy.wait()


def downward(phi, bands, received, near, before, weights, radiation_adjoint):
    boxes = near.shape[0]
    anywhere = pl.BlockSpec(memory_space=pl.ANY)
    ready = [
        pltpu.with_memory_space_constraint(array, pltpu.VMEM)
        for array in (near, before, weights, radiation_adjoint)
    ]
    return pl.pallas_call(
        down_kernel,
        in_specs=[pl.BlockSpec(memory_space=pltpu.SMEM)]
        + [pl.BlockSpec(memory_space=pltpu.VMEM)] * 4
        + [anywhere] * (1 + len(received)),
        out_specs=pl.BlockSpec(memory_space=pltpu.HBM),
        out_shape=jax.ShapeDtypeStruct(near.shape, F32),
        scratch_shapes=[
            pltpu.VMEM(bands.shape, BF16),
            pltpu.VMEM(near.shape, F32),
            pltpu.SemaphoreType.DMA((boxes + 1 + len(received),)),
        ],
        compiler_params=pltpu.CompilerParams(vmem_limit_bytes=32 * MIB),
        cost_estimate=pl.CostEstimate(
            flops=2 * 10**9, bytes_accessed=7 * MIB, transcendentals=0
        ),
        name="downward",
    )(phi, *ready, bands, *received)


def shift(block, axis, step):
    count = lax.axis_size(axis)
    pairs = [(i, i + step) for i in range(count) if 0 <= i + step < count]
    return lax.ppermute(block, axis, pairs)


def lists_of(partners, vector_ids, pair_count):
    used = jnp.arange(partners.shape[1])[None, :] < pair_count[:, None]
    names = jnp.where(used, partners, NOWHERE)
    return jnp.stack([names, vector_ids], axis=2).reshape(-1, 2)


def parent_bands(spread, shares):
    axes = ("box", "theta", "phi") if shares == lax.axis_size("box") else ("theta", "phi")
    return lax.all_to_all(spread, axes, split_axis=0, concat_axis=0, tiled=True)


def staged_bands(incoming, shares):
    axes = ("box", "theta") if shares == lax.axis_size("box") else ("theta",)
    phi_size = lax.axis_size("phi")
    phi = lax.axis_index("phi")
    bands = incoming.reshape(-1, phi_size, *incoming.shape[1:])
    bands = lax.all_to_all(bands, axes, split_axis=0, concat_axis=0, tiled=True)
    received = []
    for distance in range(1, phi_size):
        piece = lax.dynamic_index_in_dim(bands, (phi + distance) % phi_size, 1, keepdims=False)
        ring = [(place, (place + distance) % phi_size) for place in range(phi_size)]
        received.append(lax.ppermute(piece, "phi", ring))
    return phi.astype(jnp.int32).reshape(1), bands, received


def translation_lines(lists, translation, shares, per_group):
    operator_total, _, theta_band, phi_band = translation.shape
    rank = lax.axis_index("box")
    if shares < lax.axis_size("box"):
        table = translation.reshape(operator_total, -1)
        base = ((rank - 1) * per_group).astype(jnp.int32).reshape(1)
        return couplings(lists, base, table, per_group, 3 * per_group)
    if shares == 2:
        other = lax.ppermute(lists, "box", [(0, 1), (1, 0)])
        lists = jnp.where(
            rank == 0, jnp.concatenate([lists, other]), jnp.concatenate([other, lists])
        )
    part = theta_band // shares
    table = lax.dynamic_slice_in_dim(translation, rank * part, part, axis=2)
    table = table.reshape(operator_total, -1)
    total = shares * per_group
    return couplings(lists, jnp.zeros((1,), jnp.int32), table, total, total)


def per_device(
    shares,
    up_weights,
    down_weights,
    coeffs,
    near_blocks,
    near_ids,
    near_count,
    radiation,
    partners,
    vector_ids,
    pair_count,
    translation,
):
    every = ("box", "theta", "phi")
    per_group = lax.axis_size("theta") * lax.axis_size("phi")
    low = shift(coeffs, every, 1)
    spread = upward(coeffs, radiation, up_weights, shares * per_group)
    radiation_adjoint = adjoint(radiation)
    lists = lists_of(partners, vector_ids, pair_count)
    spread, lists = lax.optimization_barrier((spread, lists))
    lines = translation_lines(lists, translation, shares, per_group)
    listed = near_slots(near_ids, near_count, lax.axis_index(every))
    spread, lines, radiation_adjoint, listed = lax.optimization_barrier(
        (spread, lines, radiation_adjoint, listed)
    )
    parents = parent_bands(spread, shares)
    near = near_field(listed, near_blocks, low, 0)
    near, late = lax.optimization_barrier((near, coeffs))
    high = shift(late, every, -1)
    parents, near = lax.optimization_barrier((parents, near))
    sources = [parents]
    if shares < lax.axis_size("box"):
        sources = [shift(parents, "box", 1), parents, shift(parents, "box", -1)]
    incoming = translate(lines, sources)
    incoming, near = lax.optimization_barrier((incoming, near))
    phi, bands, received = staged_bands(incoming, shares)
    near = near_field(listed, near_blocks, coeffs, 1, near)
    ready = near_field(
        listed, near_blocks, high, 2, keep=(near, down_weights, radiation_adjoint)
    )
    return downward(phi, bands, received, *ready)


def solution(mesh):
    box_size, theta_size, phi_size = (mesh.shape[axis] for axis in ("box", "theta", "phi"))
    shares = box_size if box_size <= 2 and TU // theta_size % box_size == 0 else 1
    up_weights, down_weights = operators(shares, theta_size, phi_size)
    in_specs = (
        P(),
        P(),
        P(("box", "theta", "phi"), None, None, None),
        P(("box", "theta", "phi"), None, None, None, None),
        P(("box", "theta", "phi"), None),
        P(("box", "theta", "phi")),
        P(("box", "theta", "phi"), None, None, None),
        P("box", None),
        P("box", None),
        P("box"),
        P(None, None, "theta", "phi"),
    )
    out_specs = P(("box", "theta", "phi"), None, None, None)
    mapped = jax.shard_map(
        functools.partial(per_device, shares),
        mesh=mesh,
        in_specs=in_specs,
        out_specs=out_specs,
        check_vma=False,
    )

    def product(*arrays):
        return mapped(jnp.asarray(up_weights), jnp.asarray(down_weights), *arrays)

    return product
```

```python
import functools
import math

import jax
import jax.numpy as jnp
import ml_dtypes
import numpy as np
from jax import lax
from jax.experimental import pallas as pl
from jax.experimental.pallas import tpu as pltpu
from jax.sharding import PartitionSpec as P

TL = 8
PL = 16
TU = 16
PU = 32

WEIGHT_UP = (-0.0546875, 0.8203125, 0.2734375, -0.0390625)
WEIGHT_DOWN = (-0.0390625, 0.2734375, 0.8203125, -0.0546875)
PHASE_SCALE = 1.3

F32 = jnp.float32
BF16 = jnp.bfloat16
MIB = 2**20
GROUP = 2
NOWHERE = -(2**20)


def lagrange(rows, columns, wrap):
    matrix = np.zeros((rows, columns))
    for row in range(rows):
        weights = WEIGHT_UP if row % 2 else WEIGHT_DOWN
        for order in range(4):
            node = row // 2 + row % 2 - 2 + order
            node = node % columns if wrap else min(max(node, 0), columns - 1)
            matrix[row, node] += weights[order]
    return matrix


def split_weights(matrix):
    high = matrix.astype(ml_dtypes.bfloat16)
    low = (matrix - high.astype(np.float64)).astype(ml_dtypes.bfloat16)
    return high, low


def operators(shares, theta_size, phi_size):
    theta_part = TU // theta_size // shares
    order = np.arange(TU * PU).reshape(theta_size, shares, theta_part, phi_size, PU // phi_size)
    order = order.transpose(1, 0, 3, 2, 4).reshape(-1)
    interp = np.kron(lagrange(TU, TL, False), lagrange(PU, PL, True))
    theta = math.pi * (np.arange(TU) + 0.5) / TU
    azimuth = 2.0 * math.pi * (np.arange(PU) + 0.5) / PU
    up, down = [], []
    for octant in range(4):
        sign_x = 2 * (octant % 2) - 1
        sign_y = 2 * (octant // 2 % 2) - 1
        sign_z = 2 * (octant // 4) - 1
        angle = PHASE_SCALE * (
            sign_x * np.sin(theta)[:, None] * np.cos(azimuth)[None]
            + sign_y * np.sin(theta)[:, None] * np.sin(azimuth)[None]
            + sign_z * np.cos(theta)[:, None]
        ).reshape(-1, 1)
        cos_high, cos_low = split_weights((np.cos(angle) * interp)[order])
        sin_high, sin_low = split_weights((np.sin(angle) * interp)[order])
        high = np.concatenate([cos_high, sin_high], axis=1)
        low = np.concatenate([cos_low, sin_low], axis=1)
        up.append(np.concatenate([high, low], axis=0))
        down += [cos_high.T, sin_high.T]
    return np.concatenate(up, axis=1), np.concatenate(down, axis=0)


def in_hbm(*arrays):
    return [pltpu.with_memory_space_constraint(array, pltpu.HBM) for array in arrays]


def dot(a, b):
    return jnp.dot(a, b, preferred_element_type=F32)


def side_by_side(real, imag):
    return jnp.concatenate([real, imag], axis=1)


def complex_columns(real, imag):
    return jnp.concatenate([side_by_side(real, imag), side_by_side(-imag, real)], axis=0)


def up_kernel(x_hbm, rad_hbm, w_hbm, out_hbm, x_ref, rad_ref, w_ref, right, result, sems):
    boxes, _, _, rhs = x_ref.shape
    points = rad_ref.shape[2]
    copies = [
        pltpu.make_async_copy(source, target, sems.at[place])
        for place, (source, target) in enumerate(
            ((x_hbm, x_ref), (rad_hbm, rad_ref), (w_hbm, w_ref))
        )
    ]
    for copy in copies:
        copy.start()
    copies[0].wait()
    copies[1].wait()
    half = boxes // 2
    for octant in range(boxes):
        left = side_by_side(rad_ref[octant, 0], rad_ref[octant, 1])
        straight = dot(left, complex_columns(x_ref[octant, 0], x_ref[octant, 1])).astype(BF16)
        real, imag = straight[:, :rhs], straight[:, rhs:]
        if octant < half:
            swapped = side_by_side(-imag, real)
        else:
            swapped = side_by_side(imag, -real)
        place = octant if octant < half else boxes - 1 - octant
        start = 2 * place * points
        right[octant // half, start : start + points] = straight
        right[octant // half, start + points : start + 2 * points] = swapped
    copies[2].wait()
    total = dot(w_ref[...], right[0]) + dot(w_ref[...], right[1])
    samples = total.shape[0] // 2
    total = total[:samples] + total[samples:]
    result[...] = total.astype(BF16).reshape(result.shape)
    pltpu.sync_copy(result, out_hbm)


def upward(coeffs, radiation, weights, groups):
    boxes, _, basis, rhs = coeffs.shape
    rows, columns = weights.shape
    samples = rows // 2
    hbm = pl.BlockSpec(memory_space=pltpu.HBM)
    return pl.pallas_call(
        up_kernel,
        in_specs=[hbm] * 3,
        out_specs=hbm,
        out_shape=pltpu.HBM((groups, samples // groups, 2 * rhs), BF16),
        scratch_shapes=[
            pltpu.VMEM(coeffs.shape, BF16),
            pltpu.VMEM(radiation.shape, BF16),
            pltpu.VMEM(weights.shape, BF16),
            pltpu.VMEM((2, columns, 2 * rhs), BF16),
            pltpu.VMEM((groups, samples // groups, 2 * rhs), BF16),
            pltpu.SemaphoreType.DMA((3,)),
        ],
        compiler_params=pltpu.CompilerParams(vmem_limit_bytes=32 * MIB),
        cost_estimate=pl.CostEstimate(
            flops=2 * 10**9, bytes_accessed=4 * MIB, transcendentals=0
        ),
        name="upward",
    )(*in_hbm(coeffs, radiation, weights))


def coupling_kernel(lists_ref, base_ref, table_ref, out_ref):
    rows = lists_ref.shape[0]
    samples = table_ref.shape[1] // 2
    _, targets, columns = out_ref.shape
    slots = rows // targets
    selector = (
        lax.broadcasted_iota(jnp.int32, (rows, table_ref.shape[0]), 1) == lists_ref[:, 1:2]
    )
    chosen = dot(selector.astype(BF16), table_ref[...]).astype(BF16)
    wide = lax.broadcasted_iota(jnp.int32, (rows, columns), 1) // samples
    match = wide + base_ref[0] == lists_ref[:, 0:1]
    spread = lax.broadcasted_iota(jnp.int32, (samples, columns), 0) == (
        lax.broadcasted_iota(jnp.int32, (samples, columns), 1) % samples
    )
    gather = (
        lax.broadcasted_iota(jnp.int32, (targets, rows), 1) // slots
        == lax.broadcasted_iota(jnp.int32, (targets, rows), 0)
    ).astype(BF16)
    tile = spread.astype(BF16)
    for part in range(2):
        lines = dot(chosen[:, part * samples : (part + 1) * samples], tile)
        out_ref[part] = dot(gather, jnp.where(match, lines, 0.0).astype(BF16))


def couplings(lists, base, table, targets, names):
    shape = (2, targets, names * (table.shape[1] // 2))
    vmem = pl.BlockSpec(memory_space=pltpu.VMEM)
    return pl.pallas_call(
        coupling_kernel,
        in_specs=[vmem, pl.BlockSpec(memory_space=pltpu.SMEM), vmem],
        out_specs=vmem,
        out_shape=jax.ShapeDtypeStruct(shape, F32),
        compiler_params=pltpu.CompilerParams(vmem_limit_bytes=16 * MIB),
        cost_estimate=pl.CostEstimate(
            flops=2 * 10**8, bytes_accessed=2 * 2**20, transcendentals=0
        ),
        name="coupling",
    )(lists, base, table)


def translate_kernel(lines_hbm, *refs):
    count = (len(refs) - 5) // 2
    sources, out_hbm = refs[:count], refs[count]
    held, lines, matrix, result, sems = refs[count + 1 :][:count], *refs[2 * count + 1 :]
    targets, samples, width = result.shape
    rhs = width // 2
    copies = [
        pltpu.make_async_copy(source, target, sems.at[place])
        for place, (source, target) in enumerate(zip((lines_hbm, *sources), (lines, *held)))
    ]
    for copy in copies:
        copy.start()
    copies[0].wait()
    columns = matrix.shape[1]
    row = lax.broadcasted_iota(jnp.int32, (samples, columns), 0)
    diagonal = row == lax.broadcasted_iota(jnp.int32, (samples, columns), 1) % samples
    for part in range(2):
        for target in range(targets):
            line = jnp.broadcast_to(lines[part, target : target + 1], diagonal.shape)
            start = (part * targets + target) * samples
            matrix[start : start + samples] = jnp.where(diagonal, line, 0.0).astype(BF16)
    total = None
    start = 0
    for place, source in enumerate(held):
        copies[1 + place].wait()
        stop = start + source.shape[0] * samples
        part = dot(matrix[:, start:stop], source[...].reshape(stop - start, width))
        total = part if total is None else total + part
        start = stop
    half = targets * samples
    real = total[:half, :rhs] - total[half:, rhs:]
    imag = total[:half, rhs:] + total[half:, :rhs]
    result[...] = jnp.concatenate([real, imag], axis=1).astype(BF16).reshape(result.shape)
    pltpu.sync_copy(result, out_hbm)


def translate(lines, sources):
    _, samples, width = sources[0].shape
    _, targets, columns = lines.shape
    shape = (targets, samples, width)
    hbm = pl.BlockSpec(memory_space=pltpu.HBM)
    anywhere = pl.BlockSpec(memory_space=pl.ANY)
    return pl.pallas_call(
        translate_kernel,
        in_specs=[hbm] + [anywhere] * len(sources),
        out_specs=hbm,
        out_shape=pltpu.HBM(shape, BF16),
        scratch_shapes=[
            *[pltpu.VMEM(source.shape, BF16) for source in sources],
            pltpu.VMEM(lines.shape, F32),
            pltpu.VMEM((2 * targets * samples, columns), BF16),
            pltpu.VMEM(shape, BF16),
            pltpu.SemaphoreType.DMA((1 + len(sources),)),
        ],
        compiler_params=pltpu.CompilerParams(vmem_limit_bytes=24 * MIB),
        cost_estimate=pl.CostEstimate(
            flops=10**9, bytes_accessed=2 * MIB, transcendentals=0
        ),
        name="translate",
    )(*in_hbm(lines), *sources)


def near_kernel(first, begun, kept, *refs):
    refs = list(refs)
    listed, blocks_hbm, held = refs[:3]
    before_hbm = refs[3] if begun else None
    kept_hbm = refs[3 + begun : 3 + begun + kept]
    out_ref = refs[3 + begun + kept]
    kept_refs = refs[4 + begun + kept : 4 + begun + 2 * kept]
    blocks, wide, total_ref, sems = refs[4 + begun + 2 * kept :]
    boxes, _, basis, rhs = held.shape
    most = blocks_hbm.shape[0]
    starts = [listed[first, most + box] for box in range(boxes + 1)]

    def by_box(source, target, turn):
        return [
            pltpu.make_async_copy(
                source.at[box], target.at[box], sems.at[most + turn * boxes + box]
            )
            for box in range(boxes)
        ]

    before_copies = by_box(before_hbm, total_ref, 0) if begun else []
    out_copies = [] if kept else by_box(total_ref, out_ref, 1)
    kept_copies = [
        pltpu.make_async_copy(kept_hbm[place], kept_refs[place], sems.at[most + 2 * boxes + place])
        for place in range(kept)
    ]

    def block_copy(place):
        block = listed[first, place] // boxes
        return pltpu.make_async_copy(blocks_hbm.at[block], blocks.at[place], sems.at[place])

    def fetch(place, carry):
        block_copy(place).start()
        return carry

    lax.fori_loop(0, starts[boxes], fetch, 0)
    for copy in before_copies + kept_copies:
        copy.start()
    for place in range(boxes):
        wide[place] = complex_columns(held[place, 0], held[place, 1])

    def landed(place, carry):
        block_copy(place).wait()
        return carry

    lax.fori_loop(0, starts[boxes], landed, 0)
    for copy in before_copies:
        copy.wait()

    def group(box, begin, size):
        left, right = [], []
        for step in range(size):
            place = starts[box] + begin + step
            valid = place < starts[box + 1]
            place = jnp.where(valid, place, 0)
            real, imag = blocks[place, 0], blocks[place, 1]
            real = jnp.where(valid, real, jnp.zeros_like(real))
            imag = jnp.where(valid, imag, jnp.zeros_like(imag))
            left.append(side_by_side(real, imag))
            right.append(wide[jnp.where(valid, listed[first, place] % boxes, 0)])
        return dot(jnp.concatenate(left, axis=1), jnp.concatenate(right, axis=0))

    possible = [(boxes - box, boxes, box + 1)[first] for box in range(boxes)]
    sizes = [min(count, 3 if count < 7 else 4) for count in possible]
    for box in range(boxes):
        part = group(box, 0, sizes[box])
        if begun:
            total_ref[box, 0] += part[:, :rhs]
            total_ref[box, 1] += part[:, rhs:]
        else:
            total_ref[box, 0] = part[:, :rhs]
            total_ref[box, 1] = part[:, rhs:]
    for box in range(boxes):

        def more(index, carry, box=box):
            part = group(box, sizes[box] + GROUP * index, GROUP)
            total_ref[box, 0] += part[:, :rhs]
            total_ref[box, 1] += part[:, rhs:]
            return carry

        rest = starts[box + 1] - starts[box] - sizes[box]
        lax.fori_loop(0, (jnp.maximum(rest, 0) + GROUP - 1) // GROUP, more, 0)
        if out_copies:
            out_copies[box].start()
    for copy in out_copies + kept_copies:
        copy.wait()


def near_slots(ids, used, rank):
    boxes, slots = ids.shape
    total = boxes * slots
    source = ids - (rank - 1) * boxes
    source = jnp.where(jnp.arange(slots) < used[:, None], source, -1).reshape(-1)
    wanted = (source >= 0) & (source // boxes == jnp.arange(3)[:, None])
    earlier = jnp.arange(total)[None, :] < jnp.arange(total)[:, None]
    place = jnp.sum((wanted[:, None, :] & earlier).astype(jnp.int32), axis=2)
    code = jnp.arange(total) * boxes + source % boxes
    chosen = wanted[:, None, :] & (place[:, None, :] == jnp.arange(total)[:, None])
    listed = jnp.sum(jnp.where(chosen, code, 0), axis=2)
    before = jnp.arange(total) // slots < jnp.arange(boxes + 1)[:, None]
    starts = jnp.sum((wanted[:, None, :] & before).astype(jnp.int32), axis=2)
    return jnp.concatenate([listed, starts], axis=1).astype(jnp.int32)


def near_field(listed, blocks, source, first, before=None, keep=()):
    boxes, slots, _, basis, _ = blocks.shape
    blocks = blocks.reshape(boxes * slots, *blocks.shape[2:])
    rhs = source.shape[3]
    begun, kept = before is not None, len(keep)
    hbm = pl.BlockSpec(memory_space=pltpu.HBM)
    smem = pl.BlockSpec(memory_space=pltpu.SMEM)
    vmem = pl.BlockSpec(memory_space=pltpu.VMEM)
    shape = (boxes, 2, basis, rhs)
    scratch = [
        pltpu.VMEM(blocks.shape, BF16),
        pltpu.VMEM((boxes, 2 * basis, 2 * rhs), BF16),
        pltpu.VMEM(shape, F32),
        pltpu.SemaphoreType.DMA((boxes * slots + 2 * boxes + kept,)),
    ]
    kernel = functools.partial(near_kernel, first, begun, kept)
    if kept:
        del scratch[2]
        inner = kernel

        def kernel(*refs):
            place = 3 + begun + kept
            inner(*refs[:-1], refs[place], refs[-1])

    return pl.pallas_call(
        kernel,
        in_specs=[smem, hbm, vmem] + [hbm] * (begun + kept),
        out_specs=[vmem] * (1 + kept) if kept else hbm,
        out_shape=[
            pltpu.VMEM(shape, F32),
            *[pltpu.VMEM(array.shape, array.dtype) for array in keep],
        ]
        if kept
        else pltpu.HBM(shape, F32),
        scratch_shapes=scratch,
        compiler_params=pltpu.CompilerParams(vmem_limit_bytes=32 * MIB),
        cost_estimate=pl.CostEstimate(
            flops=10**11 if first == 2 else 2 * 10**9, bytes_accessed=8 * MIB, transcendentals=0
        ),
        name=("near_low", "near_own", "near_high")[first],
    )(
        listed,
        *in_hbm(blocks),
        source,
        *in_hbm(*([before] if begun else []), *keep),
    )


def adjoint_kernel(rad_ref, out_hbm, held):
    for box in range(rad_ref.shape[0]):
        held[box] = side_by_side(rad_ref[box, 0].T, rad_ref[box, 1].T)
    pltpu.sync_copy(held, out_hbm)


def adjoint(radiation):
    boxes, _, points, basis = radiation.shape
    return pl.pallas_call(
        adjoint_kernel,
        in_specs=[pl.BlockSpec(memory_space=pltpu.VMEM)],
        out_specs=pl.BlockSpec(memory_space=pltpu.HBM),
        scratch_shapes=[pltpu.VMEM((boxes, basis, 2 * points), BF16)],
        out_shape=pltpu.HBM((boxes, basis, 2 * points), BF16),
        cost_estimate=pl.CostEstimate(
            flops=10**6, bytes_accessed=2 * MIB, transcendentals=0
        ),
        name="adjoint",
    )(radiation)


def down_kernel(phi_ref, near_ref, before_ref, w_ref, adjoint_ref, *refs):
    bands_ref, received = refs[0], refs[1:-4]
    out_hbm, field, held, sems = refs[-4:]
    boxes, _, width = adjoint_ref.shape
    points = width // 2
    rhs = held.shape[3]
    phi = phi_ref[0]
    phi_size = field.shape[1]
    pairs = [(bands_ref.at[:, phi], field.at[:, phi])]
    for distance, piece in enumerate(received, 1):
        pairs.append((piece, field.at[:, lax.rem(phi + phi_size - distance, phi_size)]))
    copies = [
        pltpu.make_async_copy(source, target, sems.at[boxes + place])
        for place, (source, target) in enumerate(pairs)
    ]
    out_copies = [
        pltpu.make_async_copy(held.at[box], out_hbm.at[box], sems.at[box]) for box in range(boxes)
    ]
    for copy in copies:
        copy.start()
    for copy in copies:
        copy.wait()
    mixed = dot(w_ref[...], field[...].reshape(w_ref.shape[1], 2 * rhs))
    for octant in range(boxes // 2):
        start = 2 * octant * points
        cos_part = mixed[start : start + points]
        sin_part = mixed[start + points : start + 2 * points]
        cos_re, cos_im = cos_part[:, :rhs], cos_part[:, rhs:]
        sin_re, sin_im = sin_part[:, :rhs], sin_part[:, rhs:]
        leaves = (
            (octant, cos_re + sin_im, cos_im - sin_re),
            (boxes - 1 - octant, cos_re - sin_im, cos_im + sin_re),
        )
        for box, real, imag in leaves:
            real, imag = real.astype(BF16), imag.astype(BF16)
            right = jnp.concatenate([side_by_side(real, imag), side_by_side(imag, -real)], axis=0)
            far = dot(adjoint_ref[box], right)
            held[box, 0] = near_ref[box, 0] + before_ref[box, 0] + far[:, :rhs]
            held[box, 1] = near_ref[box, 1] + before_ref[box, 1] + far[:, rhs:]
            out_copies[box].start()
    for copy in out_copies:
        copy.wait()


def downward(phi, bands, received, near, before, weights, radiation_adjoint):
    boxes = near.shape[0]
    anywhere = pl.BlockSpec(memory_space=pl.ANY)
    ready = [
        pltpu.with_memory_space_constraint(array, pltpu.VMEM)
        for array in (near, before, weights, radiation_adjoint)
    ]
    return pl.pallas_call(
        down_kernel,
        in_specs=[pl.BlockSpec(memory_space=pltpu.SMEM)]
        + [pl.BlockSpec(memory_space=pltpu.VMEM)] * 4
        + [anywhere] * (1 + len(received)),
        out_specs=pl.BlockSpec(memory_space=pltpu.HBM),
        out_shape=jax.ShapeDtypeStruct(near.shape, F32),
        scratch_shapes=[
            pltpu.VMEM(bands.shape, BF16),
            pltpu.VMEM(near.shape, F32),
            pltpu.SemaphoreType.DMA((boxes + 1 + len(received),)),
        ],
        compiler_params=pltpu.CompilerParams(vmem_limit_bytes=32 * MIB),
        cost_estimate=pl.CostEstimate(
            flops=2 * 10**9, bytes_accessed=7 * MIB, transcendentals=0
        ),
        name="downward",
    )(phi, *ready, bands, *received)


def shift(block, axis, step):
    count = lax.axis_size(axis)
    pairs = [(i, i + step) for i in range(count) if 0 <= i + step < count]
    return lax.ppermute(block, axis, pairs)


def lists_of(partners, vector_ids, pair_count):
    used = jnp.arange(partners.shape[1])[None, :] < pair_count[:, None]
    names = jnp.where(used, partners, NOWHERE)
    return jnp.stack([names, vector_ids], axis=2).reshape(-1, 2)


def parent_bands(spread, shares):
    axes = ("box", "theta", "phi") if shares == lax.axis_size("box") else ("theta", "phi")
    return lax.all_to_all(spread, axes, split_axis=0, concat_axis=0, tiled=True)


def staged_bands(incoming, shares):
    axes = ("box", "theta") if shares == lax.axis_size("box") else ("theta",)
    phi_size = lax.axis_size("phi")
    phi = lax.axis_index("phi")
    bands = incoming.reshape(-1, phi_size, *incoming.shape[1:])
    bands = lax.all_to_all(bands, axes, split_axis=0, concat_axis=0, tiled=True)
    received = []
    for distance in range(1, phi_size):
        piece = lax.dynamic_index_in_dim(bands, (phi + distance) % phi_size, 1, keepdims=False)
        ring = [(place, (place + distance) % phi_size) for place in range(phi_size)]
        received.append(lax.ppermute(piece, "phi", ring))
    return phi.astype(jnp.int32).reshape(1), bands, received


def translation_lines(lists, translation, shares, per_group):
    operator_total, _, theta_band, phi_band = translation.shape
    rank = lax.axis_index("box")
    if shares < lax.axis_size("box"):
        table = translation.reshape(operator_total, -1)
        base = ((rank - 1) * per_group).astype(jnp.int32).reshape(1)
        return couplings(lists, base, table, per_group, 3 * per_group)
    if shares == 2:
        other = lax.ppermute(lists, "box", [(0, 1), (1, 0)])
        lists = jnp.where(
            rank == 0, jnp.concatenate([lists, other]), jnp.concatenate([other, lists])
        )
    part = theta_band // shares
    table = lax.dynamic_slice_in_dim(translation, rank * part, part, axis=2)
    table = table.reshape(operator_total, -1)
    total = shares * per_group
    return couplings(lists, jnp.zeros((1,), jnp.int32), table, total, total)


def per_device(
    shares,
    up_weights,
    down_weights,
    coeffs,
    near_blocks,
    near_ids,
    near_count,
    radiation,
    partners,
    vector_ids,
    pair_count,
    translation,
):
    every = ("box", "theta", "phi")
    per_group = lax.axis_size("theta") * lax.axis_size("phi")
    low = shift(coeffs, every, 1)
    spread = upward(coeffs, radiation, up_weights, shares * per_group)
    radiation_adjoint = adjoint(radiation)
    lists = lists_of(partners, vector_ids, pair_count)
    lines = translation_lines(lists, translation, shares, per_group)
    listed = near_slots(near_ids, near_count, lax.axis_index(every))
    spread, radiation_adjoint = lax.optimization_barrier((spread, radiation_adjoint))
    parents = parent_bands(spread, shares)
    lines, listed = lax.optimization_barrier((lines, listed))
    near = near_field(listed, near_blocks, low, 0)
    near, late = lax.optimization_barrier((near, coeffs))
    high = shift(late, every, -1)
    parents, near = lax.optimization_barrier((parents, near))
    sources = [parents]
    if shares < lax.axis_size("box"):
        sources = [shift(parents, "box", 1), parents, shift(parents, "box", -1)]
    incoming = translate(lines, sources)
    incoming, near = lax.optimization_barrier((incoming, near))
    phi, bands, received = staged_bands(incoming, shares)
    near = near_field(listed, near_blocks, coeffs, 1, near)
    ready = near_field(
        listed, near_blocks, high, 2, keep=(near, down_weights, radiation_adjoint)
    )
    return downward(phi, bands, received, *ready)


def solution(mesh):
    box_size, theta_size, phi_size = (mesh.shape[axis] for axis in ("box", "theta", "phi"))
    shares = box_size if box_size <= 2 and TU // theta_size % box_size == 0 else 1
    up_weights, down_weights = operators(shares, theta_size, phi_size)
    in_specs = (
        P(),
        P(),
        P(("box", "theta", "phi"), None, None, None),
        P(("box", "theta", "phi"), None, None, None, None),
        P(("box", "theta", "phi"), None),
        P(("box", "theta", "phi")),
        P(("box", "theta", "phi"), None, None, None),
        P("box", None),
        P("box", None),
        P("box"),
        P(None, None, "theta", "phi"),
    )
    out_specs = P(("box", "theta", "phi"), None, None, None)
    mapped = jax.shard_map(
        functools.partial(per_device, shares),
        mesh=mesh,
        in_specs=in_specs,
        out_specs=out_specs,
        check_vma=False,
    )

    def product(*arrays):
        return mapped(jnp.asarray(up_weights), jnp.asarray(down_weights), *arrays)

    return product
```

```python
import functools
import math

import jax
import jax.numpy as jnp
import ml_dtypes
import numpy as np
from jax import lax
from jax.experimental import pallas as pl
from jax.experimental.pallas import tpu as pltpu
from jax.sharding import PartitionSpec as P

TL = 8
PL = 16
TU = 16
PU = 32

WEIGHT_UP = (-0.0546875, 0.8203125, 0.2734375, -0.0390625)
WEIGHT_DOWN = (-0.0390625, 0.2734375, 0.8203125, -0.0546875)
PHASE_SCALE = 1.3

F32 = jnp.float32
BF16 = jnp.bfloat16
MIB = 2**20
GROUP = 2
NOWHERE = -(2**20)


def lagrange(rows, columns, wrap):
    matrix = np.zeros((rows, columns))
    for row in range(rows):
        weights = WEIGHT_UP if row % 2 else WEIGHT_DOWN
        for order in range(4):
            node = row // 2 + row % 2 - 2 + order
            node = node % columns if wrap else min(max(node, 0), columns - 1)
            matrix[row, node] += weights[order]
    return matrix


def split_weights(matrix):
    high = matrix.astype(ml_dtypes.bfloat16)
    low = (matrix - high.astype(np.float64)).astype(ml_dtypes.bfloat16)
    return high, low


def operators(shares, theta_size, phi_size):
    theta_part = TU // theta_size // shares
    order = np.arange(TU * PU).reshape(theta_size, shares, theta_part, phi_size, PU // phi_size)
    order = order.transpose(1, 0, 3, 2, 4).reshape(-1)
    interp = np.kron(lagrange(TU, TL, False), lagrange(PU, PL, True))
    theta = math.pi * (np.arange(TU) + 0.5) / TU
    azimuth = 2.0 * math.pi * (np.arange(PU) + 0.5) / PU
    up, down = [], []
    for octant in range(4):
        sign_x = 2 * (octant % 2) - 1
        sign_y = 2 * (octant // 2 % 2) - 1
        sign_z = 2 * (octant // 4) - 1
        angle = PHASE_SCALE * (
            sign_x * np.sin(theta)[:, None] * np.cos(azimuth)[None]
            + sign_y * np.sin(theta)[:, None] * np.sin(azimuth)[None]
            + sign_z * np.cos(theta)[:, None]
        ).reshape(-1, 1)
        cos_high, cos_low = split_weights((np.cos(angle) * interp)[order])
        sin_high, sin_low = split_weights((np.sin(angle) * interp)[order])
        high = np.concatenate([cos_high, sin_high], axis=1)
        low = np.concatenate([cos_low, sin_low], axis=1)
        up.append(np.concatenate([high, low], axis=0))
        down += [cos_high.T, sin_high.T]
    down = np.concatenate(down, axis=0)
    down = down.reshape(down.shape[0], shares * theta_size, phi_size, -1).transpose(2, 0, 1, 3)
    return np.concatenate(up, axis=1), down.reshape(phi_size, down.shape[1], -1)


def in_hbm(*arrays):
    return [pltpu.with_memory_space_constraint(array, pltpu.HBM) for array in arrays]


def dot(a, b):
    return jnp.dot(a, b, preferred_element_type=F32)


def side_by_side(real, imag):
    return jnp.concatenate([real, imag], axis=1)


def complex_columns(real, imag):
    return jnp.concatenate([side_by_side(real, imag), side_by_side(-imag, real)], axis=0)


def up_kernel(x_hbm, rad_hbm, w_hbm, out_hbm, x_ref, rad_ref, w_ref, right, result, sems):
    boxes, _, _, rhs = x_ref.shape
    points = rad_ref.shape[2]
    copies = [
        pltpu.make_async_copy(source, target, sems.at[place])
        for place, (source, target) in enumerate(
            ((x_hbm, x_ref), (rad_hbm, rad_ref), (w_hbm, w_ref))
        )
    ]
    for copy in copies:
        copy.start()
    copies[0].wait()
    copies[1].wait()
    half = boxes // 2
    for octant in range(boxes):
        left = side_by_side(rad_ref[octant, 0], rad_ref[octant, 1])
        straight = dot(left, complex_columns(x_ref[octant, 0], x_ref[octant, 1])).astype(BF16)
        real, imag = straight[:, :rhs], straight[:, rhs:]
        if octant < half:
            swapped = side_by_side(-imag, real)
        else:
            swapped = side_by_side(imag, -real)
        place = octant if octant < half else boxes - 1 - octant
        start = 2 * place * points
        right[octant // half, start : start + points] = straight
        right[octant // half, start + points : start + 2 * points] = swapped
    copies[2].wait()
    total = dot(w_ref[...], right[0]) + dot(w_ref[...], right[1])
    samples = total.shape[0] // 2
    total = total[:samples] + total[samples:]
    result[...] = total.astype(BF16).reshape(result.shape)
    pltpu.sync_copy(result, out_hbm)


def upward(coeffs, radiation, weights, groups):
    boxes, _, basis, rhs = coeffs.shape
    rows, columns = weights.shape
    samples = rows // 2
    hbm = pl.BlockSpec(memory_space=pltpu.HBM)
    return pl.pallas_call(
        up_kernel,
        in_specs=[hbm] * 3,
        out_specs=hbm,
        out_shape=pltpu.HBM((groups, samples // groups, 2 * rhs), BF16),
        scratch_shapes=[
            pltpu.VMEM(coeffs.shape, BF16),
            pltpu.VMEM(radiation.shape, BF16),
            pltpu.VMEM(weights.shape, BF16),
            pltpu.VMEM((2, columns, 2 * rhs), BF16),
            pltpu.VMEM((groups, samples // groups, 2 * rhs), BF16),
            pltpu.SemaphoreType.DMA((3,)),
        ],
        compiler_params=pltpu.CompilerParams(vmem_limit_bytes=32 * MIB),
        cost_estimate=pl.CostEstimate(
            flops=2 * 10**9, bytes_accessed=4 * MIB, transcendentals=0
        ),
        name="upward",
    )(*in_hbm(coeffs, radiation, weights))


def coupling_kernel(lists_ref, base_ref, table_ref, out_ref):
    rows = lists_ref.shape[0]
    samples = table_ref.shape[1] // 2
    _, targets, columns = out_ref.shape
    slots = rows // targets
    selector = (
        lax.broadcasted_iota(jnp.int32, (rows, table_ref.shape[0]), 1) == lists_ref[:, 1:2]
    )
    chosen = dot(selector.astype(BF16), table_ref[...]).astype(BF16)
    wide = lax.broadcasted_iota(jnp.int32, (rows, columns), 1) // samples
    match = wide + base_ref[0] == lists_ref[:, 0:1]
    spread = lax.broadcasted_iota(jnp.int32, (samples, columns), 0) == (
        lax.broadcasted_iota(jnp.int32, (samples, columns), 1) % samples
    )
    gather = (
        lax.broadcasted_iota(jnp.int32, (targets, rows), 1) // slots
        == lax.broadcasted_iota(jnp.int32, (targets, rows), 0)
    ).astype(BF16)
    tile = spread.astype(BF16)
    for part in range(2):
        lines = dot(chosen[:, part * samples : (part + 1) * samples], tile)
        out_ref[part] = dot(gather, jnp.where(match, lines, 0.0).astype(BF16))


def couplings(lists, base, table, targets, names):
    shape = (2, targets, names * (table.shape[1] // 2))
    vmem = pl.BlockSpec(memory_space=pltpu.VMEM)
    return pl.pallas_call(
        coupling_kernel,
        in_specs=[vmem, pl.BlockSpec(memory_space=pltpu.SMEM), vmem],
        out_specs=vmem,
        out_shape=jax.ShapeDtypeStruct(shape, F32),
        compiler_params=pltpu.CompilerParams(vmem_limit_bytes=16 * MIB),
        cost_estimate=pl.CostEstimate(
            flops=2 * 10**8, bytes_accessed=2 * 2**20, transcendentals=0
        ),
        name="coupling",
    )(lists, base, table)


def translate_kernel(lines_hbm, *refs):
    count = (len(refs) - 5) // 2
    sources, out_hbm = refs[:count], refs[count]
    held, lines, matrix, result, sems = refs[count + 1 :][:count], *refs[2 * count + 1 :]
    targets, samples, width = result.shape
    rhs = width // 2
    copies = [
        pltpu.make_async_copy(source, target, sems.at[place])
        for place, (source, target) in enumerate(zip((lines_hbm, *sources), (lines, *held)))
    ]
    for copy in copies:
        copy.start()
    copies[0].wait()
    columns = matrix.shape[1]
    row = lax.broadcasted_iota(jnp.int32, (samples, columns), 0)
    diagonal = row == lax.broadcasted_iota(jnp.int32, (samples, columns), 1) % samples
    for part in range(2):
        for target in range(targets):
            line = jnp.broadcast_to(lines[part, target : target + 1], diagonal.shape)
            start = (part * targets + target) * samples
            matrix[start : start + samples] = jnp.where(diagonal, line, 0.0).astype(BF16)
    total = None
    start = 0
    for place, source in enumerate(held):
        copies[1 + place].wait()
        stop = start + source.shape[0] * samples
        part = dot(matrix[:, start:stop], source[...].reshape(stop - start, width))
        total = part if total is None else total + part
        start = stop
    half = targets * samples
    real = total[:half, :rhs] - total[half:, rhs:]
    imag = total[:half, rhs:] + total[half:, :rhs]
    result[...] = jnp.concatenate([real, imag], axis=1).astype(BF16).reshape(result.shape)
    pltpu.sync_copy(result, out_hbm)


def translate(lines, sources):
    _, samples, width = sources[0].shape
    _, targets, columns = lines.shape
    shape = (targets, samples, width)
    hbm = pl.BlockSpec(memory_space=pltpu.HBM)
    anywhere = pl.BlockSpec(memory_space=pl.ANY)
    return pl.pallas_call(
        translate_kernel,
        in_specs=[hbm] + [anywhere] * len(sources),
        out_specs=hbm,
        out_shape=pltpu.HBM(shape, BF16),
        scratch_shapes=[
            *[pltpu.VMEM(source.shape, BF16) for source in sources],
            pltpu.VMEM(lines.shape, F32),
            pltpu.VMEM((2 * targets * samples, columns), BF16),
            pltpu.VMEM(shape, BF16),
            pltpu.SemaphoreType.DMA((1 + len(sources),)),
        ],
        compiler_params=pltpu.CompilerParams(vmem_limit_bytes=24 * MIB),
        cost_estimate=pl.CostEstimate(
            flops=10**9, bytes_accessed=2 * MIB, transcendentals=0
        ),
        name="translate",
    )(*in_hbm(lines), *sources)


def near_kernel(first, begun, kept, *refs):
    refs = list(refs)
    listed, blocks_hbm, held = refs[:3]
    before_hbm = refs[3] if begun else None
    kept_hbm = refs[3 + begun : 3 + begun + kept]
    out_ref = refs[3 + begun + kept]
    kept_refs = refs[4 + begun + kept : 4 + begun + 2 * kept]
    blocks, wide, total_ref, *earlier, sems = refs[4 + begun + 2 * kept :]
    held_back = begun and kept
    boxes, _, basis, rhs = held.shape
    most = blocks_hbm.shape[0]
    starts = [listed[first, most + box] for box in range(boxes + 1)]

    def by_box(source, target, turn):
        return [
            pltpu.make_async_copy(
                source.at[box], target.at[box], sems.at[most + turn * boxes + box]
            )
            for box in range(boxes)
        ]

    before_copies = by_box(before_hbm, earlier[0] if held_back else total_ref, 0) if begun else []
    out_copies = [] if kept else by_box(total_ref, out_ref, 1)
    kept_copies = [
        pltpu.make_async_copy(kept_hbm[place], kept_refs[place], sems.at[most + 2 * boxes + place])
        for place in range(kept)
    ]

    def block_copy(place):
        block = listed[first, place] // boxes
        return pltpu.make_async_copy(blocks_hbm.at[block], blocks.at[place], sems.at[place])

    def fetch(place, carry):
        block_copy(place).start()
        return carry

    lax.fori_loop(0, starts[boxes], fetch, 0)
    for copy in before_copies + kept_copies:
        copy.start()
    for place in range(boxes):
        wide[place] = complex_columns(held[place, 0], held[place, 1])

    def landed(place, carry):
        block_copy(place).wait()
        return carry

    lax.fori_loop(0, starts[boxes], landed, 0)
    if not held_back:
        for copy in before_copies:
            copy.wait()

    def group(box, begin, size):
        left, right = [], []
        for step in range(size):
            place = starts[box] + begin + step
            valid = place < starts[box + 1]
            place = jnp.where(valid, place, 0)
            real, imag = blocks[place, 0], blocks[place, 1]
            real = jnp.where(valid, real, jnp.zeros_like(real))
            imag = jnp.where(valid, imag, jnp.zeros_like(imag))
            left.append(side_by_side(real, imag))
            right.append(wide[jnp.where(valid, listed[first, place] % boxes, 0)])
        return dot(jnp.concatenate(left, axis=1), jnp.concatenate(right, axis=0))

    possible = [(boxes - box, boxes, box + 1)[first] for box in range(boxes)]
    sizes = [min(count, 3 if count < 7 else 4) for count in possible]
    for box in range(boxes):
        part = group(box, 0, sizes[box])
        if begun and not held_back:
            total_ref[box, 0] += part[:, :rhs]
            total_ref[box, 1] += part[:, rhs:]
        else:
            total_ref[box, 0] = part[:, :rhs]
            total_ref[box, 1] = part[:, rhs:]
    for box in range(boxes):

        def more(index, carry, box=box):
            part = group(box, sizes[box] + GROUP * index, GROUP)
            total_ref[box, 0] += part[:, :rhs]
            total_ref[box, 1] += part[:, rhs:]
            return carry

        rest = starts[box + 1] - starts[box] - sizes[box]
        lax.fori_loop(0, (jnp.maximum(rest, 0) + GROUP - 1) // GROUP, more, 0)
        if out_copies:
            out_copies[box].start()
    for copy in out_copies + kept_copies:
        copy.wait()
    if held_back:
        for box in range(boxes):
            before_copies[box].wait()
            total_ref[box] += earlier[0][box]


def near_slots(ids, used, rank):
    boxes, slots = ids.shape
    total = boxes * slots
    source = ids - (rank - 1) * boxes
    source = jnp.where(jnp.arange(slots) < used[:, None], source, -1).reshape(-1)
    wanted = (source >= 0) & (source // boxes == jnp.arange(3)[:, None])
    earlier = jnp.arange(total)[None, :] < jnp.arange(total)[:, None]
    place = jnp.sum((wanted[:, None, :] & earlier).astype(jnp.int32), axis=2)
    code = jnp.arange(total) * boxes + source % boxes
    chosen = wanted[:, None, :] & (place[:, None, :] == jnp.arange(total)[:, None])
    listed = jnp.sum(jnp.where(chosen, code, 0), axis=2)
    before = jnp.arange(total) // slots < jnp.arange(boxes + 1)[:, None]
    starts = jnp.sum((wanted[:, None, :] & before).astype(jnp.int32), axis=2)
    return jnp.concatenate([listed, starts], axis=1).astype(jnp.int32)


def near_field(listed, blocks, source, first, before=None, keep=()):
    boxes, slots, _, basis, _ = blocks.shape
    blocks = blocks.reshape(boxes * slots, *blocks.shape[2:])
    rhs = source.shape[3]
    begun, kept = before is not None, len(keep)
    hbm = pl.BlockSpec(memory_space=pltpu.HBM)
    smem = pl.BlockSpec(memory_space=pltpu.SMEM)
    vmem = pl.BlockSpec(memory_space=pltpu.VMEM)
    shape = (boxes, 2, basis, rhs)
    scratch = [
        pltpu.VMEM(blocks.shape, BF16),
        pltpu.VMEM((boxes, 2 * basis, 2 * rhs), BF16),
        pltpu.VMEM(shape, F32),
        pltpu.SemaphoreType.DMA((boxes * slots + 2 * boxes + kept,)),
    ]
    kernel = functools.partial(near_kernel, first, begun, kept)
    if kept:
        del scratch[2]
        if begun:
            scratch.insert(2, pltpu.VMEM(shape, F32))
        inner = kernel

        def kernel(*refs):
            place, tail = 3 + begun + kept, 1 + begun
            inner(*refs[:-tail], refs[place], *refs[-tail:])

    return pl.pallas_call(
        kernel,
        in_specs=[smem, hbm, vmem] + [hbm] * (begun + kept),
        out_specs=[vmem] * (1 + kept) if kept else hbm,
        out_shape=[
            pltpu.VMEM(shape, F32),
            *[pltpu.VMEM(array.shape, array.dtype) for array in keep],
        ]
        if kept
        else pltpu.HBM(shape, F32),
        scratch_shapes=scratch,
        compiler_params=pltpu.CompilerParams(vmem_limit_bytes=32 * MIB),
        cost_estimate=pl.CostEstimate(
            flops=10**11 if first == 2 else 2 * 10**9, bytes_accessed=8 * MIB, transcendentals=0
        ),
        name=("near_low", "near_own", "near_high")[first],
    )(
        listed,
        *in_hbm(blocks),
        source,
        *in_hbm(*([before] if begun else []), *keep),
    )


def adjoint_kernel(rad_ref, out_hbm, held):
    for box in range(rad_ref.shape[0]):
        held[box] = side_by_side(rad_ref[box, 0].T, rad_ref[box, 1].T)
    pltpu.sync_copy(held, out_hbm)


def adjoint(radiation):
    boxes, _, points, basis = radiation.shape
    return pl.pallas_call(
        adjoint_kernel,
        in_specs=[pl.BlockSpec(memory_space=pltpu.VMEM)],
        out_specs=pl.BlockSpec(memory_space=pltpu.HBM),
        scratch_shapes=[pltpu.VMEM((boxes, basis, 2 * points), BF16)],
        out_shape=pltpu.HBM((boxes, basis, 2 * points), BF16),
        cost_estimate=pl.CostEstimate(
            flops=10**6, bytes_accessed=2 * MIB, transcendentals=0
        ),
        name="adjoint",
    )(radiation)


def down_kernel(phi_ref, near_ref, w_ref, adjoint_ref, *refs):
    pieces, (out_hbm, held, sems) = refs[:-3], refs[-3:]
    boxes, _, width = adjoint_ref.shape
    points = width // 2
    rhs = held.shape[3]
    phi = phi_ref[0]
    phi_size = len(pieces)
    out_copies = [
        pltpu.make_async_copy(held.at[box], out_hbm.at[box], sems.at[box]) for box in range(boxes)
    ]
    places = [lax.rem(phi + distance, phi_size) for distance in range(phi_size)]
    left = jnp.concatenate([w_ref[place] for place in places], axis=1)
    right = jnp.concatenate([piece[...].reshape(-1, 2 * rhs) for piece in pieces], axis=0)
    mixed = dot(left, right)
    for octant in range(boxes // 2):
        start = 2 * octant * points
        cos_part = mixed[start : start + points]
        sin_part = mixed[start + points : start + 2 * points]
        cos_re, cos_im = cos_part[:, :rhs], cos_part[:, rhs:]
        sin_re, sin_im = sin_part[:, :rhs], sin_part[:, rhs:]
        leaves = (
            (octant, cos_re + sin_im, cos_im - sin_re),
            (boxes - 1 - octant, cos_re - sin_im, cos_im + sin_re),
        )
        for box, real, imag in leaves:
            real, imag = real.astype(BF16), imag.astype(BF16)
            right = jnp.concatenate([side_by_side(real, imag), side_by_side(imag, -real)], axis=0)
            far = dot(adjoint_ref[box], right)
            held[box, 0] = near_ref[box, 0] + far[:, :rhs]
            held[box, 1] = near_ref[box, 1] + far[:, rhs:]
            out_copies[box].start()
    for copy in out_copies:
        copy.wait()


def downward(phi, pieces, near, weights, radiation_adjoint):
    boxes = near.shape[0]
    vmem = pl.BlockSpec(memory_space=pltpu.VMEM)
    ready = [
        pltpu.with_memory_space_constraint(array, pltpu.VMEM)
        for array in (near, weights, radiation_adjoint)
    ]
    return pl.pallas_call(
        down_kernel,
        in_specs=[pl.BlockSpec(memory_space=pltpu.SMEM)] + [vmem] * (3 + len(pieces)),
        out_specs=pl.BlockSpec(memory_space=pltpu.HBM),
        out_shape=jax.ShapeDtypeStruct(near.shape, F32),
        scratch_shapes=[
            pltpu.VMEM(near.shape, F32),
            pltpu.SemaphoreType.DMA((boxes,)),
        ],
        compiler_params=pltpu.CompilerParams(vmem_limit_bytes=32 * MIB),
        cost_estimate=pl.CostEstimate(
            flops=2 * 10**9, bytes_accessed=7 * MIB, transcendentals=0
        ),
        name="downward",
    )(phi, *ready, *pieces)


def shift(block, axis, step):
    count = lax.axis_size(axis)
    pairs = [(i, i + step) for i in range(count) if 0 <= i + step < count]
    return lax.ppermute(block, axis, pairs)


def lists_of(partners, vector_ids, pair_count):
    used = jnp.arange(partners.shape[1])[None, :] < pair_count[:, None]
    names = jnp.where(used, partners, NOWHERE)
    return jnp.stack([names, vector_ids], axis=2).reshape(-1, 2)


def parent_bands(spread, shares):
    axes = ("box", "theta", "phi") if shares == lax.axis_size("box") else ("theta", "phi")
    return lax.all_to_all(spread, axes, split_axis=0, concat_axis=0, tiled=True)


def staged_bands(incoming, shares):
    axes = ("box", "theta") if shares == lax.axis_size("box") else ("theta",)
    phi_size = lax.axis_size("phi")
    phi = lax.axis_index("phi")
    bands = incoming.reshape(-1, phi_size, *incoming.shape[1:])
    bands = lax.all_to_all(bands, axes, split_axis=0, concat_axis=0, tiled=True)
    received = []
    for distance in [0, *range(phi_size - 1, 0, -1)]:
        piece = lax.dynamic_index_in_dim(bands, (phi + distance) % phi_size, 1, keepdims=False)
        if distance:
            ring = [(place, (place + distance) % phi_size) for place in range(phi_size)]
            piece = lax.ppermute(piece, "phi", ring)
        received.append(piece)
    return phi.astype(jnp.int32).reshape(1), received


def translation_lines(lists, translation, shares, per_group):
    operator_total, _, theta_band, phi_band = translation.shape
    rank = lax.axis_index("box")
    if shares < lax.axis_size("box"):
        table = translation.reshape(operator_total, -1)
        base = ((rank - 1) * per_group).astype(jnp.int32).reshape(1)
        return couplings(lists, base, table, per_group, 3 * per_group)
    if shares == 2:
        other = lax.ppermute(lists, "box", [(0, 1), (1, 0)])
        lists = jnp.where(
            rank == 0, jnp.concatenate([lists, other]), jnp.concatenate([other, lists])
        )
    part = theta_band // shares
    table = lax.dynamic_slice_in_dim(translation, rank * part, part, axis=2)
    table = table.reshape(operator_total, -1)
    total = shares * per_group
    return couplings(lists, jnp.zeros((1,), jnp.int32), table, total, total)


def per_device(
    shares,
    up_weights,
    down_weights,
    coeffs,
    near_blocks,
    near_ids,
    near_count,
    radiation,
    partners,
    vector_ids,
    pair_count,
    translation,
):
    every = ("box", "theta", "phi")
    per_group = lax.axis_size("theta") * lax.axis_size("phi")
    low = shift(coeffs, every, 1)
    spread = upward(coeffs, radiation, up_weights, shares * per_group)
    radiation_adjoint = adjoint(radiation)
    lists = lists_of(partners, vector_ids, pair_count)
    spread, lists = lax.optimization_barrier((spread, lists))
    lines = translation_lines(lists, translation, shares, per_group)
    listed = near_slots(near_ids, near_count, lax.axis_index(every))
    spread, lines, radiation_adjoint, listed = lax.optimization_barrier(
        (spread, lines, radiation_adjoint, listed)
    )
    parents = parent_bands(spread, shares)
    near = near_field(listed, near_blocks, low, 0)
    near, late = lax.optimization_barrier((near, coeffs))
    high = shift(late, every, -1)
    parents, near = lax.optimization_barrier((parents, near))
    sources = [parents]
    if shares < lax.axis_size("box"):
        sources = [shift(parents, "box", 1), parents, shift(parents, "box", -1)]
    incoming = translate(lines, sources)
    incoming, near = lax.optimization_barrier((incoming, near))
    phi, pieces = staged_bands(incoming, shares)
    near = near_field(listed, near_blocks, coeffs, 1, near)
    ready = near_field(
        listed, near_blocks, high, 2, near, keep=(down_weights, radiation_adjoint)
    )
    return downward(phi, pieces, *ready)


def solution(mesh):
    box_size, theta_size, phi_size = (mesh.shape[axis] for axis in ("box", "theta", "phi"))
    shares = box_size if box_size <= 2 and TU // theta_size % box_size == 0 else 1
    up_weights, down_weights = operators(shares, theta_size, phi_size)
    in_specs = (
        P(),
        P(),
        P(("box", "theta", "phi"), None, None, None),
        P(("box", "theta", "phi"), None, None, None, None),
        P(("box", "theta", "phi"), None),
        P(("box", "theta", "phi")),
        P(("box", "theta", "phi"), None, None, None),
        P("box", None),
        P("box", None),
        P("box"),
        P(None, None, "theta", "phi"),
    )
    out_specs = P(("box", "theta", "phi"), None, None, None)
    mapped = jax.shard_map(
        functools.partial(per_device, shares),
        mesh=mesh,
        in_specs=in_specs,
        out_specs=out_specs,
        check_vma=False,
    )

    def product(*arrays):
        return mapped(jnp.asarray(up_weights), jnp.asarray(down_weights), *arrays)

    return product
```
